256 devices in a mesh: ax: 4 (over z_lo), rad: 8 (over y, core), az: 8 (over x, z_hi).
Axes of the slice: x: 4, y: 4, z: 8 (z_hi: 2, z_lo: 4; z = z_hi * 4 + z_lo), core: 2. Of those that a mesh axis runs over, the one named last changes fastest.
Arguments:
- positions: float32 [3, 4, 8, 131072], P(None, 'ax', 'rad', 'az'), may hold values from 0 to 0.1
- velocity: float32 [3, 4, 8, 131072], P(None, 'ax', 'rad', 'az'), may hold values from -6 to 6
- diameter: float32 [4, 8, 131072], P('ax', 'rad', 'az'), may hold values from 0.02 to 0.1
- cell_index: int32 [4, 8, 131072], P('ax', 'rad', 'az'), may hold values from 0 to 32767
- pair_list: int32 [2, 4, 8, 262144], P(None, 'ax', 'rad', 'az'), may hold values from 0 to 34815, as said below
- live_pairs: int32 [4, 8, 8], P('ax', 'rad', 'az'), may hold values from 8192 to 32768, as said below
- gas_velocity: float32 [3, 32, 128, 2048], P(None, 'ax', 'rad', 'az'), may hold values from -6 to 6
Outputs:
- disturbance: float32 [3, 4, 8, 131072], P(None, 'ax', 'rad', 'az')
- drag_source: float32 [3, 32, 128, 2048], P(None, 'ax', 'rad', 'az')
The draws below stay inside these ranges and needn't reach their ends.
Inputs may be any that keep to these rules, and one draw needn't show every extreme that they name: pair_list[0] is an own droplet, under 16384; a partner on a neighbouring device lies among that device's last 2048 droplets (q from 14336) or first 2048 droplets (q under 2 * 16384 + 2048); an own partner differs from the first droplet. `live_pairs`: slots at and beyond the count are padding and are ignored.
All inputs are finite; a program needn't handle non-finite values.
Results may differ from the reference program's by a relative error of at most 0.0003.
Values sent between devices are 32-bit elements; how exact they have to be, the bound alone decides.
No kernel may reach another device: no remote copies, remote signals or barrier semaphores. Data moves between devices by JAX's collectives and lax.ppermute only.
A program may use at most 128 MiB of HBM per device.

```python
import math
import jax
import jax.numpy as jnp
from jax import lax

CX = 8
CR = 16
CA = 256
NP = 16384
PAIRS = 32768
BAND = 2048
CELLS = 32768
NX = 32
NR = 128
NA = 2048
N_AX = 4
N_RAD = 8
N_AZ = 8


def draw_pair_list(key, part):
    key = jax.random.fold_in(key, 11)
    key_head, key_kind, key_step, key_lower, key_upper = jax.random.split(key, 5)
    grid_shape = (N_AX, N_RAD, N_AZ, PAIRS)
    head_index = jax.random.randint(key_head, grid_shape, 0, NP)
    pair_kind = jax.random.randint(key_kind, grid_shape, 0, 4)
    step_local = jax.random.randint(key_step, grid_shape, 1, NP)
    local_other = NP + (head_index + step_local) % NP
    lower_other = jax.random.randint(key_lower, grid_shape, NP - BAND, NP)
    upper_other = jax.random.randint(key_upper, grid_shape, 2 * NP, 2 * NP + BAND)
    tail_index = jnp.where(pair_kind < 2, local_other, jnp.where(pair_kind == 2, lower_other, upper_other))
    slot_number = jnp.arange(PAIRS)
    tail_index = jnp.where(slot_number == 0, NP - BAND, tail_index)
    tail_index = jnp.where(slot_number == 1, 2 * NP + BAND - 1, tail_index)
    head_index = jnp.where(slot_number == 0, 0, head_index)
    stacked = jnp.stack([head_index, tail_index])
    return stacked.reshape(2, N_AX, N_RAD, N_AZ * PAIRS).astype(jnp.int32)


def draw_live_pairs(key, part):
    key = jax.random.fold_in(key, 7)
    key_count, key_top, key_bottom = jax.random.split(key, 3)
    device_total = N_AX * N_RAD * N_AZ
    counts = jax.random.randint(key_count, (device_total,), PAIRS // 4, PAIRS + 1)
    top_slot = jax.random.randint(key_top, (), 0, device_total)
    bottom_slot = (top_slot + 1 + jax.random.randint(key_bottom, (), 0, device_total - 1)) % device_total
    slot_number = jnp.arange(device_total)
    counts = jnp.where(slot_number == bottom_slot, PAIRS // 4, counts)
    counts = jnp.where(slot_number == top_slot, PAIRS, counts)
    return counts.reshape(N_AX, N_RAD, N_AZ).astype(jnp.int32)


def set_ends(drawn, own_key, least, top_value):
    longest = drawn.shape.index(max(drawn.shape))
    spots = []
    for shift in (0, 1):
        where = [jax.random.randint(jax.random.fold_in(own_key, axis), (), 0, length) for axis, length in enumerate(drawn.shape)]
        where[longest] = (where[longest] + shift) % drawn.shape[longest]
        spots.append(tuple(where))
    return drawn.at[spots[0]].set(least).at[spots[1]].set(top_value)


def steps_of(own_key, dims, cuts, least, top_value):
    loudness, own = 1.0, jax.random.fold_in(own_key, 6)
    for position, blocks in cuts:
        heights = jnp.exp(jax.random.uniform(jax.random.fold_in(own, position), (blocks,), jnp.float32, least / len(cuts), top_value / len(cuts)))
        loudness = loudness * jnp.repeat(heights, dims[position] // blocks).reshape([-1 if axis == position else 1 for axis in range(len(dims))])
    return loudness


def gaussian(key, dims, deviation, most, cuts=(), held_as=jnp.bfloat16):
    drawn = deviation * jax.random.normal(key, dims, jnp.float32)
    if cuts:
        drawn = drawn * steps_of(key, dims, cuts, -0.22, 0.18)
    return jnp.clip(drawn, -most, most).astype(held_as)


def setup_inputs(seed: int = 0) -> dict:
    seeds = jax.random.split(jax.random.key(seed), 8)
    return {
        "positions": jnp.clip(0.1 * jax.random.uniform(seeds[0], (3, N_AX, N_RAD, N_AZ * NP), jnp.float32) ** steps_of(seeds[0], (3, N_AX, N_RAD, N_AZ * NP), ((1, 4), (2, 8), (3, 8)), -0.2, 0.2), 0.0, 0.1),
        "velocity": gaussian(seeds[1], (3, N_AX, N_RAD, N_AZ * NP), 1.0, 6.0, ((1, 4), (2, 8), (3, 8)), jnp.float32),
        "diameter": jnp.clip(jnp.exp(math.log(0.1) - 1.609438 * jax.random.uniform(seeds[2], (N_AX, N_RAD, N_AZ * NP), jnp.float32) ** steps_of(seeds[2], (N_AX, N_RAD, N_AZ * NP), ((0, 4), (1, 8), (2, 8)), -0.2, 0.2)), 0.02, 0.1),
        "cell_index": set_ends(jax.random.randint(seeds[3], (N_AX, N_RAD, N_AZ * NP), 0, CELLS), jax.random.fold_in(seeds[3], 1), 0, CELLS - 1).astype(jnp.int32),
        "pair_list": draw_pair_list(jax.random.fold_in(seeds[7], 71), 0),
        "live_pairs": draw_live_pairs(jax.random.fold_in(seeds[7], 71), 0),
        "gas_velocity": gaussian(seeds[6], (3, NX, NR, NA), 1.0, 6.0, ((1, 4), (2, 8), (3, 8)), jnp.float32),
    }


piep_coef = 1.0
drag_coef = 20.0

def gauss_taps():
    offsets = jnp.arange(-2, 3).astype(jnp.float32)
    raw_taps = jnp.exp(-0.5 * offsets * offsets)
    return raw_taps / jnp.sum(raw_taps)

def reach_weight(radius, squared_gap):
    spread = squared_gap + radius * radius
    return radius * radius * radius / (spread * jnp.sqrt(spread))

def smooth_zero(field, axis_number, kernel_taps):
    out_length = field.shape[axis_number]
    pad_spec = [(0, 0)] * field.ndim
    pad_spec[axis_number] = (2, 2)
    padded = jnp.pad(field, pad_spec)
    total = jnp.zeros_like(field)
    for tap_number in range(5):
        total = total + kernel_taps[tap_number] * lax.slice_in_dim(padded, tap_number, tap_number + out_length, axis=axis_number)
    return total

def smooth_wrap(field, kernel_taps):
    out_length = field.shape[3]
    padded = jnp.concatenate([field[..., -2:], field, field[..., :2]], axis=3)
    total = jnp.zeros_like(field)
    for tap_number in range(5):
        total = total + kernel_taps[tap_number] * lax.slice_in_dim(padded, tap_number, tap_number + out_length, axis=3)
    return total

def pair_slab(slab):
    state_slab, head_slab, tail_slab, live_slab = slab
    shell_slab = jnp.concatenate([jnp.roll(state_slab, 1, axis=2), state_slab, jnp.roll(state_slab, -1, axis=2)], axis=3)
    near_state = jnp.take_along_axis(state_slab, head_slab[None], axis=3)
    far_state = jnp.take_along_axis(shell_slab, tail_slab[None], axis=3)
    separation = far_state[0:3] - near_state[0:3]
    squared_gap = lax.optimization_barrier(jnp.sum(separation * separation, axis=0))
    live_mask = (jnp.arange(PAIRS)[None, None, :] < live_slab[..., None]).astype(jnp.float32)
    weight_far = reach_weight(far_state[6], squared_gap)
    weight_near = reach_weight(near_state[6], squared_gap)
    to_head = piep_coef * (weight_far * live_mask)[None] * far_state[3:6]
    to_tail = piep_coef * (weight_near * live_mask)[None] * near_state[3:6]
    rad_index = jnp.arange(N_RAD)[:, None, None]
    az_index = jnp.arange(N_AZ)[None, :, None]
    accumulated = jnp.zeros((3, N_RAD, N_AZ, 3 * NP), jnp.float32)
    accumulated = accumulated.at[:, rad_index, az_index, head_slab + NP].add(to_head)
    accumulated = accumulated.at[:, rad_index, az_index, tail_slab].add(to_tail)
    correction = accumulated[..., NP:2 * NP]
    correction = correction + jnp.roll(accumulated[..., 2 * NP:], 1, axis=2)
    correction = correction + jnp.roll(accumulated[..., :NP], -1, axis=2)
    return correction

def reference(positions, velocity, diameter, cell_index, pair_list, live_pairs, gas_velocity):
    grid_pos = positions.reshape(3, N_AX, N_RAD, N_AZ, NP)
    grid_vel = velocity.reshape(3, N_AX, N_RAD, N_AZ, NP)
    diam_blocks = diameter.reshape(1, N_AX, N_RAD, N_AZ, NP)
    radius = 0.5 * diam_blocks
    cell_blocks = cell_index.reshape(N_AX, N_RAD, N_AZ, NP)
    gas_blocks = gas_velocity.reshape(3, N_AX, CX, N_RAD, CR, N_AZ, CA).transpose(0, 1, 3, 5, 2, 4, 6).reshape(3, N_AX, N_RAD, N_AZ, CELLS)
    seen_gas = jnp.take_along_axis(gas_blocks, cell_blocks[None], axis=4)
    slip_velocity = seen_gas - grid_vel
    droplet_state = jnp.concatenate([grid_pos, slip_velocity, radius], axis=0)
    pair_blocks = pair_list.reshape(2, N_AX, N_RAD, N_AZ, PAIRS)
    correction = lax.map(pair_slab, (droplet_state.transpose(1, 0, 2, 3, 4), pair_blocks[0], pair_blocks[1], live_pairs))
    correction = correction.transpose(1, 0, 2, 3, 4)
    force = drag_coef * diam_blocks * (slip_velocity + correction)
    ax_index = jnp.arange(N_AX)[:, None, None, None]
    rad_index = jnp.arange(N_RAD)[None, :, None, None]
    az_index = jnp.arange(N_AZ)[None, None, :, None]
    deposit = jnp.zeros((3, N_AX, N_RAD, N_AZ, CELLS), jnp.float32)
    deposit = deposit.at[:, ax_index, rad_index, az_index, cell_blocks].add(-force)
    deposit = deposit.reshape(3, N_AX, N_RAD, N_AZ, CX, CR, CA).transpose(0, 1, 4, 2, 5, 3, 6).reshape(3, NX, NR, NA)
    kernel_taps = gauss_taps()
    smoothed = smooth_zero(deposit, 1, kernel_taps)
    smoothed = smooth_zero(smoothed, 2, kernel_taps)
    smoothed = smooth_wrap(smoothed, kernel_taps)
    disturbance = correction.reshape(3, N_AX, N_RAD, N_AZ * NP)
    return (disturbance, smoothed)
```

```python
import jax
import jax.numpy as jnp
from jax import lax
from jax.experimental import pallas as pl
from jax.experimental.pallas import tpu as pltpu
from jax.sharding import PartitionSpec as P

piep_coef = 1.0
drag_coef = 20.0

LANES = 128
ROWS = 8
BLOCK = 2048
BAND_BLOCKS = 16
GAS_STEP = 5
HEAD_STEP = 6
DEAD = 1 << 29

NT = (((1,), (1,)), ((), ()))
ANY = pl.ANY
VMEM = pltpu.VMEM
SMEM = pltpu.SMEM


def params(megabytes=40):
    return pltpu.CompilerParams(vmem_limit_bytes=megabytes << 20)


def lane_gather(table, index):
    numbers = lax.GatherDimensionNumbers(
        offset_dims=(),
        collapsed_slice_dims=(1,),
        start_index_map=(1,),
        operand_batching_dims=(0,),
        start_indices_batching_dims=(0,),
    )
    return lax.gather(
        table,
        index[..., None],
        numbers,
        slice_sizes=(1, 1),
        mode=lax.GatherScatterMode.PROMISE_IN_BOUNDS,
    )


def sort_network(regs, place, levels):
    sub = lax.broadcasted_iota(jnp.int32, (ROWS, LANES), 0)
    lane = lax.broadcasted_iota(jnp.int32, (ROWS, LANES), 1)
    count = len(regs)

    def bit_fill(bit, v):
        if bit >= levels:
            return 0
        kind, k = place[bit]
        if kind == "v":
            return -((v >> k) & 1)
        return -(((sub if kind == "s" else lane) >> k) & 1)

    flip = [0] * count
    for level in range(1, levels + 1):
        fills = {}
        for v in range(count):
            kind, k = place[level] if level < levels else ("v", 99)
            key = (v >> k) & 1 if kind == "v" else 0
            if key not in fills:
                fills[key] = bit_fill(level, v)
            new = fills[key]
            if isinstance(new, int) and isinstance(flip[v], int):
                if new != flip[v]:
                    regs[v] = ~regs[v]
            else:
                regs[v] = regs[v] ^ (new ^ flip[v])
            flip[v] = new
        for bit in reversed(range(level)):
            kind, k = place[bit]
            step = 1 << k
            if kind == "v":
                for v in range(count):
                    if not v & step:
                        a, b = regs[v], regs[v | step]
                        regs[v], regs[v | step] = jnp.minimum(a, b), jnp.maximum(a, b)
            else:
                axis, size, where = (0, ROWS, sub) if kind == "s" else (1, LANES, lane)
                lower = (where & step) == 0
                for v in range(count):
                    x = regs[v]
                    ahead = pltpu.roll(x, size - step, axis)
                    behind = ahead if 2 * step == size else pltpu.roll(x, step, axis)
                    regs[v] = jnp.where(lower, jnp.minimum(x, ahead), jnp.maximum(x, behind))
    return regs


def split_two(x):
    high = x.astype(jnp.bfloat16).astype(jnp.float32)
    return high, x - high


def split_three(x):
    high, rest = split_two(x)
    mid, low = split_two(rest)
    return high, mid, low


def packed_row(ref, row):
    return jnp.broadcast_to(ref[row : row + 1, :], (16, LANES)).astype(jnp.bfloat16)


def one_hot_rows(low, count, iota16):
    one = jnp.ones((16, LANES), jnp.bfloat16)
    zero = jnp.zeros((16, LANES), jnp.bfloat16)
    return jnp.concatenate(
        [jnp.where(low - float(16 * k) == iota16, one, zero) for k in range(count // 16)], axis=0
    )


def spread_rows(rel, parts, iota16):
    hit = rel == iota16
    zero = jnp.zeros((16, LANES), jnp.bfloat16)
    return jnp.concatenate(
        [jnp.concatenate([jnp.where(hit, p, zero) for p in part], axis=1) for part in parts], axis=0
    )


def row_iota():
    return lax.broadcasted_iota(jnp.int32, (16, LANES), 0).astype(jnp.float32).astype(jnp.bfloat16)


def droplet_kernel(
    cell_ref, gas_ref, pos_ref, vel_ref, diam_ref,
    table_ref, keys_ref, ends_ref,
    gas_rows, flipped, ends_smem, seen, idx, val, sem,
):
    regs = []
    sub = lax.broadcasted_iota(jnp.int32, (ROWS, LANES), 0)
    lane = lax.broadcasted_iota(jnp.int32, (ROWS, LANES), 1)
    for v in range(16):
        own = (v % 2) * 1024 + sub * LANES + lane
        regs.append(cell_ref[v * ROWS : (v + 1) * ROWS, :] * BLOCK + own)
    place = [("l", k) for k in range(7)] + [("s", k) for k in range(3)] + [("v", 0)]
    regs = sort_network(regs, place, 11)
    keys = jnp.concatenate(regs, axis=0)
    keys_ref[...] = keys
    turned = lax.shift_right_logical(keys, 19).T
    flipped[0:8, :] = turned[0:8, :]
    flipped[8:16, :] = turned[120:128, :]
    ends_ref[...] = flipped[...]
    copy = pltpu.make_async_copy(flipped, ends_smem, sem)
    copy.start()
    for r in range(16):
        rows = slice(r * ROWS, (r + 1) * ROWS)
        for c in range(3):
            for half in range(2):
                gas_rows[rows, half * 4 + c, :] = gas_ref[c, rows, half * LANES : (half + 1) * LANES]
    copy.wait()
    iota16 = row_iota()

    def one_block(db, carry):
        group_rows = pl.ds(pl.multiple_of(db * 16, 16), 16)
        group_keys = keys_ref[group_rows, :]
        idx[0] = lax.shift_right_logical(group_keys, 19)
        idx[1] = lax.shift_right_logical(group_keys, 11) & (LANES - 1)
        idx[2] = lax.shift_right_logical(group_keys, 18) & 1
        firsts = [ends_smem[0, db * 16 + g] for g in range(16)]
        trips = jnp.int32(0)
        for g in range(16):
            trips = jnp.maximum(trips, ends_smem[15, db * 16 + g] - firsts[g])
        trips = trips // GAS_STEP + 1

        def one_trip(t, found):
            out = []
            for g in range(16):
                row = jnp.broadcast_to(idx[0, g : g + 1, :], (ROWS, LANES))
                low = jnp.broadcast_to(idx[1, g : g + 1, :], (ROWS, LANES))
                base = jnp.minimum(firsts[g] + t * GAS_STEP, LANES)
                total = found[g]
                for u in range(GAS_STEP):
                    got = lane_gather(gas_rows[base + u], low)
                    total = jnp.where(row == base + u, got, total)
                out.append(total)
            return tuple(out)

        found = lax.fori_loop(
            0, trips, one_trip, tuple(jnp.zeros((ROWS, LANES), jnp.float32) for _ in range(16))
        )
        for g in range(16):
            upper = jnp.broadcast_to(idx[2, g : g + 1, :], (ROWS, LANES)) == 1
            seen[g] = jnp.where(upper, pltpu.roll(found[g], 4, 0), found[g])
        place_in = group_keys & (BLOCK - 1)
        val[0] = lax.shift_right_logical(place_in, 7).astype(jnp.float32)
        val[1] = (place_in & (LANES - 1)).astype(jnp.float32)
        for c in range(3):
            for n, part in enumerate(split_three(seen[:, c, :])):
                val[2 + 3 * c + n] = part
        total = jnp.zeros((48, LANES), jnp.float32)
        for g in range(16):
            rel = packed_row(val.at[0], g)
            hot = one_hot_rows(packed_row(val.at[1], g), LANES, iota16)
            parts = [[packed_row(val.at[2 + 3 * c + n], g) for n in range(3)] for c in range(3)]
            total = total + lax.dot_general(
                spread_rows(rel, parts, iota16),
                jnp.concatenate([hot, hot, hot], axis=1),
                NT,
                preferred_element_type=jnp.float32,
            )
        for c in range(3):
            table_ref[group_rows, c, :] = pos_ref[c, group_rows, :]
            table_ref[group_rows, 3 + c, :] = total[16 * c : 16 * c + 16] - vel_ref[c, group_rows, :]
        table_ref[group_rows, 6, :] = 0.5 * diam_ref[group_rows, :]
        table_ref[group_rows, 7, :] = jnp.zeros((16, LANES), jnp.float32)
        return carry

    lax.fori_loop(0, 8, one_block, 0)


def droplet_states(cells, gas, pos, vel, diam):
    f32, i32 = jnp.float32, jnp.int32
    return pl.pallas_call(
        droplet_kernel,
        name="droplet_states",
        out_shape=(
            jax.ShapeDtypeStruct((128, ROWS, LANES), f32),
            jax.ShapeDtypeStruct((128, LANES), i32),
            jax.ShapeDtypeStruct((16, LANES), i32),
        ),
        scratch_shapes=[
            VMEM((144, ROWS, LANES), f32),
            VMEM((16, LANES), i32),
            SMEM((16, LANES), i32),
            VMEM((16, ROWS, LANES), f32),
            VMEM((3, 16, LANES), i32),
            VMEM((11, 16, LANES), f32),
            pltpu.SemaphoreType.DMA,
        ],
        compiler_params=params(),
    )(cells, gas, pos, vel, diam)


def pair_sort_kernel(live_ref, pairs_ref, keys_ref, ends_ref):
    live = live_ref[0, 0]
    sub = lax.broadcasted_iota(jnp.int32, (ROWS, LANES), 0)
    lane = lax.broadcasted_iota(jnp.int32, (ROWS, LANES), 1)
    regs = []
    for v in range(32):
        rows = slice(v * ROWS, (v + 1) * ROWS)
        slot = v * 1024 + sub * LANES + lane
        head = pairs_ref[0, rows, :]
        tail = pairs_ref[1, rows, :] - 7 * BLOCK
        bucket = lax.shift_right_logical(tail, 11)
        turn = -(bucket & 1) & (8 * BLOCK - 1)
        key = (bucket << 25) | ((head ^ turn) << 11) | (tail & (BLOCK - 1))
        regs.append(jnp.where(slot < live, key, DEAD))
    place = (
        [("v", k) for k in range(4)]
        + [("s", k) for k in range(3)]
        + [("v", 4)]
        + [("l", k) for k in range(7)]
    )
    regs = sort_network(regs, place, 15)
    for half in range(2):
        rows = regs[16 * half : 16 * half + 16]
        keys_ref[half] = jnp.concatenate(rows, axis=0).T
        head_row, tail_row = [], []
        least_head = least_tail = jnp.full((ROWS, LANES), 1 << 20, jnp.int32)
        most_head = most_tail = jnp.full((ROWS, LANES), -1, jnp.int32)
        for key in rows:
            used = key < DEAD
            bucket = lax.shift_right_logical(key, 25)
            head = lax.shift_right_logical(key, 18) & (LANES - 1)
            head = head ^ (-(bucket & 1) & (LANES - 1))
            least_head = jnp.minimum(least_head, jnp.where(used, head, 1 << 20))
            most_head = jnp.maximum(most_head, jnp.where(used, head, -1))
            least_tail = jnp.minimum(least_tail, jnp.where(used, bucket, 1 << 20))
            most_tail = jnp.maximum(most_tail, jnp.where(used, bucket, -1))
        for n, x in enumerate((least_head, most_head, least_tail, most_tail)):
            reduce = jnp.max if n % 2 else jnp.min
            row = 4 * half + n
            ends_ref[row : row + 1, :] = reduce(x, axis=0, keepdims=True)


def pair_sort(live, pairs):
    return pl.pallas_call(
        pair_sort_kernel,
        name="pair_sort",
        out_shape=(
            jax.ShapeDtypeStruct((2, LANES, LANES), jnp.int32),
            jax.ShapeDtypeStruct((ROWS, LANES), jnp.int32),
        ),
        in_specs=[pl.BlockSpec(memory_space=SMEM), pl.BlockSpec(memory_space=VMEM)],
        compiler_params=params(),
    )(live, pairs)


def pair_kernel(
    live_ref, ends_ref, keys_ref, own_ref, before_ref, after_ref,
    corr_ref, lower_ref, upper_ref,
    table, head_sum, tail_sum, near, far, idx, val, sems,
):
    copies = [
        pltpu.make_async_copy(before_ref, table.at[0:16], sems.at[0]),
        pltpu.make_async_copy(own_ref, table.at[16:144], sems.at[1]),
        pltpu.make_async_copy(after_ref, table.at[144:160], sems.at[2]),
    ]
    for copy in copies:
        copy.start()
    head_sum[...] = jnp.zeros_like(head_sum)
    tail_sum[...] = jnp.zeros_like(tail_sum)
    for copy in copies:
        copy.wait()
    iota16 = row_iota()
    live = live_ref[0, 0]

    def one_set(number, carry):
        half = number & 1
        first = pl.multiple_of((number >> 1) * ROWS, ROWS)
        keys = keys_ref[half, pl.ds(first, ROWS), :]
        used = keys < DEAD
        bucket = lax.shift_right_logical(keys, 25)
        odd = bucket & 1
        head = (lax.shift_right_logical(keys, 11) & (8 * BLOCK - 1)) ^ (-odd & (8 * BLOCK - 1))
        head_row = jnp.where(used, lax.shift_right_logical(head, 7), -1)
        head_low = head & (LANES - 1)
        tail_row = jnp.where(used, bucket * 16 + (lax.shift_right_logical(keys, 7) & 15), -1)
        tail_low = keys & (LANES - 1)
        idx[0] = head_row
        idx[1] = head_low
        idx[2] = tail_row
        idx[3] = tail_low
        val[0] = head_row.astype(jnp.float32)
        val[1] = head_low.astype(jnp.float32)
        val[2] = tail_row.astype(jnp.float32)
        val[3] = tail_low.astype(jnp.float32)

        head_first, tail_first = [], []
        head_span = tail_span = jnp.int32(0)
        for g in range(ROWS):
            least = ends_ref[4 * half, first + g]
            head_span = jnp.maximum(head_span, ends_ref[4 * half + 1, first + g] - least + 1)
            head_first.append(jnp.minimum(least, LANES))
            least = ends_ref[4 * half + 2, first + g]
            tail_span = jnp.maximum(tail_span, ends_ref[4 * half + 3, first + g] - least + 1)
            tail_first.append(jnp.minimum(least, 10))

        def head_trip(t, found):
            out = []
            for g in range(ROWS):
                row = jnp.broadcast_to(idx[0, g : g + 1, :], (ROWS, LANES))
                low = jnp.broadcast_to(idx[1, g : g + 1, :], (ROWS, LANES))
                base = jnp.minimum(head_first[g] + t * HEAD_STEP, LANES)
                total = found[g]
                for u in range(HEAD_STEP):
                    got = lane_gather(table[16 + base + u], low)
                    total = jnp.where(row == base + u, got, total)
                out.append(total)
            return tuple(out)

        def tail_trip(t, found):
            out = []
            for g in range(ROWS):
                row = jnp.broadcast_to(idx[2, g : g + 1, :], (ROWS, LANES))
                low = jnp.broadcast_to(idx[3, g : g + 1, :], (ROWS, LANES))
                base = jnp.minimum(tail_first[g] + t, 10) * 16
                total = found[g]
                for u in range(16):
                    got = lane_gather(table[base + u], low)
                    total = jnp.where(row == base + u, got, total)
                out.append(total)
            return tuple(out)

        blank = tuple(jnp.zeros((ROWS, LANES), jnp.float32) for _ in range(ROWS))
        got_near = lax.fori_loop(0, (head_span + HEAD_STEP - 1) // HEAD_STEP, head_trip, blank)
        got_far = lax.fori_loop(0, tail_span, tail_trip, blank)
        for g in range(ROWS):
            near[g] = got_near[g]
            far[g] = got_far[g]
        gap = jnp.zeros((ROWS, LANES), jnp.float32)
        for c in range(3):
            apart = far[:, c, :] - near[:, c, :]
            gap = gap + apart * apart
        far_radius, near_radius = far[:, 6, :], near[:, 6, :]
        far_ratio = far_radius * lax.rsqrt(gap + far_radius * far_radius)
        near_ratio = near_radius * lax.rsqrt(gap + near_radius * near_radius)
        weight_far = jnp.where(used, piep_coef * far_ratio * far_ratio * far_ratio, 0.0)
        weight_near = jnp.where(used, piep_coef * near_ratio * near_ratio * near_ratio, 0.0)
        for c in range(3):
            for n, part in enumerate(split_two(weight_far * far[:, 3 + c, :])):
                val[4 + 2 * c + n] = part
            for n, part in enumerate(split_two(weight_near * near[:, 3 + c, :])):
                val[10 + 2 * c + n] = part

        def add_heads(t, carry):
            for g in range(ROWS):
                base = jnp.minimum(head_first[g] + 16 * t, LANES)
                rel = packed_row(val.at[0], g) - base.astype(jnp.float32).astype(jnp.bfloat16)
                hot = one_hot_rows(packed_row(val.at[1], g), LANES, iota16)
                parts = [[packed_row(val.at[4 + 2 * c + n], g) for n in range(2)] for c in range(3)]
                out = lax.dot_general(
                    spread_rows(rel, parts, iota16),
                    jnp.concatenate([hot, hot], axis=1),
                    NT,
                    preferred_element_type=jnp.float32,
                )
                for c in range(3):
                    head_sum[c, pl.ds(base, 16), :] += out[16 * c : 16 * c + 16]
            return carry

        def add_tails(t, carry):
            for g in range(ROWS):
                base = jnp.minimum(tail_first[g] + t, 10) * 16
                rel = packed_row(val.at[2], g) - base.astype(jnp.float32).astype(jnp.bfloat16)
                hot = one_hot_rows(packed_row(val.at[3], g), LANES, iota16)
                parts = [[packed_row(val.at[10 + 2 * c + n], g) for n in range(2)] for c in range(3)]
                out = lax.dot_general(
                    spread_rows(rel, parts, iota16),
                    jnp.concatenate([hot, hot], axis=1),
                    NT,
                    preferred_element_type=jnp.float32,
                )
                rows = pl.ds(pl.multiple_of(base, 16), 16)
                for c in range(3):
                    tail_sum[c, rows, :] += out[16 * c : 16 * c + 16]
            return carry

        lax.fori_loop(0, (head_span + 15) // 16, add_heads, 0)
        lax.fori_loop(0, tail_span, add_tails, 0)
        return carry

    lax.fori_loop(0, 2 * ((live + 2047) // 2048), one_set, 0)
    corr_ref[...] = head_sum[:, 0:128, :] + tail_sum[:, 16:144, :]
    lower_ref[...] = tail_sum[:, 0:16, :]
    upper_ref[...] = tail_sum[:, 144:160, :]


def pair_forces(live, ends, keys, own, before, after):
    f32, i32 = jnp.float32, jnp.int32
    smem, vmem = pl.BlockSpec(memory_space=SMEM), pl.BlockSpec(memory_space=VMEM)
    hbm = pl.BlockSpec(memory_space=ANY)
    return pl.pallas_call(
        pair_kernel,
        name="pair_forces",
        out_shape=(
            jax.ShapeDtypeStruct((3, 128, LANES), f32),
            jax.ShapeDtypeStruct((3, 16, LANES), f32),
            jax.ShapeDtypeStruct((3, 16, LANES), f32),
        ),
        in_specs=[smem, smem, vmem, hbm, hbm, hbm],
        scratch_shapes=[
            VMEM((176, ROWS, LANES), f32),
            VMEM((3, 144, LANES), f32),
            VMEM((3, 176, LANES), f32),
            VMEM((ROWS, ROWS, LANES), f32),
            VMEM((ROWS, ROWS, LANES), f32),
            VMEM((4, ROWS, LANES), i32),
            VMEM((16, ROWS, LANES), f32),
            pltpu.SemaphoreType.DMA((3,)),
        ],
        compiler_params=params(),
    )(live, ends, keys, own, before, after)


def deposit_kernel(
    ends_ref, keys_ref, table_ref, corr_ref, lower_ref, upper_ref,
    out_ref, total_ref,
    cells, force, got, val,
):
    iota16 = row_iota()
    cells[...] = jnp.zeros_like(cells)
    total_ref[...] = corr_ref[...]
    total_ref[:, 0:16, :] += lower_ref[...]
    total_ref[:, 112:128, :] += upper_ref[...]

    def one_block(db, carry):
        rows = pl.ds(pl.multiple_of(db * 16, 16), 16)
        scale = (-2.0 * drag_coef) * table_ref[rows, 6, :]
        for c in range(3):
            push = scale * (table_ref[rows, 3 + c, :] + total_ref[c, rows, :])
            force[:, c, :] = push[0:8]
            force[:, 4 + c, :] = push[8:16]
        keys = keys_ref[rows, :]
        own = lax.shift_right_logical(keys, 7) & 15
        low = keys & (LANES - 1)
        tables = [force[k] for k in range(ROWS)]
        for g in range(16):
            pick = jnp.broadcast_to(own[g : g + 1, :], (ROWS, LANES))
            at = jnp.broadcast_to(low[g : g + 1, :], (ROWS, LANES))
            inner = pick & 7
            found = jnp.zeros((ROWS, LANES), jnp.float32)
            for k in range(ROWS):
                found = jnp.where(inner == k, lane_gather(tables[k], at), found)
            got[g] = jnp.where(pick >= 8, pltpu.roll(found, 4, 0), found)
        val[0] = lax.shift_right_logical(keys, 19).astype(jnp.float32)
        val[1] = (lax.shift_right_logical(keys, 11) & (2 * LANES - 1)).astype(jnp.float32)
        for c in range(3):
            for n, part in enumerate(split_two(got[:, c, :])):
                val[2 + 2 * c + n] = part
        firsts = [ends_ref[0, db * 16 + g] for g in range(16)]
        span = jnp.int32(0)
        for g in range(16):
            span = jnp.maximum(span, ends_ref[15, db * 16 + g] - firsts[g] + 1)

        def add_cells(t, carry):
            for g in range(16):
                base = jnp.minimum(firsts[g] + 16 * t, LANES)
                rel = packed_row(val.at[0], g) - base.astype(jnp.float32).astype(jnp.bfloat16)
                hot = one_hot_rows(packed_row(val.at[1], g), 2 * LANES, iota16)
                parts = [[packed_row(val.at[2 + 2 * c + n], g) for n in range(2)] for c in range(3)]
                out = lax.dot_general(
                    spread_rows(rel, parts, iota16),
                    jnp.concatenate([hot, hot], axis=1),
                    NT,
                    preferred_element_type=jnp.float32,
                )
                for c in range(3):
                    for half in range(2):
                        part = out[16 * c : 16 * c + 16, half * LANES : (half + 1) * LANES]
                        cells[2 * c + half, pl.ds(base, 16), :] += part
            return carry

        lax.fori_loop(0, (span + 15) // 16, add_cells, 0)
        return carry

    lax.fori_loop(0, 8, one_block, 0)
    for c in range(3):
        for half in range(2):
            out_ref[c, :, half * LANES : (half + 1) * LANES] = cells[2 * c + half, 0:128, :]


def deposits(ends, keys, table, corr, lower, upper):
    f32 = jnp.float32
    smem, vmem = pl.BlockSpec(memory_space=SMEM), pl.BlockSpec(memory_space=VMEM)
    return pl.pallas_call(
        deposit_kernel,
        name="deposits",
        out_shape=(
            jax.ShapeDtypeStruct((3, 128, 2 * LANES), f32),
            jax.ShapeDtypeStruct((3, 128, LANES), f32),
        ),
        in_specs=[smem, vmem, vmem, vmem, vmem, vmem],
        scratch_shapes=[
            VMEM((6, 144, LANES), f32),
            VMEM((ROWS, ROWS, LANES), f32),
            VMEM((16, ROWS, LANES), f32),
            VMEM((8, 16, LANES), f32),
        ],
        compiler_params=params(),
    )(ends, keys, table, corr, lower, upper)


def with_halo(x, sides, width, wrap):
    for axis, dim in sides:
        count, length = (lax.axis_size(axis), x.shape[dim])
        up = [(i, (i + 1) % count) for i in range(count if wrap else count - 1)]
        down = [(j, i) for i, j in up]
        last = lax.slice_in_dim(x, length - width, length, axis=dim)
        leading = lax.slice_in_dim(x, 0, width, axis=dim)
        before = lax.ppermute(last, axis, up)
        after = lax.ppermute(leading, axis, down)
        x = jnp.concatenate([before, x, after], axis=dim)
    return x


def from_behind(x, axis, by):
    count = lax.axis_size(axis)
    return lax.ppermute(x, axis, [(i, (i + by) % count) for i in range(count)])


def gauss_taps():
    offsets = jnp.arange(-2, 3).astype(jnp.float32)
    raw_taps = jnp.exp(-0.5 * offsets * offsets)
    return raw_taps / jnp.sum(raw_taps)


def taps_valid(padded, axis_number, kernel_taps):
    out_length = padded.shape[axis_number] - 4
    total = jnp.zeros(
        padded.shape[:axis_number] + (out_length,) + padded.shape[axis_number + 1 :], jnp.float32
    )
    for tap_number in range(5):
        total = total + kernel_taps[tap_number] * lax.slice_in_dim(
            padded, tap_number, tap_number + out_length, axis=axis_number
        )
    return total


def per_device(positions, velocity, diameter, cell_index, pair_list, live_pairs, gas_velocity):
    live = live_pairs.reshape(1, 1)
    table, cell_keys, cell_ends = droplet_states(
        cell_index.reshape(128, LANES),
        gas_velocity.reshape(3, 128, 2 * LANES),
        positions.reshape(3, 128, LANES),
        velocity.reshape(3, 128, LANES),
        diameter.reshape(128, LANES),
    )
    before = from_behind(table[128 - BAND_BLOCKS :], "az", 1)
    after = from_behind(table[:BAND_BLOCKS], "az", -1)
    pair_keys, pair_ends = pair_sort(live, pair_list.reshape(2, 256, LANES))
    corr, lower, upper = pair_forces(live, pair_ends, pair_keys, table, before, after)
    from_upper = from_behind(lower, "az", -1)
    from_lower = from_behind(upper, "az", 1)
    deposit, correction = deposits(cell_ends, cell_keys, table, corr, from_lower, from_upper)
    deposit = deposit.reshape(gas_velocity.shape)
    kernel_taps = gauss_taps()
    padded = with_halo(deposit, (("ax", 1), ("rad", 2)), 2, False)
    padded = with_halo(padded, (("az", 3),), 2, True)
    smoothed = taps_valid(padded, 1, kernel_taps)
    smoothed = taps_valid(smoothed, 2, kernel_taps)
    smoothed = taps_valid(smoothed, 3, kernel_taps)
    return (correction.reshape(positions.shape), smoothed)


def solution(mesh):
    return jax.shard_map(
        per_device,
        mesh=mesh,
        in_specs=(
            P(None, "ax", "rad", "az"),
            P(None, "ax", "rad", "az"),
            P("ax", "rad", "az"),
            P("ax", "rad", "az"),
            P(None, "ax", "rad", "az"),
            P("ax", "rad", "az"),
            P(None, "ax", "rad", "az"),
        ),
        out_specs=(P(None, "ax", "rad", "az"), P(None, "ax", "rad", "az")),
        check_vma=False,
    )
```

```python
import functools
import math

import jax
import jax.numpy as jnp
from jax import lax
from jax.experimental import pallas as pl
from jax.experimental.pallas import tpu as pltpu
from jax.sharding import PartitionSpec as P

piep_coef = 1.0
drag_coef = 20.0

LANES = 128
ROWS = 8
BLOCK = 2048
BAND_BLOCKS = 16
GAS_STEP = 5
HEAD_STEP = 6
DEAD = 1 << 29

NT = (((1,), (1,)), ((), ()))
ANY = pl.ANY
VMEM = pltpu.VMEM
SMEM = pltpu.SMEM


def params(megabytes=40):
    return pltpu.CompilerParams(vmem_limit_bytes=megabytes << 20)


def lane_gather(table, index):
    numbers = lax.GatherDimensionNumbers(
        offset_dims=(),
        collapsed_slice_dims=(1,),
        start_index_map=(1,),
        operand_batching_dims=(0,),
        start_indices_batching_dims=(0,),
    )
    return lax.gather(
        table,
        index[..., None],
        numbers,
        slice_sizes=(1, 1),
        mode=lax.GatherScatterMode.PROMISE_IN_BOUNDS,
    )


def sort_network(regs, place, levels):
    sub = lax.broadcasted_iota(jnp.int32, (ROWS, LANES), 0)
    lane = lax.broadcasted_iota(jnp.int32, (ROWS, LANES), 1)
    count = len(regs)

    def bit_fill(bit, v):
        if bit >= levels:
            return 0
        kind, k = place[bit]
        if kind == "v":
            return -((v >> k) & 1)
        return -(((sub if kind == "s" else lane) >> k) & 1)

    flip = [0] * count
    for level in range(1, levels + 1):
        fills = {}
        for v in range(count):
            kind, k = place[level] if level < levels else ("v", 99)
            key = (v >> k) & 1 if kind == "v" else 0
            if key not in fills:
                fills[key] = bit_fill(level, v)
            new = fills[key]
            if isinstance(new, int) and isinstance(flip[v], int):
                if new != flip[v]:
                    regs[v] = ~regs[v]
            else:
                regs[v] = regs[v] ^ (new ^ flip[v])
            flip[v] = new
        for bit in reversed(range(level)):
            kind, k = place[bit]
            step = 1 << k
            if kind == "v":
                for v in range(count):
                    if not v & step:
                        a, b = regs[v], regs[v | step]
                        regs[v], regs[v | step] = jnp.minimum(a, b), jnp.maximum(a, b)
            else:
                axis, size, where = (0, ROWS, sub) if kind == "s" else (1, LANES, lane)
                lower = (where & step) == 0
                for v in range(count):
                    x = regs[v]
                    ahead = pltpu.roll(x, size - step, axis)
                    behind = ahead if 2 * step == size else pltpu.roll(x, step, axis)
                    regs[v] = jnp.where(lower, jnp.minimum(x, ahead), jnp.maximum(x, behind))
    return regs


def split_two(x):
    high = x.astype(jnp.bfloat16).astype(jnp.float32)
    return high, x - high


def split_three(x):
    high, rest = split_two(x)
    mid, low = split_two(rest)
    return high, mid, low


def packed_row(ref, row):
    return jnp.broadcast_to(ref[row : row + 1, :], (16, LANES)).astype(jnp.bfloat16)


def one_hot_rows(low, count, iota16):
    one = jnp.ones((16, LANES), jnp.bfloat16)
    zero = jnp.zeros((16, LANES), jnp.bfloat16)
    return jnp.concatenate(
        [jnp.where(low - float(16 * k) == iota16, one, zero) for k in range(count // 16)], axis=0
    )


def spread_add(rel, parts, hot, iota16):
    hit = rel == iota16
    zero = jnp.zeros((16, LANES), jnp.bfloat16)
    rows = jnp.concatenate([jnp.where(hit, p, zero) for part in parts for p in part], axis=0)
    out = lax.dot_general(rows, hot, NT, preferred_element_type=jnp.float32)
    total = out[0:48]
    for s in range(1, len(parts)):
        total = total + out[48 * s : 48 * s + 48]
    return total


def row_iota():
    return lax.broadcasted_iota(jnp.int32, (16, LANES), 0).astype(jnp.float32).astype(jnp.bfloat16)


def droplet_kernel(
    cell_ref, gas_ref, pos_ref, vel_ref, diam_ref,
    table_ref, keys_ref, ends_ref,
    gas_rows, flipped, ends_smem, seen, idx, val, sem,
):
    regs = []
    sub = lax.broadcasted_iota(jnp.int32, (ROWS, LANES), 0)
    lane = lax.broadcasted_iota(jnp.int32, (ROWS, LANES), 1)
    for v in range(16):
        own = (v % 2) * 1024 + sub * LANES + lane
        regs.append(cell_ref[v * ROWS : (v + 1) * ROWS, :] * BLOCK + own)
    place = [("l", k) for k in range(7)] + [("s", k) for k in range(3)] + [("v", 0)]
    regs = sort_network(regs, place, 11)
    keys = jnp.concatenate(regs, axis=0)
    keys_ref[...] = keys
    turned = lax.shift_right_logical(keys, 19).T
    flipped[0:8, :] = turned[0:8, :]
    flipped[8:16, :] = turned[120:128, :]
    ends_ref[...] = flipped[...]
    copy = pltpu.make_async_copy(flipped, ends_smem, sem)
    copy.start()
    for r in range(16):
        rows = slice(r * ROWS, (r + 1) * ROWS)
        for c in range(3):
            for half in range(2):
                gas_rows[rows, half * 4 + c, :] = gas_ref[c, rows, half * LANES : (half + 1) * LANES]
    copy.wait()
    iota16 = row_iota()

    def one_block(db, carry):
        group_rows = pl.ds(pl.multiple_of(db * 16, 16), 16)
        group_keys = keys_ref[group_rows, :]
        idx[0] = lax.shift_right_logical(group_keys, 19)
        idx[1] = lax.shift_right_logical(group_keys, 11) & (LANES - 1)
        idx[2] = lax.shift_right_logical(group_keys, 18) & 1
        firsts = [ends_smem[0, db * 16 + g] for g in range(16)]
        trips = jnp.int32(0)
        for g in range(16):
            trips = jnp.maximum(trips, ends_smem[15, db * 16 + g] - firsts[g])
        trips = trips // GAS_STEP + 1

        def one_trip(t, found):
            out = []
            for g in range(16):
                row = jnp.broadcast_to(idx[0, g : g + 1, :], (ROWS, LANES))
                low = jnp.broadcast_to(idx[1, g : g + 1, :], (ROWS, LANES))
                base = jnp.minimum(firsts[g] + t * GAS_STEP, LANES)
                total = found[g]
                for u in range(GAS_STEP):
                    got = lane_gather(gas_rows[base + u], low)
                    total = jnp.where(row == base + u, got, total)
                out.append(total)
            return tuple(out)

        found = lax.fori_loop(
            0, trips, one_trip, tuple(jnp.zeros((ROWS, LANES), jnp.float32) for _ in range(16))
        )
        for g in range(16):
            upper = jnp.broadcast_to(idx[2, g : g + 1, :], (ROWS, LANES)) == 1
            seen[g] = jnp.where(upper, pltpu.roll(found[g], 4, 0), found[g])
        place_in = group_keys & (BLOCK - 1)
        val[0] = lax.shift_right_logical(place_in, 7).astype(jnp.float32)
        val[1] = (place_in & (LANES - 1)).astype(jnp.float32)
        for c in range(3):
            for n, part in enumerate(split_three(seen[:, c, :])):
                val[2 + 3 * c + n] = part
        total = jnp.zeros((48, LANES), jnp.float32)
        for g in range(16):
            rel = packed_row(val.at[0], g)
            hot = one_hot_rows(packed_row(val.at[1], g), LANES, iota16)
            parts = [[packed_row(val.at[2 + 3 * c + n], g) for c in range(3)] for n in range(3)]
            total = total + spread_add(rel, parts, hot, iota16)
        for c in range(3):
            table_ref[group_rows, c, :] = pos_ref[c, group_rows, :]
            table_ref[group_rows, 3 + c, :] = total[16 * c : 16 * c + 16] - vel_ref[c, group_rows, :]
        table_ref[group_rows, 6, :] = 0.5 * diam_ref[group_rows, :]
        table_ref[group_rows, 7, :] = jnp.zeros((16, LANES), jnp.float32)
        return carry

    lax.fori_loop(0, 8, one_block, 0)


def droplet_states(cells, gas, pos, vel, diam):
    f32, i32 = jnp.float32, jnp.int32
    return pl.pallas_call(
        droplet_kernel,
        name="droplet_states",
        out_shape=(
            jax.ShapeDtypeStruct((128, ROWS, LANES), f32),
            jax.ShapeDtypeStruct((128, LANES), i32),
            jax.ShapeDtypeStruct((16, LANES), i32),
        ),
        scratch_shapes=[
            VMEM((144, ROWS, LANES), f32),
            VMEM((16, LANES), i32),
            SMEM((16, LANES), i32),
            VMEM((16, ROWS, LANES), f32),
            VMEM((3, 16, LANES), i32),
            VMEM((11, 16, LANES), f32),
            pltpu.SemaphoreType.DMA,
        ],
        compiler_params=params(),
    )(cells, gas, pos, vel, diam)


def pair_sort_kernel(live_ref, pairs_ref, keys_ref, ends_ref):
    live = live_ref[0, 0]
    sub = lax.broadcasted_iota(jnp.int32, (ROWS, LANES), 0)
    lane = lax.broadcasted_iota(jnp.int32, (ROWS, LANES), 1)
    regs = []
    for v in range(32):
        rows = slice(v * ROWS, (v + 1) * ROWS)
        slot = v * 1024 + sub * LANES + lane
        head = pairs_ref[0, rows, :]
        tail = pairs_ref[1, rows, :] - 7 * BLOCK
        bucket = lax.shift_right_logical(tail, 11)
        turn = -(bucket & 1) & (8 * BLOCK - 1)
        key = (bucket << 25) | ((head ^ turn) << 11) | (tail & (BLOCK - 1))
        regs.append(jnp.where(slot < live, key, DEAD))
    place = (
        [("v", k) for k in range(4)]
        + [("s", k) for k in range(3)]
        + [("v", 4)]
        + [("l", k) for k in range(7)]
    )
    regs = sort_network(regs, place, 15)
    for half in range(2):
        rows = regs[16 * half : 16 * half + 16]
        keys_ref[half] = jnp.concatenate(rows, axis=0).T
        head_row, tail_row = [], []
        least_head = least_tail = jnp.full((ROWS, LANES), 1 << 20, jnp.int32)
        most_head = most_tail = jnp.full((ROWS, LANES), -1, jnp.int32)
        for key in rows:
            used = key < DEAD
            bucket = lax.shift_right_logical(key, 25)
            head = lax.shift_right_logical(key, 18) & (LANES - 1)
            head = head ^ (-(bucket & 1) & (LANES - 1))
            least_head = jnp.minimum(least_head, jnp.where(used, head, 1 << 20))
            most_head = jnp.maximum(most_head, jnp.where(used, head, -1))
            least_tail = jnp.minimum(least_tail, jnp.where(used, bucket, 1 << 20))
            most_tail = jnp.maximum(most_tail, jnp.where(used, bucket, -1))
        for n, x in enumerate((least_head, most_head, least_tail, most_tail)):
            reduce = jnp.max if n % 2 else jnp.min
            row = 4 * half + n
            ends_ref[row : row + 1, :] = reduce(x, axis=0, keepdims=True)


def pair_sort(live, pairs):
    return pl.pallas_call(
        pair_sort_kernel,
        name="pair_sort",
        out_shape=(
            jax.ShapeDtypeStruct((2, LANES, LANES), jnp.int32),
            jax.ShapeDtypeStruct((ROWS, LANES), jnp.int32),
        ),
        in_specs=[pl.BlockSpec(memory_space=SMEM), pl.BlockSpec(memory_space=VMEM)],
        compiler_params=params(),
    )(live, pairs)


def pair_kernel(
    live_ref, ends_ref, keys_ref, own_ref, before_ref, after_ref,
    corr_ref, lower_ref, upper_ref,
    table, head_sum, tail_sum, near, far, idx, val, sems,
):
    copies = [
        pltpu.make_async_copy(before_ref, table.at[0:16], sems.at[0]),
        pltpu.make_async_copy(own_ref, table.at[16:144], sems.at[1]),
        pltpu.make_async_copy(after_ref, table.at[144:160], sems.at[2]),
    ]
    for copy in copies:
        copy.start()
    head_sum[...] = jnp.zeros_like(head_sum)
    tail_sum[...] = jnp.zeros_like(tail_sum)
    for copy in copies:
        copy.wait()
    iota16 = row_iota()
    live = live_ref[0, 0]

    def one_set(number, carry):
        half = number & 1
        first = pl.multiple_of((number >> 1) * ROWS, ROWS)
        keys = keys_ref[half, pl.ds(first, ROWS), :]
        used = keys < DEAD
        bucket = lax.shift_right_logical(keys, 25)
        odd = bucket & 1
        head = (lax.shift_right_logical(keys, 11) & (8 * BLOCK - 1)) ^ (-odd & (8 * BLOCK - 1))
        head_row = jnp.where(used, lax.shift_right_logical(head, 7), -1)
        head_low = head & (LANES - 1)
        tail_row = jnp.where(used, bucket * 16 + (lax.shift_right_logical(keys, 7) & 15), -1)
        tail_low = keys & (LANES - 1)
        idx[0] = head_row
        idx[1] = head_low
        idx[2] = tail_row
        idx[3] = tail_low
        val[0] = head_row.astype(jnp.float32)
        val[1] = head_low.astype(jnp.float32)
        val[2] = tail_row.astype(jnp.float32)
        val[3] = tail_low.astype(jnp.float32)

        head_first, tail_first = [], []
        head_span = tail_span = jnp.int32(0)
        for g in range(ROWS):
            least = ends_ref[4 * half, first + g]
            head_span = jnp.maximum(head_span, ends_ref[4 * half + 1, first + g] - least + 1)
            head_first.append(jnp.minimum(least, LANES))
            least = ends_ref[4 * half + 2, first + g]
            tail_span = jnp.maximum(tail_span, ends_ref[4 * half + 3, first + g] - least + 1)
            tail_first.append(jnp.minimum(least, 10))

        def head_trip(t, found):
            out = []
            for g in range(ROWS):
                row = jnp.broadcast_to(idx[0, g : g + 1, :], (ROWS, LANES))
                low = jnp.broadcast_to(idx[1, g : g + 1, :], (ROWS, LANES))
                base = jnp.minimum(head_first[g] + t * HEAD_STEP, LANES)
                total = found[g]
                for u in range(HEAD_STEP):
                    got = lane_gather(table[16 + base + u], low)
                    total = jnp.where(row == base + u, got, total)
                out.append(total)
            return tuple(out)

        def tail_trip(t, found):
            out = []
            for g in range(ROWS):
                row = jnp.broadcast_to(idx[2, g : g + 1, :], (ROWS, LANES))
                low = jnp.broadcast_to(idx[3, g : g + 1, :], (ROWS, LANES))
                base = jnp.minimum(tail_first[g] + t, 10) * 16
                total = found[g]
                for u in range(16):
                    got = lane_gather(table[base + u], low)
                    total = jnp.where(row == base + u, got, total)
                out.append(total)
            return tuple(out)

        blank = tuple(jnp.zeros((ROWS, LANES), jnp.float32) for _ in range(ROWS))
        got_near = lax.fori_loop(0, (head_span + HEAD_STEP - 1) // HEAD_STEP, head_trip, blank)
        got_far = lax.fori_loop(0, tail_span, tail_trip, blank)
        for g in range(ROWS):
            near[g] = got_near[g]
            far[g] = got_far[g]
        gap = jnp.zeros((ROWS, LANES), jnp.float32)
        for c in range(3):
            apart = far[:, c, :] - near[:, c, :]
            gap = gap + apart * apart
        far_radius, near_radius = far[:, 6, :], near[:, 6, :]
        far_ratio = far_radius * lax.rsqrt(gap + far_radius * far_radius)
        near_ratio = near_radius * lax.rsqrt(gap + near_radius * near_radius)
        weight_far = jnp.where(used, piep_coef * far_ratio * far_ratio * far_ratio, 0.0)
        weight_near = jnp.where(used, piep_coef * near_ratio * near_ratio * near_ratio, 0.0)
        for c in range(3):
            for n, part in enumerate(split_two(weight_far * far[:, 3 + c, :])):
                val[4 + 2 * c + n] = part
            for n, part in enumerate(split_two(weight_near * near[:, 3 + c, :])):
                val[10 + 2 * c + n] = part

        def add_heads(t, carry):
            for g in range(ROWS):
                base = jnp.minimum(head_first[g] + 16 * t, LANES)
                rel = packed_row(val.at[0], g) - base.astype(jnp.float32).astype(jnp.bfloat16)
                hot = one_hot_rows(packed_row(val.at[1], g), LANES, iota16)
                parts = [[packed_row(val.at[4 + 2 * c + n], g) for c in range(3)] for n in range(2)]
                out = spread_add(rel, parts, hot, iota16)
                for c in range(3):
                    head_sum[c, pl.ds(base, 16), :] += out[16 * c : 16 * c + 16]
            return carry

        def add_tails(t, carry):
            for g in range(ROWS):
                base = jnp.minimum(tail_first[g] + t, 10) * 16
                rel = packed_row(val.at[2], g) - base.astype(jnp.float32).astype(jnp.bfloat16)
                hot = one_hot_rows(packed_row(val.at[3], g), LANES, iota16)
                parts = [[packed_row(val.at[10 + 2 * c + n], g) for c in range(3)] for n in range(2)]
                out = spread_add(rel, parts, hot, iota16)
                rows = pl.ds(pl.multiple_of(base, 16), 16)
                for c in range(3):
                    tail_sum[c, rows, :] += out[16 * c : 16 * c + 16]
            return carry

        lax.fori_loop(0, (head_span + 15) // 16, add_heads, 0)
        lax.fori_loop(0, tail_span, add_tails, 0)
        return carry

    lax.fori_loop(0, 2 * ((live + 2047) // 2048), one_set, 0)
    corr_ref[...] = head_sum[:, 0:128, :] + tail_sum[:, 16:144, :]
    lower_ref[...] = tail_sum[:, 0:16, :]
    upper_ref[...] = tail_sum[:, 144:160, :]


def pair_forces(live, ends, keys, own, before, after):
    f32, i32 = jnp.float32, jnp.int32
    smem, vmem = pl.BlockSpec(memory_space=SMEM), pl.BlockSpec(memory_space=VMEM)
    hbm = pl.BlockSpec(memory_space=ANY)
    return pl.pallas_call(
        pair_kernel,
        name="pair_forces",
        out_shape=(
            jax.ShapeDtypeStruct((3, 128, LANES), f32),
            jax.ShapeDtypeStruct((3, 16, LANES), f32),
            jax.ShapeDtypeStruct((3, 16, LANES), f32),
        ),
        in_specs=[smem, smem, vmem, hbm, hbm, hbm],
        scratch_shapes=[
            VMEM((176, ROWS, LANES), f32),
            VMEM((3, 144, LANES), f32),
            VMEM((3, 176, LANES), f32),
            VMEM((ROWS, ROWS, LANES), f32),
            VMEM((ROWS, ROWS, LANES), f32),
            VMEM((4, ROWS, LANES), i32),
            VMEM((16, ROWS, LANES), f32),
            pltpu.SemaphoreType.DMA((3,)),
        ],
        compiler_params=params(),
    )(live, ends, keys, own, before, after)


def deposit_kernel(
    ends_ref, keys_ref, table_ref, corr_ref, lower_ref, upper_ref,
    out_ref, total_ref, first_ref, last_ref,
    cells, force, got, val,
):
    iota16 = row_iota()
    cells[...] = jnp.zeros_like(cells)
    total_ref[...] = corr_ref[...]
    total_ref[:, 0:16, :] += lower_ref[...]
    total_ref[:, 112:128, :] += upper_ref[...]

    def one_block(db, carry):
        rows = pl.ds(pl.multiple_of(db * 16, 16), 16)
        scale = (-2.0 * drag_coef) * table_ref[rows, 6, :]
        for c in range(3):
            push = scale * (table_ref[rows, 3 + c, :] + total_ref[c, rows, :])
            force[:, c, :] = push[0:8]
            force[:, 4 + c, :] = push[8:16]
        keys = keys_ref[rows, :]
        own = lax.shift_right_logical(keys, 7) & 15
        low = keys & (LANES - 1)
        tables = [force[k] for k in range(ROWS)]
        for g in range(16):
            pick = jnp.broadcast_to(own[g : g + 1, :], (ROWS, LANES))
            at = jnp.broadcast_to(low[g : g + 1, :], (ROWS, LANES))
            inner = pick & 7
            found = jnp.zeros((ROWS, LANES), jnp.float32)
            for k in range(ROWS):
                found = jnp.where(inner == k, lane_gather(tables[k], at), found)
            got[g] = jnp.where(pick >= 8, pltpu.roll(found, 4, 0), found)
        val[0] = lax.shift_right_logical(keys, 19).astype(jnp.float32)
        val[1] = (lax.shift_right_logical(keys, 11) & (2 * LANES - 1)).astype(jnp.float32)
        for c in range(3):
            for n, part in enumerate(split_two(got[:, c, :])):
                val[2 + 2 * c + n] = part
        firsts = [ends_ref[0, db * 16 + g] for g in range(16)]
        span = jnp.int32(0)
        for g in range(16):
            span = jnp.maximum(span, ends_ref[15, db * 16 + g] - firsts[g] + 1)

        def add_cells(t, carry):
            for g in range(16):
                base = jnp.minimum(firsts[g] + 16 * t, LANES)
                rel = packed_row(val.at[0], g) - base.astype(jnp.float32).astype(jnp.bfloat16)
                hot = one_hot_rows(packed_row(val.at[1], g), 2 * LANES, iota16)
                parts = [[packed_row(val.at[2 + 2 * c + n], g) for c in range(3)] for n in range(2)]
                out = spread_add(rel, parts, hot, iota16)
                for c in range(3):
                    for half in range(2):
                        part = out[16 * c : 16 * c + 16, half * LANES : (half + 1) * LANES]
                        cells[2 * c + half, pl.ds(base, 16), :] += part
            return carry

        lax.fori_loop(0, (span + 15) // 16, add_cells, 0)
        return carry

    lax.fori_loop(0, 8, one_block, 0)
    for c in range(3):
        for half in range(2):
            columns = slice(half * LANES, (half + 1) * LANES)
            out_ref[c, :, columns] = cells[2 * c + half, 0:128, :]
            first_ref[c, :, columns] = cells[2 * c + half, 0:32, :]
            last_ref[c, :, columns] = cells[2 * c + half, 96:128, :]


def deposits(ends, keys, table, corr, lower, upper):
    f32 = jnp.float32
    smem, vmem = pl.BlockSpec(memory_space=SMEM), pl.BlockSpec(memory_space=VMEM)
    return pl.pallas_call(
        deposit_kernel,
        name="deposits",
        out_shape=(
            jax.ShapeDtypeStruct((3, 128, 2 * LANES), f32),
            jax.ShapeDtypeStruct((3, 128, LANES), f32),
            jax.ShapeDtypeStruct((3, 32, 2 * LANES), f32),
            jax.ShapeDtypeStruct((3, 32, 2 * LANES), f32),
        ),
        in_specs=[smem, vmem, vmem, vmem, vmem, vmem],
        scratch_shapes=[
            VMEM((6, 144, LANES), f32),
            VMEM((ROWS, ROWS, LANES), f32),
            VMEM((16, ROWS, LANES), f32),
            VMEM((8, 16, LANES), f32),
        ],
        compiler_params=params(),
    )(ends, keys, table, corr, lower, upper)


def axial_kernel(taps, cells_ref, before_ref, after_ref, out_ref, first_ref, last_ref):
    for c in range(3):
        padded = jnp.concatenate([before_ref[c], cells_ref[c], after_ref[c]], axis=0)
        total = taps[0] * padded[0:128]
        for k in range(1, 5):
            total = total + taps[k] * padded[16 * k : 16 * k + 128]
        out_ref[c] = total
        for a in range(8):
            first_ref[c, 2 * a : 2 * a + 2, :] = total[16 * a : 16 * a + 2]
            last_ref[c, 2 * a : 2 * a + 2, :] = total[16 * a + 14 : 16 * a + 16]


def radial_kernel(taps, cells_ref, before_ref, after_ref, out_ref, first_ref, last_ref, padded):
    lane = lax.broadcasted_iota(jnp.int32, (LANES, LANES), 1)
    edges = jnp.zeros((LANES, LANES), jnp.float32)
    for c in range(3):
        for a in range(8):
            padded[0:2, :] = before_ref[c, 2 * a : 2 * a + 2, :]
            padded[2:18, :] = cells_ref[c, 16 * a : 16 * a + 16, :]
            padded[18:20, :] = after_ref[c, 2 * a : 2 * a + 2, :]
            total = taps[0] * padded[0:16, :]
            for k in range(1, 5):
                total = total + taps[k] * padded[k : k + 16, :]
            out_ref[c, 16 * a : 16 * a + 16, :] = total
        left, right = out_ref[c, :, 0:LANES], out_ref[c, :, LANES:]
        if c:
            left = pltpu.roll(left, 2 * c, 1)
        right = pltpu.roll(right, 10 + 2 * c, 1)
        edges = jnp.where((lane >> 1) == c, left, edges)
        edges = jnp.where((lane >> 1) == 4 + c, right, edges)
    turned = edges.T
    first_ref[...] = turned[0:8]
    last_ref[...] = turned[8:16]


def azimuthal_kernel(taps, cells_ref, before_ref, after_ref, out_ref):
    lane = lax.broadcasted_iota(jnp.int32, (LANES, LANES), 1)
    rest = jnp.zeros((LANES - 16, LANES), jnp.float32)
    edges = jnp.concatenate([after_ref[...], before_ref[...], rest], axis=0).T
    for c in range(3):
        ahead = pltpu.roll(edges, LANES - 2 * c, 1) if c else edges
        halo = jnp.where(lane < 64, ahead, pltpu.roll(edges, 118 - 2 * c, 1))
        left, right = cells_ref[c, :, 0:LANES], cells_ref[c, :, LANES:]
        out_left, out_right = taps[2] * left, taps[2] * right
        for k in (1, 2):
            tap = taps[2 + k]
            inner = lane < LANES - k
            x, y, z = (pltpu.roll(v, LANES - k, 1) for v in (left, right, halo))
            out_left = out_left + tap * jnp.where(inner, x, y)
            out_right = out_right + tap * jnp.where(inner, y, z)
            inner = lane >= k
            x, y, z = (pltpu.roll(v, k, 1) for v in (left, right, halo))
            out_left = out_left + tap * jnp.where(inner, x, z)
            out_right = out_right + tap * jnp.where(inner, y, x)
        out_ref[c, :, 0:LANES] = out_left
        out_ref[c, :, LANES:] = out_right


def filtered(deposit, first, last):
    f32 = jnp.float32
    raw = [math.exp(-0.5 * k * k) for k in range(-2, 3)]
    taps = [x / sum(raw) for x in raw]
    whole = jax.ShapeDtypeStruct(deposit.shape, f32)
    radial_face = jax.ShapeDtypeStruct((3, 16, 2 * LANES), f32)
    edge = jax.ShapeDtypeStruct((8, LANES), f32)
    cells, first, last = pl.pallas_call(
        functools.partial(axial_kernel, taps),
        name="axial_filter",
        out_shape=(whole, radial_face, radial_face),
        compiler_params=params(),
    )(deposit, shifted(last, "ax", 1, False), shifted(first, "ax", -1, False))
    cells, first, last = pl.pallas_call(
        functools.partial(radial_kernel, taps),
        name="radial_filter",
        out_shape=(whole, edge, edge),
        scratch_shapes=[VMEM((24, 2 * LANES), f32)],
        compiler_params=params(),
    )(cells, shifted(last, "rad", 1, False), shifted(first, "rad", -1, False))
    return pl.pallas_call(
        functools.partial(azimuthal_kernel, taps),
        name="azimuthal_filter",
        out_shape=whole,
        compiler_params=params(),
    )(cells, shifted(last, "az", 1, True), shifted(first, "az", -1, True))


def shifted(x, axis, by, wrap):
    count = lax.axis_size(axis)
    pairs = [(i, (i + by) % count) for i in range(count)]
    return lax.ppermute(x, axis, [p for p in pairs if wrap or p[1] - p[0] == by])


def per_device(positions, velocity, diameter, cell_index, pair_list, live_pairs, gas_velocity):
    live = live_pairs.reshape(1, 1)
    table, cell_keys, cell_ends = droplet_states(
        cell_index.reshape(128, LANES),
        gas_velocity.reshape(3, 128, 2 * LANES),
        positions.reshape(3, 128, LANES),
        velocity.reshape(3, 128, LANES),
        diameter.reshape(128, LANES),
    )
    before = shifted(table[128 - BAND_BLOCKS :], "az", 1, True)
    after = shifted(table[:BAND_BLOCKS], "az", -1, True)
    pair_keys, pair_ends = pair_sort(live, pair_list.reshape(2, 256, LANES))
    corr, lower, upper = pair_forces(live, pair_ends, pair_keys, table, before, after)
    from_upper = shifted(lower, "az", -1, True)
    from_lower = shifted(upper, "az", 1, True)
    deposit, correction, first, last = deposits(
        cell_ends, cell_keys, table, corr, from_lower, from_upper
    )
    smoothed = filtered(deposit, first, last)
    return (correction.reshape(positions.shape), smoothed.reshape(gas_velocity.shape))


def solution(mesh):
    return jax.shard_map(
        per_device,
        mesh=mesh,
        in_specs=(
            P(None, "ax", "rad", "az"),
            P(None, "ax", "rad", "az"),
            P("ax", "rad", "az"),
            P("ax", "rad", "az"),
            P(None, "ax", "rad", "az"),
            P("ax", "rad", "az"),
            P(None, "ax", "rad", "az"),
        ),
        out_specs=(P(None, "ax", "rad", "az"), P(None, "ax", "rad", "az")),
        check_vma=False,
    )
```

```python
import functools
import math

import jax
import jax.numpy as jnp
from jax import lax
from jax.experimental import pallas as pl
from jax.experimental.pallas import tpu as pltpu
from jax.sharding import PartitionSpec as P

piep_coef = 1.0
drag_coef = 20.0

LANES = 128
ROWS = 8
BLOCK = 2048
GAS_WINDOW = 10
HEAD_WINDOW = 10
DEAD = 1 << 29

NT = (((1,), (1,)), ((), ()))
ANY = pl.ANY
VMEM = pltpu.VMEM
SMEM = pltpu.SMEM


def params(megabytes=40):
    return pltpu.CompilerParams(vmem_limit_bytes=megabytes << 20)


def lane_gather(table, index):
    numbers = lax.GatherDimensionNumbers(
        offset_dims=(),
        collapsed_slice_dims=(1,),
        start_index_map=(1,),
        operand_batching_dims=(0,),
        start_indices_batching_dims=(0,),
    )
    return lax.gather(
        table,
        index[..., None],
        numbers,
        slice_sizes=(1, 1),
        mode=lax.GatherScatterMode.PROMISE_IN_BOUNDS,
    )


def sort_network(regs, place, levels):
    sub = lax.broadcasted_iota(jnp.int32, (ROWS, LANES), 0)
    lane = lax.broadcasted_iota(jnp.int32, (ROWS, LANES), 1)
    count = len(regs)

    def bit_fill(bit, v):
        if bit >= levels:
            return 0
        kind, k = place[bit]
        if kind == "v":
            return -((v >> k) & 1)
        return -(((sub if kind == "s" else lane) >> k) & 1)

    flip = [0] * count
    for level in range(1, levels + 1):
        fills = {}
        for v in range(count):
            kind, k = place[level] if level < levels else ("v", 99)
            key = (v >> k) & 1 if kind == "v" else 0
            if key not in fills:
                fills[key] = bit_fill(level, v)
            new = fills[key]
            if isinstance(new, int) and isinstance(flip[v], int):
                if new != flip[v]:
                    regs[v] = ~regs[v]
            else:
                regs[v] = regs[v] ^ (new ^ flip[v])
            flip[v] = new
        for bit in reversed(range(level)):
            kind, k = place[bit]
            step = 1 << k
            if kind == "v":
                for v in range(count):
                    if not v & step:
                        a, b = regs[v], regs[v | step]
                        regs[v], regs[v | step] = jnp.minimum(a, b), jnp.maximum(a, b)
            else:
                axis, size, where = (0, ROWS, sub) if kind == "s" else (1, LANES, lane)
                lower = (where & step) == 0
                for v in range(count):
                    x = regs[v]
                    ahead = pltpu.roll(x, size - step, axis)
                    behind = ahead if 2 * step == size else pltpu.roll(x, step, axis)
                    regs[v] = jnp.where(lower, jnp.minimum(x, ahead), jnp.maximum(x, behind))
    return regs


def split_two(x):
    high = x.astype(jnp.bfloat16).astype(jnp.float32)
    return high, x - high


def split_three(x):
    high, rest = split_two(x)
    mid, low = split_two(rest)
    return high, mid, low


def packed_row(ref, row):
    return jnp.broadcast_to(ref[row : row + 1, :], (16, LANES)).astype(jnp.bfloat16)


def one_hot_rows(low, count, iota16):
    one = jnp.ones((16, LANES), jnp.bfloat16)
    zero = jnp.zeros((16, LANES), jnp.bfloat16)
    return jnp.concatenate(
        [jnp.where(low - float(16 * k) == iota16, one, zero) for k in range(count // 16)], axis=0
    )


def spread_add(rel, parts, hot, iota16):
    hit = rel == iota16
    zero = jnp.zeros((16, LANES), jnp.bfloat16)
    rows = jnp.concatenate([jnp.where(hit, p, zero) for part in parts for p in part], axis=0)
    out = lax.dot_general(rows, hot, NT, preferred_element_type=jnp.float32)
    total = out[0:48]
    for s in range(1, len(parts)):
        total = total + out[48 * s : 48 * s + 48]
    return total


def row_iota():
    return lax.broadcasted_iota(jnp.int32, (16, LANES), 0).astype(jnp.float32).astype(jnp.bfloat16)


def rows_of(block):
    start = block * 16
    return pl.ds(start if isinstance(block, int) else pl.multiple_of(start, 16), 16)


def wide(ref, *at):
    return jnp.broadcast_to(ref[at[:-1] + (slice(at[-1], at[-1] + 1),)], (ROWS, LANES))


def window(table, first, count, row, low, found):
    for u in range(count):
        found = jnp.where(row == first + u, lane_gather(table[first + u], low), found)
    return found


def running_max(x, count):
    x = jnp.broadcast_to(x, (ROWS, LANES))
    step = 1
    while step < count:
        x = jnp.maximum(x, pltpu.roll(x, LANES - step, 1))
        step *= 2
    return x


def fill_gas_rows(gas_ref, gas_rows):
    for r in range(16):
        rows = slice(r * ROWS, (r + 1) * ROWS)
        for c in range(3):
            for half in range(2):
                gas_rows[rows, half * 4 + c, :] = gas_ref[c, rows, half * LANES : (half + 1) * LANES]


def gas_index(block, keys_ref, slot):
    idx = slot[0]
    keys = keys_ref[rows_of(block), :]
    idx[0] = lax.shift_right_logical(keys, 19)
    idx[1] = lax.shift_right_logical(keys, 11) & (LANES - 1)


def gas_gather(block, g, ends, gas_rows, slot):
    idx, found = slot[0], slot[1]
    zero = jnp.zeros((ROWS, LANES), jnp.float32)
    first = ends[0, block * 16 + g]
    found[g] = window(gas_rows, first, GAS_WINDOW, wide(idx, 0, g), wide(idx, 1, g), zero)


def gas_rest(block, ends, gas_rows, slot):
    idx, found = slot[0], slot[1]

    @pl.when(ends[16, block * 16] >= GAS_WINDOW)
    def _():
        def one(g, carry):
            first = ends[0, block * 16 + g]
            row = jnp.broadcast_to(idx[0, pl.ds(g, 1), :], (ROWS, LANES))
            low = jnp.broadcast_to(idx[1, pl.ds(g, 1), :], (ROWS, LANES))

            def trip(t, total):
                base = jnp.minimum(first + GAS_WINDOW * t, LANES)
                return window(gas_rows, base, GAS_WINDOW, row, low, total)

            trips = (ends[15, block * 16 + g] - first) // GAS_WINDOW + 1
            found[g] = lax.fori_loop(1, trips, trip, found[g])
            return carry

        lax.fori_loop(0, 16, one, 0)


def seen_values(block, keys_ref, slot):
    idx, found, val = slot
    keys = keys_ref[rows_of(block), :]
    upper = (keys & (1 << 18)) != 0
    place_in = keys & (BLOCK - 1)
    val[0] = lax.shift_right_logical(place_in, 7).astype(jnp.float32)
    val[1] = (place_in & (LANES - 1)).astype(jnp.float32)
    for c in range(3):
        seen = jnp.where(upper, found[:, 4 + c, :], found[:, c, :])
        for n, part in enumerate(split_three(seen)):
            val[2 + 3 * c + n] = part


def seen_in_order(g, slot, iota16):
    val = slot[2]
    rel = packed_row(val.at[0], g)
    hot = one_hot_rows(packed_row(val.at[1], g), LANES, iota16)
    parts = [[packed_row(val.at[2 + 3 * c + n], g) for c in range(3)] for n in range(3)]
    return spread_add(rel, parts, hot, iota16)


def write_states(block, total, pos_ref, vel_ref, diam_ref, out_ref, out_rows):
    rows = rows_of(block)
    for c in range(3):
        out_ref[out_rows, c, :] = pos_ref[c, rows, :]
        out_ref[out_rows, 3 + c, :] = total[16 * c : 16 * c + 16] - vel_ref[c, rows, :]
    out_ref[out_rows, 6, :] = 0.5 * diam_ref[rows, :]
    out_ref[out_rows, 7, :] = jnp.zeros((16, LANES), jnp.float32)


def states_step(gather, scatter, keys_ref, ends, gas_rows, iota16, arrays):
    total = jnp.zeros((48, LANES), jnp.float32)
    if gather:
        gas_index(gather[0], keys_ref, gather[1])
    if scatter:
        seen_values(scatter[0], keys_ref, scatter[1])
    for g in range(16):
        if gather:
            gas_gather(gather[0], g, ends, gas_rows, gather[1])
        if scatter:
            total = total + seen_in_order(g, scatter[1], iota16)
    if scatter:
        write_states(scatter[0], total, *arrays, *scatter[2:])
    if gather:
        gas_rest(gather[0], ends, gas_rows, gather[1])


def edge_states_kernel(
    cell_hbm, gas_hbm, pos_hbm, vel_hbm, diam_hbm,
    keys_ref, ends_ref, first_ref, last_ref,
    cell_ref, gas_ref, pos_ref, vel_ref, diam_ref,
    gas_rows, ends, idx_a, found_a, val_a, idx_b, found_b, val_b, sems,
):
    sources = (cell_hbm, gas_hbm, pos_hbm, vel_hbm, diam_hbm)
    places = (cell_ref, gas_ref, pos_ref, vel_ref, diam_ref)
    copies = [
        pltpu.make_async_copy(x, y, sems.at[n]) for n, (x, y) in enumerate(zip(sources, places))
    ]
    for copy in copies:
        copy.start()
    copies[0].wait()
    sub = lax.broadcasted_iota(jnp.int32, (ROWS, LANES), 0)
    lane = lax.broadcasted_iota(jnp.int32, (ROWS, LANES), 1)
    regs = []
    for v in range(16):
        own = (v % 2) * 1024 + sub * LANES + lane
        regs.append(cell_ref[v * ROWS : (v + 1) * ROWS, :] * BLOCK + own)
    place = [("l", k) for k in range(7)] + [("s", k) for k in range(3)] + [("v", 0)]
    regs = sort_network(regs, place, 11)
    keys = jnp.concatenate(regs, axis=0)
    keys_ref[...] = keys
    turned = lax.shift_right_logical(keys, 19).T
    ends_ref[0:8, :] = turned[0:8]
    ends_ref[8:16, :] = turned[120:128]
    ends_ref[16:24, :] = running_max(turned[127:128] - turned[0:1], 16)
    copy = pltpu.make_async_copy(ends_ref, ends, sems.at[5])
    copy.start()
    copies[1].wait()
    fill_gas_rows(gas_ref, gas_rows)
    for other in copies[2:]:
        other.wait()
    copy.wait()
    iota16 = row_iota()
    a, b = (idx_a, found_a, val_a), (idx_b, found_b, val_b)
    whole = slice(0, 16)
    step = functools.partial(
        states_step, keys_ref=keys_ref, ends=ends, gas_rows=gas_rows, iota16=iota16,
        arrays=(pos_ref, vel_ref, diam_ref),
    )
    step((0, a), None)
    step((7, b), (0, a, first_ref, whole))
    step(None, (7, b, last_ref, whole))


def slots(rows, parts, dtype=jnp.float32):
    one = [VMEM((2, 16, LANES), jnp.int32), VMEM((16, ROWS, LANES), dtype), VMEM((parts, rows, LANES), dtype)]
    return one + one


def edge_states(cells, gas, pos, vel, diam):
    f32, i32 = jnp.float32, jnp.int32
    arrays = (cells, gas, pos, vel, diam)
    return pl.pallas_call(
        edge_states_kernel,
        name="edge_states",
        out_shape=(
            jax.ShapeDtypeStruct((128, LANES), i32),
            jax.ShapeDtypeStruct((24, LANES), i32),
            jax.ShapeDtypeStruct((16, ROWS, LANES), f32),
            jax.ShapeDtypeStruct((16, ROWS, LANES), f32),
        ),
        in_specs=[pl.BlockSpec(memory_space=pltpu.HBM)] * 5,
        scratch_shapes=[VMEM(x.shape, x.dtype) for x in arrays]
        + [VMEM((144, ROWS, LANES), f32), SMEM((24, LANES), i32)]
        + slots(16, 11)
        + [pltpu.SemaphoreType.DMA((6,))],
        compiler_params=params(),
    )(*arrays)


def inner_states_kernel(
    ends, keys_ref, gas_ref, pos_ref, vel_ref, diam_ref, first_ref, last_ref,
    table_ref,
    gas_rows, idx_a, found_a, val_a, idx_b, found_b, val_b,
):
    fill_gas_rows(gas_ref, gas_rows)
    iota16 = row_iota()
    a, b = (idx_a, found_a, val_a), (idx_b, found_b, val_b)
    step = functools.partial(
        states_step, keys_ref=keys_ref, ends=ends, gas_rows=gas_rows, iota16=iota16,
        arrays=(pos_ref, vel_ref, diam_ref),
    )
    table_ref[0:16] = first_ref[...]
    table_ref[112:128] = last_ref[...]
    step((1, a), None)

    def two(k, carry):
        block = 2 * k + 1
        step((block + 1, b), (block, a, table_ref, rows_of(block)))
        step((jnp.minimum(block + 2, 6), a), (block + 1, b, table_ref, rows_of(block + 1)))
        return carry

    lax.fori_loop(0, 3, two, 0)


def inner_states(ends, keys, gas, pos, vel, diam, first, last):
    f32 = jnp.float32
    return pl.pallas_call(
        inner_states_kernel,
        name="inner_states",
        out_shape=jax.ShapeDtypeStruct((128, ROWS, LANES), f32),
        in_specs=[pl.BlockSpec(memory_space=SMEM)] + [pl.BlockSpec(memory_space=VMEM)] * 7,
        scratch_shapes=[VMEM((144, ROWS, LANES), f32)] + slots(16, 11),
        compiler_params=params(),
    )(ends, keys, gas, pos, vel, diam, first, last)


def pair_sort_kernel(live_ref, pairs_ref, keys_ref, ends_ref):
    live = live_ref[0, 0]
    sub = lax.broadcasted_iota(jnp.int32, (ROWS, LANES), 0)
    lane = lax.broadcasted_iota(jnp.int32, (ROWS, LANES), 1)
    regs = []
    for v in range(32):
        rows = slice(v * ROWS, (v + 1) * ROWS)
        slot = v * 1024 + sub * LANES + lane
        head = pairs_ref[0, rows, :]
        tail = pairs_ref[1, rows, :] - 7 * BLOCK
        bucket = lax.shift_right_logical(tail, 11)
        turn = -(bucket & 1) & (8 * BLOCK - 1)
        key = (bucket << 25) | ((head ^ turn) << 11) | (tail & (BLOCK - 1))
        regs.append(jnp.where(slot < live, key, DEAD))
    place = (
        [("v", k) for k in range(4)]
        + [("s", k) for k in range(3)]
        + [("v", 4)]
        + [("l", k) for k in range(7)]
    )
    regs = sort_network(regs, place, 15)
    for half in range(2):
        rows = regs[16 * half : 16 * half + 16]
        keys_ref[half] = jnp.concatenate(rows, axis=0).T
        least_head = least_tail = jnp.full((ROWS, LANES), 1 << 20, jnp.int32)
        most_head = most_tail = jnp.full((ROWS, LANES), -1, jnp.int32)
        for key in rows:
            used = key < DEAD
            bucket = lax.shift_right_logical(key, 25)
            head = lax.shift_right_logical(key, 18) & (LANES - 1)
            head = head ^ (-(bucket & 1) & (LANES - 1))
            least_head = jnp.minimum(least_head, jnp.where(used, head, 1 << 20))
            most_head = jnp.maximum(most_head, jnp.where(used, head, -1))
            least_tail = jnp.minimum(least_tail, jnp.where(used, bucket, 1 << 20))
            most_tail = jnp.maximum(most_tail, jnp.where(used, bucket, -1))
        first = 8 * half
        for n, (low, high, cap) in enumerate(
            ((least_head, most_head, LANES), (least_tail, most_tail, 10))
        ):
            low = jnp.min(low, axis=0, keepdims=True)
            high = jnp.max(high, axis=0, keepdims=True)
            ends_ref[first + 2 * n : first + 2 * n + 1, :] = jnp.minimum(low, cap)
            ends_ref[first + 2 * n + 1 : first + 2 * n + 2, :] = high
            ends_ref[first + 4 + n : first + 5 + n, :] = running_max(high - low + 1, ROWS)[0:1]
        ends_ref[first + 6 : first + 8, :] = jnp.zeros((2, LANES), jnp.int32)


def pair_sort(live, pairs):
    return pl.pallas_call(
        pair_sort_kernel,
        name="pair_sort",
        out_shape=(
            jax.ShapeDtypeStruct((2, LANES, LANES), jnp.int32),
            jax.ShapeDtypeStruct((16, LANES), jnp.int32),
        ),
        in_specs=[pl.BlockSpec(memory_space=SMEM), pl.BlockSpec(memory_space=VMEM)],
        compiler_params=params(),
    )(live, pairs)


def pair_index(number, keys_ref, slot):
    idx, val = slot[0], slot[3]
    half = number & 1
    first = pl.multiple_of((number >> 1) * ROWS, ROWS)
    keys = keys_ref[half, pl.ds(first, ROWS), :]
    used = keys < DEAD
    bucket = lax.shift_right_logical(keys, 25)
    turn = -(bucket & 1) & (8 * BLOCK - 1)
    head = (lax.shift_right_logical(keys, 11) & (8 * BLOCK - 1)) ^ turn
    head_row = jnp.where(used, lax.shift_right_logical(head, 7), -1)
    tail_row = jnp.where(used, bucket * 16 + (lax.shift_right_logical(keys, 7) & 15), -1)
    for n, x in enumerate((head_row + 16, head & (LANES - 1), tail_row, keys & (LANES - 1))):
        idx[n] = x
        val[n] = (x - 16 if n == 0 else x).astype(jnp.float32)
    val[16] = used.astype(jnp.float32)


def pair_gather(number, g, ends, table, slot):
    idx, near, far = slot[0:3]
    at = 8 * (number & 1)
    group = (number >> 1) * ROWS + g
    zero = jnp.zeros((ROWS, LANES), jnp.float32)
    first = ends[at, group] + 16
    near[g] = window(table, first, HEAD_WINDOW, wide(idx, 0, g), wide(idx, 1, g), zero)
    first = ends[at + 2, group] * 16
    far[g] = window(table, first, 16, wide(idx, 2, g), wide(idx, 3, g), zero)


def pair_gather_rest(number, ends, table, slot):
    idx, near, far = slot[0:3]
    at = 8 * (number & 1)
    start = (number >> 1) * ROWS

    @pl.when((ends[at + 4, start] > HEAD_WINDOW) | (ends[at + 5, start] > 1))
    def _():
        def one(g, carry):
            row, low, tail_row, tail_low = (
                jnp.broadcast_to(idx[n, pl.ds(g, 1), :], (ROWS, LANES)) for n in range(4)
            )
            first, most = ends[at, start + g], ends[at + 1, start + g]

            def head(t, total):
                base = jnp.minimum(first + HEAD_WINDOW * t, LANES) + 16
                return window(table, base, HEAD_WINDOW, row, low, total)

            near[g] = lax.fori_loop(1, (most - first) // HEAD_WINDOW + 1, head, near[g])

            def tail(t, total):
                return window(table, t * 16, 16, tail_row, tail_low, total)

            first, most = ends[at + 2, start + g], ends[at + 3, start + g]
            far[g] = lax.fori_loop(first + 1, most + 1, tail, far[g])
            return carry

        lax.fori_loop(0, ROWS, one, 0)


def pair_values(slot):
    near, far, val = slot[1:4]
    used = val[16]
    gap = jnp.zeros((ROWS, LANES), jnp.float32)
    for c in range(3):
        apart = far[:, c, :] - near[:, c, :]
        gap = gap + apart * apart
    far_radius, near_radius = far[:, 6, :], near[:, 6, :]
    far_ratio = far_radius * lax.rsqrt(gap + far_radius * far_radius)
    near_ratio = near_radius * lax.rsqrt(gap + near_radius * near_radius)
    weight_far = jnp.where(used > 0.0, piep_coef * far_ratio * far_ratio * far_ratio, 0.0)
    weight_near = jnp.where(used > 0.0, piep_coef * near_ratio * near_ratio * near_ratio, 0.0)
    for c in range(3):
        for n, part in enumerate(split_two(weight_far * far[:, 3 + c, :])):
            val[4 + 2 * c + n] = part
        for n, part in enumerate(split_two(weight_near * near[:, 3 + c, :])):
            val[10 + 2 * c + n] = part


def pair_add(g, base, side, slot, sums, iota16):
    val = slot[3]

    def row(n):
        if isinstance(g, int):
            return packed_row(val.at[n], g)
        return jnp.broadcast_to(val[n, pl.ds(g, 1), :], (16, LANES)).astype(jnp.bfloat16)

    rel = row(2 * side) - jnp.asarray(base, jnp.int32).astype(jnp.float32).astype(jnp.bfloat16)
    hot = one_hot_rows(row(2 * side + 1), LANES, iota16)
    parts = [[row(4 + 6 * side + 2 * c + n) for c in range(3)] for n in range(2)]
    out = spread_add(rel, parts, hot, iota16)
    for c in range(3):
        sums[c, pl.ds(base, 16), :] += out[16 * c : 16 * c + 16]


def pair_scatter(number, g, ends, slot, head_sum, tail_sum, iota16):
    at = 8 * (number & 1)
    group = (number >> 1) * ROWS + g
    pair_add(g, ends[at, group], 0, slot, head_sum, iota16)
    pair_add(g, pl.multiple_of(ends[at + 2, group] * 16, 16), 1, slot, tail_sum, iota16)


def pair_scatter_rest(number, ends, slot, head_sum, tail_sum, iota16):
    at = 8 * (number & 1)
    start = (number >> 1) * ROWS

    @pl.when((ends[at + 4, start] > 16) | (ends[at + 5, start] > 1))
    def _():
        def one(g, carry):
            first, most = ends[at, start + g], ends[at + 1, start + g]

            def head(t, carry):
                base = jnp.minimum(first + 16 * t, LANES)
                pair_add(g, base, 0, slot, head_sum, iota16)
                return carry

            lax.fori_loop(1, (most - first) // 16 + 1, head, 0)

            def tail(t, carry):
                pair_add(g, pl.multiple_of(t * 16, 16), 1, slot, tail_sum, iota16)
                return carry

            first, most = ends[at + 2, start + g], ends[at + 3, start + g]
            lax.fori_loop(first + 1, most + 1, tail, 0)
            return carry

        lax.fori_loop(0, ROWS, one, 0)


def pair_kernel(
    live_ref, ends, keys_ref, own_ref, before_ref, after_ref,
    corr_ref, lower_ref, upper_ref,
    table, head_sum, tail_sum,
    idx_a, near_a, far_a, val_a, idx_b, near_b, far_b, val_b, sems,
):
    copies = [
        pltpu.make_async_copy(before_ref, table.at[0:16], sems.at[0]),
        pltpu.make_async_copy(own_ref, table.at[16:144], sems.at[1]),
        pltpu.make_async_copy(after_ref, table.at[144:160], sems.at[2]),
    ]
    for copy in copies:
        copy.start()
    head_sum[...] = jnp.zeros_like(head_sum)
    tail_sum[...] = jnp.zeros_like(tail_sum)
    for copy in copies:
        copy.wait()
    iota16 = row_iota()
    a = (idx_a, near_a, far_a, val_a)
    b = (idx_b, near_b, far_b, val_b)
    count = 2 * ((live_ref[0, 0] + 2047) // 2048)

    def step(gather, slot, scatter, other):
        pair_index(gather, keys_ref, slot)
        if other:
            pair_values(other)
        for g in range(ROWS):
            pair_gather(gather, g, ends, table, slot)
            if other:
                pair_scatter(scatter, g, ends, other, head_sum, tail_sum, iota16)
        pair_gather_rest(gather, ends, table, slot)
        if other:
            pair_scatter_rest(scatter, ends, other, head_sum, tail_sum, iota16)

    step(jnp.int32(0), a, None, None)

    def two(k, carry):
        step(2 * k + 1, b, 2 * k, a)
        step(jnp.minimum(2 * k + 2, count - 1), a, 2 * k + 1, b)
        return carry

    lax.fori_loop(0, count // 2, two, 0)
    corr_ref[...] = head_sum[:, 0:128, :] + tail_sum[:, 16:144, :]
    lower_ref[...] = tail_sum[:, 0:16, :]
    upper_ref[...] = tail_sum[:, 144:160, :]


def pair_forces(live, ends, keys, own, before, after):
    f32, i32 = jnp.float32, jnp.int32
    smem, vmem = pl.BlockSpec(memory_space=SMEM), pl.BlockSpec(memory_space=VMEM)
    hbm = pl.BlockSpec(memory_space=ANY)
    slot = [
        VMEM((4, ROWS, LANES), i32),
        VMEM((ROWS, ROWS, LANES), f32),
        VMEM((ROWS, ROWS, LANES), f32),
        VMEM((17, ROWS, LANES), f32),
    ]
    return pl.pallas_call(
        pair_kernel,
        name="pair_forces",
        out_shape=(
            jax.ShapeDtypeStruct((3, 128, LANES), f32),
            jax.ShapeDtypeStruct((3, 16, LANES), f32),
            jax.ShapeDtypeStruct((3, 16, LANES), f32),
        ),
        in_specs=[smem, smem, vmem, hbm, hbm, hbm],
        scratch_shapes=[
            VMEM((176, ROWS, LANES), f32),
            VMEM((3, 144, LANES), f32),
            VMEM((3, 176, LANES), f32),
        ]
        + slot
        + slot
        + [pltpu.SemaphoreType.DMA((3,))],
        compiler_params=params(),
    )(live, ends, keys, own, before, after)


def force_gather(block, keys_ref, table_ref, total_ref, slot):
    force, got, val = slot
    rows = rows_of(block)
    scale = (-2.0 * drag_coef) * table_ref[rows, 6, :]
    for c in range(3):
        push = scale * (table_ref[rows, 3 + c, :] + total_ref[c, rows, :])
        force[:, c, :] = push[0:8]
        force[:, 4 + c, :] = push[8:16]
    keys = keys_ref[rows, :]
    val[0] = lax.shift_right_logical(keys, 19).astype(jnp.float32)
    val[1] = (lax.shift_right_logical(keys, 11) & (2 * LANES - 1)).astype(jnp.float32)
    inner = lax.shift_right_logical(keys, 7) & 7
    low = keys & (LANES - 1)
    tables = [force[k] for k in range(ROWS)]
    for g in range(16):
        pick = jnp.broadcast_to(inner[g : g + 1, :], (ROWS, LANES))
        at = jnp.broadcast_to(low[g : g + 1, :], (ROWS, LANES))
        found = jnp.zeros((ROWS, LANES), jnp.float32)
        for k in range(ROWS):
            found = jnp.where(pick == k, lane_gather(tables[k], at), found)
        got[g] = found
    upper = (keys & 1024) != 0
    for c in range(3):
        pushed = jnp.where(upper, got[:, 4 + c, :], got[:, c, :])
        for n, part in enumerate(split_two(pushed)):
            val[2 + 2 * c + n] = part


def force_add(g, base, slot, cells, iota16):
    val = slot[2]

    def row(n):
        if isinstance(g, int):
            return packed_row(val.at[n], g)
        return jnp.broadcast_to(val[n, pl.ds(g, 1), :], (16, LANES)).astype(jnp.bfloat16)

    rel = row(0) - base.astype(jnp.float32).astype(jnp.bfloat16)
    hot = one_hot_rows(row(1), 2 * LANES, iota16)
    parts = [[row(2 + 2 * c + n) for c in range(3)] for n in range(2)]
    out = spread_add(rel, parts, hot, iota16)
    for c in range(3):
        for half in range(2):
            part = out[16 * c : 16 * c + 16, half * LANES : (half + 1) * LANES]
            cells[2 * c + half, pl.ds(base, 16), :] += part


def force_rest(block, ends, slot, cells, iota16):
    @pl.when(ends[16, block * 16] >= 16)
    def _():
        def one(g, carry):
            first, most = ends[0, block * 16 + g], ends[15, block * 16 + g]

            def trip(t, carry):
                force_add(g, jnp.minimum(first + 16 * t, LANES), slot, cells, iota16)
                return carry

            lax.fori_loop(1, (most - first) // 16 + 1, trip, 0)
            return carry

        lax.fori_loop(0, 16, one, 0)


def deposit_step(gather, scatter, ends, keys_ref, table_ref, total_ref, cells, iota16):
    if gather:
        force_gather(gather[0], keys_ref, table_ref, total_ref, gather[1])
    if scatter:
        for g in range(16):
            force_add(g, ends[0, scatter[0] * 16 + g], scatter[1], cells, iota16)
        force_rest(scatter[0], ends, scatter[1], cells, iota16)


def inner_deposit_kernel(
    ends, keys_ref, table_ref, corr_ref,
    cells,
    force_a, got_a, val_a, force_b, got_b, val_b,
):
    cells[...] = jnp.zeros_like(cells)
    a, b = (force_a, got_a, val_a), (force_b, got_b, val_b)
    step = functools.partial(
        deposit_step, ends=ends, keys_ref=keys_ref, table_ref=table_ref, total_ref=corr_ref,
        cells=cells, iota16=row_iota(),
    )
    step((1, a), None)

    def two(k, carry):
        block = 2 * k + 1
        step((block + 1, b), (block, a))
        step((jnp.minimum(block + 2, 6), a), (block + 1, b))
        return carry

    lax.fori_loop(0, 3, two, 0)


def force_slots():
    f32 = jnp.float32
    one = [VMEM((ROWS, ROWS, LANES), f32), VMEM((16, ROWS, LANES), f32), VMEM((8, 16, LANES), f32)]
    return one + one


def inner_deposit(ends, keys, table, corr):
    smem, vmem = pl.BlockSpec(memory_space=SMEM), pl.BlockSpec(memory_space=VMEM)
    return pl.pallas_call(
        inner_deposit_kernel,
        name="inner_deposit",
        out_shape=jax.ShapeDtypeStruct((6, 144, LANES), jnp.float32),
        in_specs=[smem, vmem, vmem, vmem],
        scratch_shapes=force_slots(),
        compiler_params=params(),
    )(ends, keys, table, corr)


def edge_deposit_kernel(
    ends, keys_ref, table_ref, corr_ref, lower_ref, upper_ref, inner_ref,
    out_ref, total_ref, first_ref, last_ref,
    cells, force_a, got_a, val_a, force_b, got_b, val_b,
):
    cells[...] = inner_ref[...]
    total_ref[...] = corr_ref[...]
    total_ref[:, 0:16, :] += lower_ref[...]
    total_ref[:, 112:128, :] += upper_ref[...]
    a, b = (force_a, got_a, val_a), (force_b, got_b, val_b)
    step = functools.partial(
        deposit_step, ends=ends, keys_ref=keys_ref, table_ref=table_ref, total_ref=total_ref,
        cells=cells, iota16=row_iota(),
    )
    step((0, a), None)
    step((7, b), (0, a))
    step(None, (7, b))
    for c in range(3):
        for half in range(2):
            columns = slice(half * LANES, (half + 1) * LANES)
            out_ref[c, :, columns] = cells[2 * c + half, 0:128, :]
            first_ref[c, :, columns] = cells[2 * c + half, 0:32, :]
            last_ref[c, :, columns] = cells[2 * c + half, 96:128, :]


def edge_deposit(ends, keys, table, corr, lower, upper, inner):
    f32 = jnp.float32
    smem, vmem = pl.BlockSpec(memory_space=SMEM), pl.BlockSpec(memory_space=VMEM)
    return pl.pallas_call(
        edge_deposit_kernel,
        name="edge_deposit",
        out_shape=(
            jax.ShapeDtypeStruct((3, 128, 2 * LANES), f32),
            jax.ShapeDtypeStruct((3, 128, LANES), f32),
            jax.ShapeDtypeStruct((3, 32, 2 * LANES), f32),
            jax.ShapeDtypeStruct((3, 32, 2 * LANES), f32),
        ),
        in_specs=[smem] + [vmem] * 6,
        scratch_shapes=[VMEM((6, 144, LANES), f32)] + force_slots(),
        compiler_params=params(),
    )(ends, keys, table, corr, lower, upper, inner)


def axial_kernel(taps, cells_ref, before_ref, after_ref, out_ref, first_ref, last_ref):
    for c in range(3):
        padded = jnp.concatenate([before_ref[c], cells_ref[c], after_ref[c]], axis=0)
        total = taps[0] * padded[0:128]
        for k in range(1, 5):
            total = total + taps[k] * padded[16 * k : 16 * k + 128]
        out_ref[c] = total
        for a in range(8):
            first_ref[c, 2 * a : 2 * a + 2, :] = total[16 * a : 16 * a + 2]
            last_ref[c, 2 * a : 2 * a + 2, :] = total[16 * a + 14 : 16 * a + 16]


def radial_kernel(taps, cells_ref, before_ref, after_ref, out_ref, first_ref, last_ref, padded):
    lane = lax.broadcasted_iota(jnp.int32, (LANES, LANES), 1)
    edges = jnp.zeros((LANES, LANES), jnp.float32)
    for c in range(3):
        for a in range(8):
            padded[0:2, :] = before_ref[c, 2 * a : 2 * a + 2, :]
            padded[2:18, :] = cells_ref[c, 16 * a : 16 * a + 16, :]
            padded[18:20, :] = after_ref[c, 2 * a : 2 * a + 2, :]
            total = taps[0] * padded[0:16, :]
            for k in range(1, 5):
                total = total + taps[k] * padded[k : k + 16, :]
            out_ref[c, 16 * a : 16 * a + 16, :] = total
        left, right = out_ref[c, :, 0:LANES], out_ref[c, :, LANES:]
        if c:
            left = pltpu.roll(left, 2 * c, 1)
        right = pltpu.roll(right, 10 + 2 * c, 1)
        edges = jnp.where((lane >> 1) == c, left, edges)
        edges = jnp.where((lane >> 1) == 4 + c, right, edges)
    turned = edges.T
    first_ref[...] = turned[0:8]
    last_ref[...] = turned[8:16]


def azimuthal_kernel(taps, cells_ref, before_ref, after_ref, out_ref):
    lane = lax.broadcasted_iota(jnp.int32, (LANES, LANES), 1)
    rest = jnp.zeros((LANES - 16, LANES), jnp.float32)
    edges = jnp.concatenate([after_ref[...], before_ref[...], rest], axis=0).T
    for c in range(3):
        ahead = pltpu.roll(edges, LANES - 2 * c, 1) if c else edges
        halo = jnp.where(lane < 64, ahead, pltpu.roll(edges, 118 - 2 * c, 1))
        left, right = cells_ref[c, :, 0:LANES], cells_ref[c, :, LANES:]
        out_left, out_right = taps[2] * left, taps[2] * right
        for k in (1, 2):
            tap = taps[2 + k]
            inner = lane < LANES - k
            x, y, z = (pltpu.roll(v, LANES - k, 1) for v in (left, right, halo))
            out_left = out_left + tap * jnp.where(inner, x, y)
            out_right = out_right + tap * jnp.where(inner, y, z)
            inner = lane >= k
            x, y, z = (pltpu.roll(v, k, 1) for v in (left, right, halo))
            out_left = out_left + tap * jnp.where(inner, x, z)
            out_right = out_right + tap * jnp.where(inner, y, x)
        out_ref[c, :, 0:LANES] = out_left
        out_ref[c, :, LANES:] = out_right


def filtered(deposit, first, last):
    f32 = jnp.float32
    raw = [math.exp(-0.5 * k * k) for k in range(-2, 3)]
    taps = [x / sum(raw) for x in raw]
    whole = jax.ShapeDtypeStruct(deposit.shape, f32)
    radial_face = jax.ShapeDtypeStruct((3, 16, 2 * LANES), f32)
    edge = jax.ShapeDtypeStruct((8, LANES), f32)
    cells, first, last = pl.pallas_call(
        functools.partial(axial_kernel, taps),
        name="axial_filter",
        out_shape=(whole, radial_face, radial_face),
        compiler_params=params(),
    )(deposit, shifted(last, "ax", 1, False), shifted(first, "ax", -1, False))
    cells, first, last = pl.pallas_call(
        functools.partial(radial_kernel, taps),
        name="radial_filter",
        out_shape=(whole, edge, edge),
        scratch_shapes=[VMEM((24, 2 * LANES), f32)],
        compiler_params=params(),
    )(cells, shifted(last, "rad", 1, False), shifted(first, "rad", -1, False))
    return pl.pallas_call(
        functools.partial(azimuthal_kernel, taps),
        name="azimuthal_filter",
        out_shape=whole,
        compiler_params=params(),
    )(cells, shifted(last, "az", 1, True), shifted(first, "az", -1, True))


def shifted(x, axis, by, wrap):
    count = lax.axis_size(axis)
    pairs = [(i, (i + by) % count) for i in range(count)]
    return lax.ppermute(x, axis, [p for p in pairs if wrap or p[1] - p[0] == by])


def per_device(positions, velocity, diameter, cell_index, pair_list, live_pairs, gas_velocity):
    live = live_pairs.reshape(1, 1)
    cells = cell_index.reshape(128, LANES)
    gas = gas_velocity.reshape(3, 128, 2 * LANES)
    pos = positions.reshape(3, 128, LANES)
    vel = velocity.reshape(3, 128, LANES)
    diam = diameter.reshape(128, LANES)
    cell_keys, cell_ends, first, last = edge_states(cells, gas, pos, vel, diam)
    before = shifted(last, "az", 1, True)
    after = shifted(first, "az", -1, True)
    table = inner_states(cell_ends, cell_keys, gas, pos, vel, diam, first, last)
    pair_keys, pair_ends = pair_sort(live, pair_list.reshape(2, 256, LANES))
    corr, lower, upper = pair_forces(live, pair_ends, pair_keys, table, before, after)
    from_upper = shifted(lower, "az", -1, True)
    from_lower = shifted(upper, "az", 1, True)
    inner = inner_deposit(cell_ends, cell_keys, table, corr)
    deposit, correction, first, last = edge_deposit(
        cell_ends, cell_keys, table, corr, from_lower, from_upper, inner
    )
    smoothed = filtered(deposit, first, last)
    return (correction.reshape(positions.shape), smoothed.reshape(gas_velocity.shape))


def solution(mesh):
    return jax.shard_map(
        per_device,
        mesh=mesh,
        in_specs=(
            P(None, "ax", "rad", "az"),
            P(None, "ax", "rad", "az"),
            P("ax", "rad", "az"),
            P("ax", "rad", "az"),
            P(None, "ax", "rad", "az"),
            P("ax", "rad", "az"),
            P(None, "ax", "rad", "az"),
        ),
        out_specs=(P(None, "ax", "rad", "az"), P(None, "ax", "rad", "az")),
        check_vma=False,
    )
```

```python
import functools
import math

import jax
import jax.numpy as jnp
from jax import lax
from jax.experimental import pallas as pl
from jax.experimental.pallas import tpu as pltpu
from jax.sharding import PartitionSpec as P

piep_coef = 1.0
drag_coef = 20.0

LANES = 128
ROWS = 8
BLOCK = 2048
GAS_WINDOW = 10
HEAD_WINDOW = 10
DEAD = 1 << 29

NT = (((1,), (1,)), ((), ()))
VMEM = pltpu.VMEM
SMEM = pltpu.SMEM


def params(megabytes=40):
    return pltpu.CompilerParams(vmem_limit_bytes=megabytes << 20)


def lane_gather(table, index):
    numbers = lax.GatherDimensionNumbers(
        offset_dims=(),
        collapsed_slice_dims=(1,),
        start_index_map=(1,),
        operand_batching_dims=(0,),
        start_indices_batching_dims=(0,),
    )
    return lax.gather(
        table,
        index[..., None],
        numbers,
        slice_sizes=(1, 1),
        mode=lax.GatherScatterMode.PROMISE_IN_BOUNDS,
    )


def sort_network(regs, place, levels):
    sub = lax.broadcasted_iota(jnp.int32, (ROWS, LANES), 0)
    lane = lax.broadcasted_iota(jnp.int32, (ROWS, LANES), 1)
    count = len(regs)

    def bit_fill(bit, v):
        if bit >= levels:
            return 0
        kind, k = place[bit]
        if kind == "v":
            return -((v >> k) & 1)
        return -(((sub if kind == "s" else lane) >> k) & 1)

    flip = [0] * count
    for level in range(1, levels + 1):
        fills = {}
        for v in range(count):
            kind, k = place[level] if level < levels else ("v", 99)
            key = (v >> k) & 1 if kind == "v" else 0
            if key not in fills:
                fills[key] = bit_fill(level, v)
            new = fills[key]
            if isinstance(new, int) and isinstance(flip[v], int):
                if new != flip[v]:
                    regs[v] = ~regs[v]
            else:
                regs[v] = regs[v] ^ (new ^ flip[v])
            flip[v] = new
        for bit in reversed(range(level)):
            kind, k = place[bit]
            step = 1 << k
            if kind == "v":
                for v in range(count):
                    if not v & step:
                        a, b = regs[v], regs[v | step]
                        regs[v], regs[v | step] = jnp.minimum(a, b), jnp.maximum(a, b)
            else:
                axis, size, where = (0, ROWS, sub) if kind == "s" else (1, LANES, lane)
                lower = (where & step) == 0
                for v in range(count):
                    x = regs[v]
                    ahead = pltpu.roll(x, size - step, axis)
                    behind = ahead if 2 * step == size else pltpu.roll(x, step, axis)
                    regs[v] = jnp.where(lower, jnp.minimum(x, ahead), jnp.maximum(x, behind))
    return regs


def split_two(x):
    high = x.astype(jnp.bfloat16).astype(jnp.float32)
    return high, x - high


def split_three(x):
    high, rest = split_two(x)
    mid, low = split_two(rest)
    return high, mid, low


def packed_row(ref, row):
    return jnp.broadcast_to(ref[row : row + 1, :], (16, LANES)).astype(jnp.bfloat16)


def one_hot_rows(low, iota):
    one = jnp.ones((16, LANES), jnp.bfloat16)
    zero = jnp.zeros((16, LANES), jnp.bfloat16)
    return jnp.concatenate(
        [jnp.where(low == iota[k : k + 16, :], one, zero) for k in range(0, iota.shape[0], 16)],
        axis=0,
    )


def spread_rows(rel, parts, iota):
    hit = rel == iota[0:16, :]
    zero = jnp.zeros((16, LANES), jnp.bfloat16)
    return jnp.concatenate([jnp.where(hit, p, zero) for part in parts for p in part], axis=0)


def spread_add(rows, hots):
    out = lax.dot_general(
        jnp.concatenate(rows, axis=1) if len(rows) > 1 else rows[0],
        jnp.concatenate(hots, axis=1) if len(hots) > 1 else hots[0],
        NT,
        preferred_element_type=jnp.float32,
    )
    total = out[0:48]
    for s in range(48, out.shape[0], 48):
        total = total + out[s : s + 48]
    return total


def fill_iota(iota):
    rows = lax.broadcasted_iota(jnp.int32, iota.shape, 0)
    iota[...] = rows.astype(jnp.float32).astype(jnp.bfloat16)


def rows_of(block):
    start = block * 16
    return pl.ds(start if isinstance(block, int) else pl.multiple_of(start, 16), 16)


def wide(ref, *at):
    return jnp.broadcast_to(ref[at[:-1] + (slice(at[-1], at[-1] + 1),)], (ROWS, LANES))


def window(table, first, count, row, low, found):
    rel = row - first
    for u in range(count):
        found = jnp.where(rel == u, lane_gather(table[first + u], low), found)
    return found


def running_max(x, count):
    x = jnp.broadcast_to(x, (ROWS, LANES))
    step = 1
    while step < count:
        x = jnp.maximum(x, pltpu.roll(x, LANES - step, 1))
        step *= 2
    return x


def fill_gas_rows(gas_ref, gas_rows):
    for r in range(16):
        rows = slice(r * ROWS, (r + 1) * ROWS)
        for c in range(3):
            for half in range(2):
                gas_rows[rows, half * 4 + c, :] = gas_ref[c, rows, half * LANES : (half + 1) * LANES]


def gas_index(block, keys_ref, slot):
    idx = slot[0]
    keys = keys_ref[rows_of(block), :]
    idx[0] = lax.shift_right_logical(keys, 19)
    idx[1] = lax.shift_right_logical(keys, 11) & (LANES - 1)


def gas_gather(block, g, ends, gas_rows, slot):
    idx, found = slot[0], slot[1]
    zero = jnp.zeros((ROWS, LANES), jnp.float32)
    first = ends[0, block * 16 + g]
    found[g] = window(gas_rows, first, GAS_WINDOW, wide(idx, 0, g), wide(idx, 1, g), zero)


def gas_rest(block, ends, gas_rows, slot):
    idx, found = slot[0], slot[1]

    @pl.when(ends[16, block * 16] >= GAS_WINDOW)
    def _():
        def one(g, carry):
            first = ends[0, block * 16 + g]
            row = jnp.broadcast_to(idx[0, pl.ds(g, 1), :], (ROWS, LANES))
            low = jnp.broadcast_to(idx[1, pl.ds(g, 1), :], (ROWS, LANES))

            def trip(t, total):
                base = jnp.minimum(first + GAS_WINDOW * t, LANES)
                return window(gas_rows, base, GAS_WINDOW, row, low, total)

            trips = (ends[15, block * 16 + g] - first) // GAS_WINDOW + 1
            found[g] = lax.fori_loop(1, trips, trip, found[g])
            return carry

        lax.fori_loop(0, 16, one, 0)


def seen_values(block, keys_ref, slot):
    idx, found, val = slot
    keys = keys_ref[rows_of(block), :]
    upper = (keys & (1 << 18)) != 0
    place_in = keys & (BLOCK - 1)
    val[0] = lax.shift_right_logical(place_in, 7).astype(jnp.float32)
    val[1] = (place_in & (LANES - 1)).astype(jnp.float32)
    for c in range(3):
        seen = jnp.where(upper, found[:, 4 + c, :], found[:, c, :])
        for n, part in enumerate(split_three(seen)):
            val[2 + 3 * c + n] = part


def seen_in_order(groups, slot, iota):
    val = slot[2]
    rows, hots = [], []
    for g in groups:
        parts = [[packed_row(val.at[2 + 3 * c + n], g) for c in range(3)] for n in range(3)]
        rows.append(spread_rows(packed_row(val.at[0], g), parts, iota))
        hots.append(one_hot_rows(packed_row(val.at[1], g), iota))
    return spread_add(rows, hots)


def write_states(block, total, pos_ref, vel_ref, diam_ref, out_ref, out_rows):
    rows = rows_of(block)
    for c in range(3):
        out_ref[out_rows, c, :] = pos_ref[c, rows, :]
        out_ref[out_rows, 3 + c, :] = total[16 * c : 16 * c + 16] - vel_ref[c, rows, :]
    out_ref[out_rows, 6, :] = 0.5 * diam_ref[rows, :]
    out_ref[out_rows, 7, :] = jnp.zeros((16, LANES), jnp.float32)


def states_step(gather, scatter, keys_ref, ends, gas_rows, iota, arrays):
    total = jnp.zeros((48, LANES), jnp.float32)
    if gather:
        gas_index(gather[0], keys_ref, gather[1])
    if scatter:
        seen_values(scatter[0], keys_ref, scatter[1])
    for g in range(16):
        if gather:
            gas_gather(gather[0], g, ends, gas_rows, gather[1])
        if scatter and g % 2:
            total = total + seen_in_order((g - 1, g), scatter[1], iota)
    if scatter:
        write_states(scatter[0], total, *arrays, *scatter[2:])
    if gather:
        gas_rest(gather[0], ends, gas_rows, gather[1])


def edge_states_kernel(
    cell_hbm, gas_hbm, pos_hbm, vel_hbm, diam_hbm,
    keys_ref, ends_ref, first_ref, last_ref,
    cell_ref, gas_ref, pos_ref, vel_ref, diam_ref,
    gas_rows, iota, ends, idx_a, found_a, val_a, idx_b, found_b, val_b, sems,
):
    sources = (cell_hbm, gas_hbm, pos_hbm, vel_hbm, diam_hbm)
    places = (cell_ref, gas_ref, pos_ref, vel_ref, diam_ref)
    copies = [
        pltpu.make_async_copy(x, y, sems.at[n]) for n, (x, y) in enumerate(zip(sources, places))
    ]
    for copy in copies:
        copy.start()
    copies[0].wait()
    sub = lax.broadcasted_iota(jnp.int32, (ROWS, LANES), 0)
    lane = lax.broadcasted_iota(jnp.int32, (ROWS, LANES), 1)
    regs = []
    for v in range(16):
        own = (v % 2) * 1024 + sub * LANES + lane
        regs.append(cell_ref[v * ROWS : (v + 1) * ROWS, :] * BLOCK + own)
    place = [("l", k) for k in range(7)] + [("s", k) for k in range(3)] + [("v", 0)]
    regs = sort_network(regs, place, 11)
    keys = jnp.concatenate(regs, axis=0)
    keys_ref[...] = keys
    turned = lax.shift_right_logical(keys, 19).T
    ends_ref[0:8, :] = turned[0:8]
    ends_ref[8:16, :] = turned[120:128]
    ends_ref[16:24, :] = running_max(turned[127:128] - turned[0:1], 16)
    copy = pltpu.make_async_copy(ends_ref, ends, sems.at[5])
    copy.start()
    copies[1].wait()
    fill_gas_rows(gas_ref, gas_rows)
    for other in copies[2:]:
        other.wait()
    copy.wait()
    fill_iota(iota)
    a, b = (idx_a, found_a, val_a), (idx_b, found_b, val_b)
    whole = slice(0, 16)
    step = functools.partial(
        states_step, keys_ref=keys_ref, ends=ends, gas_rows=gas_rows, iota=iota,
        arrays=(pos_ref, vel_ref, diam_ref),
    )
    step((0, a), None)
    step((7, b), (0, a, first_ref, whole))
    step(None, (7, b, last_ref, whole))


def slots(rows, parts, dtype=jnp.float32):
    one = [VMEM((2, 16, LANES), jnp.int32), VMEM((16, ROWS, LANES), dtype), VMEM((parts, rows, LANES), dtype)]
    return one + one


def edge_states(cells, gas, pos, vel, diam):
    f32, i32 = jnp.float32, jnp.int32
    arrays = (cells, gas, pos, vel, diam)
    return pl.pallas_call(
        edge_states_kernel,
        name="edge_states",
        out_shape=(
            jax.ShapeDtypeStruct((128, LANES), i32),
            jax.ShapeDtypeStruct((24, LANES), i32),
            jax.ShapeDtypeStruct((16, ROWS, LANES), f32),
            jax.ShapeDtypeStruct((16, ROWS, LANES), f32),
        ),
        in_specs=[pl.BlockSpec(memory_space=pltpu.HBM)] * 5,
        scratch_shapes=[VMEM(x.shape, x.dtype) for x in arrays]
        + [VMEM((144, ROWS, LANES), f32), VMEM((LANES, LANES), jnp.bfloat16), SMEM((24, LANES), i32)]
        + slots(16, 11)
        + [pltpu.SemaphoreType.DMA((6,))],
        compiler_params=params(60),
    )(*arrays)


def inner_states_kernel(
    ends, keys_ref, gas_ref, pos_ref, vel_ref, diam_ref, first_ref, last_ref,
    table_ref,
    gas_rows, iota, idx_a, found_a, val_a, idx_b, found_b, val_b,
):
    fill_gas_rows(gas_ref, gas_rows)
    fill_iota(iota)
    a, b = (idx_a, found_a, val_a), (idx_b, found_b, val_b)
    step = functools.partial(
        states_step, keys_ref=keys_ref, ends=ends, gas_rows=gas_rows, iota=iota,
        arrays=(pos_ref, vel_ref, diam_ref),
    )
    table_ref[0:16] = first_ref[...]
    table_ref[112:128] = last_ref[...]
    step((1, a), None)

    def two(k, carry):
        block = 2 * k + 1
        step((block + 1, b), (block, a, table_ref, rows_of(block)))
        step((jnp.minimum(block + 2, 6), a), (block + 1, b, table_ref, rows_of(block + 1)))
        return carry

    lax.fori_loop(0, 3, two, 0)


def inner_states(ends, keys, gas, pos, vel, diam, first, last):
    f32 = jnp.float32
    return pl.pallas_call(
        inner_states_kernel,
        name="inner_states",
        out_shape=jax.ShapeDtypeStruct((128, ROWS, LANES), f32),
        in_specs=[pl.BlockSpec(memory_space=SMEM)] + [pl.BlockSpec(memory_space=VMEM)] * 7,
        scratch_shapes=[VMEM((144, ROWS, LANES), f32), VMEM((LANES, LANES), jnp.bfloat16)]
        + slots(16, 11),
        compiler_params=params(),
    )(ends, keys, gas, pos, vel, diam, first, last)


def pair_sort_kernel(live_ref, pairs_ref, keys_ref, ends_ref):
    live = live_ref[0, 0]
    sub = lax.broadcasted_iota(jnp.int32, (ROWS, LANES), 0)
    lane = lax.broadcasted_iota(jnp.int32, (ROWS, LANES), 1)
    regs = []
    for v in range(32):
        rows = slice(v * ROWS, (v + 1) * ROWS)
        slot = v * 1024 + sub * LANES + lane
        head = pairs_ref[0, rows, :]
        tail = pairs_ref[1, rows, :] - 7 * BLOCK
        bucket = lax.shift_right_logical(tail, 11)
        turn = -(bucket & 1) & (8 * BLOCK - 1)
        key = (bucket << 25) | ((head ^ turn) << 11) | (tail & (BLOCK - 1))
        regs.append(jnp.where(slot < live, key, DEAD))
    place = (
        [("v", k) for k in range(4)]
        + [("s", k) for k in range(3)]
        + [("v", 4)]
        + [("l", k) for k in range(7)]
    )
    regs = sort_network(regs, place, 15)
    for half in range(2):
        rows = regs[16 * half : 16 * half + 16]
        keys_ref[half] = jnp.concatenate(rows, axis=0).T
        least_head = least_tail = jnp.full((ROWS, LANES), 1 << 20, jnp.int32)
        most_head = most_tail = jnp.full((ROWS, LANES), -1, jnp.int32)
        for key in rows:
            used = key < DEAD
            bucket = lax.shift_right_logical(key, 25)
            head = lax.shift_right_logical(key, 18) & (LANES - 1)
            head = head ^ (-(bucket & 1) & (LANES - 1))
            least_head = jnp.minimum(least_head, jnp.where(used, head, 1 << 20))
            most_head = jnp.maximum(most_head, jnp.where(used, head, -1))
            least_tail = jnp.minimum(least_tail, jnp.where(used, bucket, 1 << 20))
            most_tail = jnp.maximum(most_tail, jnp.where(used, bucket, -1))
        first = 8 * half
        for n, (low, high, cap) in enumerate(
            ((least_head, most_head, LANES), (least_tail, most_tail, 10))
        ):
            low = jnp.min(low, axis=0, keepdims=True)
            high = jnp.max(high, axis=0, keepdims=True)
            ends_ref[first + 2 * n : first + 2 * n + 1, :] = jnp.minimum(low, cap)
            ends_ref[first + 2 * n + 1 : first + 2 * n + 2, :] = high
            ends_ref[first + 4 + n : first + 5 + n, :] = running_max(high - low + 1, ROWS)[0:1]
        ends_ref[first + 6 : first + 8, :] = running_max(high, ROWS)[0:2]


def pair_sort(live, pairs):
    return pl.pallas_call(
        pair_sort_kernel,
        name="pair_sort",
        out_shape=(
            jax.ShapeDtypeStruct((2, LANES, LANES), jnp.int32),
            jax.ShapeDtypeStruct((16, LANES), jnp.int32),
        ),
        in_specs=[pl.BlockSpec(memory_space=SMEM), pl.BlockSpec(memory_space=VMEM)],
        compiler_params=params(),
    )(live, pairs)


def pair_index(number, keys_ref, slot):
    idx, val = slot[0], slot[3]
    half = number & 1
    first = pl.multiple_of((number >> 1) * ROWS, ROWS)
    keys = keys_ref[half, pl.ds(first, ROWS), :]
    used = keys < DEAD
    bucket = lax.shift_right_logical(keys, 25)
    turn = -(bucket & 1) & (8 * BLOCK - 1)
    head = (lax.shift_right_logical(keys, 11) & (8 * BLOCK - 1)) ^ turn
    head_row = jnp.where(used, lax.shift_right_logical(head, 7), -1)
    tail_row = jnp.where(used, bucket * 16 + (lax.shift_right_logical(keys, 7) & 15), -1)
    for n, x in enumerate((head_row + 16, head & (LANES - 1), tail_row, keys & (LANES - 1))):
        idx[n] = x
        val[n] = (x - 16 if n == 0 else x).astype(jnp.float32)
    val[16] = used.astype(jnp.float32)


def pair_gather(number, g, ends, table, slot):
    idx, near, far = slot[0:3]
    at = 8 * (number & 1)
    group = (number >> 1) * ROWS + g
    zero = jnp.zeros((ROWS, LANES), jnp.float32)
    first = ends[at, group] + 16
    near[g] = window(table, first, HEAD_WINDOW, wide(idx, 0, g), wide(idx, 1, g), zero)
    first = ends[at + 2, group] * 16
    far[g] = window(table, first, 16, wide(idx, 2, g), wide(idx, 3, g), zero)


def pair_gather_rest(number, ends, table, slot):
    idx, near, far = slot[0:3]
    at = 8 * (number & 1)
    start = (number >> 1) * ROWS

    @pl.when((ends[at + 4, start] > HEAD_WINDOW) | (ends[at + 5, start] > 1))
    def _():
        def one(g, carry):
            row, low, tail_row, tail_low = (
                jnp.broadcast_to(idx[n, pl.ds(g, 1), :], (ROWS, LANES)) for n in range(4)
            )
            first, most = ends[at, start + g], ends[at + 1, start + g]

            def head(t, total):
                base = jnp.minimum(first + HEAD_WINDOW * t, LANES) + 16
                return window(table, base, HEAD_WINDOW, row, low, total)

            near[g] = lax.fori_loop(1, (most - first) // HEAD_WINDOW + 1, head, near[g])

            def tail(t, total):
                return window(table, t * 16, 16, tail_row, tail_low, total)

            first, most = ends[at + 2, start + g], ends[at + 3, start + g]
            far[g] = lax.fori_loop(first + 1, most + 1, tail, far[g])
            return carry

        lax.fori_loop(0, ROWS, one, 0)


def pair_values(slot):
    near, far, val = slot[1:4]
    used = val[16]
    gap = jnp.zeros((ROWS, LANES), jnp.float32)
    for c in range(3):
        apart = far[:, c, :] - near[:, c, :]
        gap = gap + apart * apart
    far_radius, near_radius = far[:, 6, :], near[:, 6, :]
    far_ratio = far_radius * lax.rsqrt(gap + far_radius * far_radius)
    near_ratio = near_radius * lax.rsqrt(gap + near_radius * near_radius)
    weight_far = jnp.where(used > 0.0, piep_coef * far_ratio * far_ratio * far_ratio, 0.0)
    weight_near = jnp.where(used > 0.0, piep_coef * near_ratio * near_ratio * near_ratio, 0.0)
    for c in range(3):
        for n, part in enumerate(split_two(weight_far * far[:, 3 + c, :])):
            val[4 + 2 * c + n] = part
        for n, part in enumerate(split_two(weight_near * near[:, 3 + c, :])):
            val[10 + 2 * c + n] = part


def pair_rows(g, base, side, slot, iota):
    val = slot[3]

    def row(n):
        if isinstance(g, int):
            return packed_row(val.at[n], g)
        return jnp.broadcast_to(val[n, pl.ds(g, 1), :], (16, LANES)).astype(jnp.bfloat16)

    rel = row(2 * side) - jnp.asarray(base, jnp.int32).astype(jnp.float32).astype(jnp.bfloat16)
    parts = [[row(4 + 6 * side + 2 * c + n) for c in range(3)] for n in range(2)]
    return spread_rows(rel, parts, iota), one_hot_rows(row(2 * side + 1), iota)


def add_rows(sums, base, out):
    for c in range(3):
        sums[c, pl.ds(base, 16), :] += out[16 * c : 16 * c + 16]


def pair_add_heads(g, base, slot, head_sum, iota):
    rows, hot = pair_rows(g, base, 0, slot, iota)
    add_rows(head_sum, base, spread_add([rows], [hot]))


def pair_add_tails(groups, bucket, slot, tail_sum, iota):
    base = pl.multiple_of(bucket * 16, 16)
    pieces = [pair_rows(g, base, 1, slot, iota) for g in groups]
    add_rows(tail_sum, base, spread_add([p[0] for p in pieces], [p[1] for p in pieces]))


def pair_scatter(number, g, ends, slot, head_sum, tail_sum, iota):
    at = 8 * (number & 1)
    start = (number >> 1) * ROWS
    pair_add_heads(g, ends[at, start + g], slot, head_sum, iota)
    if g % 4 == 3:
        pair_add_tails(range(g - 3, g + 1), ends[at + 2, start], slot, tail_sum, iota)


def pair_scatter_rest(number, ends, slot, head_sum, tail_sum, iota):
    at = 8 * (number & 1)
    start = (number >> 1) * ROWS

    @pl.when(ends[at + 4, start] > 16)
    def _():
        def one(g, carry):
            first, most = ends[at, start + g], ends[at + 1, start + g]

            def head(t, carry):
                pair_add_heads(g, jnp.minimum(first + 16 * t, LANES), slot, head_sum, iota)
                return carry

            lax.fori_loop(1, (most - first) // 16 + 1, head, 0)
            return carry

        lax.fori_loop(0, ROWS, one, 0)

    def tail(bucket, carry):
        pair_add_tails(range(0, 4), bucket, slot, tail_sum, iota)
        pair_add_tails(range(4, 8), bucket, slot, tail_sum, iota)
        return carry

    lax.fori_loop(ends[at + 2, start] + 1, ends[at + 6, start] + 1, tail, 0)


def pair_kernel(
    live_ref, ends, keys_ref, own_ref, before_ref, after_ref,
    corr_ref, lower_ref, upper_ref,
    table, head_sum, tail_sum, iota,
    idx_a, near_a, far_a, val_a, idx_b, near_b, far_b, val_b,
):
    table[0:16] = before_ref[...]
    table[16:144] = own_ref[...]
    table[144:160] = after_ref[...]
    head_sum[...] = jnp.zeros_like(head_sum)
    tail_sum[...] = jnp.zeros_like(tail_sum)
    fill_iota(iota)
    a = (idx_a, near_a, far_a, val_a)
    b = (idx_b, near_b, far_b, val_b)
    count = 2 * ((live_ref[0, 0] + 2047) // 2048)

    def step(gather, slot, scatter, other):
        pair_index(gather, keys_ref, slot)
        if other:
            pair_values(other)
        for g in range(ROWS):
            pair_gather(gather, g, ends, table, slot)
            if other:
                pair_scatter(scatter, g, ends, other, head_sum, tail_sum, iota)
        pair_gather_rest(gather, ends, table, slot)
        if other:
            pair_scatter_rest(scatter, ends, other, head_sum, tail_sum, iota)

    step(jnp.int32(0), a, None, None)

    def two(k, carry):
        step(2 * k + 1, b, 2 * k, a)
        step(jnp.minimum(2 * k + 2, count - 1), a, 2 * k + 1, b)
        return carry

    lax.fori_loop(0, count // 2, two, 0)
    corr_ref[...] = head_sum[:, 0:128, :] + tail_sum[:, 16:144, :]
    lower_ref[...] = tail_sum[:, 0:16, :]
    upper_ref[...] = tail_sum[:, 144:160, :]


def pair_forces(live, ends, keys, own, before, after):
    f32, i32 = jnp.float32, jnp.int32
    smem, vmem = pl.BlockSpec(memory_space=SMEM), pl.BlockSpec(memory_space=VMEM)
    slot = [
        VMEM((4, ROWS, LANES), i32),
        VMEM((ROWS, ROWS, LANES), f32),
        VMEM((ROWS, ROWS, LANES), f32),
        VMEM((17, ROWS, LANES), f32),
    ]
    return pl.pallas_call(
        pair_kernel,
        name="pair_forces",
        out_shape=(
            jax.ShapeDtypeStruct((3, 128, LANES), f32),
            jax.ShapeDtypeStruct((3, 16, LANES), f32),
            jax.ShapeDtypeStruct((3, 16, LANES), f32),
        ),
        in_specs=[smem, smem, vmem, vmem, vmem, vmem],
        scratch_shapes=[
            VMEM((176, ROWS, LANES), f32),
            VMEM((3, 144, LANES), f32),
            VMEM((3, 176, LANES), f32),
            VMEM((LANES, LANES), jnp.bfloat16),
        ]
        + slot
        + slot,
        compiler_params=params(),
    )(live, ends, keys, own, before, after)


def force_gather(block, keys_ref, table_ref, total_ref, slot):
    force, got, val = slot
    rows = rows_of(block)
    scale = (-2.0 * drag_coef) * table_ref[rows, 6, :]
    for c in range(3):
        push = scale * (table_ref[rows, 3 + c, :] + total_ref[c, rows, :])
        force[:, c, :] = push[0:8]
        force[:, 4 + c, :] = push[8:16]
    keys = keys_ref[rows, :]
    val[0] = lax.shift_right_logical(keys, 19).astype(jnp.float32)
    val[1] = (lax.shift_right_logical(keys, 11) & (2 * LANES - 1)).astype(jnp.float32)
    inner = lax.shift_right_logical(keys, 7) & 7
    low = keys & (LANES - 1)
    tables = [force[k] for k in range(ROWS)]
    for g in range(16):
        pick = jnp.broadcast_to(inner[g : g + 1, :], (ROWS, LANES))
        at = jnp.broadcast_to(low[g : g + 1, :], (ROWS, LANES))
        found = jnp.zeros((ROWS, LANES), jnp.float32)
        for k in range(ROWS):
            found = jnp.where(pick == k, lane_gather(tables[k], at), found)
        got[g] = found
    upper = (keys & 1024) != 0
    for c in range(3):
        pushed = jnp.where(upper, got[:, 4 + c, :], got[:, c, :])
        for n, part in enumerate(split_two(pushed)):
            val[2 + 2 * c + n] = part


def force_add(g, base, slot, cells, iota):
    val = slot[2]

    def row(n):
        if isinstance(g, int):
            return packed_row(val.at[n], g)
        return jnp.broadcast_to(val[n, pl.ds(g, 1), :], (16, LANES)).astype(jnp.bfloat16)

    rel = row(0) - base.astype(jnp.float32).astype(jnp.bfloat16)
    parts = [[row(2 + 2 * c + n) for c in range(3)] for n in range(2)]
    out = spread_add([spread_rows(rel, parts, iota)], [one_hot_rows(row(1), iota)])
    for c in range(3):
        for half in range(2):
            part = out[16 * c : 16 * c + 16, half * LANES : (half + 1) * LANES]
            cells[2 * c + half, pl.ds(base, 16), :] += part


def force_rest(block, ends, slot, cells, iota):
    @pl.when(ends[16, block * 16] >= 16)
    def _():
        def one(g, carry):
            first, most = ends[0, block * 16 + g], ends[15, block * 16 + g]

            def trip(t, carry):
                force_add(g, jnp.minimum(first + 16 * t, LANES), slot, cells, iota)
                return carry

            lax.fori_loop(1, (most - first) // 16 + 1, trip, 0)
            return carry

        lax.fori_loop(0, 16, one, 0)


def deposit_step(gather, scatter, ends, keys_ref, table_ref, total_ref, cells, iota):
    if gather:
        force_gather(gather[0], keys_ref, table_ref, total_ref, gather[1])
    if scatter:
        for g in range(16):
            force_add(g, ends[0, scatter[0] * 16 + g], scatter[1], cells, iota)
        force_rest(scatter[0], ends, scatter[1], cells, iota)


def inner_deposit_kernel(
    ends, keys_ref, table_ref, corr_ref,
    cells,
    iota, force_a, got_a, val_a, force_b, got_b, val_b,
):
    fill_iota(iota)
    cells[...] = jnp.zeros_like(cells)
    a, b = (force_a, got_a, val_a), (force_b, got_b, val_b)
    step = functools.partial(
        deposit_step, ends=ends, keys_ref=keys_ref, table_ref=table_ref, total_ref=corr_ref,
        cells=cells, iota=iota,
    )
    step((1, a), None)

    def two(k, carry):
        block = 2 * k + 1
        step((block + 1, b), (block, a))
        step((jnp.minimum(block + 2, 6), a), (block + 1, b))
        return carry

    lax.fori_loop(0, 3, two, 0)


def force_slots():
    f32 = jnp.float32
    one = [VMEM((ROWS, ROWS, LANES), f32), VMEM((16, ROWS, LANES), f32), VMEM((8, 16, LANES), f32)]
    return [VMEM((2 * LANES, LANES), jnp.bfloat16)] + one + one


def inner_deposit(ends, keys, table, corr):
    smem, vmem = pl.BlockSpec(memory_space=SMEM), pl.BlockSpec(memory_space=VMEM)
    return pl.pallas_call(
        inner_deposit_kernel,
        name="inner_deposit",
        out_shape=jax.ShapeDtypeStruct((6, 144, LANES), jnp.float32),
        in_specs=[smem, vmem, vmem, vmem],
        scratch_shapes=force_slots(),
        compiler_params=params(),
    )(ends, keys, table, corr)


def edge_deposit_kernel(
    ends, keys_ref, table_ref, corr_ref, lower_ref, upper_ref, inner_ref,
    out_ref, total_ref, first_ref, last_ref,
    cells, iota, force_a, got_a, val_a, force_b, got_b, val_b,
):
    fill_iota(iota)
    cells[...] = inner_ref[...]
    total_ref[...] = corr_ref[...]
    total_ref[:, 0:16, :] += lower_ref[...]
    total_ref[:, 112:128, :] += upper_ref[...]
    a, b = (force_a, got_a, val_a), (force_b, got_b, val_b)
    step = functools.partial(
        deposit_step, ends=ends, keys_ref=keys_ref, table_ref=table_ref, total_ref=total_ref,
        cells=cells, iota=iota,
    )
    step((0, a), None)
    step((7, b), (0, a))
    step(None, (7, b))
    for c in range(3):
        for half in range(2):
            columns = slice(half * LANES, (half + 1) * LANES)
            out_ref[c, :, columns] = cells[2 * c + half, 0:128, :]
            first_ref[c, :, columns] = cells[2 * c + half, 0:32, :]
            last_ref[c, :, columns] = cells[2 * c + half, 96:128, :]


def edge_deposit(ends, keys, table, corr, lower, upper, inner):
    f32 = jnp.float32
    smem, vmem = pl.BlockSpec(memory_space=SMEM), pl.BlockSpec(memory_space=VMEM)
    return pl.pallas_call(
        edge_deposit_kernel,
        name="edge_deposit",
        out_shape=(
            jax.ShapeDtypeStruct((3, 128, 2 * LANES), f32),
            jax.ShapeDtypeStruct((3, 128, LANES), f32),
            jax.ShapeDtypeStruct((3, 32, 2 * LANES), f32),
            jax.ShapeDtypeStruct((3, 32, 2 * LANES), f32),
        ),
        in_specs=[smem] + [vmem] * 6,
        scratch_shapes=[VMEM((6, 144, LANES), f32)] + force_slots(),
        compiler_params=params(),
    )(ends, keys, table, corr, lower, upper, inner)


def axial_kernel(taps, cells_ref, before_ref, after_ref, out_ref, first_ref, last_ref):
    for c in range(3):
        padded = jnp.concatenate([before_ref[c], cells_ref[c], after_ref[c]], axis=0)
        total = taps[0] * padded[0:128]
        for k in range(1, 5):
            total = total + taps[k] * padded[16 * k : 16 * k + 128]
        out_ref[c] = total
        for a in range(8):
            first_ref[c, 2 * a : 2 * a + 2, :] = total[16 * a : 16 * a + 2]
            last_ref[c, 2 * a : 2 * a + 2, :] = total[16 * a + 14 : 16 * a + 16]


def radial_kernel(taps, cells_ref, before_ref, after_ref, out_ref, first_ref, last_ref, padded):
    lane = lax.broadcasted_iota(jnp.int32, (LANES, LANES), 1)
    edges = jnp.zeros((LANES, LANES), jnp.float32)
    for c in range(3):
        for a in range(8):
            padded[0:2, :] = before_ref[c, 2 * a : 2 * a + 2, :]
            padded[2:18, :] = cells_ref[c, 16 * a : 16 * a + 16, :]
            padded[18:20, :] = after_ref[c, 2 * a : 2 * a + 2, :]
            total = taps[0] * padded[0:16, :]
            for k in range(1, 5):
                total = total + taps[k] * padded[k : k + 16, :]
            out_ref[c, 16 * a : 16 * a + 16, :] = total
        left, right = out_ref[c, :, 0:LANES], out_ref[c, :, LANES:]
        if c:
            left = pltpu.roll(left, 2 * c, 1)
        right = pltpu.roll(right, 10 + 2 * c, 1)
        edges = jnp.where((lane >> 1) == c, left, edges)
        edges = jnp.where((lane >> 1) == 4 + c, right, edges)
    turned = edges.T
    first_ref[...] = turned[0:8]
    last_ref[...] = turned[8:16]


def azimuthal_kernel(taps, cells_ref, before_ref, after_ref, out_ref):
    lane = lax.broadcasted_iota(jnp.int32, (LANES, LANES), 1)
    rest = jnp.zeros((LANES - 16, LANES), jnp.float32)
    edges = jnp.concatenate([after_ref[...], before_ref[...], rest], axis=0).T
    for c in range(3):
        ahead = pltpu.roll(edges, LANES - 2 * c, 1) if c else edges
        halo = jnp.where(lane < 64, ahead, pltpu.roll(edges, 118 - 2 * c, 1))
        left, right = cells_ref[c, :, 0:LANES], cells_ref[c, :, LANES:]
        out_left, out_right = taps[2] * left, taps[2] * right
        for k in (1, 2):
            tap = taps[2 + k]
            inner = lane < LANES - k
            x, y, z = (pltpu.roll(v, LANES - k, 1) for v in (left, right, halo))
            out_left = out_left + tap * jnp.where(inner, x, y)
            out_right = out_right + tap * jnp.where(inner, y, z)
            inner = lane >= k
            x, y, z = (pltpu.roll(v, k, 1) for v in (left, right, halo))
            out_left = out_left + tap * jnp.where(inner, x, z)
            out_right = out_right + tap * jnp.where(inner, y, x)
        out_ref[c, :, 0:LANES] = out_left
        out_ref[c, :, LANES:] = out_right


def filtered(deposit, first, last):
    f32 = jnp.float32
    raw = [math.exp(-0.5 * k * k) for k in range(-2, 3)]
    taps = [x / sum(raw) for x in raw]
    whole = jax.ShapeDtypeStruct(deposit.shape, f32)
    radial_face = jax.ShapeDtypeStruct((3, 16, 2 * LANES), f32)
    edge = jax.ShapeDtypeStruct((8, LANES), f32)
    cells, first, last = pl.pallas_call(
        functools.partial(axial_kernel, taps),
        name="axial_filter",
        out_shape=(whole, radial_face, radial_face),
        compiler_params=params(),
    )(deposit, shifted(last, "ax", 1, False), shifted(first, "ax", -1, False))
    cells, first, last = pl.pallas_call(
        functools.partial(radial_kernel, taps),
        name="radial_filter",
        out_shape=(whole, edge, edge),
        scratch_shapes=[VMEM((24, 2 * LANES), f32)],
        compiler_params=params(),
    )(cells, shifted(last, "rad", 1, False), shifted(first, "rad", -1, False))
    return pl.pallas_call(
        functools.partial(azimuthal_kernel, taps),
        name="azimuthal_filter",
        out_shape=whole,
        compiler_params=params(),
    )(cells, shifted(last, "az", 1, True), shifted(first, "az", -1, True))


def shifted(x, axis, by, wrap):
    count = lax.axis_size(axis)
    pairs = [(i, (i + by) % count) for i in range(count)]
    return lax.ppermute(x, axis, [p for p in pairs if wrap or p[1] - p[0] == by])


def per_device(positions, velocity, diameter, cell_index, pair_list, live_pairs, gas_velocity):
    live = live_pairs.reshape(1, 1)
    cells = cell_index.reshape(128, LANES)
    gas = gas_velocity.reshape(3, 128, 2 * LANES)
    pos = positions.reshape(3, 128, LANES)
    vel = velocity.reshape(3, 128, LANES)
    diam = diameter.reshape(128, LANES)
    cell_keys, cell_ends, first, last = edge_states(cells, gas, pos, vel, diam)
    before = shifted(last, "az", 1, True)
    after = shifted(first, "az", -1, True)
    table = inner_states(cell_ends, cell_keys, gas, pos, vel, diam, first, last)
    pair_keys, pair_ends = pair_sort(live, pair_list.reshape(2, 256, LANES))
    corr, lower, upper = pair_forces(live, pair_ends, pair_keys, table, before, after)
    from_upper = shifted(lower, "az", -1, True)
    from_lower = shifted(upper, "az", 1, True)
    inner = inner_deposit(cell_ends, cell_keys, table, corr)
    deposit, correction, first, last = edge_deposit(
        cell_ends, cell_keys, table, corr, from_lower, from_upper, inner
    )
    smoothed = filtered(deposit, first, last)
    return (correction.reshape(positions.shape), smoothed.reshape(gas_velocity.shape))


def solution(mesh):
    return jax.shard_map(
        per_device,
        mesh=mesh,
        in_specs=(
            P(None, "ax", "rad", "az"),
            P(None, "ax", "rad", "az"),
            P("ax", "rad", "az"),
            P("ax", "rad", "az"),
            P(None, "ax", "rad", "az"),
            P("ax", "rad", "az"),
            P(None, "ax", "rad", "az"),
        ),
        out_specs=(P(None, "ax", "rad", "az"), P(None, "ax", "rad", "az")),
        check_vma=False,
    )
```

```python
import functools
import math

import jax
import jax.numpy as jnp
from jax import lax
from jax.experimental import pallas as pl
from jax.experimental.pallas import tpu as pltpu
from jax.sharding import PartitionSpec as P

piep_coef = 1.0
drag_coef = 20.0

LANES = 128
ROWS = 8
BLOCK = 2048
GAS_WINDOW = 10
BUCKET = 1024
BUCKETS = 20
HEAD_WINDOW = 10
DEAD = 1 << 29

NT = (((1,), (1,)), ((), ()))
VMEM = pltpu.VMEM
SMEM = pltpu.SMEM


def params(megabytes=40):
    return pltpu.CompilerParams(vmem_limit_bytes=megabytes << 20)


def lane_gather(table, index):
    numbers = lax.GatherDimensionNumbers(
        offset_dims=(),
        collapsed_slice_dims=(1,),
        start_index_map=(1,),
        operand_batching_dims=(0,),
        start_indices_batching_dims=(0,),
    )
    return lax.gather(
        table,
        index[..., None],
        numbers,
        slice_sizes=(1, 1),
        mode=lax.GatherScatterMode.PROMISE_IN_BOUNDS,
    )


def sort_network(regs, place, levels):
    sub = lax.broadcasted_iota(jnp.int32, (ROWS, LANES), 0)
    lane = lax.broadcasted_iota(jnp.int32, (ROWS, LANES), 1)
    count = len(regs)

    def bit_fill(bit, v):
        if bit >= levels:
            return 0
        kind, k = place[bit]
        if kind == "v":
            return -((v >> k) & 1)
        return -(((sub if kind == "s" else lane) >> k) & 1)

    flip = [0] * count
    for level in range(1, levels + 1):
        fills = {}
        for v in range(count):
            kind, k = place[level] if level < levels else ("v", 99)
            key = (v >> k) & 1 if kind == "v" else 0
            if key not in fills:
                fills[key] = bit_fill(level, v)
            new = fills[key]
            if isinstance(new, int) and isinstance(flip[v], int):
                if new != flip[v]:
                    regs[v] = ~regs[v]
            else:
                regs[v] = regs[v] ^ (new ^ flip[v])
            flip[v] = new
        for bit in reversed(range(level)):
            kind, k = place[bit]
            step = 1 << k
            if kind == "v":
                for v in range(count):
                    if not v & step:
                        a, b = regs[v], regs[v | step]
                        regs[v], regs[v | step] = jnp.minimum(a, b), jnp.maximum(a, b)
            else:
                axis, size, where = (0, ROWS, sub) if kind == "s" else (1, LANES, lane)
                lower = (where & step) == 0
                for v in range(count):
                    x = regs[v]
                    ahead = pltpu.roll(x, size - step, axis)
                    behind = ahead if 2 * step == size else pltpu.roll(x, step, axis)
                    regs[v] = jnp.where(lower, jnp.minimum(x, ahead), jnp.maximum(x, behind))
    return regs


def split_two(x):
    high = x.astype(jnp.bfloat16).astype(jnp.float32)
    return high, x - high


def split_three(x):
    high, rest = split_two(x)
    mid, low = split_two(rest)
    return high, mid, low


def packed_row(ref, row):
    return jnp.broadcast_to(ref[row : row + 1, :], (16, LANES)).astype(jnp.bfloat16)


def one_hot_rows(low, iota):
    one = jnp.ones((16, LANES), jnp.bfloat16)
    zero = jnp.zeros((16, LANES), jnp.bfloat16)
    return jnp.concatenate(
        [jnp.where(low == iota[k : k + 16, :], one, zero) for k in range(0, iota.shape[0], 16)],
        axis=0,
    )


def spread_rows(rel, parts, iota):
    hit = rel == iota[0:16, :]
    zero = jnp.zeros((16, LANES), jnp.bfloat16)
    return jnp.concatenate([jnp.where(hit, p, zero) for part in parts for p in part], axis=0)


def spread_add(rows, hots):
    out = lax.dot_general(
        jnp.concatenate(rows, axis=1) if len(rows) > 1 else rows[0],
        jnp.concatenate(hots, axis=1) if len(hots) > 1 else hots[0],
        NT,
        preferred_element_type=jnp.float32,
    )
    total = out[0:48]
    for s in range(48, out.shape[0], 48):
        total = total + out[s : s + 48]
    return total


def fill_iota(iota):
    rows = lax.broadcasted_iota(jnp.int32, iota.shape, 0)
    iota[...] = rows.astype(jnp.float32).astype(jnp.bfloat16)


def rows_of(block):
    start = block * 16
    return pl.ds(start if isinstance(block, int) else pl.multiple_of(start, 16), 16)


def wide(ref, *at):
    return jnp.broadcast_to(ref[at[:-1] + (slice(at[-1], at[-1] + 1),)], (ROWS, LANES))


def window(table, first, count, row, low, found):
    rel = row - first
    for u in range(count):
        found = jnp.where(rel == u, lane_gather(table[first + u], low), found)
    return found


def running_max(x, count):
    x = jnp.broadcast_to(x, (ROWS, LANES))
    step = 1
    while step < count:
        x = jnp.maximum(x, pltpu.roll(x, LANES - step, 1))
        step *= 2
    return x


def fill_gas_rows(gas_ref, gas_rows):
    for r in range(16):
        rows = slice(r * ROWS, (r + 1) * ROWS)
        for c in range(3):
            for half in range(2):
                gas_rows[rows, half * 4 + c, :] = gas_ref[c, rows, half * LANES : (half + 1) * LANES]


def gas_index(block, keys_ref, slot):
    idx = slot[0]
    keys = keys_ref[rows_of(block), :]
    idx[0] = lax.shift_right_logical(keys, 19)
    idx[1] = lax.shift_right_logical(keys, 11) & (LANES - 1)


def gas_gather(block, g, ends, gas_rows, slot):
    idx, found = slot[0], slot[1]
    zero = jnp.zeros((ROWS, LANES), jnp.float32)
    first = ends[0, block * 16 + g]
    found[g] = window(gas_rows, first, GAS_WINDOW, wide(idx, 0, g), wide(idx, 1, g), zero)


def gas_rest(block, ends, gas_rows, slot):
    idx, found = slot[0], slot[1]

    @pl.when(ends[16, block * 16] >= GAS_WINDOW)
    def _():
        def one(g, carry):
            first = ends[0, block * 16 + g]
            row = jnp.broadcast_to(idx[0, pl.ds(g, 1), :], (ROWS, LANES))
            low = jnp.broadcast_to(idx[1, pl.ds(g, 1), :], (ROWS, LANES))

            def trip(t, total):
                base = jnp.minimum(first + GAS_WINDOW * t, LANES)
                return window(gas_rows, base, GAS_WINDOW, row, low, total)

            trips = (ends[15, block * 16 + g] - first) // GAS_WINDOW + 1
            found[g] = lax.fori_loop(1, trips, trip, found[g])
            return carry

        lax.fori_loop(0, 16, one, 0)


def seen_values(block, keys_ref, slot):
    idx, found, val = slot
    keys = keys_ref[rows_of(block), :]
    upper = (keys & (1 << 18)) != 0
    place_in = keys & (BLOCK - 1)
    val[0] = lax.shift_right_logical(place_in, 7).astype(jnp.float32)
    val[1] = (place_in & (LANES - 1)).astype(jnp.float32)
    for c in range(3):
        seen = jnp.where(upper, found[:, 4 + c, :], found[:, c, :])
        for n, part in enumerate(split_three(seen)):
            val[2 + 3 * c + n] = part


def seen_in_order(groups, slot, iota):
    val = slot[2]
    rows, hots = [], []
    for g in groups:
        parts = [[packed_row(val.at[2 + 3 * c + n], g) for c in range(3)] for n in range(3)]
        rows.append(spread_rows(packed_row(val.at[0], g), parts, iota))
        hots.append(one_hot_rows(packed_row(val.at[1], g), iota))
    return spread_add(rows, hots)


def write_states(block, total, pos_ref, vel_ref, diam_ref, out_ref, out_rows):
    rows = rows_of(block)
    for c in range(3):
        out_ref[out_rows, c, :] = pos_ref[c, rows, :]
        out_ref[out_rows, 3 + c, :] = total[16 * c : 16 * c + 16] - vel_ref[c, rows, :]
    out_ref[out_rows, 6, :] = 0.5 * diam_ref[rows, :]
    out_ref[out_rows, 7, :] = jnp.zeros((16, LANES), jnp.float32)


def states_step(gather, scatter, keys_ref, ends, gas_rows, iota, arrays):
    total = jnp.zeros((48, LANES), jnp.float32)
    if gather:
        gas_index(gather[0], keys_ref, gather[1])
    if scatter:
        seen_values(scatter[0], keys_ref, scatter[1])
    for g in range(16):
        if gather:
            gas_gather(gather[0], g, ends, gas_rows, gather[1])
        if scatter and g % 2:
            total = total + seen_in_order((g - 1, g), scatter[1], iota)
    if scatter:
        write_states(scatter[0], total, *arrays, *scatter[2:])
    if gather:
        gas_rest(gather[0], ends, gas_rows, gather[1])


def edge_states_kernel(
    cell_hbm, gas_hbm, pos_hbm, vel_hbm, diam_hbm,
    keys_ref, ends_ref, first_ref, last_ref,
    cell_ref, gas_ref, pos_ref, vel_ref, diam_ref,
    gas_rows, iota, ends, idx_a, found_a, val_a, idx_b, found_b, val_b, sems,
):
    sources = (cell_hbm, gas_hbm, pos_hbm, vel_hbm, diam_hbm)
    places = (cell_ref, gas_ref, pos_ref, vel_ref, diam_ref)
    copies = [
        pltpu.make_async_copy(x, y, sems.at[n]) for n, (x, y) in enumerate(zip(sources, places))
    ]
    for copy in copies:
        copy.start()
    copies[0].wait()
    sub = lax.broadcasted_iota(jnp.int32, (ROWS, LANES), 0)
    lane = lax.broadcasted_iota(jnp.int32, (ROWS, LANES), 1)
    regs = []
    for v in range(16):
        own = (v % 2) * 1024 + sub * LANES + lane
        regs.append(cell_ref[v * ROWS : (v + 1) * ROWS, :] * BLOCK + own)
    place = [("l", k) for k in range(7)] + [("s", k) for k in range(3)] + [("v", 0)]
    regs = sort_network(regs, place, 11)
    keys = jnp.concatenate(regs, axis=0)
    keys_ref[...] = keys
    turned = lax.shift_right_logical(keys, 19).T
    ends_ref[0:8, :] = turned[0:8]
    ends_ref[8:16, :] = turned[120:128]
    ends_ref[16:24, :] = running_max(turned[127:128] - turned[0:1], 16)
    copy = pltpu.make_async_copy(ends_ref, ends, sems.at[5])
    copy.start()
    copies[1].wait()
    fill_gas_rows(gas_ref, gas_rows)
    for other in copies[2:]:
        other.wait()
    copy.wait()
    fill_iota(iota)
    a, b = (idx_a, found_a, val_a), (idx_b, found_b, val_b)
    whole = slice(0, 16)
    step = functools.partial(
        states_step, keys_ref=keys_ref, ends=ends, gas_rows=gas_rows, iota=iota,
        arrays=(pos_ref, vel_ref, diam_ref),
    )
    step((0, a), None)
    step((7, b), (0, a, first_ref, whole))
    step(None, (7, b, last_ref, whole))


def slots(rows, parts, dtype=jnp.float32):
    one = [VMEM((2, 16, LANES), jnp.int32), VMEM((16, ROWS, LANES), dtype), VMEM((parts, rows, LANES), dtype)]
    return one + one


def edge_states(cells, gas, pos, vel, diam):
    f32, i32 = jnp.float32, jnp.int32
    arrays = (cells, gas, pos, vel, diam)
    return pl.pallas_call(
        edge_states_kernel,
        name="edge_states",
        out_shape=(
            jax.ShapeDtypeStruct((128, LANES), i32),
            jax.ShapeDtypeStruct((24, LANES), i32),
            jax.ShapeDtypeStruct((16, ROWS, LANES), f32),
            jax.ShapeDtypeStruct((16, ROWS, LANES), f32),
        ),
        in_specs=[pl.BlockSpec(memory_space=pltpu.HBM)] * 5,
        scratch_shapes=[VMEM(x.shape, x.dtype) for x in arrays]
        + [VMEM((144, ROWS, LANES), f32), VMEM((LANES, LANES), jnp.bfloat16), SMEM((24, LANES), i32)]
        + slots(16, 11)
        + [pltpu.SemaphoreType.DMA((6,))],
        compiler_params=params(60),
    )(*arrays)


def inner_states_kernel(
    ends, keys_ref, gas_ref, pos_ref, vel_ref, diam_ref, first_ref, last_ref,
    table_ref,
    gas_rows, iota, idx_a, found_a, val_a, idx_b, found_b, val_b,
):
    fill_gas_rows(gas_ref, gas_rows)
    fill_iota(iota)
    a, b = (idx_a, found_a, val_a), (idx_b, found_b, val_b)
    step = functools.partial(
        states_step, keys_ref=keys_ref, ends=ends, gas_rows=gas_rows, iota=iota,
        arrays=(pos_ref, vel_ref, diam_ref),
    )
    table_ref[0:16] = first_ref[...]
    table_ref[112:128] = last_ref[...]
    step((1, a), None)

    def two(k, carry):
        block = 2 * k + 1
        step((block + 1, b), (block, a, table_ref, rows_of(block)))
        step((jnp.minimum(block + 2, 6), a), (block + 1, b, table_ref, rows_of(block + 1)))
        return carry

    lax.fori_loop(0, 3, two, 0)


def inner_states(ends, keys, gas, pos, vel, diam, first, last):
    f32 = jnp.float32
    return pl.pallas_call(
        inner_states_kernel,
        name="inner_states",
        out_shape=jax.ShapeDtypeStruct((128, ROWS, LANES), f32),
        in_specs=[pl.BlockSpec(memory_space=SMEM)] + [pl.BlockSpec(memory_space=VMEM)] * 7,
        scratch_shapes=[VMEM((144, ROWS, LANES), f32), VMEM((LANES, LANES), jnp.bfloat16)]
        + slots(16, 11),
        compiler_params=params(),
    )(ends, keys, gas, pos, vel, diam, first, last)


def pair_sort_kernel(live_ref, pairs_ref, keys_ref, ends_ref):
    live = live_ref[0, 0]
    sub = lax.broadcasted_iota(jnp.int32, (ROWS, LANES), 0)
    lane = lax.broadcasted_iota(jnp.int32, (ROWS, LANES), 1)
    regs = []
    for v in range(32):
        rows = slice(v * ROWS, (v + 1) * ROWS)
        slot = v * 1024 + sub * LANES + lane
        head = pairs_ref[0, rows, :]
        tail = pairs_ref[1, rows, :] - 7 * BLOCK
        own = tail - BLOCK
        inside = (own >= 0) & (own < 8 * BLOCK)
        tail = jnp.where(inside, jnp.maximum(own, head) + BLOCK, tail)
        head = jnp.where(inside, jnp.minimum(own, head), head)
        bucket = lax.shift_right_logical(tail, 10)
        turn = -(bucket & 1) & (8 * BLOCK - 1)
        key = (bucket << 24) | ((head ^ turn) << 10) | (tail & (BUCKET - 1))
        regs.append(jnp.where(slot < live, key, DEAD))
    place = (
        [("v", k) for k in range(4)]
        + [("s", k) for k in range(3)]
        + [("v", 4)]
        + [("l", k) for k in range(7)]
    )
    regs = sort_network(regs, place, 15)
    for half in range(2):
        rows = regs[16 * half : 16 * half + 16]
        keys_ref[half] = jnp.concatenate(rows, axis=0).T
        least_head = least_tail = jnp.full((ROWS, LANES), 1 << 20, jnp.int32)
        most_head = most_tail = jnp.full((ROWS, LANES), -1, jnp.int32)
        for key in rows:
            used = key < DEAD
            bucket = lax.shift_right_logical(key, 24)
            head = lax.shift_right_logical(key, 17) & (LANES - 1)
            head = head ^ (-(bucket & 1) & (LANES - 1))
            least_head = jnp.minimum(least_head, jnp.where(used, head, 1 << 20))
            most_head = jnp.maximum(most_head, jnp.where(used, head, -1))
            least_tail = jnp.minimum(least_tail, jnp.where(used, bucket, 1 << 20))
            most_tail = jnp.maximum(most_tail, jnp.where(used, bucket, -1))
        for n, x in enumerate((least_head, most_head, least_tail, most_tail)):
            reduce = jnp.max if n % 2 else jnp.min
            row = 4 * half + n
            bound = (LANES, LANES, BUCKETS, BUCKETS)[n]
            ends_ref[row : row + 1, :] = jnp.minimum(reduce(x, axis=0, keepdims=True), bound)


def pair_sort(live, pairs):
    return pl.pallas_call(
        pair_sort_kernel,
        name="pair_sort",
        out_shape=(
            jax.ShapeDtypeStruct((2, LANES, LANES), jnp.int32),
            jax.ShapeDtypeStruct((ROWS, LANES), jnp.int32),
        ),
        in_specs=[pl.BlockSpec(memory_space=SMEM), pl.BlockSpec(memory_space=VMEM)],
        compiler_params=params(),
    )(live, pairs)


def take_items(state, groups, ends):
    items = []
    for _ in range(ROWS):
        g, bucket, head = state
        valid = g < groups
        seen = jnp.minimum(g, 2 * LANES - 1)
        at, lane = 4 * (seen & 1), seen >> 1
        items.append((seen, jnp.where(valid, bucket, -1), head, bucket * 8))
        more_heads = head + HEAD_WINDOW <= ends[at + 1, lane]
        more_tails = bucket < ends[at + 3, lane]
        step = jnp.where(more_heads | more_tails, 0, 1)
        g = jnp.minimum(g + step, 2 * LANES)
        seen = jnp.minimum(g, 2 * LANES - 1)
        at, lane = 4 * (seen & 1), seen >> 1
        head = jnp.where(more_heads, head + HEAD_WINDOW, ends[at, lane])
        same = jnp.where(more_heads, bucket, bucket + 1)
        bucket = jnp.where(step == 1, ends[at + 2, lane], same)
        state = (g, bucket, head)
    return items, state


def pair_gather(k, item, keys_ref, table, slot):
    key_rows, rel_rows, near, far = slot[0:4]
    g, bucket, first, tail_first = item
    keys = jnp.broadcast_to(keys_ref[g & 1, pl.ds(g >> 1, 1), :], (ROWS, LANES))
    of_bucket = lax.shift_right_logical(keys, 24)
    turn = -(of_bucket & 1) & (8 * BLOCK - 1)
    head = (lax.shift_right_logical(keys, 10) & (8 * BLOCK - 1)) ^ turn
    rel = lax.shift_right_logical(head, 7) - first
    tail_row = lax.shift_right_logical(keys, 7) & 7
    used = (of_bucket == bucket) & (rel >= 0) & (rel < HEAD_WINDOW)
    key_rows[k : k + 1, :] = jnp.where(used, keys, DEAD)[0:1]
    rel_rows[k : k + 1, :] = rel[0:1]
    zero = jnp.zeros((ROWS, LANES), jnp.float32)
    low = head & (LANES - 1)
    found = zero
    for u in range(HEAD_WINDOW):
        found = jnp.where(rel == u, lane_gather(table[16 + first + u], low), found)
    near[k] = found
    low = keys & (LANES - 1)
    found = zero
    for u in range(8):
        found = jnp.where(tail_row == u, lane_gather(table[tail_first + u], low), found)
    far[k] = found


def pair_values(slot):
    key_rows, rel_rows, near, far, val = slot
    keys = key_rows[...]
    used = keys < DEAD
    turn = -(lax.shift_right_logical(keys, 24) & 1) & (LANES - 1)
    val[0] = rel_rows[...].astype(jnp.float32)
    val[1] = ((lax.shift_right_logical(keys, 10) & (LANES - 1)) ^ turn).astype(jnp.float32)
    val[2] = (lax.shift_right_logical(keys, 7) & 7).astype(jnp.float32)
    val[3] = (keys & (LANES - 1)).astype(jnp.float32)
    gap = jnp.zeros((ROWS, LANES), jnp.float32)
    for c in range(3):
        apart = far[:, c, :] - near[:, c, :]
        gap = gap + apart * apart
    far_radius, near_radius = far[:, 6, :], near[:, 6, :]
    far_ratio = far_radius * lax.rsqrt(gap + far_radius * far_radius)
    near_ratio = near_radius * lax.rsqrt(gap + near_radius * near_radius)
    weight_far = jnp.where(used, piep_coef * far_ratio * far_ratio * far_ratio, 0.0)
    weight_near = jnp.where(used, piep_coef * near_ratio * near_ratio * near_ratio, 0.0)
    for c in range(3):
        for n, part in enumerate(split_two(weight_far * far[:, 3 + c, :])):
            val[4 + 3 * n + c] = part
        for n, part in enumerate(split_two(weight_near * near[:, 3 + c, :])):
            val[10 + 3 * n + c] = part


def pair_scatter(k, item, slot, head_sum, tail_sum, iota, iota8):
    val = slot[4]
    first, tail_first = item
    parts = [[packed_row(val.at[4 + 3 * n + c], k) for c in range(3)] for n in range(2)]
    rows = spread_rows(packed_row(val.at[0], k), parts, iota)
    out = spread_add([rows], [one_hot_rows(packed_row(val.at[1], k), iota)])
    for c in range(3):
        head_sum[c, pl.ds(first, 16), :] += out[16 * c : 16 * c + 16]

    hit = packed_row(val.at[2], k) == iota8[...]
    zero = jnp.zeros((16, LANES), jnp.bfloat16)
    tiles = []
    for n in range(10, 16, 2):
        both = jnp.concatenate([wide(val, n, k), wide(val, n + 1, k)], axis=0)
        tiles.append(jnp.where(hit, both.astype(jnp.bfloat16), zero))
    out = lax.dot_general(
        jnp.concatenate(tiles, axis=0),
        one_hot_rows(packed_row(val.at[3], k), iota),
        NT,
        preferred_element_type=jnp.float32,
    )
    at = pl.ds(pl.multiple_of(tail_first, 8), 8)
    for c in range(3):
        tail_sum[c, at, :] += out[8 * c : 8 * c + 8] + out[24 + 8 * c : 32 + 8 * c]


def pair_kernel(
    live_ref, ends, keys_ref, own_ref, before_ref, after_ref,
    corr_ref, lower_ref, upper_ref,
    table, head_sum, tail_sum, iota, iota8,
    key_a, rel_a, near_a, far_a, val_a, key_b, rel_b, near_b, far_b, val_b,
):
    table[0:16] = before_ref[...]
    table[16:144] = own_ref[...]
    table[144:160] = after_ref[...]
    table[160:168] = jnp.zeros((8, ROWS, LANES), jnp.float32)
    head_sum[...] = jnp.zeros_like(head_sum)
    tail_sum[...] = jnp.zeros_like(tail_sum)
    fill_iota(iota)
    rows = lax.broadcasted_iota(jnp.int32, iota8.shape, 0) & 7
    iota8[...] = rows.astype(jnp.float32).astype(jnp.bfloat16)
    a = (key_a, rel_a, near_a, far_a, val_a)
    b = (key_b, rel_b, near_b, far_b, val_b)
    groups = (live_ref[0, 0] + LANES - 1) // LANES

    def step(state, slot, pending, other):
        items, state = take_items(state, groups, ends)
        if other:
            pair_values(other)
        for k in range(ROWS):
            pair_gather(k, items[k], keys_ref, table, slot)
            if other:
                pair_scatter(k, pending[k], other, head_sum, tail_sum, iota, iota8)
        return tuple(item[2:4] for item in items), state, items[0][1] >= 0

    start = (jnp.int32(0), ends[2, 0], ends[0, 0])
    carry = step(start, a, None, None)

    def two(carry):
        pending, state, _ = carry
        pending, state, _ = step(state, b, pending, a)
        return step(state, a, pending, b)

    lax.while_loop(lambda carry: carry[2], two, carry)
    corr_ref[...] = head_sum[:, 0:128, :] + tail_sum[:, 16:144, :]
    lower_ref[...] = tail_sum[:, 0:16, :]
    upper_ref[...] = tail_sum[:, 144:160, :]


def pair_forces(live, ends, keys, own, before, after):
    f32, i32 = jnp.float32, jnp.int32
    smem, vmem = pl.BlockSpec(memory_space=SMEM), pl.BlockSpec(memory_space=VMEM)
    slot = [
        VMEM((ROWS, LANES), i32),
        VMEM((ROWS, LANES), i32),
        VMEM((ROWS, ROWS, LANES), f32),
        VMEM((ROWS, ROWS, LANES), f32),
        VMEM((16, ROWS, LANES), f32),
    ]
    return pl.pallas_call(
        pair_kernel,
        name="pair_forces",
        out_shape=(
            jax.ShapeDtypeStruct((3, 128, LANES), f32),
            jax.ShapeDtypeStruct((3, 16, LANES), f32),
            jax.ShapeDtypeStruct((3, 16, LANES), f32),
        ),
        in_specs=[smem, smem, vmem, vmem, vmem, vmem],
        scratch_shapes=[
            VMEM((168, ROWS, LANES), f32),
            VMEM((3, 144, LANES), f32),
            VMEM((3, 168, LANES), f32),
            VMEM((LANES, LANES), jnp.bfloat16),
            VMEM((16, LANES), jnp.bfloat16),
        ]
        + slot
        + slot,
        compiler_params=params(),
    )(live, ends, keys, own, before, after)


def force_gather(block, keys_ref, table_ref, total_ref, slot):
    force, got, val = slot
    rows = rows_of(block)
    scale = (-2.0 * drag_coef) * table_ref[rows, 6, :]
    for c in range(3):
        push = scale * (table_ref[rows, 3 + c, :] + total_ref[c, rows, :])
        force[:, c, :] = push[0:8]
        force[:, 4 + c, :] = push[8:16]
    keys = keys_ref[rows, :]
    val[0] = lax.shift_right_logical(keys, 19).astype(jnp.float32)
    val[1] = (lax.shift_right_logical(keys, 11) & (2 * LANES - 1)).astype(jnp.float32)
    inner = lax.shift_right_logical(keys, 7) & 7
    low = keys & (LANES - 1)
    tables = [force[k] for k in range(ROWS)]
    for g in range(16):
        pick = jnp.broadcast_to(inner[g : g + 1, :], (ROWS, LANES))
        at = jnp.broadcast_to(low[g : g + 1, :], (ROWS, LANES))
        found = jnp.zeros((ROWS, LANES), jnp.float32)
        for k in range(ROWS):
            found = jnp.where(pick == k, lane_gather(tables[k], at), found)
        got[g] = found
    upper = (keys & 1024) != 0
    for c in range(3):
        pushed = jnp.where(upper, got[:, 4 + c, :], got[:, c, :])
        for n, part in enumerate(split_two(pushed)):
            val[2 + 2 * c + n] = part


def force_add(g, base, slot, cells, iota):
    val = slot[2]

    def row(n):
        if isinstance(g, int):
            return packed_row(val.at[n], g)
        return jnp.broadcast_to(val[n, pl.ds(g, 1), :], (16, LANES)).astype(jnp.bfloat16)

    rel = row(0) - base.astype(jnp.float32).astype(jnp.bfloat16)
    parts = [[row(2 + 2 * c + n) for c in range(3)] for n in range(2)]
    out = spread_add([spread_rows(rel, parts, iota)], [one_hot_rows(row(1), iota)])
    for c in range(3):
        for half in range(2):
            part = out[16 * c : 16 * c + 16, half * LANES : (half + 1) * LANES]
            cells[2 * c + half, pl.ds(base, 16), :] += part


def force_rest(block, ends, slot, cells, iota):
    @pl.when(ends[16, block * 16] >= 16)
    def _():
        def one(g, carry):
            first, most = ends[0, block * 16 + g], ends[15, block * 16 + g]

            def trip(t, carry):
                force_add(g, jnp.minimum(first + 16 * t, LANES), slot, cells, iota)
                return carry

            lax.fori_loop(1, (most - first) // 16 + 1, trip, 0)
            return carry

        lax.fori_loop(0, 16, one, 0)


def deposit_step(gather, scatter, ends, keys_ref, table_ref, total_ref, cells, iota):
    if gather:
        force_gather(gather[0], keys_ref, table_ref, total_ref, gather[1])
    if scatter:
        for g in range(16):
            force_add(g, ends[0, scatter[0] * 16 + g], scatter[1], cells, iota)
        force_rest(scatter[0], ends, scatter[1], cells, iota)


def inner_deposit_kernel(
    ends, keys_ref, table_ref, corr_ref,
    cells,
    iota, force_a, got_a, val_a, force_b, got_b, val_b,
):
    fill_iota(iota)
    cells[...] = jnp.zeros_like(cells)
    a, b = (force_a, got_a, val_a), (force_b, got_b, val_b)
    step = functools.partial(
        deposit_step, ends=ends, keys_ref=keys_ref, table_ref=table_ref, total_ref=corr_ref,
        cells=cells, iota=iota,
    )
    step((1, a), None)

    def two(k, carry):
        block = 2 * k + 1
        step((block + 1, b), (block, a))
        step((jnp.minimum(block + 2, 6), a), (block + 1, b))
        return carry

    lax.fori_loop(0, 3, two, 0)


def force_slots():
    f32 = jnp.float32
    one = [VMEM((ROWS, ROWS, LANES), f32), VMEM((16, ROWS, LANES), f32), VMEM((8, 16, LANES), f32)]
    return [VMEM((2 * LANES, LANES), jnp.bfloat16)] + one + one


def inner_deposit(ends, keys, table, corr):
    smem, vmem = pl.BlockSpec(memory_space=SMEM), pl.BlockSpec(memory_space=VMEM)
    return pl.pallas_call(
        inner_deposit_kernel,
        name="inner_deposit",
        out_shape=jax.ShapeDtypeStruct((6, 144, LANES), jnp.float32),
        in_specs=[smem, vmem, vmem, vmem],
        scratch_shapes=force_slots(),
        compiler_params=params(),
    )(ends, keys, table, corr)


def edge_deposit_kernel(
    ends, keys_ref, table_ref, corr_ref, lower_ref, upper_ref, inner_ref,
    out_ref, total_ref, first_ref, last_ref,
    cells, iota, force_a, got_a, val_a, force_b, got_b, val_b,
):
    fill_iota(iota)
    cells[...] = inner_ref[...]
    total_ref[...] = corr_ref[...]
    total_ref[:, 0:16, :] += lower_ref[...]
    total_ref[:, 112:128, :] += upper_ref[...]
    a, b = (force_a, got_a, val_a), (force_b, got_b, val_b)
    step = functools.partial(
        deposit_step, ends=ends, keys_ref=keys_ref, table_ref=table_ref, total_ref=total_ref,
        cells=cells, iota=iota,
    )
    step((0, a), None)
    step((7, b), (0, a))
    step(None, (7, b))
    for c in range(3):
        for half in range(2):
            columns = slice(half * LANES, (half + 1) * LANES)
            out_ref[c, :, columns] = cells[2 * c + half, 0:128, :]
            first_ref[c, :, columns] = cells[2 * c + half, 0:32, :]
            last_ref[c, :, columns] = cells[2 * c + half, 96:128, :]


def edge_deposit(ends, keys, table, corr, lower, upper, inner):
    f32 = jnp.float32
    smem, vmem = pl.BlockSpec(memory_space=SMEM), pl.BlockSpec(memory_space=VMEM)
    return pl.pallas_call(
        edge_deposit_kernel,
        name="edge_deposit",
        out_shape=(
            jax.ShapeDtypeStruct((3, 128, 2 * LANES), f32),
            jax.ShapeDtypeStruct((3, 128, LANES), f32),
            jax.ShapeDtypeStruct((3, 32, 2 * LANES), f32),
            jax.ShapeDtypeStruct((3, 32, 2 * LANES), f32),
        ),
        in_specs=[smem] + [vmem] * 6,
        scratch_shapes=[VMEM((6, 144, LANES), f32)] + force_slots(),
        compiler_params=params(),
    )(ends, keys, table, corr, lower, upper, inner)


def axial_kernel(taps, cells_ref, before_ref, after_ref, out_ref, first_ref, last_ref):
    for c in range(3):
        padded = jnp.concatenate([before_ref[c], cells_ref[c], after_ref[c]], axis=0)
        total = taps[0] * padded[0:128]
        for k in range(1, 5):
            total = total + taps[k] * padded[16 * k : 16 * k + 128]
        out_ref[c] = total
        for a in range(8):
            first_ref[c, 2 * a : 2 * a + 2, :] = total[16 * a : 16 * a + 2]
            last_ref[c, 2 * a : 2 * a + 2, :] = total[16 * a + 14 : 16 * a + 16]


def radial_kernel(taps, cells_ref, before_ref, after_ref, out_ref, first_ref, last_ref, padded):
    lane = lax.broadcasted_iota(jnp.int32, (LANES, LANES), 1)
    edges = jnp.zeros((LANES, LANES), jnp.float32)
    for c in range(3):
        for a in range(8):
            padded[0:2, :] = before_ref[c, 2 * a : 2 * a + 2, :]
            padded[2:18, :] = cells_ref[c, 16 * a : 16 * a + 16, :]
            padded[18:20, :] = after_ref[c, 2 * a : 2 * a + 2, :]
            total = taps[0] * padded[0:16, :]
            for k in range(1, 5):
                total = total + taps[k] * padded[k : k + 16, :]
            out_ref[c, 16 * a : 16 * a + 16, :] = total
        left, right = out_ref[c, :, 0:LANES], out_ref[c, :, LANES:]
        if c:
            left = pltpu.roll(left, 2 * c, 1)
        right = pltpu.roll(right, 10 + 2 * c, 1)
        edges = jnp.where((lane >> 1) == c, left, edges)
        edges = jnp.where((lane >> 1) == 4 + c, right, edges)
    turned = edges.T
    first_ref[...] = turned[0:8]
    last_ref[...] = turned[8:16]


def azimuthal_kernel(taps, cells_ref, before_ref, after_ref, out_ref):
    lane = lax.broadcasted_iota(jnp.int32, (LANES, LANES), 1)
    rest = jnp.zeros((LANES - 16, LANES), jnp.float32)
    edges = jnp.concatenate([after_ref[...], before_ref[...], rest], axis=0).T
    for c in range(3):
        ahead = pltpu.roll(edges, LANES - 2 * c, 1) if c else edges
        halo = jnp.where(lane < 64, ahead, pltpu.roll(edges, 118 - 2 * c, 1))
        left, right = cells_ref[c, :, 0:LANES], cells_ref[c, :, LANES:]
        out_left, out_right = taps[2] * left, taps[2] * right
        for k in (1, 2):
            tap = taps[2 + k]
            inner = lane < LANES - k
            x, y, z = (pltpu.roll(v, LANES - k, 1) for v in (left, right, halo))
            out_left = out_left + tap * jnp.where(inner, x, y)
            out_right = out_right + tap * jnp.where(inner, y, z)
            inner = lane >= k
            x, y, z = (pltpu.roll(v, k, 1) for v in (left, right, halo))
            out_left = out_left + tap * jnp.where(inner, x, z)
            out_right = out_right + tap * jnp.where(inner, y, x)
        out_ref[c, :, 0:LANES] = out_left
        out_ref[c, :, LANES:] = out_right


def filtered(deposit, first, last):
    f32 = jnp.float32
    raw = [math.exp(-0.5 * k * k) for k in range(-2, 3)]
    taps = [x / sum(raw) for x in raw]
    whole = jax.ShapeDtypeStruct(deposit.shape, f32)
    radial_face = jax.ShapeDtypeStruct((3, 16, 2 * LANES), f32)
    edge = jax.ShapeDtypeStruct((8, LANES), f32)
    cells, first, last = pl.pallas_call(
        functools.partial(axial_kernel, taps),
        name="axial_filter",
        out_shape=(whole, radial_face, radial_face),
        compiler_params=params(),
    )(deposit, shifted(last, "ax", 1, False), shifted(first, "ax", -1, False))
    cells, first, last = pl.pallas_call(
        functools.partial(radial_kernel, taps),
        name="radial_filter",
        out_shape=(whole, edge, edge),
        scratch_shapes=[VMEM((24, 2 * LANES), f32)],
        compiler_params=params(),
    )(cells, shifted(last, "rad", 1, False), shifted(first, "rad", -1, False))
    return pl.pallas_call(
        functools.partial(azimuthal_kernel, taps),
        name="azimuthal_filter",
        out_shape=whole,
        compiler_params=params(),
    )(cells, shifted(last, "az", 1, True), shifted(first, "az", -1, True))


def shifted(x, axis, by, wrap):
    count = lax.axis_size(axis)
    pairs = [(i, (i + by) % count) for i in range(count)]
    return lax.ppermute(x, axis, [p for p in pairs if wrap or p[1] - p[0] == by])


def per_device(positions, velocity, diameter, cell_index, pair_list, live_pairs, gas_velocity):
    live = live_pairs.reshape(1, 1)
    cells = cell_index.reshape(128, LANES)
    gas = gas_velocity.reshape(3, 128, 2 * LANES)
    pos = positions.reshape(3, 128, LANES)
    vel = velocity.reshape(3, 128, LANES)
    diam = diameter.reshape(128, LANES)
    cell_keys, cell_ends, first, last = edge_states(cells, gas, pos, vel, diam)
    before = shifted(last, "az", 1, True)
    after = shifted(first, "az", -1, True)
    table = inner_states(cell_ends, cell_keys, gas, pos, vel, diam, first, last)
    pair_keys, pair_ends = pair_sort(live, pair_list.reshape(2, 256, LANES))
    corr, lower, upper = pair_forces(live, pair_ends, pair_keys, table, before, after)
    from_upper = shifted(lower, "az", -1, True)
    from_lower = shifted(upper, "az", 1, True)
    inner = inner_deposit(cell_ends, cell_keys, table, corr)
    deposit, correction, first, last = edge_deposit(
        cell_ends, cell_keys, table, corr, from_lower, from_upper, inner
    )
    smoothed = filtered(deposit, first, last)
    return (correction.reshape(positions.shape), smoothed.reshape(gas_velocity.shape))


def solution(mesh):
    return jax.shard_map(
        per_device,
        mesh=mesh,
        in_specs=(
            P(None, "ax", "rad", "az"),
            P(None, "ax", "rad", "az"),
            P("ax", "rad", "az"),
            P("ax", "rad", "az"),
            P(None, "ax", "rad", "az"),
            P("ax", "rad", "az"),
            P(None, "ax", "rad", "az"),
        ),
        out_specs=(P(None, "ax", "rad", "az"), P(None, "ax", "rad", "az")),
        check_vma=False,
    )
```

```python
import functools
import math

import jax
import jax.numpy as jnp
from jax import lax
from jax.experimental import pallas as pl
from jax.experimental.pallas import tpu as pltpu
from jax.sharding import PartitionSpec as P

piep_coef = 1.0
drag_coef = 20.0

LANES = 128
ROWS = 8
BLOCK = 2048
GAS_WINDOW = 10
BUCKET = 1024
BUCKETS = 20
NEAR_BUCKETS = 4
NEAR_HEADS = 6
OWN_HEADS = 10
DEAD = 1 << 29

NT = (((1,), (1,)), ((), ()))
VMEM = pltpu.VMEM
SMEM = pltpu.SMEM


def params(megabytes=40):
    return pltpu.CompilerParams(vmem_limit_bytes=megabytes << 20)


def lane_gather(table, index):
    numbers = lax.GatherDimensionNumbers(
        offset_dims=(),
        collapsed_slice_dims=(1,),
        start_index_map=(1,),
        operand_batching_dims=(0,),
        start_indices_batching_dims=(0,),
    )
    return lax.gather(
        table,
        index[..., None],
        numbers,
        slice_sizes=(1, 1),
        mode=lax.GatherScatterMode.PROMISE_IN_BOUNDS,
    )


def swap_bits(regs, m, kind, k):
    axis, size = (0, ROWS) if kind == "s" else (1, LANES)
    step = 1 << k
    lower = (lax.broadcasted_iota(jnp.int32, (ROWS, LANES), axis) & step) == 0
    for v in range(len(regs)):
        if not v & (1 << m):
            x, y = regs[v], regs[v | (1 << m)]
            regs[v] = jnp.where(lower, x, pltpu.roll(y, step, axis))
            regs[v | (1 << m)] = jnp.where(lower, pltpu.roll(x, size - step, axis), y)


def sort_network(regs, final, resident):
    levels = len(final)
    at, held = list(range(levels)), resident
    for level in range(1, levels + 1):
        for bit in reversed(range(resident, level)):
            if bit != held:
                at[held], at[bit] = at[bit], at[held]
                held = bit
    place = [None] * levels
    for bit in range(levels):
        place[at[bit]] = final[bit]
    held = resident

    def fill(bit, v):
        if bit >= levels or bit == 0:
            return 0
        kind, k = place[bit]
        if kind == "v":
            return -((v >> k) & 1)
        where = lax.broadcasted_iota(jnp.int32, (ROWS, LANES), 0 if kind == "s" else 1)
        return -((where >> k) & 1)

    for level in range(1, levels + 1):
        fills = {}
        for v in range(len(regs)):
            key = tuple(
                (v >> place[bit][1]) & 1 if bit < levels and place[bit][0] == "v" else 0
                for bit in (level - 1, level)
            )
            if key not in fills:
                fills[key] = fill(level, v) ^ fill(level - 1, v)
            flip = fills[key]
            if isinstance(flip, int):
                if flip:
                    regs[v] = ~regs[v]
            else:
                regs[v] = regs[v] ^ flip
        for bit in reversed(range(level)):
            if bit >= resident and bit != held:
                swap_bits(regs, place[held][1], *place[bit])
                place[held], place[bit] = place[bit], place[held]
                held = bit
            step = 1 << place[bit][1]
            for v in range(len(regs)):
                if not v & step:
                    x, y = regs[v], regs[v | step]
                    regs[v], regs[v | step] = jnp.minimum(x, y), jnp.maximum(x, y)
    return regs


def split_two(x):
    high = x.astype(jnp.bfloat16).astype(jnp.float32)
    return high, x - high


def split_three(x):
    high, rest = split_two(x)
    mid, low = split_two(rest)
    return high, mid, low


def packed_row(ref, row):
    return jnp.broadcast_to(ref[row : row + 1, :], (16, LANES)).astype(jnp.bfloat16)


def one_hot_rows(low, iota):
    one = jnp.ones((16, LANES), jnp.bfloat16)
    zero = jnp.zeros((16, LANES), jnp.bfloat16)
    return jnp.concatenate(
        [jnp.where(low == iota[k : k + 16, :], one, zero) for k in range(0, iota.shape[0], 16)],
        axis=0,
    )


def spread_rows(rel, parts, iota):
    hit = rel == iota[0:16, :]
    zero = jnp.zeros((16, LANES), jnp.bfloat16)
    return jnp.concatenate([jnp.where(hit, p, zero) for part in parts for p in part], axis=0)


def spread_add(rows, hots):
    out = lax.dot_general(
        jnp.concatenate(rows, axis=1) if len(rows) > 1 else rows[0],
        jnp.concatenate(hots, axis=1) if len(hots) > 1 else hots[0],
        NT,
        preferred_element_type=jnp.float32,
    )
    total = out[0:48]
    for s in range(48, out.shape[0], 48):
        total = total + out[s : s + 48]
    return total


def fill_iota(iota):
    rows = lax.broadcasted_iota(jnp.int32, iota.shape, 0)
    iota[...] = rows.astype(jnp.float32).astype(jnp.bfloat16)


def rows_of(block):
    start = block * 16
    return pl.ds(start if isinstance(block, int) else pl.multiple_of(start, 16), 16)


def wide(ref, *at):
    return jnp.broadcast_to(ref[at[:-1] + (slice(at[-1], at[-1] + 1),)], (ROWS, LANES))


def window(table, first, count, row, low, found):
    rel = row - first
    for u in range(count):
        found = jnp.where(rel == u, lane_gather(table[first + u], low), found)
    return found


def running_max(x, count):
    x = jnp.broadcast_to(x, (ROWS, LANES))
    step = 1
    while step < count:
        x = jnp.maximum(x, pltpu.roll(x, LANES - step, 1))
        step *= 2
    return x


def fill_gas_rows(gas_ref, gas_rows):
    for r in range(16):
        rows = slice(r * ROWS, (r + 1) * ROWS)
        for c in range(3):
            for half in range(2):
                gas_rows[rows, half * 4 + c, :] = gas_ref[c, rows, half * LANES : (half + 1) * LANES]


def gas_index(block, keys_ref, slot):
    idx = slot[0]
    keys = keys_ref[rows_of(block), :]
    idx[0] = lax.shift_right_logical(keys, 19)
    idx[1] = lax.shift_right_logical(keys, 11) & (LANES - 1)


def gas_gather(block, g, ends, gas_rows, slot):
    idx, found = slot[0], slot[1]
    zero = jnp.zeros((ROWS, LANES), jnp.float32)
    first = ends[0, block * 16 + g]
    found[g] = window(gas_rows, first, GAS_WINDOW, wide(idx, 0, g), wide(idx, 1, g), zero)


def gas_rest(block, ends, gas_rows, slot):
    idx, found = slot[0], slot[1]

    @pl.when(ends[2, block * 16] >= GAS_WINDOW)
    def _():
        def one(g, carry):
            first = ends[0, block * 16 + g]
            row = jnp.broadcast_to(idx[0, pl.ds(g, 1), :], (ROWS, LANES))
            low = jnp.broadcast_to(idx[1, pl.ds(g, 1), :], (ROWS, LANES))

            def trip(t, total):
                base = jnp.minimum(first + GAS_WINDOW * t, LANES)
                return window(gas_rows, base, GAS_WINDOW, row, low, total)

            trips = (ends[1, block * 16 + g] - first) // GAS_WINDOW + 1
            found[g] = lax.fori_loop(1, trips, trip, found[g])
            return carry

        lax.fori_loop(0, 16, one, 0)


def seen_values(block, keys_ref, slot):
    idx, found, val = slot
    keys = keys_ref[rows_of(block), :]
    upper = (keys & (1 << 18)) != 0
    place_in = keys & (BLOCK - 1)
    val[0] = lax.shift_right_logical(place_in, 7).astype(jnp.float32)
    val[1] = (place_in & (LANES - 1)).astype(jnp.float32)
    for c in range(3):
        seen = jnp.where(upper, found[:, 4 + c, :], found[:, c, :])
        for n, part in enumerate(split_three(seen)):
            val[2 + 3 * c + n] = part


def seen_in_order(groups, slot, iota):
    val = slot[2]
    rows, hots = [], []
    for g in groups:
        parts = [[packed_row(val.at[2 + 3 * c + n], g) for c in range(3)] for n in range(3)]
        rows.append(spread_rows(packed_row(val.at[0], g), parts, iota))
        hots.append(one_hot_rows(packed_row(val.at[1], g), iota))
    return spread_add(rows, hots)


def write_states(block, total, pos_ref, vel_ref, diam_ref, out_ref, out_rows):
    rows = rows_of(block)
    for c in range(3):
        out_ref[out_rows, c, :] = pos_ref[c, rows, :]
        out_ref[out_rows, 3 + c, :] = total[16 * c : 16 * c + 16] - vel_ref[c, rows, :]
    out_ref[out_rows, 6, :] = 0.5 * diam_ref[rows, :]
    out_ref[out_rows, 7, :] = jnp.zeros((16, LANES), jnp.float32)


def states_step(gather, scatter, keys_ref, ends, gas_rows, iota, arrays):
    total = jnp.zeros((48, LANES), jnp.float32)
    if gather:
        gas_index(gather[0], keys_ref, gather[1])
    if scatter:
        seen_values(scatter[0], keys_ref, scatter[1])
    for g in range(16):
        if gather:
            gas_gather(gather[0], g, ends, gas_rows, gather[1])
        if scatter and g % 2:
            total = total + seen_in_order((g - 1, g), scatter[1], iota)
    if scatter:
        write_states(scatter[0], total, *arrays, *scatter[2:])
    if gather:
        gas_rest(gather[0], ends, gas_rows, gather[1])


def edge_states_kernel(
    cell_hbm, gas_hbm, pos_hbm, vel_hbm, diam_hbm,
    keys_ref, ends_ref, first_ref, last_ref,
    cell_ref, gas_ref, pos_ref, vel_ref, diam_ref,
    gas_rows, iota, ends, idx_a, found_a, val_a, idx_b, found_b, val_b, sems,
):
    sources = (cell_hbm, gas_hbm, pos_hbm, vel_hbm, diam_hbm)
    places = (cell_ref, gas_ref, pos_ref, vel_ref, diam_ref)
    copies = [
        pltpu.make_async_copy(x, y, sems.at[n]) for n, (x, y) in enumerate(zip(sources, places))
    ]
    for copy in copies:
        copy.start()
    copies[0].wait()
    sub = lax.broadcasted_iota(jnp.int32, (ROWS, LANES), 0)
    lane = lax.broadcasted_iota(jnp.int32, (ROWS, LANES), 1)
    cells = cell_ref[...].T
    regs = []
    for v in range(16):
        own = (lane & 15) * LANES + v * ROWS + sub
        regs.append(cells[v * ROWS : (v + 1) * ROWS] * BLOCK + own)
    final = [("v", k) for k in range(4)] + [("s", k) for k in range(3)] + [("l", k) for k in range(4)]
    regs = sort_network(regs, final, 3)
    keys_ref[...] = jnp.concatenate(regs, axis=0).T
    least = functools.reduce(jnp.minimum, regs)
    most = functools.reduce(jnp.maximum, regs)
    least = lax.shift_right_logical(jnp.min(least, axis=0, keepdims=True), 19)
    most = lax.shift_right_logical(jnp.max(most, axis=0, keepdims=True), 19)
    ends_ref[0:1, :] = least
    ends_ref[1:2, :] = most
    ends_ref[2:8, :] = running_max(most - least, 16)[0:6]
    copy = pltpu.make_async_copy(ends_ref, ends, sems.at[5])
    copy.start()
    copies[1].wait()
    fill_gas_rows(gas_ref, gas_rows)
    for other in copies[2:]:
        other.wait()
    copy.wait()
    fill_iota(iota)
    a, b = (idx_a, found_a, val_a), (idx_b, found_b, val_b)
    whole = slice(0, 16)
    step = functools.partial(
        states_step, keys_ref=keys_ref, ends=ends, gas_rows=gas_rows, iota=iota,
        arrays=(pos_ref, vel_ref, diam_ref),
    )
    step((0, a), None)
    step((7, b), (0, a, first_ref, whole))
    step(None, (7, b, last_ref, whole))


def slots(rows, parts, dtype=jnp.float32):
    one = [VMEM((2, 16, LANES), jnp.int32), VMEM((16, ROWS, LANES), dtype), VMEM((parts, rows, LANES), dtype)]
    return one + one


def edge_states(cells, gas, pos, vel, diam):
    f32, i32 = jnp.float32, jnp.int32
    arrays = (cells, gas, pos, vel, diam)
    return pl.pallas_call(
        edge_states_kernel,
        name="edge_states",
        out_shape=(
            jax.ShapeDtypeStruct((128, LANES), i32),
            jax.ShapeDtypeStruct((ROWS, LANES), i32),
            jax.ShapeDtypeStruct((16, ROWS, LANES), f32),
            jax.ShapeDtypeStruct((16, ROWS, LANES), f32),
        ),
        in_specs=[pl.BlockSpec(memory_space=pltpu.HBM)] * 5,
        scratch_shapes=[VMEM(x.shape, x.dtype) for x in arrays]
        + [VMEM((144, ROWS, LANES), f32), VMEM((LANES, LANES), jnp.bfloat16), SMEM((ROWS, LANES), i32)]
        + slots(16, 11)
        + [pltpu.SemaphoreType.DMA((6,))],
        compiler_params=params(60),
    )(*arrays)


def inner_states_kernel(
    ends, keys_ref, gas_ref, pos_ref, vel_ref, diam_ref, first_hbm, last_hbm,
    table_ref,
    gas_rows, iota, idx_a, found_a, val_a, idx_b, found_b, val_b, sems,
):
    copies = [
        pltpu.make_async_copy(first_hbm, table_ref.at[0:16], sems.at[0]),
        pltpu.make_async_copy(last_hbm, table_ref.at[112:128], sems.at[1]),
    ]
    for copy in copies:
        copy.start()
    table_ref[128:144] = jnp.zeros((16, ROWS, LANES), jnp.float32)
    fill_gas_rows(gas_ref, gas_rows)
    fill_iota(iota)
    a, b = (idx_a, found_a, val_a), (idx_b, found_b, val_b)
    step = functools.partial(
        states_step, keys_ref=keys_ref, ends=ends, gas_rows=gas_rows, iota=iota,
        arrays=(pos_ref, vel_ref, diam_ref),
    )
    step((1, a), None)

    def two(k, carry):
        block = 2 * k + 1
        step((block + 1, b), (block, a, table_ref, rows_of(block)))
        step((jnp.minimum(block + 2, 6), a), (block + 1, b, table_ref, rows_of(block + 1)))
        return carry

    lax.fori_loop(0, 3, two, 0)
    for copy in copies:
        copy.wait()


def inner_states(ends, keys, gas, pos, vel, diam, first, last):
    f32 = jnp.float32
    return pl.pallas_call(
        inner_states_kernel,
        name="inner_states",
        out_shape=jax.ShapeDtypeStruct((144, ROWS, LANES), f32),
        in_specs=[pl.BlockSpec(memory_space=SMEM)]
        + [pl.BlockSpec(memory_space=VMEM)] * 5
        + [pl.BlockSpec(memory_space=pltpu.HBM)] * 2,
        scratch_shapes=[VMEM((144, ROWS, LANES), f32), VMEM((LANES, LANES), jnp.bfloat16)]
        + slots(16, 11)
        + [pltpu.SemaphoreType.DMA((2,))],
        compiler_params=params(),
    )(ends, keys, gas, pos, vel, diam, first, last)


def pair_sort_kernel(live_ref, pairs_ref, keys_ref, ends_ref):
    live = live_ref[0, 0]
    sub = lax.broadcasted_iota(jnp.int32, (ROWS, LANES), 0)
    lane = lax.broadcasted_iota(jnp.int32, (ROWS, LANES), 1)
    regs = []
    for v in range(32):
        rows = slice(v * ROWS, (v + 1) * ROWS)
        slot = v * 1024 + sub * LANES + lane
        head = pairs_ref[0, rows, :]
        tail = pairs_ref[1, rows, :] - 7 * BLOCK
        own = tail - BLOCK
        inside = (own >= 0) & (own < 8 * BLOCK)
        tail = jnp.where(inside, jnp.maximum(own, head) + BLOCK, tail)
        head = jnp.where(inside, jnp.minimum(own, head), head)
        bucket = lax.shift_right_logical(tail, 10)
        bucket = jnp.where(inside, bucket + 2, jnp.where(bucket >= 18, bucket - 16, bucket))
        turn = -(bucket & 1) & (8 * BLOCK - 1)
        key = (bucket << 24) | ((head ^ turn) << 10) | (tail & (BUCKET - 1))
        regs.append(jnp.where(slot < live, key, DEAD))
    final = [("v", k) for k in range(5)] + [("s", k) for k in range(3)] + [("l", k) for k in range(7)]
    regs = sort_network(regs, final, 4)
    swap_bits(regs, 4, "s", 2)
    beyond = jnp.zeros((ROWS, LANES), jnp.float32)
    for key in regs:
        beyond = beyond + jnp.where(key < NEAR_BUCKETS << 24, 1.0, 0.0)
    beyond = jnp.sum(jnp.sum(beyond, axis=0, keepdims=True), axis=1, keepdims=True)
    ends_ref[8:16, :] = jnp.broadcast_to(beyond, (ROWS, LANES)).astype(jnp.int32)
    for half in range(2):
        rows = regs[16 * half : 16 * half + 16]
        keys_ref[half] = jnp.concatenate(rows, axis=0).T
        least_head = least_tail = jnp.full((ROWS, LANES), 1 << 20, jnp.int32)
        most_head = most_tail = jnp.full((ROWS, LANES), -1, jnp.int32)
        for key in rows:
            used = key < DEAD
            bucket = lax.shift_right_logical(key, 24)
            head = lax.shift_right_logical(key, 17) & (LANES - 1)
            head = head ^ (-(bucket & 1) & (LANES - 1))
            least_head = jnp.minimum(least_head, jnp.where(used, head, 1 << 20))
            most_head = jnp.maximum(most_head, jnp.where(used, head, -1))
            least_tail = jnp.minimum(least_tail, jnp.where(used, bucket, 1 << 20))
            most_tail = jnp.maximum(most_tail, jnp.where(used, bucket, -1))
        for n, x in enumerate((least_head, most_head, least_tail, most_tail)):
            reduce = jnp.max if n % 2 else jnp.min
            row = 4 * half + n
            bound = (LANES, LANES, BUCKETS, BUCKETS)[n]
            ends_ref[row : row + 1, :] = jnp.minimum(reduce(x, axis=0, keepdims=True), bound)


def pair_sort(live, pairs):
    return pl.pallas_call(
        pair_sort_kernel,
        name="pair_sort",
        out_shape=(
            jax.ShapeDtypeStruct((2, LANES, LANES), jnp.int32),
            jax.ShapeDtypeStruct((16, LANES), jnp.int32),
        ),
        in_specs=[pl.BlockSpec(memory_space=SMEM), pl.BlockSpec(memory_space=VMEM)],
        compiler_params=params(),
    )(live, pairs)


def take_items(state, groups, ends, part):
    low, high, heads = part
    items = []
    for _ in range(ROWS):
        g, bucket, head = state
        valid = g < groups
        seen = jnp.minimum(g, 2 * LANES - 1)
        at, lane = 4 * (seen & 1), seen >> 1
        tail_first = (jnp.minimum(bucket, high) - low) * 8
        items.append((seen, jnp.where(valid, bucket, -1), head, tail_first))
        more_heads = head + heads <= ends[at + 1, lane]
        more_tails = bucket < jnp.minimum(ends[at + 3, lane], high - 1)
        step = jnp.where(more_heads | more_tails, 0, 1)
        g = jnp.minimum(g + step, 2 * LANES)
        seen = jnp.minimum(g, 2 * LANES - 1)
        at, lane = 4 * (seen & 1), seen >> 1
        head = jnp.where(more_heads, head + heads, ends[at, lane])
        same = jnp.where(more_heads, bucket, bucket + 1)
        bucket = jnp.where(step == 1, jnp.maximum(ends[at + 2, lane], low), same)
        state = (g, bucket, head)
    return items, state


def pair_gather(k, item, keys_ref, near_table, far_table, heads, slot):
    key_rows, rel_rows, near, far = slot[0:4]
    g, bucket, first, tail_first = item
    keys = jnp.broadcast_to(keys_ref[g & 1, pl.ds(g >> 1, 1), :], (ROWS, LANES))
    of_bucket = lax.shift_right_logical(keys, 24)
    turn = -(of_bucket & 1) & (8 * BLOCK - 1)
    head = (lax.shift_right_logical(keys, 10) & (8 * BLOCK - 1)) ^ turn
    rel = lax.shift_right_logical(head, 7) - first
    tail_row = lax.shift_right_logical(keys, 7) & 7
    used = (of_bucket == bucket) & (rel >= 0) & (rel < heads)
    key_rows[k : k + 1, :] = jnp.where(used, keys, DEAD)[0:1]
    rel_rows[k : k + 1, :] = rel[0:1]
    zero = jnp.zeros((ROWS, LANES), jnp.float32)
    low = head & (LANES - 1)
    found = zero
    for u in range(heads):
        found = jnp.where(rel == u, lane_gather(near_table[first + u], low), found)
    near[k] = found
    low = keys & (LANES - 1)
    found = zero
    for u in range(8):
        found = jnp.where(tail_row == u, lane_gather(far_table[tail_first + u], low), found)
    far[k] = found


def pair_values(slot):
    key_rows, rel_rows, near, far, val = slot
    keys = key_rows[...]
    used = keys < DEAD
    turn = -(lax.shift_right_logical(keys, 24) & 1) & (LANES - 1)
    val[0] = rel_rows[...].astype(jnp.float32)
    val[1] = ((lax.shift_right_logical(keys, 10) & (LANES - 1)) ^ turn).astype(jnp.float32)
    val[2] = (lax.shift_right_logical(keys, 7) & 7).astype(jnp.float32)
    val[3] = (keys & (LANES - 1)).astype(jnp.float32)
    gap = jnp.zeros((ROWS, LANES), jnp.float32)
    for c in range(3):
        apart = far[:, c, :] - near[:, c, :]
        gap = gap + apart * apart
    far_radius, near_radius = far[:, 6, :], near[:, 6, :]
    far_ratio = far_radius * lax.rsqrt(gap + far_radius * far_radius)
    near_ratio = near_radius * lax.rsqrt(gap + near_radius * near_radius)
    weight_far = jnp.where(used, piep_coef * far_ratio * far_ratio * far_ratio, 0.0)
    weight_near = jnp.where(used, piep_coef * near_ratio * near_ratio * near_ratio, 0.0)
    for c in range(3):
        for n, part in enumerate(split_two(weight_far * far[:, 3 + c, :])):
            val[4 + 3 * n + c] = part
        for n, part in enumerate(split_two(weight_near * near[:, 3 + c, :])):
            val[10 + 3 * n + c] = part


def pair_scatter(k, item, slot, head_sum, tail_sum, iota, iota8):
    val = slot[4]
    first, tail_first = item
    parts = [[packed_row(val.at[4 + 3 * n + c], k) for c in range(3)] for n in range(2)]
    rows = spread_rows(packed_row(val.at[0], k), parts, iota)
    out = spread_add([rows], [one_hot_rows(packed_row(val.at[1], k), iota)])
    for c in range(3):
        head_sum[c, pl.ds(first, 16), :] += out[16 * c : 16 * c + 16]

    hit = packed_row(val.at[2], k) == iota8[...]
    zero = jnp.zeros((16, LANES), jnp.bfloat16)
    tiles = []
    for n in range(10, 16, 2):
        both = jnp.concatenate([wide(val, n, k), wide(val, n + 1, k)], axis=0)
        tiles.append(jnp.where(hit, both.astype(jnp.bfloat16), zero))
    out = lax.dot_general(
        jnp.concatenate(tiles, axis=0),
        one_hot_rows(packed_row(val.at[3], k), iota),
        NT,
        preferred_element_type=jnp.float32,
    )
    at = pl.ds(pl.multiple_of(tail_first, 8), 8)
    for c in range(3):
        tail_sum[c, at, :] += out[8 * c : 8 * c + 8] + out[24 + 8 * c : 32 + 8 * c]


def run_pairs(groups, start, part, ends, keys_ref, near_table, far_table, sums, iota, iota8, slots_):
    fill_iota(iota)
    rows = lax.broadcasted_iota(jnp.int32, iota8.shape, 0) & 7
    iota8[...] = rows.astype(jnp.float32).astype(jnp.bfloat16)
    a, b = slots_[0:5], slots_[5:10]

    def step(state, slot, pending, other):
        items, state = take_items(state, groups, ends, part)
        if other:
            pair_values(other)
        for k in range(ROWS):
            pair_gather(k, items[k], keys_ref, near_table, far_table, part[2], slot)
            if other:
                pair_scatter(k, pending[k], other, *sums, iota, iota8)
        return tuple(item[2:4] for item in items), state, items[0][1] >= 0

    at, lane = 4 * (start & 1), start >> 1
    state = (start, jnp.maximum(ends[at + 2, lane], part[0]), ends[at, lane])
    carry = step(state, a, None, None)

    def two(carry):
        pending, state, _ = carry
        pending, state, _ = step(state, b, pending, a)
        return step(state, a, pending, b)

    lax.while_loop(lambda carry: carry[2], two, carry)


def near_pairs_kernel(
    ends, keys_ref, table_ref, before_ref, after_ref,
    heads_ref, lower_ref, upper_ref,
    shell, head_sum, tail_sum, iota, iota8, *slots_,
):
    shell[0:16] = before_ref[...]
    shell[16:32] = after_ref[...]
    shell[32:40] = jnp.zeros((8, ROWS, LANES), jnp.float32)
    head_sum[...] = jnp.zeros_like(head_sum)
    tail_sum[...] = jnp.zeros_like(tail_sum)
    groups = (ends[8, 0] + LANES - 1) // LANES
    run_pairs(
        groups, jnp.int32(0), (0, NEAR_BUCKETS, NEAR_HEADS), ends, keys_ref, table_ref, shell,
        (head_sum, tail_sum), iota, iota8, slots_,
    )
    heads_ref[...] = head_sum[:, 0:128, :]
    lower_ref[...] = tail_sum[:, 0:16, :]
    upper_ref[...] = tail_sum[:, 16:32, :]


def own_pairs_kernel(
    live_ref, ends, keys_ref, table_ref, heads_ref,
    corr_ref,
    head_sum, tail_sum, iota, iota8, *slots_,
):
    head_sum[:, 0:128, :] = heads_ref[...]
    head_sum[:, 128:144, :] = jnp.zeros((3, 16, LANES), jnp.float32)
    tail_sum[...] = jnp.zeros_like(tail_sum)
    groups = (live_ref[0, 0] + LANES - 1) // LANES
    start = jnp.minimum(ends[8, 0] // LANES, 2 * LANES - 1)
    run_pairs(
        groups, start, (NEAR_BUCKETS, BUCKETS, OWN_HEADS), ends, keys_ref, table_ref, table_ref,
        (head_sum, tail_sum), iota, iota8, slots_,
    )
    corr_ref[...] = head_sum[:, 0:128, :] + tail_sum[:, 0:128, :]


def pair_scratch(tail_rows):
    f32, i32 = jnp.float32, jnp.int32
    slot = [
        VMEM((ROWS, LANES), i32),
        VMEM((ROWS, LANES), i32),
        VMEM((ROWS, ROWS, LANES), f32),
        VMEM((ROWS, ROWS, LANES), f32),
        VMEM((16, ROWS, LANES), f32),
    ]
    return [
        VMEM((3, 144, LANES), f32),
        VMEM((3, tail_rows, LANES), f32),
        VMEM((LANES, LANES), jnp.bfloat16),
        VMEM((16, LANES), jnp.bfloat16),
        *slot,
        *slot,
    ]


def near_pairs(ends, keys, table, before, after):
    f32 = jnp.float32
    smem, vmem = pl.BlockSpec(memory_space=SMEM), pl.BlockSpec(memory_space=VMEM)
    return pl.pallas_call(
        near_pairs_kernel,
        name="near_pairs",
        out_shape=(
            jax.ShapeDtypeStruct((3, 128, LANES), f32),
            jax.ShapeDtypeStruct((3, 16, LANES), f32),
            jax.ShapeDtypeStruct((3, 16, LANES), f32),
        ),
        in_specs=[smem, vmem, vmem, vmem, vmem],
        scratch_shapes=[VMEM((40, ROWS, LANES), f32)] + pair_scratch(40),
        compiler_params=params(),
    )(ends, keys, table, before, after)


def own_pairs(live, ends, keys, table, heads):
    smem, vmem = pl.BlockSpec(memory_space=SMEM), pl.BlockSpec(memory_space=VMEM)
    return pl.pallas_call(
        own_pairs_kernel,
        name="own_pairs",
        out_shape=jax.ShapeDtypeStruct((3, 128, LANES), jnp.float32),
        in_specs=[smem, smem, vmem, vmem, vmem],
        scratch_shapes=pair_scratch(136),
        compiler_params=params(),
    )(live, ends, keys, table, heads)


def force_gather(block, keys_ref, table_ref, total_ref, slot):
    force, got, val = slot
    rows = rows_of(block)
    scale = (-2.0 * drag_coef) * table_ref[rows, 6, :]
    for c in range(3):
        push = scale * (table_ref[rows, 3 + c, :] + total_ref[c, rows, :])
        force[:, c, :] = push[0:8]
        force[:, 4 + c, :] = push[8:16]
    keys = keys_ref[rows, :]
    val[0] = lax.shift_right_logical(keys, 19).astype(jnp.float32)
    val[1] = (lax.shift_right_logical(keys, 11) & (2 * LANES - 1)).astype(jnp.float32)
    inner = lax.shift_right_logical(keys, 7) & 7
    low = keys & (LANES - 1)
    tables = [force[k] for k in range(ROWS)]
    for g in range(16):
        pick = jnp.broadcast_to(inner[g : g + 1, :], (ROWS, LANES))
        at = jnp.broadcast_to(low[g : g + 1, :], (ROWS, LANES))
        found = jnp.zeros((ROWS, LANES), jnp.float32)
        for k in range(ROWS):
            found = jnp.where(pick == k, lane_gather(tables[k], at), found)
        got[g] = found
    upper = (keys & 1024) != 0
    for c in range(3):
        pushed = jnp.where(upper, got[:, 4 + c, :], got[:, c, :])
        for n, part in enumerate(split_two(pushed)):
            val[2 + 2 * c + n] = part


def force_add(g, base, slot, cells, iota):
    val = slot[2]

    def row(n):
        if isinstance(g, int):
            return packed_row(val.at[n], g)
        return jnp.broadcast_to(val[n, pl.ds(g, 1), :], (16, LANES)).astype(jnp.bfloat16)

    rel = row(0) - base.astype(jnp.float32).astype(jnp.bfloat16)
    parts = [[row(2 + 2 * c + n) for c in range(3)] for n in range(2)]
    out = spread_add([spread_rows(rel, parts, iota)], [one_hot_rows(row(1), iota)])
    for c in range(3):
        for half in range(2):
            part = out[16 * c : 16 * c + 16, half * LANES : (half + 1) * LANES]
            cells[2 * c + half, pl.ds(base, 16), :] += part


def force_rest(block, ends, slot, cells, iota):
    @pl.when(ends[2, block * 16] >= 16)
    def _():
        def one(g, carry):
            first, most = ends[0, block * 16 + g], ends[1, block * 16 + g]

            def trip(t, carry):
                force_add(g, jnp.minimum(first + 16 * t, LANES), slot, cells, iota)
                return carry

            lax.fori_loop(1, (most - first) // 16 + 1, trip, 0)
            return carry

        lax.fori_loop(0, 16, one, 0)


def deposit_step(gather, scatter, ends, keys_ref, table_ref, total_ref, cells, iota):
    if gather:
        force_gather(gather[0], keys_ref, table_ref, total_ref, gather[1])
    if scatter:
        for g in range(16):
            force_add(g, ends[0, scatter[0] * 16 + g], scatter[1], cells, iota)
        force_rest(scatter[0], ends, scatter[1], cells, iota)


def by_partner(axis, first, last):
    even = (lax.axis_index(axis) & 1) == 0
    return jnp.where(even, last, first), jnp.where(even, first, last)


def from_partners(axis, one, other):
    at, count = lax.axis_index(axis), lax.axis_size(axis)
    even = (at & 1) == 0
    before = jnp.where(at > 0, jnp.where(even, other, one), 0.0)
    after = jnp.where(at < count - 1, jnp.where(even, one, other), 0.0)
    return before, after


def deposit_kernel(
    ends, keys_ref, table_ref, corr_ref, lower_ref, upper_ref,
    out_ref, total_ref, one_ref, other_ref,
    cells, iota, force_a, got_a, val_a, force_b, got_b, val_b,
):
    fill_iota(iota)
    cells[...] = jnp.zeros_like(cells)
    total_ref[...] = corr_ref[...]
    total_ref[:, 0:16, :] += lower_ref[...]
    total_ref[:, 112:128, :] += upper_ref[...]
    a, b = (force_a, got_a, val_a), (force_b, got_b, val_b)
    step = functools.partial(
        deposit_step, ends=ends, keys_ref=keys_ref, table_ref=table_ref, total_ref=total_ref,
        cells=cells, iota=iota,
    )
    step((0, a), None)

    def two(k, carry):
        block = 2 * k
        step((block + 1, b), (block, a))
        step((jnp.minimum(block + 2, 7), a), (block + 1, b))
        return carry

    lax.fori_loop(0, 4, two, 0)
    for c in range(3):
        for half in range(2):
            columns = slice(half * LANES, (half + 1) * LANES)
            out_ref[c, :, columns] = cells[2 * c + half, 0:128, :]
            one, other = by_partner(
                "ax", cells[2 * c + half, 0:32, :], cells[2 * c + half, 96:128, :]
            )
            one_ref[c, :, columns] = one
            other_ref[c, :, columns] = other


def deposits(ends, keys, table, corr, lower, upper):
    f32 = jnp.float32
    smem, vmem = pl.BlockSpec(memory_space=SMEM), pl.BlockSpec(memory_space=VMEM)
    slot = [VMEM((ROWS, ROWS, LANES), f32), VMEM((16, ROWS, LANES), f32), VMEM((8, 16, LANES), f32)]
    return pl.pallas_call(
        deposit_kernel,
        name="deposits",
        out_shape=(
            jax.ShapeDtypeStruct((3, 128, 2 * LANES), f32),
            jax.ShapeDtypeStruct((3, 128, LANES), f32),
            jax.ShapeDtypeStruct((3, 32, 2 * LANES), f32),
            jax.ShapeDtypeStruct((3, 32, 2 * LANES), f32),
        ),
        in_specs=[smem] + [vmem] * 5,
        scratch_shapes=[VMEM((6, 144, LANES), f32), VMEM((2 * LANES, LANES), jnp.bfloat16)]
        + slot
        + slot,
        compiler_params=params(),
    )(ends, keys, table, corr, lower, upper)


def axial_kernel(taps, cells_ref, one_in, other_in, out_ref, one_ref, other_ref, first_ref, last_ref):
    for c in range(3):
        before, after = from_partners("ax", one_in[c], other_in[c])
        padded = jnp.concatenate([before, cells_ref[c], after], axis=0)
        total = taps[0] * padded[0:128]
        for k in range(1, 5):
            total = total + taps[k] * padded[16 * k : 16 * k + 128]
        out_ref[c] = total
        for a in range(8):
            first_ref[2 * a : 2 * a + 2, :] = total[16 * a : 16 * a + 2]
            last_ref[2 * a : 2 * a + 2, :] = total[16 * a + 14 : 16 * a + 16]
        one_ref[c], other_ref[c] = by_partner("rad", first_ref[...], last_ref[...])


def radial_kernel(
    taps, cells_ref, one_in, other_in, out_ref, first_ref, last_ref, padded, before_ref, after_ref
):
    lane = lax.broadcasted_iota(jnp.int32, (LANES, LANES), 1)
    edges = jnp.zeros((LANES, LANES), jnp.float32)
    for c in range(3):
        before_ref[...], after_ref[...] = from_partners("rad", one_in[c], other_in[c])
        for a in range(8):
            padded[0:2, :] = before_ref[2 * a : 2 * a + 2, :]
            padded[2:18, :] = cells_ref[c, 16 * a : 16 * a + 16, :]
            padded[18:20, :] = after_ref[2 * a : 2 * a + 2, :]
            total = taps[0] * padded[0:16, :]
            for k in range(1, 5):
                total = total + taps[k] * padded[k : k + 16, :]
            out_ref[c, 16 * a : 16 * a + 16, :] = total
        left, right = out_ref[c, :, 0:LANES], out_ref[c, :, LANES:]
        if c:
            left = pltpu.roll(left, 2 * c, 1)
        right = pltpu.roll(right, 10 + 2 * c, 1)
        edges = jnp.where((lane >> 1) == c, left, edges)
        edges = jnp.where((lane >> 1) == 4 + c, right, edges)
    turned = edges.T
    first_ref[...] = turned[0:8]
    last_ref[...] = turned[8:16]


def azimuthal_kernel(taps, cells_ref, before_ref, after_ref, out_ref):
    lane = lax.broadcasted_iota(jnp.int32, (LANES, LANES), 1)
    rest = jnp.zeros((LANES - 16, LANES), jnp.float32)
    edges = jnp.concatenate([after_ref[...], before_ref[...], rest], axis=0).T
    for c in range(3):
        ahead = pltpu.roll(edges, LANES - 2 * c, 1) if c else edges
        halo = jnp.where(lane < 64, ahead, pltpu.roll(edges, 118 - 2 * c, 1))
        left, right = cells_ref[c, :, 0:LANES], cells_ref[c, :, LANES:]
        out_left, out_right = taps[2] * left, taps[2] * right
        for k in (1, 2):
            tap = taps[2 + k]
            inner = lane < LANES - k
            x, y, z = (pltpu.roll(v, LANES - k, 1) for v in (left, right, halo))
            out_left = out_left + tap * jnp.where(inner, x, y)
            out_right = out_right + tap * jnp.where(inner, y, z)
            inner = lane >= k
            x, y, z = (pltpu.roll(v, k, 1) for v in (left, right, halo))
            out_left = out_left + tap * jnp.where(inner, x, z)
            out_right = out_right + tap * jnp.where(inner, y, x)
        out_ref[c, :, 0:LANES] = out_left
        out_ref[c, :, LANES:] = out_right


def filtered(deposit, one, other):
    f32 = jnp.float32
    raw = [math.exp(-0.5 * k * k) for k in range(-2, 3)]
    taps = [x / sum(raw) for x in raw]
    whole = jax.ShapeDtypeStruct(deposit.shape, f32)
    radial_face = jax.ShapeDtypeStruct((3, 16, 2 * LANES), f32)
    edge = jax.ShapeDtypeStruct((8, LANES), f32)
    cells, one, other = pl.pallas_call(
        functools.partial(axial_kernel, taps),
        name="axial_filter",
        out_shape=(whole, radial_face, radial_face),
        scratch_shapes=[VMEM((16, 2 * LANES), f32)] * 2,
        compiler_params=params(),
    )(deposit, *swapped(one, other, "ax"))
    cells, first, last = pl.pallas_call(
        functools.partial(radial_kernel, taps),
        name="radial_filter",
        out_shape=(whole, edge, edge),
        scratch_shapes=[VMEM((24, 2 * LANES), f32)] + [VMEM((16, 2 * LANES), f32)] * 2,
        compiler_params=params(),
    )(cells, *swapped(one, other, "rad"))
    return pl.pallas_call(
        functools.partial(azimuthal_kernel, taps),
        name="azimuthal_filter",
        out_shape=whole,
        compiler_params=params(),
    )(cells, shifted(last, "az", 1), shifted(first, "az", -1))


def shifted(x, axis, by):
    count = lax.axis_size(axis)
    return lax.ppermute(x, axis, [(i, (i + by) % count) for i in range(count)])


def swapped(one, other, axis):
    count = lax.axis_size(axis)

    def partner(i, odd):
        j = i + 1 if i % 2 == odd else i - 1
        return j if 0 <= j < count else i

    return [
        lax.ppermute(x, axis, [(i, partner(i, odd)) for i in range(count)])
        for odd, x in enumerate((one, other))
    ]


def per_device(positions, velocity, diameter, cell_index, pair_list, live_pairs, gas_velocity):
    live = live_pairs.reshape(1, 1)
    cells = cell_index.reshape(128, LANES)
    gas = gas_velocity.reshape(3, 128, 2 * LANES)
    pos = positions.reshape(3, 128, LANES)
    vel = velocity.reshape(3, 128, LANES)
    diam = diameter.reshape(128, LANES)
    cell_keys, cell_ends, first, last = edge_states(cells, gas, pos, vel, diam)
    before = shifted(last, "az", 1)
    after = shifted(first, "az", -1)
    table = inner_states(cell_ends, cell_keys, gas, pos, vel, diam, first, last)
    pair_keys, pair_ends = pair_sort(live, pair_list.reshape(2, 256, LANES))
    heads, lower, upper = near_pairs(pair_ends, pair_keys, table, before, after)
    from_upper = shifted(lower, "az", -1)
    from_lower = shifted(upper, "az", 1)
    corr = own_pairs(live, pair_ends, pair_keys, table, heads)
    deposit, correction, one, other = deposits(
        cell_ends, cell_keys, table, corr, from_lower, from_upper
    )
    smoothed = filtered(deposit, one, other)
    return (correction.reshape(positions.shape), smoothed.reshape(gas_velocity.shape))


def solution(mesh):
    return jax.shard_map(
        per_device,
        mesh=mesh,
        in_specs=(
            P(None, "ax", "rad", "az"),
            P(None, "ax", "rad", "az"),
            P("ax", "rad", "az"),
            P("ax", "rad", "az"),
            P(None, "ax", "rad", "az"),
            P("ax", "rad", "az"),
            P(None, "ax", "rad", "az"),
        ),
        out_specs=(P(None, "ax", "rad", "az"), P(None, "ax", "rad", "az")),
        check_vma=False,
    )
```

```python
import functools
import math

import jax
import jax.numpy as jnp
from jax import lax
from jax.experimental import pallas as pl
from jax.experimental.pallas import tpu as pltpu
from jax.sharding import PartitionSpec as P

piep_coef = 1.0
drag_coef = 20.0

LANES = 128
ROWS = 8
BLOCK = 2048
GAS_WINDOW = 10
BUCKET = 1024
BUCKETS = 20
NEAR_BUCKETS = 4
NEAR_HEADS = 6
OWN_HEADS = 10
DEAD = 1 << 29

NT = (((1,), (1,)), ((), ()))
VMEM = pltpu.VMEM
SMEM = pltpu.SMEM


def params(megabytes=40):
    return pltpu.CompilerParams(vmem_limit_bytes=megabytes << 20)


def lane_gather(table, index):
    numbers = lax.GatherDimensionNumbers(
        offset_dims=(),
        collapsed_slice_dims=(1,),
        start_index_map=(1,),
        operand_batching_dims=(0,),
        start_indices_batching_dims=(0,),
    )
    return lax.gather(
        table,
        index[..., None],
        numbers,
        slice_sizes=(1, 1),
        mode=lax.GatherScatterMode.PROMISE_IN_BOUNDS,
    )


def sort_network(regs, place, levels):
    sub = lax.broadcasted_iota(jnp.int32, (ROWS, LANES), 0)
    lane = lax.broadcasted_iota(jnp.int32, (ROWS, LANES), 1)
    count = len(regs)

    def bit_fill(bit, v):
        if bit >= levels:
            return 0
        kind, k = place[bit]
        if kind == "v":
            return -((v >> k) & 1)
        return -(((sub if kind == "s" else lane) >> k) & 1)

    flip = [0] * count
    for level in range(1, levels + 1):
        fills = {}
        for v in range(count):
            kind, k = place[level] if level < levels else ("v", 99)
            key = (v >> k) & 1 if kind == "v" else 0
            if key not in fills:
                fills[key] = bit_fill(level, v)
            new = fills[key]
            if isinstance(new, int) and isinstance(flip[v], int):
                if new != flip[v]:
                    regs[v] = ~regs[v]
            else:
                regs[v] = regs[v] ^ (new ^ flip[v])
            flip[v] = new
        for bit in reversed(range(level)):
            kind, k = place[bit]
            step = 1 << k
            if kind == "v":
                for v in range(count):
                    if not v & step:
                        a, b = regs[v], regs[v | step]
                        regs[v], regs[v | step] = jnp.minimum(a, b), jnp.maximum(a, b)
            else:
                axis, size, where = (0, ROWS, sub) if kind == "s" else (1, LANES, lane)
                lower = (where & step) == 0
                for v in range(count):
                    x = regs[v]
                    ahead = pltpu.roll(x, size - step, axis)
                    behind = ahead if 2 * step == size else pltpu.roll(x, step, axis)
                    regs[v] = jnp.where(lower, jnp.minimum(x, ahead), jnp.maximum(x, behind))
    return regs


def split_two(x):
    high = x.astype(jnp.bfloat16).astype(jnp.float32)
    return high, x - high


def split_three(x):
    high, rest = split_two(x)
    mid, low = split_two(rest)
    return high, mid, low


def packed_row(ref, row):
    return jnp.broadcast_to(ref[row : row + 1, :], (16, LANES)).astype(jnp.bfloat16)


def one_hot_rows(low, iota):
    one = jnp.ones((16, LANES), jnp.bfloat16)
    zero = jnp.zeros((16, LANES), jnp.bfloat16)
    return jnp.concatenate(
        [jnp.where(low == iota[k : k + 16, :], one, zero) for k in range(0, iota.shape[0], 16)],
        axis=0,
    )


def spread_rows(rel, parts, iota):
    hit = rel == iota[0:16, :]
    zero = jnp.zeros((16, LANES), jnp.bfloat16)
    return jnp.concatenate([jnp.where(hit, p, zero) for part in parts for p in part], axis=0)


def spread_add(rows, hots):
    out = lax.dot_general(
        jnp.concatenate(rows, axis=1) if len(rows) > 1 else rows[0],
        jnp.concatenate(hots, axis=1) if len(hots) > 1 else hots[0],
        NT,
        preferred_element_type=jnp.float32,
    )
    total = out[0:48]
    for s in range(48, out.shape[0], 48):
        total = total + out[s : s + 48]
    return total


def fill_iota(iota):
    rows = lax.broadcasted_iota(jnp.int32, iota.shape, 0)
    iota[...] = rows.astype(jnp.float32).astype(jnp.bfloat16)


def rows_of(block):
    start = block * 16
    return pl.ds(start if isinstance(block, int) else pl.multiple_of(start, 16), 16)


def wide(ref, *at):
    return jnp.broadcast_to(ref[at[:-1] + (slice(at[-1], at[-1] + 1),)], (ROWS, LANES))


def window(table, first, count, row, low, found):
    rel = row - first
    for u in range(count):
        found = jnp.where(rel == u, lane_gather(table[first + u], low), found)
    return found


def running_max(x, count):
    x = jnp.broadcast_to(x, (ROWS, LANES))
    step = 1
    while step < count:
        x = jnp.maximum(x, pltpu.roll(x, LANES - step, 1))
        step *= 2
    return x


def by_partner(axis, first, last):
    even = (lax.axis_index(axis) & 1) == 0
    return jnp.where(even, last, first), jnp.where(even, first, last)


def from_partners(axis, one, other, wrap=False):
    at, count = lax.axis_index(axis), lax.axis_size(axis)
    even = (at & 1) == 0
    before, after = jnp.where(even, other, one), jnp.where(even, one, other)
    if wrap:
        return before, after
    return jnp.where(at > 0, before, 0.0), jnp.where(at < count - 1, after, 0.0)


def fill_gas_rows(gas_ref, gas_rows):
    for r in range(16):
        rows = slice(r * ROWS, (r + 1) * ROWS)
        for c in range(3):
            for half in range(2):
                gas_rows[rows, half * 4 + c, :] = gas_ref[c, rows, half * LANES : (half + 1) * LANES]


def gas_index(block, keys_ref, slot):
    idx = slot[0]
    keys = keys_ref[rows_of(block), :]
    idx[0] = lax.shift_right_logical(keys, 19)
    idx[1] = lax.shift_right_logical(keys, 11) & (LANES - 1)


def gas_gather(block, g, ends, gas_rows, slot):
    idx, found = slot[0], slot[1]
    zero = jnp.zeros((ROWS, LANES), jnp.float32)
    first = ends[0, block * 16 + g]
    found[g] = window(gas_rows, first, GAS_WINDOW, wide(idx, 0, g), wide(idx, 1, g), zero)


def gas_rest(block, ends, gas_rows, slot):
    idx, found = slot[0], slot[1]

    @pl.when(ends[2, block * 16] >= GAS_WINDOW)
    def _():
        def one(g, carry):
            first = ends[0, block * 16 + g]
            row = jnp.broadcast_to(idx[0, pl.ds(g, 1), :], (ROWS, LANES))
            low = jnp.broadcast_to(idx[1, pl.ds(g, 1), :], (ROWS, LANES))

            def trip(t, total):
                base = jnp.minimum(first + GAS_WINDOW * t, LANES)
                return window(gas_rows, base, GAS_WINDOW, row, low, total)

            trips = (ends[1, block * 16 + g] - first) // GAS_WINDOW + 1
            found[g] = lax.fori_loop(1, trips, trip, found[g])
            return carry

        lax.fori_loop(0, 16, one, 0)


def seen_values(block, keys_ref, slot):
    idx, found, val = slot
    keys = keys_ref[rows_of(block), :]
    upper = (keys & (1 << 18)) != 0
    place_in = keys & (BLOCK - 1)
    val[0] = lax.shift_right_logical(place_in, 7).astype(jnp.float32)
    val[1] = (place_in & (LANES - 1)).astype(jnp.float32)
    for c in range(3):
        seen = jnp.where(upper, found[:, 4 + c, :], found[:, c, :])
        for n, part in enumerate(split_three(seen)):
            val[2 + 3 * c + n] = part


def seen_in_order(groups, slot, iota):
    val = slot[2]
    rows, hots = [], []
    for g in groups:
        parts = [[packed_row(val.at[2 + 3 * c + n], g) for c in range(3)] for n in range(3)]
        rows.append(spread_rows(packed_row(val.at[0], g), parts, iota))
        hots.append(one_hot_rows(packed_row(val.at[1], g), iota))
    return spread_add(rows, hots)


def write_states(block, total, pos_ref, vel_ref, diam_ref, out_ref, out_rows):
    rows = rows_of(block)
    for c in range(3):
        out_ref[out_rows, c, :] = pos_ref[c, rows, :]
        out_ref[out_rows, 3 + c, :] = total[16 * c : 16 * c + 16] - vel_ref[c, rows, :]
    out_ref[out_rows, 6, :] = 0.5 * diam_ref[rows, :]
    out_ref[out_rows, 7, :] = jnp.zeros((16, LANES), jnp.float32)


def states_step(gather, scatter, keys_ref, ends, gas_rows, iota, arrays):
    total = jnp.zeros((48, LANES), jnp.float32)
    if gather:
        gas_index(gather[0], keys_ref, gather[1])
    if scatter:
        seen_values(scatter[0], keys_ref, scatter[1])
    for g in range(16):
        if gather:
            gas_gather(gather[0], g, ends, gas_rows, gather[1])
        if scatter and g % 2:
            total = total + seen_in_order((g - 1, g), scatter[1], iota)
    if scatter:
        write_states(scatter[0], total, *arrays, *scatter[2:])
    if gather:
        gas_rest(gather[0], ends, gas_rows, gather[1])


def states_kernel(
    cell_hbm, gas_hbm, pos_hbm, vel_hbm, diam_hbm,
    keys_ref, ends_ref, table_ref, one_ref, other_ref,
    cell_ref, gas_ref, pos_ref, vel_ref, diam_ref,
    gas_rows, iota, ends, idx_a, found_a, val_a, idx_b, found_b, val_b, sems,
):
    sources = (cell_hbm, gas_hbm, pos_hbm, vel_hbm, diam_hbm)
    places = (cell_ref, gas_ref, pos_ref, vel_ref, diam_ref)
    copies = [
        pltpu.make_async_copy(x, y, sems.at[n]) for n, (x, y) in enumerate(zip(sources, places))
    ]
    for copy in copies:
        copy.start()
    copies[0].wait()
    sub = lax.broadcasted_iota(jnp.int32, (ROWS, LANES), 0)
    lane = lax.broadcasted_iota(jnp.int32, (ROWS, LANES), 1)
    cells = cell_ref[...].T
    regs = []
    for v in range(16):
        own = (lane & 15) * LANES + v * ROWS + sub
        regs.append(cells[v * ROWS : (v + 1) * ROWS] * BLOCK + own)
    place = [("v", k) for k in range(4)] + [("s", k) for k in range(3)] + [("l", k) for k in range(4)]
    regs = sort_network(regs, place, 11)
    keys_ref[...] = jnp.concatenate(regs, axis=0).T
    least = functools.reduce(jnp.minimum, regs)
    most = functools.reduce(jnp.maximum, regs)
    least = lax.shift_right_logical(jnp.min(least, axis=0, keepdims=True), 19)
    most = lax.shift_right_logical(jnp.max(most, axis=0, keepdims=True), 19)
    ends_ref[0:1, :] = least
    ends_ref[1:2, :] = most
    ends_ref[2:8, :] = running_max(most - least, 16)[0:6]
    copy = pltpu.make_async_copy(ends_ref, ends, sems.at[5])
    copy.start()
    copies[1].wait()
    fill_gas_rows(gas_ref, gas_rows)
    for other in copies[2:]:
        other.wait()
    copy.wait()
    fill_iota(iota)
    a, b = (idx_a, found_a, val_a), (idx_b, found_b, val_b)
    step = functools.partial(
        states_step, keys_ref=keys_ref, ends=ends, gas_rows=gas_rows, iota=iota,
        arrays=(pos_ref, vel_ref, diam_ref),
    )
    step((0, a), None)

    def two(k, carry):
        block = 2 * k
        step((block + 1, b), (block, a, table_ref, rows_of(block)))
        step((block + 2, a), (block + 1, b, table_ref, rows_of(block + 1)))
        return carry

    lax.fori_loop(0, 3, two, 0)
    step((7, b), (6, a, table_ref, rows_of(6)))
    step(None, (7, b, table_ref, rows_of(7)))
    table_ref[128:144] = jnp.zeros((16, ROWS, LANES), jnp.float32)
    one_ref[...], other_ref[...] = by_partner("az", table_ref[0:16], table_ref[112:128])


def slots(rows, parts, dtype=jnp.float32):
    one = [VMEM((2, 16, LANES), jnp.int32), VMEM((16, ROWS, LANES), dtype), VMEM((parts, rows, LANES), dtype)]
    return one + one


def droplet_states(cells, gas, pos, vel, diam):
    f32, i32 = jnp.float32, jnp.int32
    arrays = (cells, gas, pos, vel, diam)
    return pl.pallas_call(
        states_kernel,
        name="droplet_states",
        out_shape=(
            jax.ShapeDtypeStruct((128, LANES), i32),
            jax.ShapeDtypeStruct((ROWS, LANES), i32),
            jax.ShapeDtypeStruct((144, ROWS, LANES), f32),
            jax.ShapeDtypeStruct((16, ROWS, LANES), f32),
            jax.ShapeDtypeStruct((16, ROWS, LANES), f32),
        ),
        in_specs=[pl.BlockSpec(memory_space=pltpu.HBM)] * 5,
        scratch_shapes=[VMEM(x.shape, x.dtype) for x in arrays]
        + [VMEM((144, ROWS, LANES), f32), VMEM((LANES, LANES), jnp.bfloat16), SMEM((ROWS, LANES), i32)]
        + slots(16, 11)
        + [pltpu.SemaphoreType.DMA((6,))],
        compiler_params=params(60),
    )(*arrays)


def pair_sort_kernel(live_ref, pairs_ref, keys_ref, ends_ref):
    live = live_ref[0, 0]
    sub = lax.broadcasted_iota(jnp.int32, (ROWS, LANES), 0)
    lane = lax.broadcasted_iota(jnp.int32, (ROWS, LANES), 1)
    regs = []
    for v in range(32):
        rows = slice(v * ROWS, (v + 1) * ROWS)
        slot = v * 1024 + sub * LANES + lane
        head = pairs_ref[0, rows, :]
        tail = pairs_ref[1, rows, :] - 7 * BLOCK
        own = tail - BLOCK
        inside = (own >= 0) & (own < 8 * BLOCK)
        tail = jnp.where(inside, jnp.maximum(own, head) + BLOCK, tail)
        head = jnp.where(inside, jnp.minimum(own, head), head)
        bucket = lax.shift_right_logical(tail, 10)
        bucket = jnp.where(inside, bucket + 2, jnp.where(bucket >= 18, bucket - 16, bucket))
        turn = -(bucket & 1) & (8 * BLOCK - 1)
        key = (bucket << 24) | ((head ^ turn) << 10) | (tail & (BUCKET - 1))
        regs.append(jnp.where(slot < live, key, DEAD))
    place = (
        [("v", k) for k in range(4)]
        + [("s", k) for k in range(3)]
        + [("v", 4)]
        + [("l", k) for k in range(7)]
    )
    regs = sort_network(regs, place, 15)
    beyond = jnp.zeros((ROWS, LANES), jnp.float32)
    for key in regs:
        beyond = beyond + jnp.where(key < NEAR_BUCKETS << 24, 1.0, 0.0)
    beyond = jnp.sum(jnp.sum(beyond, axis=0, keepdims=True), axis=1, keepdims=True)
    ends_ref[8:16, :] = jnp.broadcast_to(beyond, (ROWS, LANES)).astype(jnp.int32)
    for half in range(2):
        rows = regs[16 * half : 16 * half + 16]
        keys_ref[half] = jnp.concatenate(rows, axis=0).T
        least_head = least_tail = jnp.full((ROWS, LANES), 1 << 20, jnp.int32)
        most_head = most_tail = jnp.full((ROWS, LANES), -1, jnp.int32)
        for key in rows:
            used = key < DEAD
            bucket = lax.shift_right_logical(key, 24)
            head = lax.shift_right_logical(key, 17) & (LANES - 1)
            head = head ^ (-(bucket & 1) & (LANES - 1))
            least_head = jnp.minimum(least_head, jnp.where(used, head, 1 << 20))
            most_head = jnp.maximum(most_head, jnp.where(used, head, -1))
            least_tail = jnp.minimum(least_tail, jnp.where(used, bucket, 1 << 20))
            most_tail = jnp.maximum(most_tail, jnp.where(used, bucket, -1))
        for n, x in enumerate((least_head, most_head, least_tail, most_tail)):
            reduce = jnp.max if n % 2 else jnp.min
            row = 4 * half + n
            bound = (LANES, LANES, BUCKETS, BUCKETS)[n]
            ends_ref[row : row + 1, :] = jnp.minimum(reduce(x, axis=0, keepdims=True), bound)


def pair_sort(live, pairs):
    return pl.pallas_call(
        pair_sort_kernel,
        name="pair_sort",
        out_shape=(
            jax.ShapeDtypeStruct((2, LANES, LANES), jnp.int32),
            jax.ShapeDtypeStruct((16, LANES), jnp.int32),
        ),
        in_specs=[pl.BlockSpec(memory_space=SMEM), pl.BlockSpec(memory_space=VMEM)],
        compiler_params=params(),
    )(live, pairs)


def take_items(state, groups, ends, part):
    low, high, heads = part
    items = []
    for _ in range(ROWS):
        g, bucket, head = state
        valid = g < groups
        seen = jnp.minimum(g, 2 * LANES - 1)
        at, lane = 4 * (seen & 1), seen >> 1
        items.append((seen, jnp.where(valid, bucket, -1), head, jnp.minimum(bucket, high) - low))
        more_heads = head + heads <= ends[at + 1, lane]
        more_tails = bucket < jnp.minimum(ends[at + 3, lane], high - 1)
        step = jnp.where(more_heads | more_tails, 0, 1)
        g = jnp.minimum(g + step, 2 * LANES)
        seen = jnp.minimum(g, 2 * LANES - 1)
        at, lane = 4 * (seen & 1), seen >> 1
        head = jnp.where(more_heads, head + heads, ends[at, lane])
        same = jnp.where(more_heads, bucket, bucket + 1)
        bucket = jnp.where(step == 1, jnp.maximum(ends[at + 2, lane], low), same)
        state = (g, bucket, head)
    return items, state


def pair_gather(k, item, keys_ref, near_table, far_parts, heads, slot, iota, pick):
    key_rows, rel_rows, near, far, _, hots = slot
    g, bucket, first, part = item
    keys = jnp.broadcast_to(keys_ref[g & 1, pl.ds(g >> 1, 1), :], (ROWS, LANES))
    of_bucket = lax.shift_right_logical(keys, 24)
    turn = -(of_bucket & 1) & (8 * BLOCK - 1)
    head = (lax.shift_right_logical(keys, 10) & (8 * BLOCK - 1)) ^ turn
    rel = lax.shift_right_logical(head, 7) - first
    tail_row = lax.shift_right_logical(keys, 7) & 7
    used = (of_bucket == bucket) & (rel >= 0) & (rel < heads)
    key_rows[k : k + 1, :] = jnp.where(used, keys, DEAD)[0:1]
    rel_rows[k : k + 1, :] = rel[0:1]
    zero = jnp.zeros((ROWS, LANES), jnp.float32)
    low = head & (LANES - 1)
    found = zero
    for u in range(heads):
        found = jnp.where(rel == u, lane_gather(near_table[first + u], low), found)
    near[k] = found
    low = (keys & (LANES - 1)).astype(jnp.float32)
    low = jnp.concatenate([low, low], axis=0).astype(jnp.bfloat16)
    hot = one_hot_rows(low, iota)
    hots[k] = hot
    found = jnp.dot(far_parts[part], hot, preferred_element_type=jnp.float32)
    hit = tail_row == lax.broadcasted_iota(jnp.int32, (ROWS, LANES), 0)
    masked = [jnp.where(hit, found[8 * q : 8 * q + 8], 0.0) for q in range(14)]
    masked = jnp.concatenate(masked, axis=0).astype(jnp.bfloat16)
    far[k] = jnp.dot(pick[...], masked, preferred_element_type=jnp.float32)[0:8]


def pair_values(slot):
    key_rows, rel_rows, near, far, val = slot[0:5]
    keys = key_rows[...]
    used = keys < DEAD
    turn = -(lax.shift_right_logical(keys, 24) & 1) & (LANES - 1)
    val[0] = rel_rows[...].astype(jnp.float32)
    val[1] = ((lax.shift_right_logical(keys, 10) & (LANES - 1)) ^ turn).astype(jnp.float32)
    val[2] = (lax.shift_right_logical(keys, 7) & 7).astype(jnp.float32)
    gap = jnp.zeros((ROWS, LANES), jnp.float32)
    for c in range(3):
        apart = far[:, c, :] - near[:, c, :]
        gap = gap + apart * apart
    far_radius, near_radius = far[:, 6, :], near[:, 6, :]
    far_ratio = far_radius * lax.rsqrt(gap + far_radius * far_radius)
    near_ratio = near_radius * lax.rsqrt(gap + near_radius * near_radius)
    weight_far = jnp.where(used, piep_coef * far_ratio * far_ratio * far_ratio, 0.0)
    weight_near = jnp.where(used, piep_coef * near_ratio * near_ratio * near_ratio, 0.0)
    for c in range(3):
        for n, part in enumerate(split_two(weight_far * far[:, 3 + c, :])):
            val[4 + 3 * n + c] = part
        for n, part in enumerate(split_two(weight_near * near[:, 3 + c, :])):
            val[10 + 3 * n + c] = part


def pair_scatter(k, item, slot, head_sum, tail_sum, iota, iota8):
    val, hots = slot[4:6]
    first, tail_first = item
    parts = [[packed_row(val.at[4 + 3 * n + c], k) for c in range(3)] for n in range(2)]
    rows = spread_rows(packed_row(val.at[0], k), parts, iota)
    out = spread_add([rows], [one_hot_rows(packed_row(val.at[1], k), iota)])
    for c in range(3):
        head_sum[c, pl.ds(first, 16), :] += out[16 * c : 16 * c + 16]

    hit = packed_row(val.at[2], k) == iota8[...]
    zero = jnp.zeros((16, LANES), jnp.bfloat16)
    tiles = []
    for n in range(10, 16, 2):
        both = jnp.concatenate([wide(val, n, k), wide(val, n + 1, k)], axis=0)
        tiles.append(jnp.where(hit, both.astype(jnp.bfloat16), zero))
    out = lax.dot_general(
        jnp.concatenate(tiles, axis=0),
        hots[k],
        NT,
        preferred_element_type=jnp.float32,
    )
    at = pl.ds(pl.multiple_of(tail_first, 8), 8)
    for c in range(3):
        tail_sum[c, at, :] += out[8 * c : 8 * c + 8] + out[24 + 8 * c : 32 + 8 * c]


def run_pairs(
    groups, start, part, ends, keys_ref, near_table, far_table, far_parts, sums, iota, iota8, pick, slots_
):
    fill_iota(iota)
    rows = lax.broadcasted_iota(jnp.int32, iota8.shape, 0) & 7
    iota8[...] = rows.astype(jnp.float32).astype(jnp.bfloat16)
    rows = lax.broadcasted_iota(jnp.int32, pick.shape, 0)
    columns = lax.broadcasted_iota(jnp.int32, pick.shape, 1)
    channel = lax.shift_right_logical(columns, 3)
    channel = jnp.where(channel >= 7, channel - 7, channel)
    pick[...] = jnp.where(rows == channel, 1.0, 0.0).astype(jnp.bfloat16)

    def one_bucket(n, carry):
        block = pl.ds(pl.multiple_of(n * 8, 8), 8)
        pieces = [split_two(far_table[block, c, :]) for c in range(7)]
        pieces = [p[0] for p in pieces] + [p[1] for p in pieces]
        for t in range(7):
            both = jnp.concatenate(pieces[2 * t : 2 * t + 2], axis=0)
            far_parts[n, 16 * t : 16 * t + 16, :] = both.astype(jnp.bfloat16)
        return carry

    lax.fori_loop(0, far_parts.shape[0], one_bucket, 0)
    a, b = slots_[0:6], slots_[6:12]

    def step(state, slot, pending, other):
        items, state = take_items(state, groups, ends, part)
        if other:
            pair_values(other)
        for k in range(ROWS):
            pair_gather(k, items[k], keys_ref, near_table, far_parts, part[2], slot, iota, pick)
            if other:
                pair_scatter(k, pending[k], other, *sums, iota, iota8)
        return tuple((item[2], item[3] * 8) for item in items), state, items[0][1] >= 0

    at, lane = 4 * (start & 1), start >> 1
    state = (start, jnp.maximum(ends[at + 2, lane], part[0]), ends[at, lane])
    carry = step(state, a, None, None)

    def two(carry):
        pending, state, _ = carry
        pending, state, _ = step(state, b, pending, a)
        return step(state, a, pending, b)

    lax.while_loop(lambda carry: carry[2], two, carry)


def near_pairs_kernel(
    ends, keys_ref, table_ref, one_in, other_in,
    heads_ref, one_ref, other_ref,
    shell, far_parts, head_sum, tail_sum, iota, iota8, pick, *slots_,
):
    shell[0:16], shell[16:32] = from_partners("az", one_in[...], other_in[...], True)
    shell[32:40] = jnp.zeros((8, ROWS, LANES), jnp.float32)
    head_sum[...] = jnp.zeros_like(head_sum)
    tail_sum[...] = jnp.zeros_like(tail_sum)
    groups = (ends[8, 0] + LANES - 1) // LANES
    run_pairs(
        groups, jnp.int32(0), (0, NEAR_BUCKETS, NEAR_HEADS), ends, keys_ref, table_ref, shell,
        far_parts, (head_sum, tail_sum), iota, iota8, pick, slots_,
    )
    heads_ref[...] = head_sum[:, 0:128, :]
    one_ref[...], other_ref[...] = by_partner("az", tail_sum[:, 0:16, :], tail_sum[:, 16:32, :])


def own_pairs_kernel(
    live_ref, ends, keys_ref, table_ref, heads_ref,
    corr_ref,
    far_parts, head_sum, tail_sum, iota, iota8, pick, *slots_,
):
    head_sum[:, 0:128, :] = heads_ref[...]
    head_sum[:, 128:144, :] = jnp.zeros((3, 16, LANES), jnp.float32)
    tail_sum[...] = jnp.zeros_like(tail_sum)
    groups = (live_ref[0, 0] + LANES - 1) // LANES
    start = jnp.minimum(ends[8, 0] // LANES, 2 * LANES - 1)
    run_pairs(
        groups, start, (NEAR_BUCKETS, BUCKETS, OWN_HEADS), ends, keys_ref, table_ref, table_ref,
        far_parts, (head_sum, tail_sum), iota, iota8, pick, slots_,
    )
    corr_ref[...] = head_sum[:, 0:128, :] + tail_sum[:, 0:128, :]


def pair_scratch(tail_rows):
    f32, i32 = jnp.float32, jnp.int32
    slot = [
        VMEM((ROWS, LANES), i32),
        VMEM((ROWS, LANES), i32),
        VMEM((ROWS, ROWS, LANES), f32),
        VMEM((ROWS, ROWS, LANES), f32),
        VMEM((16, ROWS, LANES), f32),
        VMEM((ROWS, LANES, LANES), jnp.bfloat16),
    ]
    return [
        VMEM((tail_rows // 8, 112, LANES), jnp.bfloat16),
        VMEM((3, 144, LANES), f32),
        VMEM((3, tail_rows, LANES), f32),
        VMEM((LANES, LANES), jnp.bfloat16),
        VMEM((16, LANES), jnp.bfloat16),
        VMEM((16, 112), jnp.bfloat16),
        *slot,
        *slot,
    ]


def near_pairs(ends, keys, table, one, other):
    f32 = jnp.float32
    smem, vmem = pl.BlockSpec(memory_space=SMEM), pl.BlockSpec(memory_space=VMEM)
    return pl.pallas_call(
        near_pairs_kernel,
        name="near_pairs",
        out_shape=(
            jax.ShapeDtypeStruct((3, 128, LANES), f32),
            jax.ShapeDtypeStruct((3, 16, LANES), f32),
            jax.ShapeDtypeStruct((3, 16, LANES), f32),
        ),
        in_specs=[smem, vmem, vmem, vmem, vmem],
        scratch_shapes=[VMEM((40, ROWS, LANES), f32)] + pair_scratch(40),
        compiler_params=params(),
    )(ends, keys, table, one, other)


def own_pairs(live, ends, keys, table, heads):
    smem, vmem = pl.BlockSpec(memory_space=SMEM), pl.BlockSpec(memory_space=VMEM)
    return pl.pallas_call(
        own_pairs_kernel,
        name="own_pairs",
        out_shape=jax.ShapeDtypeStruct((3, 128, LANES), jnp.float32),
        in_specs=[smem, smem, vmem, vmem, vmem],
        scratch_shapes=pair_scratch(136),
        compiler_params=params(),
    )(live, ends, keys, table, heads)


def force_gather(block, keys_ref, table_ref, total_ref, slot):
    force, got, val = slot
    rows = rows_of(block)
    scale = (-2.0 * drag_coef) * table_ref[rows, 6, :]
    for c in range(3):
        push = scale * (table_ref[rows, 3 + c, :] + total_ref[c, rows, :])
        force[:, c, :] = push[0:8]
        force[:, 4 + c, :] = push[8:16]
    keys = keys_ref[rows, :]
    val[0] = lax.shift_right_logical(keys, 19).astype(jnp.float32)
    val[1] = (lax.shift_right_logical(keys, 11) & (2 * LANES - 1)).astype(jnp.float32)
    inner = lax.shift_right_logical(keys, 7) & 7
    low = keys & (LANES - 1)
    tables = [force[k] for k in range(ROWS)]
    for g in range(16):
        pick = jnp.broadcast_to(inner[g : g + 1, :], (ROWS, LANES))
        at = jnp.broadcast_to(low[g : g + 1, :], (ROWS, LANES))
        found = jnp.zeros((ROWS, LANES), jnp.float32)
        for k in range(ROWS):
            found = jnp.where(pick == k, lane_gather(tables[k], at), found)
        got[g] = found
    upper = (keys & 1024) != 0
    for c in range(3):
        pushed = jnp.where(upper, got[:, 4 + c, :], got[:, c, :])
        for n, part in enumerate(split_two(pushed)):
            val[2 + 2 * c + n] = part


def force_add(g, base, slot, cells, iota):
    val = slot[2]

    def row(n):
        if isinstance(g, int):
            return packed_row(val.at[n], g)
        return jnp.broadcast_to(val[n, pl.ds(g, 1), :], (16, LANES)).astype(jnp.bfloat16)

    rel = row(0) - base.astype(jnp.float32).astype(jnp.bfloat16)
    parts = [[row(2 + 2 * c + n) for c in range(3)] for n in range(2)]
    out = spread_add([spread_rows(rel, parts, iota)], [one_hot_rows(row(1), iota)])
    for c in range(3):
        for half in range(2):
            part = out[16 * c : 16 * c + 16, half * LANES : (half + 1) * LANES]
            cells[2 * c + half, pl.ds(base, 16), :] += part


def force_rest(block, ends, slot, cells, iota):
    @pl.when(ends[2, block * 16] >= 16)
    def _():
        def one(g, carry):
            first, most = ends[0, block * 16 + g], ends[1, block * 16 + g]

            def trip(t, carry):
                force_add(g, jnp.minimum(first + 16 * t, LANES), slot, cells, iota)
                return carry

            lax.fori_loop(1, (most - first) // 16 + 1, trip, 0)
            return carry

        lax.fori_loop(0, 16, one, 0)


def deposit_step(gather, scatter, ends, keys_ref, table_ref, total_ref, cells, iota):
    if gather:
        force_gather(gather[0], keys_ref, table_ref, total_ref, gather[1])
    if scatter:
        for g in range(16):
            force_add(g, ends[0, scatter[0] * 16 + g], scatter[1], cells, iota)
        force_rest(scatter[0], ends, scatter[1], cells, iota)


def deposit_kernel(
    ends, keys_ref, table_ref, corr_ref, one_in, other_in,
    out_ref, total_ref, one_ref, other_ref,
    cells, iota, force_a, got_a, val_a, force_b, got_b, val_b,
):
    fill_iota(iota)
    cells[...] = jnp.zeros_like(cells)
    total_ref[...] = corr_ref[...]
    before, after = from_partners("az", one_in[...], other_in[...], True)
    total_ref[:, 0:16, :] += before
    total_ref[:, 112:128, :] += after
    a, b = (force_a, got_a, val_a), (force_b, got_b, val_b)
    step = functools.partial(
        deposit_step, ends=ends, keys_ref=keys_ref, table_ref=table_ref, total_ref=total_ref,
        cells=cells, iota=iota,
    )
    step((0, a), None)

    def two(k, carry):
        block = 2 * k
        step((block + 1, b), (block, a))
        step((block + 2, a), (block + 1, b))
        return carry

    lax.fori_loop(0, 3, two, 0)
    step((7, b), (6, a))
    step(None, (7, b))
    for c in range(3):
        for half in range(2):
            columns = slice(half * LANES, (half + 1) * LANES)
            out_ref[c, :, columns] = cells[2 * c + half, 0:128, :]
            one, other = by_partner(
                "ax", cells[2 * c + half, 0:32, :], cells[2 * c + half, 96:128, :]
            )
            one_ref[c, :, columns] = one
            other_ref[c, :, columns] = other


def deposits(ends, keys, table, corr, one, other):
    f32 = jnp.float32
    smem, vmem = pl.BlockSpec(memory_space=SMEM), pl.BlockSpec(memory_space=VMEM)
    slot = [VMEM((ROWS, ROWS, LANES), f32), VMEM((16, ROWS, LANES), f32), VMEM((8, 16, LANES), f32)]
    return pl.pallas_call(
        deposit_kernel,
        name="deposits",
        out_shape=(
            jax.ShapeDtypeStruct((3, 128, 2 * LANES), f32),
            jax.ShapeDtypeStruct((3, 128, LANES), f32),
            jax.ShapeDtypeStruct((3, 32, 2 * LANES), f32),
            jax.ShapeDtypeStruct((3, 32, 2 * LANES), f32),
        ),
        in_specs=[smem] + [vmem] * 5,
        scratch_shapes=[VMEM((6, 144, LANES), f32), VMEM((2 * LANES, LANES), jnp.bfloat16)]
        + slot
        + slot,
        compiler_params=params(),
    )(ends, keys, table, corr, one, other)


def axial_kernel(taps, cells_ref, one_in, other_in, out_ref, one_ref, other_ref, first_ref, last_ref):
    for c in range(3):
        before, after = from_partners("ax", one_in[c], other_in[c])
        padded = jnp.concatenate([before, cells_ref[c], after], axis=0)
        total = taps[0] * padded[0:128]
        for k in range(1, 5):
            total = total + taps[k] * padded[16 * k : 16 * k + 128]
        out_ref[c] = total
        for a in range(8):
            first_ref[2 * a : 2 * a + 2, :] = total[16 * a : 16 * a + 2]
            last_ref[2 * a : 2 * a + 2, :] = total[16 * a + 14 : 16 * a + 16]
        one_ref[c], other_ref[c] = by_partner("rad", first_ref[...], last_ref[...])


def radial_kernel(
    taps, cells_ref, one_in, other_in, out_ref, one_ref, other_ref, padded, before_ref, after_ref
):
    lane = lax.broadcasted_iota(jnp.int32, (LANES, LANES), 1)
    edges = jnp.zeros((LANES, LANES), jnp.float32)
    for c in range(3):
        before_ref[...], after_ref[...] = from_partners("rad", one_in[c], other_in[c])
        for a in range(8):
            padded[0:2, :] = before_ref[2 * a : 2 * a + 2, :]
            padded[2:18, :] = cells_ref[c, 16 * a : 16 * a + 16, :]
            padded[18:20, :] = after_ref[2 * a : 2 * a + 2, :]
            total = taps[0] * padded[0:16, :]
            for k in range(1, 5):
                total = total + taps[k] * padded[k : k + 16, :]
            out_ref[c, 16 * a : 16 * a + 16, :] = total
        left, right = out_ref[c, :, 0:LANES], out_ref[c, :, LANES:]
        if c:
            left = pltpu.roll(left, 2 * c, 1)
        right = pltpu.roll(right, 10 + 2 * c, 1)
        edges = jnp.where((lane >> 1) == c, left, edges)
        edges = jnp.where((lane >> 1) == 4 + c, right, edges)
    turned = edges.T
    one_ref[...], other_ref[...] = by_partner("az", turned[0:8], turned[8:16])


def azimuthal_kernel(taps, cells_ref, one_in, other_in, out_ref):
    lane = lax.broadcasted_iota(jnp.int32, (LANES, LANES), 1)
    rest = jnp.zeros((LANES - 16, LANES), jnp.float32)
    before, after = from_partners("az", one_in[...], other_in[...], True)
    edges = jnp.concatenate([after, before, rest], axis=0).T
    for c in range(3):
        ahead = pltpu.roll(edges, LANES - 2 * c, 1) if c else edges
        halo = jnp.where(lane < 64, ahead, pltpu.roll(edges, 118 - 2 * c, 1))
        left, right = cells_ref[c, :, 0:LANES], cells_ref[c, :, LANES:]
        out_left, out_right = taps[2] * left, taps[2] * right
        for k in (1, 2):
            tap = taps[2 + k]
            inner = lane < LANES - k
            x, y, z = (pltpu.roll(v, LANES - k, 1) for v in (left, right, halo))
            out_left = out_left + tap * jnp.where(inner, x, y)
            out_right = out_right + tap * jnp.where(inner, y, z)
            inner = lane >= k
            x, y, z = (pltpu.roll(v, k, 1) for v in (left, right, halo))
            out_left = out_left + tap * jnp.where(inner, x, z)
            out_right = out_right + tap * jnp.where(inner, y, x)
        out_ref[c, :, 0:LANES] = out_left
        out_ref[c, :, LANES:] = out_right


def filtered(deposit, one, other):
    f32 = jnp.float32
    raw = [math.exp(-0.5 * k * k) for k in range(-2, 3)]
    taps = [x / sum(raw) for x in raw]
    whole = jax.ShapeDtypeStruct(deposit.shape, f32)
    radial_face = jax.ShapeDtypeStruct((3, 16, 2 * LANES), f32)
    edge = jax.ShapeDtypeStruct((8, LANES), f32)
    cells, one, other = pl.pallas_call(
        functools.partial(axial_kernel, taps),
        name="axial_filter",
        out_shape=(whole, radial_face, radial_face),
        scratch_shapes=[VMEM((16, 2 * LANES), f32)] * 2,
        compiler_params=params(),
    )(deposit, *swapped(one, other, "ax"))
    cells, one, other = pl.pallas_call(
        functools.partial(radial_kernel, taps),
        name="radial_filter",
        out_shape=(whole, edge, edge),
        scratch_shapes=[VMEM((24, 2 * LANES), f32)] + [VMEM((16, 2 * LANES), f32)] * 2,
        compiler_params=params(),
    )(cells, *swapped(one, other, "rad"))
    return pl.pallas_call(
        functools.partial(azimuthal_kernel, taps),
        name="azimuthal_filter",
        out_shape=whole,
        compiler_params=params(),
    )(cells, *swapped(one, other, "az", True))


def swapped(one, other, axis, wrap=False):
    count = lax.axis_size(axis)

    def partner(i, odd):
        j = i + 1 if i % 2 == odd else i - 1
        return j % count if wrap or 0 <= j < count else i

    return [
        lax.ppermute(x, axis, [(i, partner(i, odd)) for i in range(count)])
        for odd, x in enumerate((one, other))
    ]


def per_device(positions, velocity, diameter, cell_index, pair_list, live_pairs, gas_velocity):
    live = live_pairs.reshape(1, 1)
    cells = cell_index.reshape(128, LANES)
    gas = gas_velocity.reshape(3, 128, 2 * LANES)
    pos = positions.reshape(3, 128, LANES)
    vel = velocity.reshape(3, 128, LANES)
    diam = diameter.reshape(128, LANES)
    cell_keys, cell_ends, table, one, other = droplet_states(cells, gas, pos, vel, diam)
    one, other = swapped(one, other, "az", True)
    pair_keys, pair_ends = pair_sort(live, pair_list.reshape(2, 256, LANES))
    heads, one, other = near_pairs(pair_ends, pair_keys, table, one, other)
    one, other = swapped(one, other, "az", True)
    corr = own_pairs(live, pair_ends, pair_keys, table, heads)
    deposit, correction, one, other = deposits(cell_ends, cell_keys, table, corr, one, other)
    smoothed = filtered(deposit, one, other)
    return (correction.reshape(positions.shape), smoothed.reshape(gas_velocity.shape))


def solution(mesh):
    return jax.shard_map(
        per_device,
        mesh=mesh,
        in_specs=(
            P(None, "ax", "rad", "az"),
            P(None, "ax", "rad", "az"),
            P("ax", "rad", "az"),
            P("ax", "rad", "az"),
            P(None, "ax", "rad", "az"),
            P("ax", "rad", "az"),
            P(None, "ax", "rad", "az"),
        ),
        out_specs=(P(None, "ax", "rad", "az"), P(None, "ax", "rad", "az")),
        check_vma=False,
    )
```

```python
import functools
import math

import jax
import jax.numpy as jnp
from jax import lax
from jax.experimental import pallas as pl
from jax.experimental.pallas import tpu as pltpu
from jax.sharding import PartitionSpec as P

piep_coef = 1.0
drag_coef = 20.0

LANES = 128
ROWS = 8
BLOCK = 2048
GAS_WINDOW = 10
BUCKET = 1024
BUCKETS = 20
NEAR_BUCKETS = 4
NEAR_HEADS = 8
OWN_HEADS = 12
DEAD = 1 << 29

NT = (((1,), (1,)), ((), ()))
VMEM = pltpu.VMEM
SMEM = pltpu.SMEM


def params(megabytes=40):
    return pltpu.CompilerParams(vmem_limit_bytes=megabytes << 20)


def lane_gather(table, index):
    numbers = lax.GatherDimensionNumbers(
        offset_dims=(),
        collapsed_slice_dims=(1,),
        start_index_map=(1,),
        operand_batching_dims=(0,),
        start_indices_batching_dims=(0,),
    )
    return lax.gather(
        table,
        index[..., None],
        numbers,
        slice_sizes=(1, 1),
        mode=lax.GatherScatterMode.PROMISE_IN_BOUNDS,
    )


def sort_network(regs, place, levels):
    sub = lax.broadcasted_iota(jnp.int32, (ROWS, LANES), 0)
    lane = lax.broadcasted_iota(jnp.int32, (ROWS, LANES), 1)
    count = len(regs)

    def bit_fill(bit, v):
        if bit >= levels:
            return 0
        kind, k = place[bit]
        if kind == "v":
            return -((v >> k) & 1)
        return -(((sub if kind == "s" else lane) >> k) & 1)

    flip = [0] * count
    for level in range(1, levels + 1):
        fills = {}
        for v in range(count):
            kind, k = place[level] if level < levels else ("v", 99)
            key = (v >> k) & 1 if kind == "v" else 0
            if key not in fills:
                fills[key] = bit_fill(level, v)
            new = fills[key]
            if isinstance(new, int) and isinstance(flip[v], int):
                if new != flip[v]:
                    regs[v] = ~regs[v]
            else:
                regs[v] = regs[v] ^ (new ^ flip[v])
            flip[v] = new
        for bit in reversed(range(level)):
            kind, k = place[bit]
            step = 1 << k
            if kind == "v":
                for v in range(count):
                    if not v & step:
                        a, b = regs[v], regs[v | step]
                        regs[v], regs[v | step] = jnp.minimum(a, b), jnp.maximum(a, b)
            else:
                axis, size, where = (0, ROWS, sub) if kind == "s" else (1, LANES, lane)
                lower = (where & step) == 0
                for v in range(count):
                    x = regs[v]
                    ahead = pltpu.roll(x, size - step, axis)
                    behind = ahead if 2 * step == size else pltpu.roll(x, step, axis)
                    regs[v] = jnp.where(lower, jnp.minimum(x, ahead), jnp.maximum(x, behind))
    return regs


def split_two(x):
    high = x.astype(jnp.bfloat16).astype(jnp.float32)
    return high, x - high


def split_three(x):
    high, rest = split_two(x)
    mid, low = split_two(rest)
    return high, mid, low


def packed_row(ref, row):
    return jnp.broadcast_to(ref[row : row + 1, :], (16, LANES)).astype(jnp.bfloat16)


def one_hot_rows(low, iota):
    one = jnp.ones((16, LANES), jnp.bfloat16)
    zero = jnp.zeros((16, LANES), jnp.bfloat16)
    return jnp.concatenate(
        [jnp.where(low == iota[k : k + 16, :], one, zero) for k in range(0, iota.shape[0], 16)],
        axis=0,
    )


def spread_rows(rel, parts, iota):
    hit = rel == iota[0:16, :]
    zero = jnp.zeros((16, LANES), jnp.bfloat16)
    return jnp.concatenate([jnp.where(hit, p, zero) for part in parts for p in part], axis=0)


def spread_add(rows, hots):
    out = lax.dot_general(
        jnp.concatenate(rows, axis=1) if len(rows) > 1 else rows[0],
        jnp.concatenate(hots, axis=1) if len(hots) > 1 else hots[0],
        NT,
        preferred_element_type=jnp.float32,
    )
    total = out[0:48]
    for s in range(48, out.shape[0], 48):
        total = total + out[s : s + 48]
    return total


def fill_iota(iota):
    rows = lax.broadcasted_iota(jnp.int32, iota.shape, 0)
    iota[...] = rows.astype(jnp.float32).astype(jnp.bfloat16)


def rows_of(block):
    start = block * 16
    return pl.ds(start if isinstance(block, int) else pl.multiple_of(start, 16), 16)


def wide(ref, *at):
    return jnp.broadcast_to(ref[at[:-1] + (slice(at[-1], at[-1] + 1),)], (ROWS, LANES))


def window(table, first, count, row, low, found):
    rel = row - first
    for u in range(count):
        found = jnp.where(rel == u, lane_gather(table[first + u], low), found)
    return found


def running_max(x, count):
    x = jnp.broadcast_to(x, (ROWS, LANES))
    step = 1
    while step < count:
        x = jnp.maximum(x, pltpu.roll(x, LANES - step, 1))
        step *= 2
    return x


def by_partner(axis, first, last):
    even = (lax.axis_index(axis) & 1) == 0
    return jnp.where(even, last, first), jnp.where(even, first, last)


def from_partners(axis, one, other, wrap=False):
    at, count = lax.axis_index(axis), lax.axis_size(axis)
    even = (at & 1) == 0
    before, after = jnp.where(even, other, one), jnp.where(even, one, other)
    if wrap:
        return before, after
    return jnp.where(at > 0, before, 0.0), jnp.where(at < count - 1, after, 0.0)


PLACE_STEP = 0.1 / 65535.0
RADIUS_LEAST = 0.01
RADIUS_STEP = 0.04 / 65535.0
SLIP_HALF = 1 << 20


def largest_slip(table, rows):
    most = jnp.zeros((ROWS, LANES), jnp.float32)
    for n in range(0, rows, ROWS):
        for c in range(3):
            most = jnp.maximum(most, jnp.abs(table[n : n + ROWS, 3 + c, :]))
    most = jnp.max(jnp.max(most, axis=0, keepdims=True), axis=1, keepdims=True)
    return jnp.broadcast_to(jnp.maximum(most, 1e-30), (ROWS, LANES))


def code_rows(table, n, largest, words):
    rows = pl.ds(n * ROWS, ROWS)

    def whole(c, least, step):
        x = ((table[rows, c, :] - least) * (1.0 / step) + 0.5).astype(jnp.int32)
        return jnp.clip(x, 0, 65535)

    x, y, z = (whole(c, 0.0, PLACE_STEP) for c in range(3))
    radius = whole(6, RADIUS_LEAST, RADIUS_STEP)
    scale = (SLIP_HALF - 1.0) / largest
    u, v, w = (
        (table[rows, 3 + c, :] * scale + (SLIP_HALF + 0.5)).astype(jnp.int32) for c in range(3)
    )
    coded = (
        x | (y << 16),
        z | (radius << 16),
        u | ((w & 2047) << 21),
        v | (lax.shift_right_logical(w, 11) << 21),
    )
    for k, word in enumerate(coded):
        words[pl.ds(n * 32 + k, ROWS, stride=4), :] = word


def decoded(words, largest):
    low = [x & 65535 for x in words[0:2]]
    high = [lax.shift_right_logical(x, 16) for x in words[0:2]]
    place = (low[0], high[0], low[1])
    radius = high[1].astype(jnp.float32) * RADIUS_STEP + RADIUS_LEAST
    mask = 2 * SLIP_HALF - 1
    third = lax.shift_right_logical(words[2], 21) | (lax.shift_right_logical(words[3], 21) << 11)
    scale = largest * (1.0 / (SLIP_HALF - 1.0))
    slip = [
        (x - SLIP_HALF).astype(jnp.float32) * scale for x in (words[2] & mask, words[3] & mask, third)
    ]
    return place, radius, slip


def fill_gas_rows(gas_ref, gas_rows):
    for r in range(16):
        rows = slice(r * ROWS, (r + 1) * ROWS)
        for c in range(3):
            for half in range(2):
                gas_rows[rows, half * 4 + c, :] = gas_ref[c, rows, half * LANES : (half + 1) * LANES]


def gas_index(block, keys_ref, slot):
    idx = slot[0]
    keys = keys_ref[rows_of(block), :]
    idx[0] = lax.shift_right_logical(keys, 19)
    idx[1] = lax.shift_right_logical(keys, 11) & (LANES - 1)


def gas_gather(block, g, ends, gas_rows, slot):
    idx, found = slot[0], slot[1]
    zero = jnp.zeros((ROWS, LANES), jnp.float32)
    first = ends[0, block * 16 + g]
    found[g] = window(gas_rows, first, GAS_WINDOW, wide(idx, 0, g), wide(idx, 1, g), zero)


def gas_rest(block, ends, gas_rows, slot):
    idx, found = slot[0], slot[1]

    @pl.when(ends[2, block * 16] >= GAS_WINDOW)
    def _():
        def one(g, carry):
            first = ends[0, block * 16 + g]
            row = jnp.broadcast_to(idx[0, pl.ds(g, 1), :], (ROWS, LANES))
            low = jnp.broadcast_to(idx[1, pl.ds(g, 1), :], (ROWS, LANES))

            def trip(t, total):
                base = jnp.minimum(first + GAS_WINDOW * t, LANES)
                return window(gas_rows, base, GAS_WINDOW, row, low, total)

            trips = (ends[1, block * 16 + g] - first) // GAS_WINDOW + 1
            found[g] = lax.fori_loop(1, trips, trip, found[g])
            return carry

        lax.fori_loop(0, 16, one, 0)


def seen_values(block, keys_ref, slot):
    idx, found, val = slot
    keys = keys_ref[rows_of(block), :]
    upper = (keys & (1 << 18)) != 0
    place_in = keys & (BLOCK - 1)
    val[0] = lax.shift_right_logical(place_in, 7).astype(jnp.float32)
    val[1] = (place_in & (LANES - 1)).astype(jnp.float32)
    for c in range(3):
        seen = jnp.where(upper, found[:, 4 + c, :], found[:, c, :])
        for n, part in enumerate(split_three(seen)):
            val[2 + 3 * c + n] = part


def seen_in_order(groups, slot, iota):
    val = slot[2]
    rows, hots = [], []
    for g in groups:
        parts = [[packed_row(val.at[2 + 3 * c + n], g) for c in range(3)] for n in range(3)]
        rows.append(spread_rows(packed_row(val.at[0], g), parts, iota))
        hots.append(one_hot_rows(packed_row(val.at[1], g), iota))
    return spread_add(rows, hots)


def write_states(block, total, pos_ref, vel_ref, diam_ref, out_ref, out_rows):
    rows = rows_of(block)
    for c in range(3):
        out_ref[out_rows, c, :] = pos_ref[c, rows, :]
        out_ref[out_rows, 3 + c, :] = total[16 * c : 16 * c + 16] - vel_ref[c, rows, :]
    out_ref[out_rows, 6, :] = 0.5 * diam_ref[rows, :]
    out_ref[out_rows, 7, :] = jnp.zeros((16, LANES), jnp.float32)


def states_step(gather, scatter, keys_ref, ends, gas_rows, iota, arrays):
    total = jnp.zeros((48, LANES), jnp.float32)
    if gather:
        gas_index(gather[0], keys_ref, gather[1])
    if scatter:
        seen_values(scatter[0], keys_ref, scatter[1])
    for g in range(16):
        if gather:
            gas_gather(gather[0], g, ends, gas_rows, gather[1])
        if scatter and g % 2:
            total = total + seen_in_order((g - 1, g), scatter[1], iota)
    if scatter:
        write_states(scatter[0], total, *arrays, *scatter[2:])
    if gather:
        gas_rest(gather[0], ends, gas_rows, gather[1])


def states_kernel(
    cell_hbm, gas_hbm, pos_hbm, vel_hbm, diam_hbm,
    keys_ref, ends_ref, table_ref, words_ref, largest_ref, one_ref, other_ref,
    cell_ref, gas_ref, pos_ref, vel_ref, diam_ref,
    gas_rows, iota, ends, idx_a, found_a, val_a, idx_b, found_b, val_b, sems,
):
    sources = (cell_hbm, gas_hbm, pos_hbm, vel_hbm, diam_hbm)
    places = (cell_ref, gas_ref, pos_ref, vel_ref, diam_ref)
    copies = [
        pltpu.make_async_copy(x, y, sems.at[n]) for n, (x, y) in enumerate(zip(sources, places))
    ]
    for copy in copies:
        copy.start()
    copies[0].wait()
    sub = lax.broadcasted_iota(jnp.int32, (ROWS, LANES), 0)
    lane = lax.broadcasted_iota(jnp.int32, (ROWS, LANES), 1)
    cells = cell_ref[...].T
    regs = []
    for v in range(16):
        own = (lane & 15) * LANES + v * ROWS + sub
        regs.append(cells[v * ROWS : (v + 1) * ROWS] * BLOCK + own)
    place = [("v", k) for k in range(4)] + [("s", k) for k in range(3)] + [("l", k) for k in range(4)]
    regs = sort_network(regs, place, 11)
    keys_ref[...] = jnp.concatenate(regs, axis=0).T
    least = functools.reduce(jnp.minimum, regs)
    most = functools.reduce(jnp.maximum, regs)
    least = lax.shift_right_logical(jnp.min(least, axis=0, keepdims=True), 19)
    most = lax.shift_right_logical(jnp.max(most, axis=0, keepdims=True), 19)
    ends_ref[0:1, :] = least
    ends_ref[1:2, :] = most
    ends_ref[2:8, :] = running_max(most - least, 16)[0:6]
    copy = pltpu.make_async_copy(ends_ref, ends, sems.at[5])
    copy.start()
    copies[1].wait()
    fill_gas_rows(gas_ref, gas_rows)
    for other in copies[2:]:
        other.wait()
    copy.wait()
    fill_iota(iota)
    a, b = (idx_a, found_a, val_a), (idx_b, found_b, val_b)
    step = functools.partial(
        states_step, keys_ref=keys_ref, ends=ends, gas_rows=gas_rows, iota=iota,
        arrays=(pos_ref, vel_ref, diam_ref),
    )
    step((0, a), None)

    def two(k, carry):
        block = 2 * k
        step((block + 1, b), (block, a, table_ref, rows_of(block)))
        step((block + 2, a), (block + 1, b, table_ref, rows_of(block + 1)))
        return carry

    lax.fori_loop(0, 3, two, 0)
    step((7, b), (6, a, table_ref, rows_of(6)))
    step(None, (7, b, table_ref, rows_of(7)))
    largest = largest_slip(table_ref, 128)
    largest_ref[...] = largest
    for n in range(16):
        code_rows(table_ref, n, largest, words_ref)
    words_ref[512:576, :] = jnp.zeros((64, LANES), jnp.int32)
    one_ref[...], other_ref[...] = by_partner("az", table_ref[0:16], table_ref[112:128])


def slots(rows, parts, dtype=jnp.float32):
    one = [VMEM((2, 16, LANES), jnp.int32), VMEM((16, ROWS, LANES), dtype), VMEM((parts, rows, LANES), dtype)]
    return one + one


def droplet_states(cells, gas, pos, vel, diam):
    f32, i32 = jnp.float32, jnp.int32
    arrays = (cells, gas, pos, vel, diam)
    return pl.pallas_call(
        states_kernel,
        name="droplet_states",
        out_shape=(
            jax.ShapeDtypeStruct((128, LANES), i32),
            jax.ShapeDtypeStruct((ROWS, LANES), i32),
            jax.ShapeDtypeStruct((128, ROWS, LANES), f32),
            jax.ShapeDtypeStruct((576, LANES), i32),
            jax.ShapeDtypeStruct((ROWS, LANES), f32),
            jax.ShapeDtypeStruct((16, ROWS, LANES), f32),
            jax.ShapeDtypeStruct((16, ROWS, LANES), f32),
        ),
        in_specs=[pl.BlockSpec(memory_space=pltpu.HBM)] * 5,
        scratch_shapes=[VMEM(x.shape, x.dtype) for x in arrays]
        + [VMEM((144, ROWS, LANES), f32), VMEM((LANES, LANES), jnp.bfloat16), SMEM((ROWS, LANES), i32)]
        + slots(16, 11)
        + [pltpu.SemaphoreType.DMA((6,))],
        compiler_params=params(60),
    )(*arrays)


def pair_sort_kernel(live_ref, pairs_ref, keys_ref, ends_ref):
    live = live_ref[0, 0]
    sub = lax.broadcasted_iota(jnp.int32, (ROWS, LANES), 0)
    lane = lax.broadcasted_iota(jnp.int32, (ROWS, LANES), 1)
    regs = []
    for v in range(32):
        rows = slice(v * ROWS, (v + 1) * ROWS)
        slot = v * 1024 + sub * LANES + lane
        head = pairs_ref[0, rows, :]
        tail = pairs_ref[1, rows, :] - 7 * BLOCK
        own = tail - BLOCK
        inside = (own >= 0) & (own < 8 * BLOCK)
        tail = jnp.where(inside, jnp.maximum(own, head) + BLOCK, tail)
        head = jnp.where(inside, jnp.minimum(own, head), head)
        bucket = lax.shift_right_logical(tail, 10)
        bucket = jnp.where(inside, bucket + 2, jnp.where(bucket >= 18, bucket - 16, bucket))
        turn = -(bucket & 1) & (8 * BLOCK - 1)
        key = (bucket << 24) | ((head ^ turn) << 10) | (tail & (BUCKET - 1))
        regs.append(jnp.where(slot < live, key, DEAD))
    place = (
        [("v", k) for k in range(4)]
        + [("s", k) for k in range(3)]
        + [("v", 4)]
        + [("l", k) for k in range(7)]
    )
    regs = sort_network(regs, place, 15)
    beyond = jnp.zeros((ROWS, LANES), jnp.float32)
    for key in regs:
        beyond = beyond + jnp.where(key < NEAR_BUCKETS << 24, 1.0, 0.0)
    beyond = jnp.sum(jnp.sum(beyond, axis=0, keepdims=True), axis=1, keepdims=True)
    ends_ref[8:16, :] = jnp.broadcast_to(beyond, (ROWS, LANES)).astype(jnp.int32)
    for half in range(2):
        rows = regs[16 * half : 16 * half + 16]
        keys_ref[half] = jnp.concatenate(rows, axis=0).T
        least_head = least_tail = jnp.full((ROWS, LANES), 1 << 20, jnp.int32)
        most_head = most_tail = jnp.full((ROWS, LANES), -1, jnp.int32)
        for key in rows:
            used = key < DEAD
            bucket = lax.shift_right_logical(key, 24)
            head = lax.shift_right_logical(key, 17) & (LANES - 1)
            head = head ^ (-(bucket & 1) & (LANES - 1))
            least_head = jnp.minimum(least_head, jnp.where(used, head, 1 << 20))
            most_head = jnp.maximum(most_head, jnp.where(used, head, -1))
            least_tail = jnp.minimum(least_tail, jnp.where(used, bucket, 1 << 20))
            most_tail = jnp.maximum(most_tail, jnp.where(used, bucket, -1))
        for n, x in enumerate((least_head, most_head, least_tail, most_tail)):
            reduce = jnp.max if n % 2 else jnp.min
            row = 4 * half + n
            bound = (LANES, LANES, BUCKETS, BUCKETS)[n]
            ends_ref[row : row + 1, :] = jnp.minimum(reduce(x, axis=0, keepdims=True), bound)


def pair_sort(live, pairs):
    return pl.pallas_call(
        pair_sort_kernel,
        name="pair_sort",
        out_shape=(
            jax.ShapeDtypeStruct((2, LANES, LANES), jnp.int32),
            jax.ShapeDtypeStruct((16, LANES), jnp.int32),
        ),
        in_specs=[pl.BlockSpec(memory_space=SMEM), pl.BlockSpec(memory_space=VMEM)],
        compiler_params=params(),
    )(live, pairs)


def take_items(state, groups, ends, part):
    low, high, heads = part
    items = []
    for _ in range(ROWS):
        g, bucket, head = state
        valid = g < groups
        seen = jnp.minimum(g, 2 * LANES - 1)
        at, lane = 4 * (seen & 1), seen >> 1
        items.append((seen, jnp.where(valid, bucket, -1), head, jnp.minimum(bucket, high) - low))
        more_heads = head + heads <= ends[at + 1, lane]
        more_tails = bucket < jnp.minimum(ends[at + 3, lane], high - 1)
        step = jnp.where(more_heads | more_tails, 0, 1)
        g = jnp.minimum(g + step, 2 * LANES)
        seen = jnp.minimum(g, 2 * LANES - 1)
        at, lane = 4 * (seen & 1), seen >> 1
        head = jnp.where(more_heads, head + heads, ends[at, lane] & -2)
        same = jnp.where(more_heads, bucket, bucket + 1)
        bucket = jnp.where(step == 1, jnp.maximum(ends[at + 2, lane], low), same)
        state = (g, bucket, head)
    return items, state


def word_window(words, first, count, pair, low):
    found = jnp.zeros((ROWS, LANES), jnp.int32)
    for u in range(count):
        rows = words[pl.ds(pl.multiple_of((first + u) * ROWS, ROWS), ROWS), :]
        found = jnp.where(pair == u, lane_gather(rows, low), found)
    return found


def pair_gather(k, item, keys_ref, near_words, far_words, heads, slot):
    key_rows, rel_rows, near, far = slot
    g, bucket, first, part = item
    keys = jnp.broadcast_to(keys_ref[g & 1, pl.ds(g >> 1, 1), :], (ROWS, LANES))
    of_bucket = lax.shift_right_logical(keys, 24)
    turn = -(of_bucket & 1) & (8 * BLOCK - 1)
    head = (lax.shift_right_logical(keys, 10) & (8 * BLOCK - 1)) ^ turn
    rel = lax.shift_right_logical(head, 7) - first
    used = (of_bucket == bucket) & (rel >= 0) & (rel < heads)
    key_rows[k : k + 1, :] = jnp.where(used, keys, DEAD)[0:1]
    rel_rows[k : k + 1, :] = rel[0:1]
    near[k] = word_window(near_words, first >> 1, heads // 2, rel >> 1, head & (LANES - 1))
    pair = lax.shift_right_logical(keys, 8) & 3
    far[k] = word_window(far_words, part * 4, 4, pair, keys & (LANES - 1))


def pair_values(slot, val, near_largest, far_largest):
    key_rows, rel_rows, near, far = slot
    keys, rel = key_rows[...], rel_rows[...]
    used = keys < DEAD
    turn = -(lax.shift_right_logical(keys, 24) & 1) & (LANES - 1)
    val[0] = rel.astype(jnp.float32)
    val[1] = ((lax.shift_right_logical(keys, 10) & (LANES - 1)) ^ turn).astype(jnp.float32)
    val[2] = (lax.shift_right_logical(keys, 7) & 7).astype(jnp.float32)
    val[3] = (keys & (LANES - 1)).astype(jnp.float32)

    def words(ref, odd):
        return [jnp.where(odd, ref[:, 4 + w, :], ref[:, w, :]) for w in range(4)]

    near_place, near_radius, near_slip = decoded(words(near, (rel & 1) == 1), near_largest)
    far_place, far_radius, far_slip = decoded(words(far, (keys & LANES) != 0), far_largest)
    gap = jnp.zeros((ROWS, LANES), jnp.float32)
    for x, y in zip(far_place, near_place):
        apart = (x - y).astype(jnp.float32)
        gap = gap + apart * apart
    gap = gap * (PLACE_STEP * PLACE_STEP)
    far_ratio = far_radius * lax.rsqrt(gap + far_radius * far_radius)
    near_ratio = near_radius * lax.rsqrt(gap + near_radius * near_radius)
    weight_far = jnp.where(used, piep_coef * far_ratio * far_ratio * far_ratio, 0.0)
    weight_near = jnp.where(used, piep_coef * near_ratio * near_ratio * near_ratio, 0.0)
    for c in range(3):
        for n, part in enumerate(split_two(weight_far * far_slip[c])):
            val[4 + 3 * n + c] = part
        for n, part in enumerate(split_two(weight_near * near_slip[c])):
            val[10 + 3 * n + c] = part


def pair_scatter(k, item, val, head_sum, tail_sum, iota, iota8):
    first, tail_first = item
    parts = [[packed_row(val.at[4 + 3 * n + c], k) for c in range(3)] for n in range(2)]
    rows = spread_rows(packed_row(val.at[0], k), parts, iota)
    out = spread_add([rows], [one_hot_rows(packed_row(val.at[1], k), iota)])
    for c in range(3):
        head_sum[c, pl.ds(first, 16), :] += out[16 * c : 16 * c + 16]

    hit = packed_row(val.at[2], k) == iota8[...]
    zero = jnp.zeros((16, LANES), jnp.bfloat16)
    tiles = []
    for n in range(10, 16, 2):
        both = jnp.concatenate([wide(val, n, k), wide(val, n + 1, k)], axis=0)
        tiles.append(jnp.where(hit, both.astype(jnp.bfloat16), zero))
    out = lax.dot_general(
        jnp.concatenate(tiles, axis=0),
        one_hot_rows(packed_row(val.at[3], k), iota),
        NT,
        preferred_element_type=jnp.float32,
    )
    at = pl.ds(pl.multiple_of(tail_first, 8), 8)
    for c in range(3):
        tail_sum[c, at, :] += out[8 * c : 8 * c + 8] + out[24 + 8 * c : 32 + 8 * c]


def run_pairs(groups, start, part, ends, keys_ref, near, far, sums, iota, iota8, scratch):
    fill_iota(iota)
    rows = lax.broadcasted_iota(jnp.int32, iota8.shape, 0) & 7
    iota8[...] = rows.astype(jnp.float32).astype(jnp.bfloat16)
    val, a, b = scratch[0], scratch[1:5], scratch[5:9]

    def step(state, slot, pending):
        items, state = take_items(state, groups, ends, part)
        if pending:
            pair_values(a, val, near[1], far[1])
        for k in range(ROWS):
            pair_gather(k, items[k], keys_ref, near[0], far[0], part[2], slot)
            if pending:
                pair_scatter(k, pending[k], val, *sums, iota, iota8)
        return tuple((item[2], item[3] * 8) for item in items), state, items[0][1] >= 0

    at, lane = 4 * (start & 1), start >> 1
    state = (start, jnp.maximum(ends[at + 2, lane], part[0]), ends[at, lane] & -2)

    def one(carry):
        pending, state, _ = carry
        carry = step(state, b, pending)
        for x, y in zip(a, b):
            x[...] = y[...]
        return carry

    lax.while_loop(lambda carry: carry[2], one, step(state, a, None))


def near_pairs_kernel(
    ends, keys_ref, words_ref, largest_ref, one_in, other_in,
    heads_ref, one_ref, other_ref,
    shell, shell_words, head_sum, tail_sum, iota, iota8, *scratch,
):
    shell[0:16], shell[16:32] = from_partners("az", one_in[...], other_in[...], True)
    shell_largest = largest_slip(shell, 32)
    for n in range(4):
        code_rows(shell, n, shell_largest, shell_words)
    shell_words[128:160, :] = jnp.zeros((32, LANES), jnp.int32)
    head_sum[...] = jnp.zeros_like(head_sum)
    tail_sum[...] = jnp.zeros_like(tail_sum)
    groups = (ends[8, 0] + LANES - 1) // LANES
    run_pairs(
        groups, jnp.int32(0), (0, NEAR_BUCKETS, NEAR_HEADS), ends, keys_ref,
        (words_ref, largest_ref[...]), (shell_words, shell_largest),
        (head_sum, tail_sum), iota, iota8, scratch,
    )
    heads_ref[...] = head_sum[:, 0:128, :]
    one_ref[...], other_ref[...] = by_partner("az", tail_sum[:, 0:16, :], tail_sum[:, 16:32, :])


def own_pairs_kernel(
    live_ref, ends, keys_ref, words_ref, largest_ref, heads_ref,
    corr_ref,
    head_sum, tail_sum, iota, iota8, *scratch,
):
    head_sum[:, 0:128, :] = heads_ref[...]
    head_sum[:, 128:144, :] = jnp.zeros((3, 16, LANES), jnp.float32)
    tail_sum[...] = jnp.zeros_like(tail_sum)
    groups = (live_ref[0, 0] + LANES - 1) // LANES
    start = jnp.minimum(ends[8, 0] // LANES, 2 * LANES - 1)
    coded = (words_ref, largest_ref[...])
    run_pairs(
        groups, start, (NEAR_BUCKETS, BUCKETS, OWN_HEADS), ends, keys_ref, coded, coded,
        (head_sum, tail_sum), iota, iota8, scratch,
    )
    corr_ref[...] = head_sum[:, 0:128, :] + tail_sum[:, 0:128, :]


def pair_scratch(tail_rows):
    f32, i32 = jnp.float32, jnp.int32
    slot = [
        VMEM((ROWS, LANES), i32),
        VMEM((ROWS, LANES), i32),
        VMEM((ROWS, ROWS, LANES), i32),
        VMEM((ROWS, ROWS, LANES), i32),
    ]
    return [
        VMEM((3, 144, LANES), f32),
        VMEM((3, tail_rows, LANES), f32),
        VMEM((LANES, LANES), jnp.bfloat16),
        VMEM((16, LANES), jnp.bfloat16),
        VMEM((16, ROWS, LANES), f32),
        *slot,
        *slot,
    ]


def near_pairs(ends, keys, words, largest, one, other):
    f32 = jnp.float32
    smem, vmem = pl.BlockSpec(memory_space=SMEM), pl.BlockSpec(memory_space=VMEM)
    return pl.pallas_call(
        near_pairs_kernel,
        name="near_pairs",
        out_shape=(
            jax.ShapeDtypeStruct((3, 128, LANES), f32),
            jax.ShapeDtypeStruct((3, 16, LANES), f32),
            jax.ShapeDtypeStruct((3, 16, LANES), f32),
        ),
        in_specs=[smem, vmem, vmem, vmem, vmem, vmem],
        scratch_shapes=[VMEM((32, ROWS, LANES), f32), VMEM((160, LANES), jnp.int32)]
        + pair_scratch(40),
        compiler_params=params(),
    )(ends, keys, words, largest, one, other)


def own_pairs(live, ends, keys, words, largest, heads):
    smem, vmem = pl.BlockSpec(memory_space=SMEM), pl.BlockSpec(memory_space=VMEM)
    return pl.pallas_call(
        own_pairs_kernel,
        name="own_pairs",
        out_shape=jax.ShapeDtypeStruct((3, 128, LANES), jnp.float32),
        in_specs=[smem, smem, vmem, vmem, vmem, vmem],
        scratch_shapes=pair_scratch(136),
        compiler_params=params(),
    )(live, ends, keys, words, largest, heads)


def force_gather(block, keys_ref, table_ref, total_ref, slot):
    force, got, val = slot
    rows = rows_of(block)
    scale = (-2.0 * drag_coef) * table_ref[rows, 6, :]
    for c in range(3):
        push = scale * (table_ref[rows, 3 + c, :] + total_ref[c, rows, :])
        force[:, c, :] = push[0:8]
        force[:, 4 + c, :] = push[8:16]
    keys = keys_ref[rows, :]
    val[0] = lax.shift_right_logical(keys, 19).astype(jnp.float32)
    val[1] = (lax.shift_right_logical(keys, 11) & (2 * LANES - 1)).astype(jnp.float32)
    inner = lax.shift_right_logical(keys, 7) & 7
    low = keys & (LANES - 1)
    tables = [force[k] for k in range(ROWS)]
    for g in range(16):
        pick = jnp.broadcast_to(inner[g : g + 1, :], (ROWS, LANES))
        at = jnp.broadcast_to(low[g : g + 1, :], (ROWS, LANES))
        found = jnp.zeros((ROWS, LANES), jnp.float32)
        for k in range(ROWS):
            found = jnp.where(pick == k, lane_gather(tables[k], at), found)
        got[g] = found
    upper = (keys & 1024) != 0
    for c in range(3):
        pushed = jnp.where(upper, got[:, 4 + c, :], got[:, c, :])
        for n, part in enumerate(split_two(pushed)):
            val[2 + 2 * c + n] = part


def force_add(g, base, slot, cells, iota):
    val = slot[2]

    def row(n):
        if isinstance(g, int):
            return packed_row(val.at[n], g)
        return jnp.broadcast_to(val[n, pl.ds(g, 1), :], (16, LANES)).astype(jnp.bfloat16)

    rel = row(0) - base.astype(jnp.float32).astype(jnp.bfloat16)
    parts = [[row(2 + 2 * c + n) for c in range(3)] for n in range(2)]
    out = spread_add([spread_rows(rel, parts, iota)], [one_hot_rows(row(1), iota)])
    for c in range(3):
        for half in range(2):
            part = out[16 * c : 16 * c + 16, half * LANES : (half + 1) * LANES]
            cells[2 * c + half, pl.ds(base, 16), :] += part


def force_rest(block, ends, slot, cells, iota):
    @pl.when(ends[2, block * 16] >= 16)
    def _():
        def one(g, carry):
            first, most = ends[0, block * 16 + g], ends[1, block * 16 + g]

            def trip(t, carry):
                force_add(g, jnp.minimum(first + 16 * t, LANES), slot, cells, iota)
                return carry

            lax.fori_loop(1, (most - first) // 16 + 1, trip, 0)
            return carry

        lax.fori_loop(0, 16, one, 0)


def deposit_step(gather, scatter, ends, keys_ref, table_ref, total_ref, cells, iota):
    if gather:
        force_gather(gather[0], keys_ref, table_ref, total_ref, gather[1])
    if scatter:
        for g in range(16):
            force_add(g, ends[0, scatter[0] * 16 + g], scatter[1], cells, iota)
        force_rest(scatter[0], ends, scatter[1], cells, iota)


def deposit_kernel(
    ends, keys_ref, table_ref, corr_ref, one_in, other_in,
    out_ref, total_ref, one_ref, other_ref,
    cells, iota, force_a, got_a, val_a, force_b, got_b, val_b,
):
    fill_iota(iota)
    cells[...] = jnp.zeros_like(cells)
    total_ref[...] = corr_ref[...]
    before, after = from_partners("az", one_in[...], other_in[...], True)
    total_ref[:, 0:16, :] += before
    total_ref[:, 112:128, :] += after
    a, b = (force_a, got_a, val_a), (force_b, got_b, val_b)
    step = functools.partial(
        deposit_step, ends=ends, keys_ref=keys_ref, table_ref=table_ref, total_ref=total_ref,
        cells=cells, iota=iota,
    )
    step((0, a), None)

    def two(k, carry):
        block = 2 * k
        step((block + 1, b), (block, a))
        step((block + 2, a), (block + 1, b))
        return carry

    lax.fori_loop(0, 3, two, 0)
    step((7, b), (6, a))
    step(None, (7, b))
    for c in range(3):
        for half in range(2):
            columns = slice(half * LANES, (half + 1) * LANES)
            out_ref[c, :, columns] = cells[2 * c + half, 0:128, :]
            one, other = by_partner(
                "ax", cells[2 * c + half, 0:32, :], cells[2 * c + half, 96:128, :]
            )
            one_ref[c, :, columns] = one
            other_ref[c, :, columns] = other


def deposits(ends, keys, table, corr, one, other):
    f32 = jnp.float32
    smem, vmem = pl.BlockSpec(memory_space=SMEM), pl.BlockSpec(memory_space=VMEM)
    slot = [VMEM((ROWS, ROWS, LANES), f32), VMEM((16, ROWS, LANES), f32), VMEM((8, 16, LANES), f32)]
    return pl.pallas_call(
        deposit_kernel,
        name="deposits",
        out_shape=(
            jax.ShapeDtypeStruct((3, 128, 2 * LANES), f32),
            jax.ShapeDtypeStruct((3, 128, LANES), f32),
            jax.ShapeDtypeStruct((3, 32, 2 * LANES), f32),
            jax.ShapeDtypeStruct((3, 32, 2 * LANES), f32),
        ),
        in_specs=[smem] + [vmem] * 5,
        scratch_shapes=[VMEM((6, 144, LANES), f32), VMEM((2 * LANES, LANES), jnp.bfloat16)]
        + slot
        + slot,
        compiler_params=params(),
    )(ends, keys, table, corr, one, other)


def axial_kernel(taps, cells_ref, one_in, other_in, out_ref, one_ref, other_ref, first_ref, last_ref):
    for c in range(3):
        before, after = from_partners("ax", one_in[c], other_in[c])
        padded = jnp.concatenate([before, cells_ref[c], after], axis=0)
        total = taps[0] * padded[0:128]
        for k in range(1, 5):
            total = total + taps[k] * padded[16 * k : 16 * k + 128]
        out_ref[c] = total
        for a in range(8):
            first_ref[2 * a : 2 * a + 2, :] = total[16 * a : 16 * a + 2]
            last_ref[2 * a : 2 * a + 2, :] = total[16 * a + 14 : 16 * a + 16]
        one_ref[c], other_ref[c] = by_partner("rad", first_ref[...], last_ref[...])


def radial_kernel(
    taps, cells_ref, one_in, other_in, out_ref, one_ref, other_ref, padded, before_ref, after_ref
):
    lane = lax.broadcasted_iota(jnp.int32, (LANES, LANES), 1)
    edges = jnp.zeros((LANES, LANES), jnp.float32)
    for c in range(3):
        before_ref[...], after_ref[...] = from_partners("rad", one_in[c], other_in[c])
        for a in range(8):
            padded[0:2, :] = before_ref[2 * a : 2 * a + 2, :]
            padded[2:18, :] = cells_ref[c, 16 * a : 16 * a + 16, :]
            padded[18:20, :] = after_ref[2 * a : 2 * a + 2, :]
            total = taps[0] * padded[0:16, :]
            for k in range(1, 5):
                total = total + taps[k] * padded[k : k + 16, :]
            out_ref[c, 16 * a : 16 * a + 16, :] = total
        left, right = out_ref[c, :, 0:LANES], out_ref[c, :, LANES:]
        if c:
            left = pltpu.roll(left, 2 * c, 1)
        right = pltpu.roll(right, 10 + 2 * c, 1)
        edges = jnp.where((lane >> 1) == c, left, edges)
        edges = jnp.where((lane >> 1) == 4 + c, right, edges)
    turned = edges.T
    one_ref[...], other_ref[...] = by_partner("az", turned[0:8], turned[8:16])


def azimuthal_kernel(taps, cells_ref, one_in, other_in, out_ref):
    lane = lax.broadcasted_iota(jnp.int32, (LANES, LANES), 1)
    rest = jnp.zeros((LANES - 16, LANES), jnp.float32)
    before, after = from_partners("az", one_in[...], other_in[...], True)
    edges = jnp.concatenate([after, before, rest], axis=0).T
    for c in range(3):
        ahead = pltpu.roll(edges, LANES - 2 * c, 1) if c else edges
        halo = jnp.where(lane < 64, ahead, pltpu.roll(edges, 118 - 2 * c, 1))
        left, right = cells_ref[c, :, 0:LANES], cells_ref[c, :, LANES:]
        out_left, out_right = taps[2] * left, taps[2] * right
        for k in (1, 2):
            tap = taps[2 + k]
            inner = lane < LANES - k
            x, y, z = (pltpu.roll(v, LANES - k, 1) for v in (left, right, halo))
            out_left = out_left + tap * jnp.where(inner, x, y)
            out_right = out_right + tap * jnp.where(inner, y, z)
            inner = lane >= k
            x, y, z = (pltpu.roll(v, k, 1) for v in (left, right, halo))
            out_left = out_left + tap * jnp.where(inner, x, z)
            out_right = out_right + tap * jnp.where(inner, y, x)
        out_ref[c, :, 0:LANES] = out_left
        out_ref[c, :, LANES:] = out_right


def filtered(deposit, one, other):
    f32 = jnp.float32
    raw = [math.exp(-0.5 * k * k) for k in range(-2, 3)]
    taps = [x / sum(raw) for x in raw]
    whole = jax.ShapeDtypeStruct(deposit.shape, f32)
    radial_face = jax.ShapeDtypeStruct((3, 16, 2 * LANES), f32)
    edge = jax.ShapeDtypeStruct((8, LANES), f32)
    cells, one, other = pl.pallas_call(
        functools.partial(axial_kernel, taps),
        name="axial_filter",
        out_shape=(whole, radial_face, radial_face),
        scratch_shapes=[VMEM((16, 2 * LANES), f32)] * 2,
        compiler_params=params(),
    )(deposit, *swapped(one, other, "ax"))
    cells, one, other = pl.pallas_call(
        functools.partial(radial_kernel, taps),
        name="radial_filter",
        out_shape=(whole, edge, edge),
        scratch_shapes=[VMEM((24, 2 * LANES), f32)] + [VMEM((16, 2 * LANES), f32)] * 2,
        compiler_params=params(),
    )(cells, *swapped(one, other, "rad"))
    return pl.pallas_call(
        functools.partial(azimuthal_kernel, taps),
        name="azimuthal_filter",
        out_shape=whole,
        compiler_params=params(),
    )(cells, *swapped(one, other, "az", True))


def swapped(one, other, axis, wrap=False):
    count = lax.axis_size(axis)

    def partner(i, odd):
        j = i + 1 if i % 2 == odd else i - 1
        return j % count if wrap or 0 <= j < count else i

    return [
        lax.ppermute(x, axis, [(i, partner(i, odd)) for i in range(count)])
        for odd, x in enumerate((one, other))
    ]


def per_device(positions, velocity, diameter, cell_index, pair_list, live_pairs, gas_velocity):
    live = live_pairs.reshape(1, 1)
    cells = cell_index.reshape(128, LANES)
    gas = gas_velocity.reshape(3, 128, 2 * LANES)
    pos = positions.reshape(3, 128, LANES)
    vel = velocity.reshape(3, 128, LANES)
    diam = diameter.reshape(128, LANES)
    cell_keys, cell_ends, table, words, largest, one, other = droplet_states(
        cells, gas, pos, vel, diam
    )
    one, other = swapped(one, other, "az", True)
    pair_keys, pair_ends = pair_sort(live, pair_list.reshape(2, 256, LANES))
    heads, one, other = near_pairs(pair_ends, pair_keys, words, largest, one, other)
    one, other = swapped(one, other, "az", True)
    corr = own_pairs(live, pair_ends, pair_keys, words, largest, heads)
    deposit, correction, one, other = deposits(cell_ends, cell_keys, table, corr, one, other)
    smoothed = filtered(deposit, one, other)
    return (correction.reshape(positions.shape), smoothed.reshape(gas_velocity.shape))


def solution(mesh):
    return jax.shard_map(
        per_device,
        mesh=mesh,
        in_specs=(
            P(None, "ax", "rad", "az"),
            P(None, "ax", "rad", "az"),
            P("ax", "rad", "az"),
            P("ax", "rad", "az"),
            P(None, "ax", "rad", "az"),
            P("ax", "rad", "az"),
            P(None, "ax", "rad", "az"),
        ),
        out_specs=(P(None, "ax", "rad", "az"), P(None, "ax", "rad", "az")),
        check_vma=False,
    )
```

```python
import functools
import math

import jax
import jax.numpy as jnp
from jax import lax
from jax.experimental import pallas as pl
from jax.experimental.pallas import tpu as pltpu
from jax.sharding import PartitionSpec as P

piep_coef = 1.0
drag_coef = 20.0

LANES = 128
ROWS = 8
BLOCK = 2048
GAS_WINDOW = 10
BUCKET = 1024
BUCKETS = 20
NEAR_BUCKETS = 4
NEAR_HEADS = 8
OWN_HEADS = 12
DEAD = 1 << 29

NT = (((1,), (1,)), ((), ()))
VMEM = pltpu.VMEM
SMEM = pltpu.SMEM


def params(megabytes=40):
    return pltpu.CompilerParams(vmem_limit_bytes=megabytes << 20)


def lane_gather(table, index):
    numbers = lax.GatherDimensionNumbers(
        offset_dims=(),
        collapsed_slice_dims=(1,),
        start_index_map=(1,),
        operand_batching_dims=(0,),
        start_indices_batching_dims=(0,),
    )
    return lax.gather(
        table,
        index[..., None],
        numbers,
        slice_sizes=(1, 1),
        mode=lax.GatherScatterMode.PROMISE_IN_BOUNDS,
    )


def sort_network(regs, place, levels):
    sub = lax.broadcasted_iota(jnp.int32, (ROWS, LANES), 0)
    lane = lax.broadcasted_iota(jnp.int32, (ROWS, LANES), 1)
    count = len(regs)

    def bit_fill(bit, v):
        if bit >= levels:
            return 0
        kind, k = place[bit]
        if kind == "v":
            return -((v >> k) & 1)
        return -(((sub if kind == "s" else lane) >> k) & 1)

    flip = [0] * count
    for level in range(1, levels + 1):
        fills = {}
        for v in range(count):
            kind, k = place[level] if level < levels else ("v", 99)
            key = (v >> k) & 1 if kind == "v" else 0
            if key not in fills:
                fills[key] = bit_fill(level, v)
            new = fills[key]
            if isinstance(new, int) and isinstance(flip[v], int):
                if new != flip[v]:
                    regs[v] = ~regs[v]
            else:
                regs[v] = regs[v] ^ (new ^ flip[v])
            flip[v] = new
        for bit in reversed(range(level)):
            kind, k = place[bit]
            step = 1 << k
            if kind == "v":
                for v in range(count):
                    if not v & step:
                        a, b = regs[v], regs[v | step]
                        regs[v], regs[v | step] = jnp.minimum(a, b), jnp.maximum(a, b)
            else:
                axis, size, where = (0, ROWS, sub) if kind == "s" else (1, LANES, lane)
                lower = (where & step) == 0
                for v in range(count):
                    x = regs[v]
                    ahead = pltpu.roll(x, size - step, axis)
                    behind = ahead if 2 * step == size else pltpu.roll(x, step, axis)
                    regs[v] = jnp.where(lower, jnp.minimum(x, ahead), jnp.maximum(x, behind))
    return regs


def split_two(x):
    high = x.astype(jnp.bfloat16).astype(jnp.float32)
    return high, x - high


def split_three(x):
    high, rest = split_two(x)
    mid, low = split_two(rest)
    return high, mid, low


def packed_row(ref, row):
    return jnp.broadcast_to(ref[row : row + 1, :], (16, LANES)).astype(jnp.bfloat16)


def one_hot_rows(low, iota):
    one = jnp.ones((16, LANES), jnp.bfloat16)
    zero = jnp.zeros((16, LANES), jnp.bfloat16)
    return jnp.concatenate(
        [jnp.where(low == iota[k : k + 16, :], one, zero) for k in range(0, iota.shape[0], 16)],
        axis=0,
    )


def spread_rows(rel, parts, iota):
    hit = rel == iota[0:16, :]
    zero = jnp.zeros((16, LANES), jnp.bfloat16)
    return jnp.concatenate([jnp.where(hit, p, zero) for part in parts for p in part], axis=0)


def block_product(rows, hots):
    zero = jnp.zeros
    lines = [
        jnp.concatenate(
            [x if m == n else zero(x.shape, x.dtype) for m in range(len(rows))], axis=1
        )
        for n, x in enumerate(rows)
    ]
    return lax.dot_general(
        jnp.concatenate(lines, axis=0),
        jnp.concatenate(hots, axis=1),
        NT,
        preferred_element_type=jnp.float32,
    )


def spread_add(rows, hots):
    out = lax.dot_general(
        jnp.concatenate(rows, axis=1) if len(rows) > 1 else rows[0],
        jnp.concatenate(hots, axis=1) if len(hots) > 1 else hots[0],
        NT,
        preferred_element_type=jnp.float32,
    )
    total = out[0:48]
    for s in range(48, out.shape[0], 48):
        total = total + out[s : s + 48]
    return total


def fill_iota(iota):
    rows = lax.broadcasted_iota(jnp.int32, iota.shape, 0)
    iota[...] = rows.astype(jnp.float32).astype(jnp.bfloat16)


def rows_of(block):
    start = block * 16
    return pl.ds(start if isinstance(block, int) else pl.multiple_of(start, 16), 16)


def wide(ref, *at):
    return jnp.broadcast_to(ref[at[:-1] + (slice(at[-1], at[-1] + 1),)], (ROWS, LANES))


def window(table, first, count, row, low, found):
    rel = row - first
    for u in range(count):
        found = jnp.where(rel == u, lane_gather(table[first + u], low), found)
    return found


def running_max(x, count):
    x = jnp.broadcast_to(x, (ROWS, LANES))
    step = 1
    while step < count:
        x = jnp.maximum(x, pltpu.roll(x, LANES - step, 1))
        step *= 2
    return x


def by_partner(axis, first, last):
    even = (lax.axis_index(axis) & 1) == 0
    return jnp.where(even, last, first), jnp.where(even, first, last)


def from_partners(axis, one, other, wrap=False):
    at, count = lax.axis_index(axis), lax.axis_size(axis)
    even = (at & 1) == 0
    before, after = jnp.where(even, other, one), jnp.where(even, one, other)
    if wrap:
        return before, after
    return jnp.where(at > 0, before, 0.0), jnp.where(at < count - 1, after, 0.0)


PLACE_STEP = 0.1 / 65535.0
RADIUS_LEAST = 0.01
RADIUS_STEP = 0.04 / 65535.0
SLIP_HALF = 1 << 20


def largest_slip(table, rows):
    most = jnp.zeros((ROWS, LANES), jnp.float32)
    for n in range(0, rows, ROWS):
        for c in range(3):
            most = jnp.maximum(most, jnp.abs(table[n : n + ROWS, 3 + c, :]))
    most = jnp.max(jnp.max(most, axis=0, keepdims=True), axis=1, keepdims=True)
    return jnp.broadcast_to(jnp.maximum(most, 1e-30), (ROWS, LANES))


def code_rows(table, n, largest, words):
    rows = pl.ds(n * ROWS, ROWS)

    def whole(c, least, step):
        x = ((table[rows, c, :] - least) * (1.0 / step) + 0.5).astype(jnp.int32)
        return jnp.clip(x, 0, 65535)

    x, y, z = (whole(c, 0.0, PLACE_STEP) for c in range(3))
    radius = whole(6, RADIUS_LEAST, RADIUS_STEP)
    scale = (SLIP_HALF - 1.0) / largest
    u, v, w = (
        (table[rows, 3 + c, :] * scale + (SLIP_HALF + 0.5)).astype(jnp.int32) for c in range(3)
    )
    coded = (
        x | (y << 16),
        z | (radius << 16),
        u | ((w & 2047) << 21),
        v | (lax.shift_right_logical(w, 11) << 21),
    )
    for k, word in enumerate(coded):
        words[pl.ds(n * 32 + k, ROWS, stride=4), :] = word


def decoded(words, largest):
    low = [x & 65535 for x in words[0:2]]
    high = [lax.shift_right_logical(x, 16) for x in words[0:2]]
    place = (low[0], high[0], low[1])
    radius = high[1].astype(jnp.float32) * RADIUS_STEP + RADIUS_LEAST
    mask = 2 * SLIP_HALF - 1
    third = lax.shift_right_logical(words[2], 21) | (lax.shift_right_logical(words[3], 21) << 11)
    scale = largest * (1.0 / (SLIP_HALF - 1.0))
    slip = [
        (x - SLIP_HALF).astype(jnp.float32) * scale for x in (words[2] & mask, words[3] & mask, third)
    ]
    return place, radius, slip


def fill_gas_rows(gas_ref, gas_rows):
    for r in range(16):
        rows = slice(r * ROWS, (r + 1) * ROWS)
        for c in range(3):
            for half in range(2):
                gas_rows[rows, half * 4 + c, :] = gas_ref[c, rows, half * LANES : (half + 1) * LANES]


def gas_index(block, keys_ref, slot):
    idx = slot[0]
    keys = keys_ref[rows_of(block), :]
    idx[0] = lax.shift_right_logical(keys, 19)
    idx[1] = lax.shift_right_logical(keys, 11) & (LANES - 1)


def gas_gather(block, g, ends, gas_rows, slot):
    idx, found = slot[0], slot[1]
    zero = jnp.zeros((ROWS, LANES), jnp.float32)
    first = ends[0, block * 16 + g]
    found[g] = window(gas_rows, first, GAS_WINDOW, wide(idx, 0, g), wide(idx, 1, g), zero)


def gas_rest(block, ends, gas_rows, slot):
    idx, found = slot[0], slot[1]

    @pl.when(ends[2, block * 16] >= GAS_WINDOW)
    def _():
        def one(g, carry):
            first = ends[0, block * 16 + g]
            row = jnp.broadcast_to(idx[0, pl.ds(g, 1), :], (ROWS, LANES))
            low = jnp.broadcast_to(idx[1, pl.ds(g, 1), :], (ROWS, LANES))

            def trip(t, total):
                base = jnp.minimum(first + GAS_WINDOW * t, LANES)
                return window(gas_rows, base, GAS_WINDOW, row, low, total)

            trips = (ends[1, block * 16 + g] - first) // GAS_WINDOW + 1
            found[g] = lax.fori_loop(1, trips, trip, found[g])
            return carry

        lax.fori_loop(0, 16, one, 0)


def seen_values(block, keys_ref, slot):
    idx, found, val = slot
    keys = keys_ref[rows_of(block), :]
    upper = (keys & (1 << 18)) != 0
    place_in = keys & (BLOCK - 1)
    val[0] = lax.shift_right_logical(place_in, 7).astype(jnp.float32)
    val[1] = (place_in & (LANES - 1)).astype(jnp.float32)
    for c in range(3):
        seen = jnp.where(upper, found[:, 4 + c, :], found[:, c, :])
        for n, part in enumerate(split_three(seen)):
            val[2 + 3 * c + n] = part


def seen_in_order(groups, slot, iota):
    val = slot[2]
    rows, hots = [], []
    for g in groups:
        parts = [[packed_row(val.at[2 + 3 * c + n], g) for c in range(3)] for n in range(3)]
        rows.append(spread_rows(packed_row(val.at[0], g), parts, iota))
        hots.append(one_hot_rows(packed_row(val.at[1], g), iota))
    return spread_add(rows, hots)


def write_states(block, total, pos_ref, vel_ref, diam_ref, out_ref, out_rows):
    rows = rows_of(block)
    for c in range(3):
        out_ref[out_rows, c, :] = pos_ref[c, rows, :]
        out_ref[out_rows, 3 + c, :] = total[16 * c : 16 * c + 16] - vel_ref[c, rows, :]
    out_ref[out_rows, 6, :] = 0.5 * diam_ref[rows, :]
    out_ref[out_rows, 7, :] = jnp.zeros((16, LANES), jnp.float32)


def states_step(gather, scatter, keys_ref, ends, gas_rows, iota, arrays):
    total = jnp.zeros((48, LANES), jnp.float32)
    if gather:
        gas_index(gather[0], keys_ref, gather[1])
    if scatter:
        seen_values(scatter[0], keys_ref, scatter[1])
    for g in range(16):
        if gather:
            gas_gather(gather[0], g, ends, gas_rows, gather[1])
        if scatter and g % 2:
            total = total + seen_in_order((g - 1, g), scatter[1], iota)
    if scatter:
        write_states(scatter[0], total, *arrays, *scatter[2:])
    if gather:
        gas_rest(gather[0], ends, gas_rows, gather[1])


def states_kernel(
    cell_hbm, gas_hbm, pos_hbm, vel_hbm, diam_hbm,
    keys_ref, ends_ref, table_ref, words_ref, largest_ref, one_ref, other_ref,
    cell_ref, gas_ref, pos_ref, vel_ref, diam_ref,
    gas_rows, iota, ends, idx_a, found_a, val_a, idx_b, found_b, val_b, sems,
):
    sources = (cell_hbm, gas_hbm, pos_hbm, vel_hbm, diam_hbm)
    places = (cell_ref, gas_ref, pos_ref, vel_ref, diam_ref)
    copies = [
        pltpu.make_async_copy(x, y, sems.at[n]) for n, (x, y) in enumerate(zip(sources, places))
    ]
    for copy in copies:
        copy.start()
    copies[0].wait()
    sub = lax.broadcasted_iota(jnp.int32, (ROWS, LANES), 0)
    lane = lax.broadcasted_iota(jnp.int32, (ROWS, LANES), 1)
    cells = cell_ref[...].T
    regs = []
    for v in range(16):
        own = (lane & 15) * LANES + v * ROWS + sub
        regs.append(cells[v * ROWS : (v + 1) * ROWS] * BLOCK + own)
    place = [("v", k) for k in range(4)] + [("s", k) for k in range(3)] + [("l", k) for k in range(4)]
    regs = sort_network(regs, place, 11)
    keys_ref[...] = jnp.concatenate(regs, axis=0).T
    least = functools.reduce(jnp.minimum, regs)
    most = functools.reduce(jnp.maximum, regs)
    least = lax.shift_right_logical(jnp.min(least, axis=0, keepdims=True), 19)
    most = lax.shift_right_logical(jnp.max(most, axis=0, keepdims=True), 19)
    ends_ref[0:1, :] = least
    ends_ref[1:2, :] = most
    ends_ref[2:8, :] = running_max(most - least, 16)[0:6]
    copy = pltpu.make_async_copy(ends_ref, ends, sems.at[5])
    copy.start()
    copies[1].wait()
    fill_gas_rows(gas_ref, gas_rows)
    for other in copies[2:]:
        other.wait()
    copy.wait()
    fill_iota(iota)
    a, b = (idx_a, found_a, val_a), (idx_b, found_b, val_b)
    step = functools.partial(
        states_step, keys_ref=keys_ref, ends=ends, gas_rows=gas_rows, iota=iota,
        arrays=(pos_ref, vel_ref, diam_ref),
    )
    step((0, a), None)

    def two(k, carry):
        block = 2 * k
        step((block + 1, b), (block, a, table_ref, rows_of(block)))
        step((block + 2, a), (block + 1, b, table_ref, rows_of(block + 1)))
        return carry

    lax.fori_loop(0, 3, two, 0)
    step((7, b), (6, a, table_ref, rows_of(6)))
    step(None, (7, b, table_ref, rows_of(7)))
    largest = largest_slip(table_ref, 128)
    largest_ref[...] = largest
    for n in range(16):
        code_rows(table_ref, n, largest, words_ref)
    words_ref[512:576, :] = jnp.zeros((64, LANES), jnp.int32)
    one_ref[...], other_ref[...] = by_partner("az", table_ref[0:16], table_ref[112:128])


def slots(rows, parts, dtype=jnp.float32):
    one = [VMEM((2, 16, LANES), jnp.int32), VMEM((16, ROWS, LANES), dtype), VMEM((parts, rows, LANES), dtype)]
    return one + one


def droplet_states(cells, gas, pos, vel, diam):
    f32, i32 = jnp.float32, jnp.int32
    arrays = (cells, gas, pos, vel, diam)
    return pl.pallas_call(
        states_kernel,
        name="droplet_states",
        out_shape=(
            jax.ShapeDtypeStruct((128, LANES), i32),
            jax.ShapeDtypeStruct((ROWS, LANES), i32),
            jax.ShapeDtypeStruct((128, ROWS, LANES), f32),
            jax.ShapeDtypeStruct((576, LANES), i32),
            jax.ShapeDtypeStruct((ROWS, LANES), f32),
            jax.ShapeDtypeStruct((16, ROWS, LANES), f32),
            jax.ShapeDtypeStruct((16, ROWS, LANES), f32),
        ),
        in_specs=[pl.BlockSpec(memory_space=pltpu.HBM)] * 5,
        scratch_shapes=[VMEM(x.shape, x.dtype) for x in arrays]
        + [VMEM((144, ROWS, LANES), f32), VMEM((LANES, LANES), jnp.bfloat16), SMEM((ROWS, LANES), i32)]
        + slots(16, 11)
        + [pltpu.SemaphoreType.DMA((6,))],
        compiler_params=params(60),
    )(*arrays)


def pair_sort_kernel(live_ref, pairs_ref, keys_ref, ends_ref):
    live = live_ref[0, 0]
    sub = lax.broadcasted_iota(jnp.int32, (ROWS, LANES), 0)
    lane = lax.broadcasted_iota(jnp.int32, (ROWS, LANES), 1)
    regs = []
    for v in range(32):
        rows = slice(v * ROWS, (v + 1) * ROWS)
        slot = v * 1024 + sub * LANES + lane
        head = pairs_ref[0, rows, :]
        tail = pairs_ref[1, rows, :] - 7 * BLOCK
        own = tail - BLOCK
        inside = (own >= 0) & (own < 8 * BLOCK)
        tail = jnp.where(inside, jnp.maximum(own, head) + BLOCK, tail)
        head = jnp.where(inside, jnp.minimum(own, head), head)
        bucket = lax.shift_right_logical(tail, 10)
        bucket = jnp.where(inside, bucket + 2, jnp.where(bucket >= 18, bucket - 16, bucket))
        turn = -(bucket & 1) & (8 * BLOCK - 1)
        key = (bucket << 24) | ((head ^ turn) << 10) | (tail & (BUCKET - 1))
        regs.append(jnp.where(slot < live, key, DEAD))
    place = (
        [("v", k) for k in range(4)]
        + [("s", k) for k in range(3)]
        + [("v", 4)]
        + [("l", k) for k in range(7)]
    )
    regs = sort_network(regs, place, 15)
    beyond = jnp.zeros((ROWS, LANES), jnp.float32)
    for key in regs:
        beyond = beyond + jnp.where(key < NEAR_BUCKETS << 24, 1.0, 0.0)
    beyond = jnp.sum(jnp.sum(beyond, axis=0, keepdims=True), axis=1, keepdims=True)
    ends_ref[8:16, :] = jnp.broadcast_to(beyond, (ROWS, LANES)).astype(jnp.int32)
    for half in range(2):
        rows = regs[16 * half : 16 * half + 16]
        keys_ref[half] = jnp.concatenate(rows, axis=0).T
        least_head = least_tail = jnp.full((ROWS, LANES), 1 << 20, jnp.int32)
        most_head = most_tail = jnp.full((ROWS, LANES), -1, jnp.int32)
        for key in rows:
            used = key < DEAD
            bucket = lax.shift_right_logical(key, 24)
            head = lax.shift_right_logical(key, 17) & (LANES - 1)
            head = head ^ (-(bucket & 1) & (LANES - 1))
            least_head = jnp.minimum(least_head, jnp.where(used, head, 1 << 20))
            most_head = jnp.maximum(most_head, jnp.where(used, head, -1))
            least_tail = jnp.minimum(least_tail, jnp.where(used, bucket, 1 << 20))
            most_tail = jnp.maximum(most_tail, jnp.where(used, bucket, -1))
        for n, x in enumerate((least_head, most_head, least_tail, most_tail)):
            reduce = jnp.max if n % 2 else jnp.min
            row = 4 * half + n
            bound = (LANES, LANES, BUCKETS, BUCKETS)[n]
            ends_ref[row : row + 1, :] = jnp.minimum(reduce(x, axis=0, keepdims=True), bound)


def pair_sort(live, pairs):
    return pl.pallas_call(
        pair_sort_kernel,
        name="pair_sort",
        out_shape=(
            jax.ShapeDtypeStruct((2, LANES, LANES), jnp.int32),
            jax.ShapeDtypeStruct((16, LANES), jnp.int32),
        ),
        in_specs=[pl.BlockSpec(memory_space=SMEM), pl.BlockSpec(memory_space=VMEM)],
        compiler_params=params(),
    )(live, pairs)


def group_ends(g, ends, part):
    g = jnp.minimum(g, 2 * LANES - 1)
    at, lane = 4 * (g & 1), g >> 1
    low, high, _ = part
    return (
        ends[at, lane] & -2,
        ends[at + 1, lane],
        jnp.maximum(ends[at + 2, lane], low),
        jnp.minimum(ends[at + 3, lane], high - 1),
    )


def take_items(state, groups, ends, part):
    low, high, heads = part
    items = []
    for _ in range(ROWS):
        g, bucket, head, now, later = state
        place = jnp.minimum(bucket, high) - low
        items.append((jnp.minimum(g, 2 * LANES - 1), jnp.where(g < groups, bucket, -1), head, place))
        ahead = group_ends(g + 2, ends, part)
        more_heads = head + heads <= now[1]
        stay = more_heads | (bucket < now[3])
        head = jnp.where(more_heads, head + heads, jnp.where(stay, now[0], later[0]))
        bucket = jnp.where(more_heads, bucket, jnp.where(stay, bucket + 1, later[2]))
        now = tuple(jnp.where(stay, x, y) for x, y in zip(now, later))
        later = tuple(jnp.where(stay, x, y) for x, y in zip(later, ahead))
        state = (jnp.where(stay, g, g + 1), bucket, head, now, later)
    return items, state


def word_window(words, first, count, pair, low):
    found = jnp.zeros((ROWS, LANES), jnp.int32)
    for u in range(count):
        rows = words[pl.ds(pl.multiple_of((first + u) * ROWS, ROWS), ROWS), :]
        found = jnp.where(pair == u, lane_gather(rows, low), found)
    return found


def pair_gather(k, item, keys_ref, near_words, far_words, heads, slot):
    key_rows, rel_rows, near, far = slot
    g, bucket, first, part = item
    keys = jnp.broadcast_to(keys_ref[g & 1, pl.ds(g >> 1, 1), :], (ROWS, LANES))
    of_bucket = lax.shift_right_logical(keys, 24)
    turn = -(of_bucket & 1) & (8 * BLOCK - 1)
    head = (lax.shift_right_logical(keys, 10) & (8 * BLOCK - 1)) ^ turn
    rel = lax.shift_right_logical(head, 7) - first
    used = (of_bucket == bucket) & (rel >= 0) & (rel < heads)
    key_rows[k : k + 1, :] = jnp.where(used, keys, DEAD)[0:1]
    rel_rows[k : k + 1, :] = rel[0:1]
    near[k] = word_window(near_words, first >> 1, heads // 2, rel >> 1, head & (LANES - 1))
    pair = lax.shift_right_logical(keys, 8) & 3
    far[k] = word_window(far_words, part * 4, 4, pair, keys & (LANES - 1))


def pair_values(slot, val, near_largest, far_largest):
    key_rows, rel_rows, near, far = slot
    keys, rel = key_rows[...], rel_rows[...]
    used = keys < DEAD
    turn = -(lax.shift_right_logical(keys, 24) & 1) & (LANES - 1)
    val[0] = rel.astype(jnp.float32)
    val[1] = ((lax.shift_right_logical(keys, 10) & (LANES - 1)) ^ turn).astype(jnp.float32)
    val[2] = (lax.shift_right_logical(keys, 7) & 7).astype(jnp.float32)
    val[3] = (keys & (LANES - 1)).astype(jnp.float32)

    def words(ref, odd):
        return [jnp.where(odd, ref[:, 4 + w, :], ref[:, w, :]) for w in range(4)]

    near_place, near_radius, near_slip = decoded(words(near, (rel & 1) == 1), near_largest)
    far_place, far_radius, far_slip = decoded(words(far, (keys & LANES) != 0), far_largest)
    gap = jnp.zeros((ROWS, LANES), jnp.float32)
    for x, y in zip(far_place, near_place):
        apart = (x - y).astype(jnp.float32)
        gap = gap + apart * apart
    gap = gap * (PLACE_STEP * PLACE_STEP)
    far_ratio = far_radius * lax.rsqrt(gap + far_radius * far_radius)
    near_ratio = near_radius * lax.rsqrt(gap + near_radius * near_radius)
    weight_far = jnp.where(used, piep_coef * far_ratio * far_ratio * far_ratio, 0.0)
    weight_near = jnp.where(used, piep_coef * near_ratio * near_ratio * near_ratio, 0.0)
    for c in range(3):
        for n, part in enumerate(split_two(weight_far * far_slip[c])):
            val[4 + 3 * n + c] = part
        for n, part in enumerate(split_two(weight_near * near_slip[c])):
            val[10 + 3 * n + c] = part


def pair_scatter(k, item, val, head_sum, tail_sum, iota, iota8):
    first, tail_first = item
    parts = [[packed_row(val.at[4 + 3 * n + c], k) for c in range(3)] for n in range(2)]
    heads = spread_rows(packed_row(val.at[0], k), parts, iota)
    hit = packed_row(val.at[2], k) == iota8[...]
    zero = jnp.zeros((16, LANES), jnp.bfloat16)
    tails = []
    for n in range(10, 16, 2):
        both = jnp.concatenate([wide(val, n, k), wide(val, n + 1, k)], axis=0)
        tails.append(jnp.where(hit, both.astype(jnp.bfloat16), zero))
    tails = jnp.concatenate(tails, axis=0)
    out = block_product(
        [heads, tails], [one_hot_rows(packed_row(val.at[n], k), iota) for n in (1, 3)]
    )
    for c in range(3):
        head_sum[c, pl.ds(first, 16), :] += out[16 * c : 16 * c + 16] + out[16 * c + 48 : 16 * c + 64]
    at = pl.ds(pl.multiple_of(tail_first, 8), 8)
    for c in range(3):
        tail_sum[c, at, :] += out[8 * c + 96 : 8 * c + 104] + out[8 * c + 120 : 8 * c + 128]


def run_pairs(groups, start, part, ends, keys_ref, near, far, sums, iota, iota8, scratch):
    fill_iota(iota)
    rows = lax.broadcasted_iota(jnp.int32, iota8.shape, 0) & 7
    iota8[...] = rows.astype(jnp.float32).astype(jnp.bfloat16)
    val, a, b = scratch[0], scratch[1:5], scratch[5:9]

    def step(state, slot, pending):
        items, state = take_items(state, groups, ends, part)
        if pending:
            pair_values(a, val, near[1], far[1])
        for k in range(ROWS):
            pair_gather(k, items[k], keys_ref, near[0], far[0], part[2], slot)
            if pending:
                pair_scatter(k, pending[k], val, *sums, iota, iota8)
        return tuple((item[2], item[3] * 8) for item in items), state, items[0][1] >= 0

    now, later = group_ends(start, ends, part), group_ends(start + 1, ends, part)
    state = (start, now[2], now[0], now, later)

    def one(carry):
        pending, state, _ = carry
        carry = step(state, b, pending)
        for x, y in zip(a, b):
            x[...] = y[...]
        return carry

    lax.while_loop(lambda carry: carry[2], one, step(state, a, None))


def near_pairs_kernel(
    ends, keys_ref, words_ref, largest_ref, one_in, other_in,
    heads_ref, one_ref, other_ref,
    shell, shell_words, head_sum, tail_sum, iota, iota8, *scratch,
):
    shell[0:16], shell[16:32] = from_partners("az", one_in[...], other_in[...], True)
    shell_largest = largest_slip(shell, 32)
    for n in range(4):
        code_rows(shell, n, shell_largest, shell_words)
    shell_words[128:160, :] = jnp.zeros((32, LANES), jnp.int32)
    head_sum[...] = jnp.zeros_like(head_sum)
    tail_sum[...] = jnp.zeros_like(tail_sum)
    groups = (ends[8, 0] + LANES - 1) // LANES
    run_pairs(
        groups, jnp.int32(0), (0, NEAR_BUCKETS, NEAR_HEADS), ends, keys_ref,
        (words_ref, largest_ref[...]), (shell_words, shell_largest),
        (head_sum, tail_sum), iota, iota8, scratch,
    )
    heads_ref[...] = head_sum[:, 0:128, :]
    one_ref[...], other_ref[...] = by_partner("az", tail_sum[:, 0:16, :], tail_sum[:, 16:32, :])


def own_pairs_kernel(
    live_ref, ends, keys_ref, words_ref, largest_ref, heads_ref,
    corr_ref,
    head_sum, tail_sum, iota, iota8, *scratch,
):
    head_sum[:, 0:128, :] = heads_ref[...]
    head_sum[:, 128:144, :] = jnp.zeros((3, 16, LANES), jnp.float32)
    tail_sum[...] = jnp.zeros_like(tail_sum)
    groups = (live_ref[0, 0] + LANES - 1) // LANES
    start = jnp.minimum(ends[8, 0] // LANES, 2 * LANES - 1)
    coded = (words_ref, largest_ref[...])
    run_pairs(
        groups, start, (NEAR_BUCKETS, BUCKETS, OWN_HEADS), ends, keys_ref, coded, coded,
        (head_sum, tail_sum), iota, iota8, scratch,
    )
    corr_ref[...] = head_sum[:, 0:128, :] + tail_sum[:, 0:128, :]


def pair_scratch(tail_rows):
    f32, i32 = jnp.float32, jnp.int32
    slot = [
        VMEM((ROWS, LANES), i32),
        VMEM((ROWS, LANES), i32),
        VMEM((ROWS, ROWS, LANES), i32),
        VMEM((ROWS, ROWS, LANES), i32),
    ]
    return [
        VMEM((3, 144, LANES), f32),
        VMEM((3, tail_rows, LANES), f32),
        VMEM((LANES, LANES), jnp.bfloat16),
        VMEM((16, LANES), jnp.bfloat16),
        VMEM((16, ROWS, LANES), f32),
        *slot,
        *slot,
    ]


def near_pairs(ends, keys, words, largest, one, other):
    f32 = jnp.float32
    smem, vmem = pl.BlockSpec(memory_space=SMEM), pl.BlockSpec(memory_space=VMEM)
    return pl.pallas_call(
        near_pairs_kernel,
        name="near_pairs",
        out_shape=(
            jax.ShapeDtypeStruct((3, 128, LANES), f32),
            jax.ShapeDtypeStruct((3, 16, LANES), f32),
            jax.ShapeDtypeStruct((3, 16, LANES), f32),
        ),
        in_specs=[smem, vmem, vmem, vmem, vmem, vmem],
        scratch_shapes=[VMEM((32, ROWS, LANES), f32), VMEM((160, LANES), jnp.int32)]
        + pair_scratch(40),
        compiler_params=params(),
    )(ends, keys, words, largest, one, other)


def own_pairs(live, ends, keys, words, largest, heads):
    smem, vmem = pl.BlockSpec(memory_space=SMEM), pl.BlockSpec(memory_space=VMEM)
    return pl.pallas_call(
        own_pairs_kernel,
        name="own_pairs",
        out_shape=jax.ShapeDtypeStruct((3, 128, LANES), jnp.float32),
        in_specs=[smem, smem, vmem, vmem, vmem, vmem],
        scratch_shapes=pair_scratch(136),
        compiler_params=params(),
    )(live, ends, keys, words, largest, heads)


def force_gather(block, keys_ref, table_ref, total_ref, slot):
    force, got, val = slot
    rows = rows_of(block)
    scale = (-2.0 * drag_coef) * table_ref[rows, 6, :]
    for c in range(3):
        push = scale * (table_ref[rows, 3 + c, :] + total_ref[c, rows, :])
        force[:, c, :] = push[0:8]
        force[:, 4 + c, :] = push[8:16]
    keys = keys_ref[rows, :]
    val[0] = lax.shift_right_logical(keys, 19).astype(jnp.float32)
    val[1] = (lax.shift_right_logical(keys, 11) & (2 * LANES - 1)).astype(jnp.float32)
    inner = lax.shift_right_logical(keys, 7) & 7
    low = keys & (LANES - 1)
    tables = [force[k] for k in range(ROWS)]
    for g in range(16):
        pick = jnp.broadcast_to(inner[g : g + 1, :], (ROWS, LANES))
        at = jnp.broadcast_to(low[g : g + 1, :], (ROWS, LANES))
        found = jnp.zeros((ROWS, LANES), jnp.float32)
        for k in range(ROWS):
            found = jnp.where(pick == k, lane_gather(tables[k], at), found)
        got[g] = found
    upper = (keys & 1024) != 0
    for c in range(3):
        pushed = jnp.where(upper, got[:, 4 + c, :], got[:, c, :])
        for n, part in enumerate(split_two(pushed)):
            val[2 + 2 * c + n] = part


def force_rows(g, base, slot, iota):
    val = slot[2]

    def row(n):
        if isinstance(g, int):
            return packed_row(val.at[n], g)
        return jnp.broadcast_to(val[n, pl.ds(g, 1), :], (16, LANES)).astype(jnp.bfloat16)

    rel = row(0) - base.astype(jnp.float32).astype(jnp.bfloat16)
    parts = [[row(2 + 2 * c + n) for c in range(3)] for n in range(2)]
    return spread_rows(rel, parts, iota), one_hot_rows(row(1), iota)


def force_add(groups, bases, slot, cells, iota):
    pieces = [force_rows(g, base, slot, iota) for g, base in zip(groups, bases)]
    out = block_product([p[0] for p in pieces], [p[1] for p in pieces])
    for n, base in enumerate(bases):
        for c in range(3):
            at = 96 * n + 16 * c
            total = out[at : at + 16] + out[at + 48 : at + 64]
            for half in range(2):
                part = total[:, half * LANES : (half + 1) * LANES]
                cells[2 * c + half, pl.ds(base, 16), :] += part


def force_rest(block, ends, slot, cells, iota):
    @pl.when(ends[2, block * 16] >= 16)
    def _():
        def one(g, carry):
            first, most = ends[0, block * 16 + g], ends[1, block * 16 + g]

            def trip(t, carry):
                force_add([g], [jnp.minimum(first + 16 * t, LANES)], slot, cells, iota)
                return carry

            lax.fori_loop(1, (most - first) // 16 + 1, trip, 0)
            return carry

        lax.fori_loop(0, 16, one, 0)


def deposit_step(gather, scatter, ends, keys_ref, table_ref, total_ref, cells, iota):
    if gather:
        force_gather(gather[0], keys_ref, table_ref, total_ref, gather[1])
    if scatter:
        for g in range(0, 16, 2):
            bases = [ends[0, scatter[0] * 16 + n] for n in (g, g + 1)]
            force_add([g, g + 1], bases, scatter[1], cells, iota)
        force_rest(scatter[0], ends, scatter[1], cells, iota)


def deposit_kernel(
    ends, keys_ref, table_ref, corr_ref, one_in, other_in,
    out_ref, total_ref, one_ref, other_ref,
    cells, iota, force_a, got_a, val_a, force_b, got_b, val_b,
):
    fill_iota(iota)
    cells[...] = jnp.zeros_like(cells)
    total_ref[...] = corr_ref[...]
    before, after = from_partners("az", one_in[...], other_in[...], True)
    total_ref[:, 0:16, :] += before
    total_ref[:, 112:128, :] += after
    a, b = (force_a, got_a, val_a), (force_b, got_b, val_b)
    step = functools.partial(
        deposit_step, ends=ends, keys_ref=keys_ref, table_ref=table_ref, total_ref=total_ref,
        cells=cells, iota=iota,
    )
    step((0, a), None)

    def two(k, carry):
        block = 2 * k
        step((block + 1, b), (block, a))
        step((block + 2, a), (block + 1, b))
        return carry

    lax.fori_loop(0, 3, two, 0)
    step((7, b), (6, a))
    step(None, (7, b))
    for c in range(3):
        for half in range(2):
            columns = slice(half * LANES, (half + 1) * LANES)
            out_ref[c, :, columns] = cells[2 * c + half, 0:128, :]
            one, other = by_partner(
                "ax", cells[2 * c + half, 0:32, :], cells[2 * c + half, 96:128, :]
            )
            one_ref[c, :, columns] = one
            other_ref[c, :, columns] = other


def deposits(ends, keys, table, corr, one, other):
    f32 = jnp.float32
    smem, vmem = pl.BlockSpec(memory_space=SMEM), pl.BlockSpec(memory_space=VMEM)
    slot = [VMEM((ROWS, ROWS, LANES), f32), VMEM((16, ROWS, LANES), f32), VMEM((8, 16, LANES), f32)]
    return pl.pallas_call(
        deposit_kernel,
        name="deposits",
        out_shape=(
            jax.ShapeDtypeStruct((3, 128, 2 * LANES), f32),
            jax.ShapeDtypeStruct((3, 128, LANES), f32),
            jax.ShapeDtypeStruct((3, 32, 2 * LANES), f32),
            jax.ShapeDtypeStruct((3, 32, 2 * LANES), f32),
        ),
        in_specs=[smem] + [vmem] * 5,
        scratch_shapes=[VMEM((6, 144, LANES), f32), VMEM((2 * LANES, LANES), jnp.bfloat16)]
        + slot
        + slot,
        compiler_params=params(),
    )(ends, keys, table, corr, one, other)


def axial_kernel(taps, cells_ref, one_in, other_in, out_ref, one_ref, other_ref, first_ref, last_ref):
    for c in range(3):
        before, after = from_partners("ax", one_in[c], other_in[c])
        padded = jnp.concatenate([before, cells_ref[c], after], axis=0)
        total = taps[0] * padded[0:128]
        for k in range(1, 5):
            total = total + taps[k] * padded[16 * k : 16 * k + 128]
        out_ref[c] = total
        for a in range(8):
            first_ref[2 * a : 2 * a + 2, :] = total[16 * a : 16 * a + 2]
            last_ref[2 * a : 2 * a + 2, :] = total[16 * a + 14 : 16 * a + 16]
        one_ref[c], other_ref[c] = by_partner("rad", first_ref[...], last_ref[...])


def radial_kernel(
    taps, cells_ref, one_in, other_in, out_ref, one_ref, other_ref, padded, before_ref, after_ref
):
    lane = lax.broadcasted_iota(jnp.int32, (LANES, LANES), 1)
    edges = jnp.zeros((LANES, LANES), jnp.float32)
    for c in range(3):
        before_ref[...], after_ref[...] = from_partners("rad", one_in[c], other_in[c])
        for a in range(8):
            padded[0:2, :] = before_ref[2 * a : 2 * a + 2, :]
            padded[2:18, :] = cells_ref[c, 16 * a : 16 * a + 16, :]
            padded[18:20, :] = after_ref[2 * a : 2 * a + 2, :]
            total = taps[0] * padded[0:16, :]
            for k in range(1, 5):
                total = total + taps[k] * padded[k : k + 16, :]
            out_ref[c, 16 * a : 16 * a + 16, :] = total
        left, right = out_ref[c, :, 0:LANES], out_ref[c, :, LANES:]
        if c:
            left = pltpu.roll(left, 2 * c, 1)
        right = pltpu.roll(right, 10 + 2 * c, 1)
        edges = jnp.where((lane >> 1) == c, left, edges)
        edges = jnp.where((lane >> 1) == 4 + c, right, edges)
    turned = edges.T
    one_ref[...], other_ref[...] = by_partner("az", turned[0:8], turned[8:16])


def azimuthal_kernel(taps, cells_ref, one_in, other_in, out_ref):
    lane = lax.broadcasted_iota(jnp.int32, (LANES, LANES), 1)
    rest = jnp.zeros((LANES - 16, LANES), jnp.float32)
    before, after = from_partners("az", one_in[...], other_in[...], True)
    edges = jnp.concatenate([after, before, rest], axis=0).T
    for c in range(3):
        ahead = pltpu.roll(edges, LANES - 2 * c, 1) if c else edges
        halo = jnp.where(lane < 64, ahead, pltpu.roll(edges, 118 - 2 * c, 1))
        left, right = cells_ref[c, :, 0:LANES], cells_ref[c, :, LANES:]
        out_left, out_right = taps[2] * left, taps[2] * right
        for k in (1, 2):
            tap = taps[2 + k]
            inner = lane < LANES - k
            x, y, z = (pltpu.roll(v, LANES - k, 1) for v in (left, right, halo))
            out_left = out_left + tap * jnp.where(inner, x, y)
            out_right = out_right + tap * jnp.where(inner, y, z)
            inner = lane >= k
            x, y, z = (pltpu.roll(v, k, 1) for v in (left, right, halo))
            out_left = out_left + tap * jnp.where(inner, x, z)
            out_right = out_right + tap * jnp.where(inner, y, x)
        out_ref[c, :, 0:LANES] = out_left
        out_ref[c, :, LANES:] = out_right


def filtered(deposit, one, other):
    f32 = jnp.float32
    raw = [math.exp(-0.5 * k * k) for k in range(-2, 3)]
    taps = [x / sum(raw) for x in raw]
    whole = jax.ShapeDtypeStruct(deposit.shape, f32)
    radial_face = jax.ShapeDtypeStruct((3, 16, 2 * LANES), f32)
    edge = jax.ShapeDtypeStruct((8, LANES), f32)
    cells, one, other = pl.pallas_call(
        functools.partial(axial_kernel, taps),
        name="axial_filter",
        out_shape=(whole, radial_face, radial_face),
        scratch_shapes=[VMEM((16, 2 * LANES), f32)] * 2,
        compiler_params=params(),
    )(deposit, *swapped(one, other, "ax"))
    cells, one, other = pl.pallas_call(
        functools.partial(radial_kernel, taps),
        name="radial_filter",
        out_shape=(whole, edge, edge),
        scratch_shapes=[VMEM((24, 2 * LANES), f32)] + [VMEM((16, 2 * LANES), f32)] * 2,
        compiler_params=params(),
    )(cells, *swapped(one, other, "rad"))
    return pl.pallas_call(
        functools.partial(azimuthal_kernel, taps),
        name="azimuthal_filter",
        out_shape=whole,
        compiler_params=params(),
    )(cells, *swapped(one, other, "az", True))


def swapped(one, other, axis, wrap=False):
    count = lax.axis_size(axis)

    def partner(i, odd):
        j = i + 1 if i % 2 == odd else i - 1
        return j % count if wrap or 0 <= j < count else i

    return [
        lax.ppermute(x, axis, [(i, partner(i, odd)) for i in range(count)])
        for odd, x in enumerate((one, other))
    ]


def per_device(positions, velocity, diameter, cell_index, pair_list, live_pairs, gas_velocity):
    live = live_pairs.reshape(1, 1)
    cells = cell_index.reshape(128, LANES)
    gas = gas_velocity.reshape(3, 128, 2 * LANES)
    pos = positions.reshape(3, 128, LANES)
    vel = velocity.reshape(3, 128, LANES)
    diam = diameter.reshape(128, LANES)
    cell_keys, cell_ends, table, words, largest, one, other = droplet_states(
        cells, gas, pos, vel, diam
    )
    one, other = swapped(one, other, "az", True)
    pair_keys, pair_ends = pair_sort(live, pair_list.reshape(2, 256, LANES))
    heads, one, other = near_pairs(pair_ends, pair_keys, words, largest, one, other)
    one, other = swapped(one, other, "az", True)
    corr = own_pairs(live, pair_ends, pair_keys, words, largest, heads)
    deposit, correction, one, other = deposits(cell_ends, cell_keys, table, corr, one, other)
    smoothed = filtered(deposit, one, other)
    return (correction.reshape(positions.shape), smoothed.reshape(gas_velocity.shape))


def solution(mesh):
    return jax.shard_map(
        per_device,
        mesh=mesh,
        in_specs=(
            P(None, "ax", "rad", "az"),
            P(None, "ax", "rad", "az"),
            P("ax", "rad", "az"),
            P("ax", "rad", "az"),
            P(None, "ax", "rad", "az"),
            P("ax", "rad", "az"),
            P(None, "ax", "rad", "az"),
        ),
        out_specs=(P(None, "ax", "rad", "az"), P(None, "ax", "rad", "az")),
        check_vma=False,
    )
```

```python
import functools
import math

import jax
import jax.numpy as jnp
from jax import lax
from jax.experimental import pallas as pl
from jax.experimental.pallas import tpu as pltpu
from jax.sharding import PartitionSpec as P

piep_coef = 1.0
drag_coef = 20.0

LANES = 128
ROWS = 8
BLOCK = 2048
GAS_WINDOW = 10
BUCKET = 1024
BUCKETS = 20
NEAR_BUCKETS = 4
NEAR_HEADS = 8
OWN_HEADS = 12
DEAD = 1 << 29

NT = (((1,), (1,)), ((), ()))
VMEM = pltpu.VMEM
SMEM = pltpu.SMEM


def params(megabytes=40):
    return pltpu.CompilerParams(vmem_limit_bytes=megabytes << 20)


def lane_gather(table, index):
    numbers = lax.GatherDimensionNumbers(
        offset_dims=(),
        collapsed_slice_dims=(1,),
        start_index_map=(1,),
        operand_batching_dims=(0,),
        start_indices_batching_dims=(0,),
    )
    return lax.gather(
        table,
        index[..., None],
        numbers,
        slice_sizes=(1, 1),
        mode=lax.GatherScatterMode.PROMISE_IN_BOUNDS,
    )


def sort_network(regs, place, levels):
    sub = lax.broadcasted_iota(jnp.int32, (ROWS, LANES), 0)
    lane = lax.broadcasted_iota(jnp.int32, (ROWS, LANES), 1)
    count = len(regs)

    def bit_fill(bit, v):
        if bit >= levels:
            return 0
        kind, k = place[bit]
        if kind == "v":
            return -((v >> k) & 1)
        return -(((sub if kind == "s" else lane) >> k) & 1)

    flip = [0] * count
    for level in range(1, levels + 1):
        fills = {}
        for v in range(count):
            kind, k = place[level] if level < levels else ("v", 99)
            key = (v >> k) & 1 if kind == "v" else 0
            if key not in fills:
                fills[key] = bit_fill(level, v)
            new = fills[key]
            if isinstance(new, int) and isinstance(flip[v], int):
                if new != flip[v]:
                    regs[v] = ~regs[v]
            else:
                regs[v] = regs[v] ^ (new ^ flip[v])
            flip[v] = new
        for bit in reversed(range(level)):
            kind, k = place[bit]
            step = 1 << k
            if kind == "v":
                for v in range(count):
                    if not v & step:
                        a, b = regs[v], regs[v | step]
                        regs[v], regs[v | step] = jnp.minimum(a, b), jnp.maximum(a, b)
            else:
                axis, size, where = (0, ROWS, sub) if kind == "s" else (1, LANES, lane)
                lower = (where & step) == 0
                for v in range(count):
                    x = regs[v]
                    ahead = pltpu.roll(x, size - step, axis)
                    behind = ahead if 2 * step == size else pltpu.roll(x, step, axis)
                    regs[v] = jnp.where(lower, jnp.minimum(x, ahead), jnp.maximum(x, behind))
    return regs


def split_two(x):
    high = x.astype(jnp.bfloat16).astype(jnp.float32)
    return high, x - high


def split_three(x):
    high, rest = split_two(x)
    mid, low = split_two(rest)
    return high, mid, low


def packed_row(ref, row):
    return jnp.broadcast_to(ref[row : row + 1, :], (16, LANES)).astype(jnp.bfloat16)


def one_hot_rows(low, iota):
    one = jnp.ones((16, LANES), jnp.bfloat16)
    zero = jnp.zeros((16, LANES), jnp.bfloat16)
    return jnp.concatenate(
        [jnp.where(low == iota[k : k + 16, :], one, zero) for k in range(0, iota.shape[0], 16)],
        axis=0,
    )


def spread_rows(rel, parts, iota):
    hit = rel == iota[0:16, :]
    zero = jnp.zeros((16, LANES), jnp.bfloat16)
    return jnp.concatenate([jnp.where(hit, p, zero) for part in parts for p in part], axis=0)


def block_product(rows, hots):
    zero = jnp.zeros
    lines = [
        jnp.concatenate(
            [x if m == n else zero(x.shape, x.dtype) for m in range(len(rows))], axis=1
        )
        for n, x in enumerate(rows)
    ]
    return lax.dot_general(
        jnp.concatenate(lines, axis=0),
        jnp.concatenate(hots, axis=1),
        NT,
        preferred_element_type=jnp.float32,
    )


def spread_add(rows, hots):
    out = lax.dot_general(
        jnp.concatenate(rows, axis=1) if len(rows) > 1 else rows[0],
        jnp.concatenate(hots, axis=1) if len(hots) > 1 else hots[0],
        NT,
        preferred_element_type=jnp.float32,
    )
    total = out[0:48]
    for s in range(48, out.shape[0], 48):
        total = total + out[s : s + 48]
    return total


def fill_iota(iota):
    rows = lax.broadcasted_iota(jnp.int32, iota.shape, 0)
    iota[...] = rows.astype(jnp.float32).astype(jnp.bfloat16)


def rows_of(block):
    start = block * 16
    return pl.ds(start if isinstance(block, int) else pl.multiple_of(start, 16), 16)


def wide(ref, *at):
    return jnp.broadcast_to(ref[at[:-1] + (slice(at[-1], at[-1] + 1),)], (ROWS, LANES))


def window(table, first, count, row, low, found):
    rel = row - first
    for u in range(count):
        found = jnp.where(rel == u, lane_gather(table[first + u], low), found)
    return found


def running_max(x, count):
    x = jnp.broadcast_to(x, (ROWS, LANES))
    step = 1
    while step < count:
        x = jnp.maximum(x, pltpu.roll(x, LANES - step, 1))
        step *= 2
    return x


def by_partner(axis, first, last):
    even = (lax.axis_index(axis) & 1) == 0
    return jnp.where(even, last, first), jnp.where(even, first, last)


def neighbours(axis):
    at, count = lax.axis_index(axis), lax.axis_size(axis)
    return lax.rem(at + count - 1, count), lax.rem(at + 1, count)


def from_partners(axis, one, other, wrap=False):
    at, count = lax.axis_index(axis), lax.axis_size(axis)
    even = (at & 1) == 0
    before, after = jnp.where(even, other, one), jnp.where(even, one, other)
    if wrap:
        return before, after
    return jnp.where(at > 0, before, 0.0), jnp.where(at < count - 1, after, 0.0)


PLACE_STEP = 0.1 / 65535.0
RADIUS_LEAST = 0.01
RADIUS_STEP = 0.04 / 65535.0
SLIP_HALF = 1 << 20


def largest_slip(table, rows):
    most = jnp.zeros((ROWS, LANES), jnp.float32)
    for n in range(0, rows, ROWS):
        for c in range(3):
            most = jnp.maximum(most, jnp.abs(table[n : n + ROWS, 3 + c, :]))
    most = jnp.max(jnp.max(most, axis=0, keepdims=True), axis=1, keepdims=True)
    return jnp.broadcast_to(jnp.maximum(most, 1e-30), (ROWS, LANES))


def code_rows(table, n, largest, words):
    rows = pl.ds(n * ROWS, ROWS)

    def whole(c, least, step):
        x = ((table[rows, c, :] - least) * (1.0 / step) + 0.5).astype(jnp.int32)
        return jnp.clip(x, 0, 65535)

    x, y, z = (whole(c, 0.0, PLACE_STEP) for c in range(3))
    radius = whole(6, RADIUS_LEAST, RADIUS_STEP)
    scale = (SLIP_HALF - 1.0) / largest
    u, v, w = (
        (table[rows, 3 + c, :] * scale + (SLIP_HALF + 0.5)).astype(jnp.int32) for c in range(3)
    )
    coded = (
        x | (y << 16),
        z | (radius << 16),
        u | ((w & 2047) << 21),
        v | (lax.shift_right_logical(w, 11) << 21),
    )
    for k, word in enumerate(coded):
        words[pl.ds(n * 32 + k, ROWS, stride=4), :] = word


def decoded(words, largest):
    low = [x & 65535 for x in words[0:2]]
    high = [lax.shift_right_logical(x, 16) for x in words[0:2]]
    place = (low[0], high[0], low[1])
    radius = high[1].astype(jnp.float32) * RADIUS_STEP + RADIUS_LEAST
    mask = 2 * SLIP_HALF - 1
    third = lax.shift_right_logical(words[2], 21) | (lax.shift_right_logical(words[3], 21) << 11)
    scale = largest * (1.0 / (SLIP_HALF - 1.0))
    slip = [
        (x - SLIP_HALF).astype(jnp.float32) * scale for x in (words[2] & mask, words[3] & mask, third)
    ]
    return place, radius, slip


def fill_gas_rows(gas_ref, gas_rows):
    for r in range(16):
        rows = slice(r * ROWS, (r + 1) * ROWS)
        for c in range(3):
            for half in range(2):
                gas_rows[rows, half * 4 + c, :] = gas_ref[c, rows, half * LANES : (half + 1) * LANES]


def gas_index(block, keys_ref, slot):
    idx = slot[0]
    keys = keys_ref[rows_of(block), :]
    idx[0] = lax.shift_right_logical(keys, 19)
    idx[1] = lax.shift_right_logical(keys, 11) & (LANES - 1)


def gas_gather(block, g, ends, gas_rows, slot):
    idx, found = slot[0], slot[1]
    zero = jnp.zeros((ROWS, LANES), jnp.float32)
    first = ends[0, block * 16 + g]
    found[g] = window(gas_rows, first, GAS_WINDOW, wide(idx, 0, g), wide(idx, 1, g), zero)


def gas_rest(block, ends, gas_rows, slot):
    idx, found = slot[0], slot[1]

    @pl.when(ends[2, block * 16] >= GAS_WINDOW)
    def _():
        def one(g, carry):
            first = ends[0, block * 16 + g]
            row = jnp.broadcast_to(idx[0, pl.ds(g, 1), :], (ROWS, LANES))
            low = jnp.broadcast_to(idx[1, pl.ds(g, 1), :], (ROWS, LANES))

            def trip(t, total):
                base = jnp.minimum(first + GAS_WINDOW * t, LANES)
                return window(gas_rows, base, GAS_WINDOW, row, low, total)

            trips = (ends[1, block * 16 + g] - first) // GAS_WINDOW + 1
            found[g] = lax.fori_loop(1, trips, trip, found[g])
            return carry

        lax.fori_loop(0, 16, one, 0)


def seen_values(block, keys_ref, slot):
    idx, found, val = slot
    keys = keys_ref[rows_of(block), :]
    upper = (keys & (1 << 18)) != 0
    place_in = keys & (BLOCK - 1)
    val[0] = lax.shift_right_logical(place_in, 7).astype(jnp.float32)
    val[1] = (place_in & (LANES - 1)).astype(jnp.float32)
    for c in range(3):
        seen = jnp.where(upper, found[:, 4 + c, :], found[:, c, :])
        for n, part in enumerate(split_three(seen)):
            val[2 + 3 * c + n] = part


def seen_in_order(groups, slot, iota):
    val = slot[2]
    rows, hots = [], []
    for g in groups:
        parts = [[packed_row(val.at[2 + 3 * c + n], g) for c in range(3)] for n in range(3)]
        rows.append(spread_rows(packed_row(val.at[0], g), parts, iota))
        hots.append(one_hot_rows(packed_row(val.at[1], g), iota))
    return spread_add(rows, hots)


def write_states(block, total, pos_ref, vel_ref, diam_ref, out_ref, out_rows):
    rows = rows_of(block)
    for c in range(3):
        out_ref[out_rows, c, :] = pos_ref[c, rows, :]
        out_ref[out_rows, 3 + c, :] = total[16 * c : 16 * c + 16] - vel_ref[c, rows, :]
    out_ref[out_rows, 6, :] = 0.5 * diam_ref[rows, :]
    out_ref[out_rows, 7, :] = jnp.zeros((16, LANES), jnp.float32)


def states_step(gather, scatter, keys_ref, ends, gas_rows, iota, arrays):
    total = jnp.zeros((48, LANES), jnp.float32)
    if gather:
        gas_index(gather[0], keys_ref, gather[1])
    if scatter:
        seen_values(scatter[0], keys_ref, scatter[1])
    for g in range(16):
        if gather:
            gas_gather(gather[0], g, ends, gas_rows, gather[1])
        if scatter and g % 2:
            total = total + seen_in_order((g - 1, g), scatter[1], iota)
    if scatter:
        write_states(scatter[0], total, *arrays, *scatter[2:])
    if gather:
        gas_rest(gather[0], ends, gas_rows, gather[1])


def states_kernel(
    cell_hbm, gas_hbm, pos_hbm, vel_hbm, diam_hbm,
    keys_ref, ends_ref, table_ref, words_ref, largest_ref, one_ref, other_ref,
    cell_ref, gas_ref, pos_ref, vel_ref, diam_ref,
    gas_rows, iota, ends, idx_a, found_a, val_a, idx_b, found_b, val_b, sems,
):
    sources = (cell_hbm, gas_hbm, pos_hbm, vel_hbm, diam_hbm)
    places = (cell_ref, gas_ref, pos_ref, vel_ref, diam_ref)
    copies = [
        pltpu.make_async_copy(x, y, sems.at[n]) for n, (x, y) in enumerate(zip(sources, places))
    ]
    for copy in copies:
        copy.start()
    copies[0].wait()
    sub = lax.broadcasted_iota(jnp.int32, (ROWS, LANES), 0)
    lane = lax.broadcasted_iota(jnp.int32, (ROWS, LANES), 1)
    cells = cell_ref[...].T
    regs = []
    for v in range(16):
        own = (lane & 15) * LANES + v * ROWS + sub
        regs.append(cells[v * ROWS : (v + 1) * ROWS] * BLOCK + own)
    place = [("v", k) for k in range(4)] + [("s", k) for k in range(3)] + [("l", k) for k in range(4)]
    regs = sort_network(regs, place, 11)
    keys_ref[...] = jnp.concatenate(regs, axis=0).T
    least = functools.reduce(jnp.minimum, regs)
    most = functools.reduce(jnp.maximum, regs)
    least = lax.shift_right_logical(jnp.min(least, axis=0, keepdims=True), 19)
    most = lax.shift_right_logical(jnp.max(most, axis=0, keepdims=True), 19)
    ends_ref[0:1, :] = least
    ends_ref[1:2, :] = most
    ends_ref[2:8, :] = running_max(most - least, 16)[0:6]
    copy = pltpu.make_async_copy(ends_ref, ends, sems.at[5])
    copy.start()
    copies[1].wait()
    fill_gas_rows(gas_ref, gas_rows)
    for other in copies[2:]:
        other.wait()
    copy.wait()
    fill_iota(iota)
    a, b = (idx_a, found_a, val_a), (idx_b, found_b, val_b)
    step = functools.partial(
        states_step, keys_ref=keys_ref, ends=ends, gas_rows=gas_rows, iota=iota,
        arrays=(pos_ref, vel_ref, diam_ref),
    )
    step((0, a), None)

    def two(k, carry):
        block = 2 * k
        step((block + 1, b), (block, a, table_ref, rows_of(block)))
        step((block + 2, a), (block + 1, b, table_ref, rows_of(block + 1)))
        return carry

    lax.fori_loop(0, 3, two, 0)
    step((7, b), (6, a, table_ref, rows_of(6)))
    step(None, (7, b, table_ref, rows_of(7)))
    largest = largest_slip(table_ref, 128)
    largest_ref[...] = largest
    for n in range(16):
        code_rows(table_ref, n, largest, words_ref)
    words_ref[512:576, :] = jnp.zeros((64, LANES), jnp.int32)
    one_ref[...], other_ref[...] = by_partner("az", table_ref[0:16], table_ref[112:128])


def slots(rows, parts, dtype=jnp.float32):
    one = [VMEM((2, 16, LANES), jnp.int32), VMEM((16, ROWS, LANES), dtype), VMEM((parts, rows, LANES), dtype)]
    return one + one


def droplet_states(cells, gas, pos, vel, diam):
    f32, i32 = jnp.float32, jnp.int32
    arrays = (cells, gas, pos, vel, diam)
    return pl.pallas_call(
        states_kernel,
        name="droplet_states",
        out_shape=(
            jax.ShapeDtypeStruct((128, LANES), i32),
            jax.ShapeDtypeStruct((ROWS, LANES), i32),
            jax.ShapeDtypeStruct((128, ROWS, LANES), f32),
            jax.ShapeDtypeStruct((576, LANES), i32),
            jax.ShapeDtypeStruct((ROWS, LANES), f32),
            jax.ShapeDtypeStruct((16, ROWS, LANES), f32),
            jax.ShapeDtypeStruct((16, ROWS, LANES), f32),
        ),
        in_specs=[pl.BlockSpec(memory_space=pltpu.HBM)] * 5,
        scratch_shapes=[VMEM(x.shape, x.dtype) for x in arrays]
        + [VMEM((144, ROWS, LANES), f32), VMEM((LANES, LANES), jnp.bfloat16), SMEM((ROWS, LANES), i32)]
        + slots(16, 11)
        + [pltpu.SemaphoreType.DMA((6,))],
        compiler_params=params(60),
    )(*arrays)


def pair_sort_kernel(live_ref, pairs_ref, keys_ref, ends_ref):
    live = live_ref[0, 0]
    sub = lax.broadcasted_iota(jnp.int32, (ROWS, LANES), 0)
    lane = lax.broadcasted_iota(jnp.int32, (ROWS, LANES), 1)
    regs = []
    for v in range(32):
        rows = slice(v * ROWS, (v + 1) * ROWS)
        slot = v * 1024 + sub * LANES + lane
        head = pairs_ref[0, rows, :]
        tail = pairs_ref[1, rows, :] - 7 * BLOCK
        own = tail - BLOCK
        inside = (own >= 0) & (own < 8 * BLOCK)
        tail = jnp.where(inside, jnp.maximum(own, head) + BLOCK, tail)
        head = jnp.where(inside, jnp.minimum(own, head), head)
        bucket = lax.shift_right_logical(tail, 10)
        bucket = jnp.where(inside, bucket + 2, jnp.where(bucket >= 18, bucket - 16, bucket))
        turn = -(bucket & 1) & (8 * BLOCK - 1)
        key = (bucket << 24) | ((head ^ turn) << 10) | (tail & (BUCKET - 1))
        regs.append(jnp.where(slot < live, key, DEAD))
    place = (
        [("v", k) for k in range(4)]
        + [("s", k) for k in range(3)]
        + [("v", 4)]
        + [("l", k) for k in range(7)]
    )
    regs = sort_network(regs, place, 15)
    beyond = jnp.zeros((ROWS, LANES), jnp.float32)
    for key in regs:
        beyond = beyond + jnp.where(key < NEAR_BUCKETS << 24, 1.0, 0.0)
    beyond = jnp.sum(jnp.sum(beyond, axis=0, keepdims=True), axis=1, keepdims=True)
    ends_ref[8:16, :] = jnp.broadcast_to(beyond, (ROWS, LANES)).astype(jnp.int32)
    for half in range(2):
        rows = regs[16 * half : 16 * half + 16]
        keys_ref[half] = jnp.concatenate(rows, axis=0).T
        least_head = least_tail = jnp.full((ROWS, LANES), 1 << 20, jnp.int32)
        most_head = most_tail = jnp.full((ROWS, LANES), -1, jnp.int32)
        for key in rows:
            used = key < DEAD
            bucket = lax.shift_right_logical(key, 24)
            head = lax.shift_right_logical(key, 17) & (LANES - 1)
            head = head ^ (-(bucket & 1) & (LANES - 1))
            least_head = jnp.minimum(least_head, jnp.where(used, head, 1 << 20))
            most_head = jnp.maximum(most_head, jnp.where(used, head, -1))
            least_tail = jnp.minimum(least_tail, jnp.where(used, bucket, 1 << 20))
            most_tail = jnp.maximum(most_tail, jnp.where(used, bucket, -1))
        for n, x in enumerate((least_head, most_head, least_tail, most_tail)):
            reduce = jnp.max if n % 2 else jnp.min
            row = 4 * half + n
            bound = (LANES, LANES, BUCKETS, BUCKETS)[n]
            ends_ref[row : row + 1, :] = jnp.minimum(reduce(x, axis=0, keepdims=True), bound)


def pair_sort(live, pairs):
    return pl.pallas_call(
        pair_sort_kernel,
        name="pair_sort",
        out_shape=(
            jax.ShapeDtypeStruct((2, LANES, LANES), jnp.int32),
            jax.ShapeDtypeStruct((16, LANES), jnp.int32),
        ),
        in_specs=[pl.BlockSpec(memory_space=SMEM), pl.BlockSpec(memory_space=VMEM)],
        compiler_params=params(),
    )(live, pairs)


def group_ends(g, ends, part):
    g = jnp.minimum(g, 2 * LANES - 1)
    at, lane = 4 * (g & 1), g >> 1
    low, high, _ = part
    return (
        ends[at, lane] & -2,
        ends[at + 1, lane],
        jnp.maximum(ends[at + 2, lane], low),
        jnp.minimum(ends[at + 3, lane], high - 1),
    )


def take_items(state, groups, ends, part):
    low, high, heads = part
    items = []
    for _ in range(ROWS):
        g, bucket, head, now, later = state
        place = jnp.minimum(bucket, high) - low
        items.append((jnp.minimum(g, 2 * LANES - 1), jnp.where(g < groups, bucket, -1), head, place))
        ahead = group_ends(g + 2, ends, part)
        more_heads = head + heads <= now[1]
        stay = more_heads | (bucket < now[3])
        head = jnp.where(more_heads, head + heads, jnp.where(stay, now[0], later[0]))
        bucket = jnp.where(more_heads, bucket, jnp.where(stay, bucket + 1, later[2]))
        now = tuple(jnp.where(stay, x, y) for x, y in zip(now, later))
        later = tuple(jnp.where(stay, x, y) for x, y in zip(later, ahead))
        state = (jnp.where(stay, g, g + 1), bucket, head, now, later)
    return items, state


def word_window(words, first, count, pair, low):
    found = jnp.zeros((ROWS, LANES), jnp.int32)
    for u in range(count):
        rows = words[pl.ds(pl.multiple_of((first + u) * ROWS, ROWS), ROWS), :]
        found = jnp.where(pair == u, lane_gather(rows, low), found)
    return found


def pair_gather(k, item, keys_ref, near_words, far_words, heads, slot):
    key_rows, rel_rows, near, far = slot
    g, bucket, first, part = item
    keys = jnp.broadcast_to(keys_ref[g & 1, pl.ds(g >> 1, 1), :], (ROWS, LANES))
    of_bucket = lax.shift_right_logical(keys, 24)
    turn = -(of_bucket & 1) & (8 * BLOCK - 1)
    head = (lax.shift_right_logical(keys, 10) & (8 * BLOCK - 1)) ^ turn
    rel = lax.shift_right_logical(head, 7) - first
    used = (of_bucket == bucket) & (rel >= 0) & (rel < heads)
    key_rows[k : k + 1, :] = jnp.where(used, keys, DEAD)[0:1]
    rel_rows[k : k + 1, :] = rel[0:1]
    near[k] = word_window(near_words, first >> 1, heads // 2, rel >> 1, head & (LANES - 1))
    pair = lax.shift_right_logical(keys, 8) & 3
    far[k] = word_window(far_words, part * 4, 4, pair, keys & (LANES - 1))


def pair_values(slot, val, near_largest, far_largest):
    key_rows, rel_rows, near, far = slot
    keys, rel = key_rows[...], rel_rows[...]
    used = keys < DEAD
    turn = -(lax.shift_right_logical(keys, 24) & 1) & (LANES - 1)
    val[0] = rel.astype(jnp.float32)
    val[1] = ((lax.shift_right_logical(keys, 10) & (LANES - 1)) ^ turn).astype(jnp.float32)
    val[2] = (lax.shift_right_logical(keys, 7) & 7).astype(jnp.float32)
    val[3] = (keys & (LANES - 1)).astype(jnp.float32)

    def words(ref, odd):
        return [jnp.where(odd, ref[:, 4 + w, :], ref[:, w, :]) for w in range(4)]

    near_place, near_radius, near_slip = decoded(words(near, (rel & 1) == 1), near_largest)
    far_place, far_radius, far_slip = decoded(words(far, (keys & LANES) != 0), far_largest)
    gap = jnp.zeros((ROWS, LANES), jnp.float32)
    for x, y in zip(far_place, near_place):
        apart = (x - y).astype(jnp.float32)
        gap = gap + apart * apart
    gap = gap * (PLACE_STEP * PLACE_STEP)
    far_ratio = far_radius * lax.rsqrt(gap + far_radius * far_radius)
    near_ratio = near_radius * lax.rsqrt(gap + near_radius * near_radius)
    weight_far = jnp.where(used, piep_coef * far_ratio * far_ratio * far_ratio, 0.0)
    weight_near = jnp.where(used, piep_coef * near_ratio * near_ratio * near_ratio, 0.0)
    for c in range(3):
        for n, part in enumerate(split_two(weight_far * far_slip[c])):
            val[4 + 3 * n + c] = part
        for n, part in enumerate(split_two(weight_near * near_slip[c])):
            val[10 + 3 * n + c] = part


def pair_scatter(k, item, val, head_sum, tail_sum, iota, iota8):
    first, tail_first = item
    parts = [[packed_row(val.at[4 + 3 * n + c], k) for c in range(3)] for n in range(2)]
    heads = spread_rows(packed_row(val.at[0], k), parts, iota)
    hit = packed_row(val.at[2], k) == iota8[...]
    zero = jnp.zeros((16, LANES), jnp.bfloat16)
    tails = []
    for n in range(10, 16, 2):
        both = jnp.concatenate([wide(val, n, k), wide(val, n + 1, k)], axis=0)
        tails.append(jnp.where(hit, both.astype(jnp.bfloat16), zero))
    tails = jnp.concatenate(tails, axis=0)
    out = block_product(
        [heads, tails], [one_hot_rows(packed_row(val.at[n], k), iota) for n in (1, 3)]
    )
    for c in range(3):
        head_sum[c, pl.ds(first, 16), :] += out[16 * c : 16 * c + 16] + out[16 * c + 48 : 16 * c + 64]
    at = pl.ds(pl.multiple_of(tail_first, 8), 8)
    for c in range(3):
        tail_sum[c, at, :] += out[8 * c + 96 : 8 * c + 104] + out[8 * c + 120 : 8 * c + 128]


def run_pairs(groups, start, part, ends, keys_ref, near, far, sums, iota, iota8, scratch):
    fill_iota(iota)
    rows = lax.broadcasted_iota(jnp.int32, iota8.shape, 0) & 7
    iota8[...] = rows.astype(jnp.float32).astype(jnp.bfloat16)
    val, a, b = scratch[0], scratch[1:5], scratch[5:9]

    def step(state, slot, pending):
        items, state = take_items(state, groups, ends, part)
        if pending:
            pair_values(a, val, near[1], far[1])
        for k in range(ROWS):
            pair_gather(k, items[k], keys_ref, near[0], far[0], part[2], slot)
            if pending:
                pair_scatter(k, pending[k], val, *sums, iota, iota8)
        return tuple((item[2], item[3] * 8) for item in items), state, items[0][1] >= 0

    now, later = group_ends(start, ends, part), group_ends(start + 1, ends, part)
    state = (start, now[2], now[0], now, later)

    def one(carry):
        pending, state, _ = carry
        carry = step(state, b, pending)
        for x, y in zip(a, b):
            x[...] = y[...]
        return carry

    lax.while_loop(lambda carry: carry[2], one, step(state, a, None))


def near_pairs_kernel(
    ends, keys_ref, words_ref, largest_ref, one_in, other_in,
    heads_ref, sent_ref,
    shell, shell_words, head_sum, tail_sum, iota, iota8, *scratch,
):
    shell[0:16], shell[16:32] = from_partners("az", one_in[...], other_in[...], True)
    shell_largest = largest_slip(shell, 32)
    for n in range(4):
        code_rows(shell, n, shell_largest, shell_words)
    shell_words[128:160, :] = jnp.zeros((32, LANES), jnp.int32)
    head_sum[...] = jnp.zeros_like(head_sum)
    tail_sum[...] = jnp.zeros_like(tail_sum)
    groups = (ends[8, 0] + LANES - 1) // LANES
    run_pairs(
        groups, jnp.int32(0), (0, NEAR_BUCKETS, NEAR_HEADS), ends, keys_ref,
        (words_ref, largest_ref[...]), (shell_words, shell_largest),
        (head_sum, tail_sum), iota, iota8, scratch,
    )
    heads_ref[...] = head_sum[:, 0:128, :]
    sent_ref[0] = tail_sum[:, 0:16, :]
    sent_ref[1] = tail_sum[:, 16:32, :]


def own_pairs_kernel(
    live_ref, ends, keys_ref, words_ref, largest_ref, heads_ref,
    corr_ref,
    head_sum, tail_sum, iota, iota8, *scratch,
):
    head_sum[:, 0:128, :] = heads_ref[...]
    head_sum[:, 128:144, :] = jnp.zeros((3, 16, LANES), jnp.float32)
    tail_sum[...] = jnp.zeros_like(tail_sum)
    groups = (live_ref[0, 0] + LANES - 1) // LANES
    start = jnp.minimum(ends[8, 0] // LANES, 2 * LANES - 1)
    coded = (words_ref, largest_ref[...])
    run_pairs(
        groups, start, (NEAR_BUCKETS, BUCKETS, OWN_HEADS), ends, keys_ref, coded, coded,
        (head_sum, tail_sum), iota, iota8, scratch,
    )
    corr_ref[...] = head_sum[:, 0:128, :] + tail_sum[:, 0:128, :]


def pair_scratch(tail_rows):
    f32, i32 = jnp.float32, jnp.int32
    slot = [
        VMEM((ROWS, LANES), i32),
        VMEM((ROWS, LANES), i32),
        VMEM((ROWS, ROWS, LANES), i32),
        VMEM((ROWS, ROWS, LANES), i32),
    ]
    return [
        VMEM((3, 144, LANES), f32),
        VMEM((3, tail_rows, LANES), f32),
        VMEM((LANES, LANES), jnp.bfloat16),
        VMEM((16, LANES), jnp.bfloat16),
        VMEM((16, ROWS, LANES), f32),
        *slot,
        *slot,
    ]


def near_pairs(ends, keys, words, largest, one, other):
    f32 = jnp.float32
    smem, vmem = pl.BlockSpec(memory_space=SMEM), pl.BlockSpec(memory_space=VMEM)
    return pl.pallas_call(
        near_pairs_kernel,
        name="near_pairs",
        out_shape=(
            jax.ShapeDtypeStruct((3, 128, LANES), f32),
            jax.ShapeDtypeStruct((2, 3, 16, LANES), f32),
        ),
        in_specs=[smem, vmem, vmem, vmem, vmem, vmem],
        scratch_shapes=[VMEM((32, ROWS, LANES), f32), VMEM((160, LANES), jnp.int32)]
        + pair_scratch(40),
        compiler_params=params(),
    )(ends, keys, words, largest, one, other)


def own_pairs(live, ends, keys, words, largest, heads):
    smem, vmem = pl.BlockSpec(memory_space=SMEM), pl.BlockSpec(memory_space=VMEM)
    return pl.pallas_call(
        own_pairs_kernel,
        name="own_pairs",
        out_shape=jax.ShapeDtypeStruct((3, 128, LANES), jnp.float32),
        in_specs=[smem, smem, vmem, vmem, vmem, vmem],
        scratch_shapes=pair_scratch(136),
        compiler_params=params(),
    )(live, ends, keys, words, largest, heads)


def force_gather(block, keys_ref, table_ref, total_ref, slot):
    force, got, val = slot
    rows = rows_of(block)
    scale = (-2.0 * drag_coef) * table_ref[rows, 6, :]
    for c in range(3):
        push = scale * (table_ref[rows, 3 + c, :] + total_ref[c, rows, :])
        force[:, c, :] = push[0:8]
        force[:, 4 + c, :] = push[8:16]
    keys = keys_ref[rows, :]
    val[0] = lax.shift_right_logical(keys, 19).astype(jnp.float32)
    val[1] = (lax.shift_right_logical(keys, 11) & (2 * LANES - 1)).astype(jnp.float32)
    inner = lax.shift_right_logical(keys, 7) & 7
    low = keys & (LANES - 1)
    tables = [force[k] for k in range(ROWS)]
    for g in range(16):
        pick = jnp.broadcast_to(inner[g : g + 1, :], (ROWS, LANES))
        at = jnp.broadcast_to(low[g : g + 1, :], (ROWS, LANES))
        found = jnp.zeros((ROWS, LANES), jnp.float32)
        for k in range(ROWS):
            found = jnp.where(pick == k, lane_gather(tables[k], at), found)
        got[g] = found
    upper = (keys & 1024) != 0
    for c in range(3):
        pushed = jnp.where(upper, got[:, 4 + c, :], got[:, c, :])
        for n, part in enumerate(split_two(pushed)):
            val[2 + 2 * c + n] = part


def force_rows(g, base, slot, iota):
    val = slot[2]

    def row(n):
        if isinstance(g, int):
            return packed_row(val.at[n], g)
        return jnp.broadcast_to(val[n, pl.ds(g, 1), :], (16, LANES)).astype(jnp.bfloat16)

    rel = row(0) - base.astype(jnp.float32).astype(jnp.bfloat16)
    parts = [[row(2 + 2 * c + n) for c in range(3)] for n in range(2)]
    return spread_rows(rel, parts, iota), one_hot_rows(row(1), iota)


def force_add(groups, bases, slot, cells, iota):
    pieces = [force_rows(g, base, slot, iota) for g, base in zip(groups, bases)]
    out = block_product([p[0] for p in pieces], [p[1] for p in pieces])
    for n, base in enumerate(bases):
        for c in range(3):
            at = 96 * n + 16 * c
            total = out[at : at + 16] + out[at + 48 : at + 64]
            for half in range(2):
                part = total[:, half * LANES : (half + 1) * LANES]
                cells[2 * c + half, pl.ds(base, 16), :] += part


def force_rest(block, ends, slot, cells, iota):
    @pl.when(ends[2, block * 16] >= 16)
    def _():
        def one(g, carry):
            first, most = ends[0, block * 16 + g], ends[1, block * 16 + g]

            def trip(t, carry):
                force_add([g], [jnp.minimum(first + 16 * t, LANES)], slot, cells, iota)
                return carry

            lax.fori_loop(1, (most - first) // 16 + 1, trip, 0)
            return carry

        lax.fori_loop(0, 16, one, 0)


def deposit_step(gather, scatter, ends, keys_ref, table_ref, total_ref, cells, iota):
    if gather:
        force_gather(gather[0], keys_ref, table_ref, total_ref, gather[1])
    if scatter:
        for g in range(16):
            force_add([g], [ends[0, scatter[0] * 16 + g]], scatter[1], cells, iota)
        force_rest(scatter[0], ends, scatter[1], cells, iota)


def deposit_kernel(
    ends, keys_ref, table_ref, corr_ref, sent_ref,
    out_ref, total_ref, one_ref, other_ref,
    cells, iota, force_a, got_a, val_a, force_b, got_b, val_b,
):
    fill_iota(iota)
    cells[...] = jnp.zeros_like(cells)
    total_ref[...] = corr_ref[...]
    lower, upper = neighbours("az")
    total_ref[:, 0:16, :] += sent_ref[lower, 1]
    total_ref[:, 112:128, :] += sent_ref[upper, 0]
    a, b = (force_a, got_a, val_a), (force_b, got_b, val_b)
    step = functools.partial(
        deposit_step, ends=ends, keys_ref=keys_ref, table_ref=table_ref, total_ref=total_ref,
        cells=cells, iota=iota,
    )
    step((0, a), None)

    def two(k, carry):
        block = 2 * k
        step((block + 1, b), (block, a))
        step((block + 2, a), (block + 1, b))
        return carry

    lax.fori_loop(0, 3, two, 0)
    step((7, b), (6, a))
    step(None, (7, b))
    for c in range(3):
        for half in range(2):
            columns = slice(half * LANES, (half + 1) * LANES)
            out_ref[c, :, columns] = cells[2 * c + half, 0:128, :]
            one, other = by_partner(
                "ax", cells[2 * c + half, 0:32, :], cells[2 * c + half, 96:128, :]
            )
            one_ref[c, :, columns] = one
            other_ref[c, :, columns] = other


def deposits(ends, keys, table, corr, sent):
    f32 = jnp.float32
    smem, vmem = pl.BlockSpec(memory_space=SMEM), pl.BlockSpec(memory_space=VMEM)
    slot = [VMEM((ROWS, ROWS, LANES), f32), VMEM((16, ROWS, LANES), f32), VMEM((8, 16, LANES), f32)]
    return pl.pallas_call(
        deposit_kernel,
        name="deposits",
        out_shape=(
            jax.ShapeDtypeStruct((3, 128, 2 * LANES), f32),
            jax.ShapeDtypeStruct((3, 128, LANES), f32),
            jax.ShapeDtypeStruct((3, 32, 2 * LANES), f32),
            jax.ShapeDtypeStruct((3, 32, 2 * LANES), f32),
        ),
        in_specs=[smem] + [vmem] * 4,
        scratch_shapes=[VMEM((6, 144, LANES), f32), VMEM((2 * LANES, LANES), jnp.bfloat16)]
        + slot
        + slot,
        compiler_params=params(),
    )(ends, keys, table, corr, sent)


def axial_kernel(taps, cells_ref, one_in, other_in, out_ref, one_ref, other_ref, first_ref, last_ref):
    for c in range(3):
        before, after = from_partners("ax", one_in[c], other_in[c])
        padded = jnp.concatenate([before, cells_ref[c], after], axis=0)
        total = taps[0] * padded[0:128]
        for k in range(1, 5):
            total = total + taps[k] * padded[16 * k : 16 * k + 128]
        out_ref[c] = total
        for a in range(8):
            first_ref[2 * a : 2 * a + 2, :] = total[16 * a : 16 * a + 2]
            last_ref[2 * a : 2 * a + 2, :] = total[16 * a + 14 : 16 * a + 16]
        one_ref[c], other_ref[c] = by_partner("rad", first_ref[...], last_ref[...])


def radial_kernel(
    taps, cells_ref, one_in, other_in, out_ref, edges_ref, padded, before_ref, after_ref
):
    lane = lax.broadcasted_iota(jnp.int32, (LANES, LANES), 1)
    edges = jnp.zeros((LANES, LANES), jnp.float32)
    for c in range(3):
        before_ref[...], after_ref[...] = from_partners("rad", one_in[c], other_in[c])
        for a in range(8):
            padded[0:2, :] = before_ref[2 * a : 2 * a + 2, :]
            padded[2:18, :] = cells_ref[c, 16 * a : 16 * a + 16, :]
            padded[18:20, :] = after_ref[2 * a : 2 * a + 2, :]
            total = taps[0] * padded[0:16, :]
            for k in range(1, 5):
                total = total + taps[k] * padded[k : k + 16, :]
            out_ref[c, 16 * a : 16 * a + 16, :] = total
        left, right = out_ref[c, :, 0:LANES], out_ref[c, :, LANES:]
        if c:
            left = pltpu.roll(left, 2 * c, 1)
        right = pltpu.roll(right, 10 + 2 * c, 1)
        edges = jnp.where((lane >> 1) == c, left, edges)
        edges = jnp.where((lane >> 1) == 4 + c, right, edges)
    edges_ref[...] = edges.T[0:16]


def inner_azimuthal_kernel(taps, cells_ref, out_ref):
    lane = lax.broadcasted_iota(jnp.int32, (LANES, LANES), 1)
    for c in range(3):
        left, right = cells_ref[c, :, 0:LANES], cells_ref[c, :, LANES:]
        out_left, out_right = taps[2] * left, taps[2] * right
        for k in (1, 2):
            tap = taps[2 + k]
            inner = lane < LANES - k
            x, y = (pltpu.roll(v, LANES - k, 1) for v in (left, right))
            out_left = out_left + tap * jnp.where(inner, x, y)
            out_right = out_right + tap * jnp.where(inner, y, 0.0)
            inner = lane >= k
            x, y = (pltpu.roll(v, k, 1) for v in (left, right))
            out_left = out_left + tap * jnp.where(inner, x, 0.0)
            out_right = out_right + tap * jnp.where(inner, y, x)
        out_ref[c, :, 0:LANES] = out_left
        out_ref[c, :, LANES:] = out_right


def azimuthal_kernel(taps, inner_ref, edges_ref, out_ref):
    lane = lax.broadcasted_iota(jnp.int32, (LANES, LANES), 1)
    rest = jnp.zeros((LANES - 16, LANES), jnp.float32)
    lower, upper = neighbours("az")
    edges = jnp.concatenate([edges_ref[upper, 0:8], edges_ref[lower, 8:16], rest], axis=0).T
    for c in range(3):
        out_left, out_right = inner_ref[c, :, 0:LANES], inner_ref[c, :, LANES:]
        for k in (1, 2):
            x = pltpu.roll(edges, (118 - 2 * c + k) % LANES, 1)
            out_left = out_left + taps[2 - k] * jnp.where(lane < k, x, 0.0)
            y = pltpu.roll(edges, LANES - 2 * c - k, 1)
            out_right = out_right + taps[2 + k] * jnp.where(lane >= LANES - k, y, 0.0)
        out_ref[c, :, 0:LANES] = out_left
        out_ref[c, :, LANES:] = out_right


def filtered(deposit, one, other):
    f32 = jnp.float32
    raw = [math.exp(-0.5 * k * k) for k in range(-2, 3)]
    taps = [x / sum(raw) for x in raw]
    whole = jax.ShapeDtypeStruct(deposit.shape, f32)
    radial_face = jax.ShapeDtypeStruct((3, 16, 2 * LANES), f32)
    edge = jax.ShapeDtypeStruct((16, LANES), f32)
    cells, one, other = pl.pallas_call(
        functools.partial(axial_kernel, taps),
        name="axial_filter",
        out_shape=(whole, radial_face, radial_face),
        scratch_shapes=[VMEM((16, 2 * LANES), f32)] * 2,
        compiler_params=params(),
    )(deposit, *swapped(one, other, "ax"))
    cells, edges = pl.pallas_call(
        functools.partial(radial_kernel, taps),
        name="radial_filter",
        out_shape=(whole, edge),
        scratch_shapes=[VMEM((24, 2 * LANES), f32)] + [VMEM((16, 2 * LANES), f32)] * 2,
        compiler_params=params(),
    )(cells, *swapped(one, other, "rad"))
    edges = lax.all_gather(edges, "az")
    inner = pl.pallas_call(
        functools.partial(inner_azimuthal_kernel, taps),
        name="inner_azimuthal_filter",
        out_shape=whole,
        compiler_params=params(),
    )(cells)
    return pl.pallas_call(
        functools.partial(azimuthal_kernel, taps),
        name="azimuthal_filter",
        out_shape=whole,
        compiler_params=params(),
    )(inner, edges)


def swapped(one, other, axis, wrap=False):
    count = lax.axis_size(axis)

    def partner(i, odd):
        j = i + 1 if i % 2 == odd else i - 1
        return j % count if wrap or 0 <= j < count else i

    return [
        lax.ppermute(x, axis, [(i, partner(i, odd)) for i in range(count)])
        for odd, x in enumerate((one, other))
    ]


def per_device(positions, velocity, diameter, cell_index, pair_list, live_pairs, gas_velocity):
    live = live_pairs.reshape(1, 1)
    cells = cell_index.reshape(128, LANES)
    gas = gas_velocity.reshape(3, 128, 2 * LANES)
    pos = positions.reshape(3, 128, LANES)
    vel = velocity.reshape(3, 128, LANES)
    diam = diameter.reshape(128, LANES)
    cell_keys, cell_ends, table, words, largest, one, other = droplet_states(
        cells, gas, pos, vel, diam
    )
    one, other = swapped(one, other, "az", True)
    pair_keys, pair_ends = pair_sort(live, pair_list.reshape(2, 256, LANES))
    heads, sent = near_pairs(pair_ends, pair_keys, words, largest, one, other)
    sent = lax.all_gather(sent, "az")
    corr = own_pairs(live, pair_ends, pair_keys, words, largest, heads)
    deposit, correction, one, other = deposits(cell_ends, cell_keys, table, corr, sent)
    smoothed = filtered(deposit, one, other)
    return (correction.reshape(positions.shape), smoothed.reshape(gas_velocity.shape))


def solution(mesh):
    return jax.shard_map(
        per_device,
        mesh=mesh,
        in_specs=(
            P(None, "ax", "rad", "az"),
            P(None, "ax", "rad", "az"),
            P("ax", "rad", "az"),
            P("ax", "rad", "az"),
            P(None, "ax", "rad", "az"),
            P("ax", "rad", "az"),
            P(None, "ax", "rad", "az"),
        ),
        out_specs=(P(None, "ax", "rad", "az"), P(None, "ax", "rad", "az")),
        check_vma=False,
    )
```

```python
import functools
import math

import jax
import jax.numpy as jnp
from jax import lax
from jax.experimental import pallas as pl
from jax.experimental.pallas import tpu as pltpu
from jax.sharding import PartitionSpec as P

piep_coef = 1.0
drag_coef = 20.0

LANES = 128
ROWS = 8
BLOCK = 2048
GAS_WINDOW = 12
BUCKET = 1024
BUCKETS = 20
NEAR_BUCKETS = 4
NEAR_HEADS = 8
OWN_HEADS = 12
DEAD = 1 << 29

NT = (((1,), (1,)), ((), ()))
VMEM = pltpu.VMEM
SMEM = pltpu.SMEM


def params(megabytes=40):
    return pltpu.CompilerParams(vmem_limit_bytes=megabytes << 20)


def lane_gather(table, index):
    numbers = lax.GatherDimensionNumbers(
        offset_dims=(),
        collapsed_slice_dims=(1,),
        start_index_map=(1,),
        operand_batching_dims=(0,),
        start_indices_batching_dims=(0,),
    )
    return lax.gather(
        table,
        index[..., None],
        numbers,
        slice_sizes=(1, 1),
        mode=lax.GatherScatterMode.PROMISE_IN_BOUNDS,
    )


def sort_network(regs, place, levels):
    sub = lax.broadcasted_iota(jnp.int32, (ROWS, LANES), 0)
    lane = lax.broadcasted_iota(jnp.int32, (ROWS, LANES), 1)
    count = len(regs)

    def bit_fill(bit, v):
        if bit >= levels:
            return 0
        kind, k = place[bit]
        if kind == "v":
            return -((v >> k) & 1)
        return -(((sub if kind == "s" else lane) >> k) & 1)

    flip = [0] * count
    for level in range(1, levels + 1):
        fills = {}
        for v in range(count):
            kind, k = place[level] if level < levels else ("v", 99)
            key = (v >> k) & 1 if kind == "v" else 0
            if key not in fills:
                fills[key] = bit_fill(level, v)
            new = fills[key]
            if isinstance(new, int) and isinstance(flip[v], int):
                if new != flip[v]:
                    regs[v] = ~regs[v]
            else:
                regs[v] = regs[v] ^ (new ^ flip[v])
            flip[v] = new
        for bit in reversed(range(level)):
            kind, k = place[bit]
            step = 1 << k
            if kind == "v":
                for v in range(count):
                    if not v & step:
                        a, b = regs[v], regs[v | step]
                        regs[v], regs[v | step] = jnp.minimum(a, b), jnp.maximum(a, b)
            else:
                axis, size, where = (0, ROWS, sub) if kind == "s" else (1, LANES, lane)
                lower = (where & step) == 0
                for v in range(count):
                    x = regs[v]
                    ahead = pltpu.roll(x, size - step, axis)
                    behind = ahead if 2 * step == size else pltpu.roll(x, step, axis)
                    regs[v] = jnp.where(lower, jnp.minimum(x, ahead), jnp.maximum(x, behind))
    return regs


def split_two(x):
    high = x.astype(jnp.bfloat16).astype(jnp.float32)
    return high, x - high


def split_three(x):
    high, rest = split_two(x)
    mid, low = split_two(rest)
    return high, mid, low


def packed_row(ref, row):
    return jnp.broadcast_to(ref[row : row + 1, :], (16, LANES)).astype(jnp.bfloat16)


def one_hot_rows(low, iota):
    one = jnp.ones((16, LANES), jnp.bfloat16)
    zero = jnp.zeros((16, LANES), jnp.bfloat16)
    return jnp.concatenate(
        [jnp.where(low == iota[k : k + 16, :], one, zero) for k in range(0, iota.shape[0], 16)],
        axis=0,
    )


def spread_rows(rel, parts, iota):
    hit = rel == iota[0:16, :]
    zero = jnp.zeros((16, LANES), jnp.bfloat16)
    return jnp.concatenate([jnp.where(hit, p, zero) for part in parts for p in part], axis=0)


def block_product(rows, hots):
    zero = jnp.zeros
    lines = [
        jnp.concatenate(
            [x if m == n else zero(x.shape, x.dtype) for m in range(len(rows))], axis=1
        )
        for n, x in enumerate(rows)
    ]
    return lax.dot_general(
        jnp.concatenate(lines, axis=0),
        jnp.concatenate(hots, axis=1),
        NT,
        preferred_element_type=jnp.float32,
    )


def spread_add(rows, hots):
    out = lax.dot_general(
        jnp.concatenate(rows, axis=1) if len(rows) > 1 else rows[0],
        jnp.concatenate(hots, axis=1) if len(hots) > 1 else hots[0],
        NT,
        preferred_element_type=jnp.float32,
    )
    total = out[0:48]
    for s in range(48, out.shape[0], 48):
        total = total + out[s : s + 48]
    return total


def fill_iota(iota):
    rows = lax.broadcasted_iota(jnp.int32, iota.shape, 0)
    iota[...] = rows.astype(jnp.float32).astype(jnp.bfloat16)


def rows_of(block):
    start = block * 16
    return pl.ds(start if isinstance(block, int) else pl.multiple_of(start, 16), 16)


def wide(ref, *at):
    return jnp.broadcast_to(ref[at[:-1] + (slice(at[-1], at[-1] + 1),)], (ROWS, LANES))


def window(table, first, count, row, low, found):
    rel = row - first
    for u in range(count):
        found = jnp.where(rel == u, lane_gather(table[first + u], low), found)
    return found


def running_max(x, count):
    x = jnp.broadcast_to(x, (ROWS, LANES))
    step = 1
    while step < count:
        x = jnp.maximum(x, pltpu.roll(x, LANES - step, 1))
        step *= 2
    return x


def by_partner(axis, first, last):
    even = (lax.axis_index(axis) & 1) == 0
    return jnp.where(even, last, first), jnp.where(even, first, last)


def from_partners(axis, one, other, wrap=False):
    at, count = lax.axis_index(axis), lax.axis_size(axis)
    even = (at & 1) == 0
    before, after = jnp.where(even, other, one), jnp.where(even, one, other)
    if wrap:
        return before, after
    return jnp.where(at > 0, before, 0.0), jnp.where(at < count - 1, after, 0.0)


PLACE_STEP = 0.1 / 65535.0
RADIUS_LEAST = 0.01
RADIUS_STEP = 0.04 / 65535.0
SLIP_HALF = 1 << 20


def largest_slip(table, rows):
    most = jnp.zeros((ROWS, LANES), jnp.float32)
    for n in range(0, rows, ROWS):
        for c in range(3):
            most = jnp.maximum(most, jnp.abs(table[n : n + ROWS, 3 + c, :]))
    most = jnp.max(jnp.max(most, axis=0, keepdims=True), axis=1, keepdims=True)
    return jnp.broadcast_to(jnp.maximum(most, 1e-30), (ROWS, LANES))


def code_rows(table, n, largest, words):
    rows = pl.ds(n * ROWS, ROWS)

    def whole(c, least, step):
        x = ((table[rows, c, :] - least) * (1.0 / step) + 0.5).astype(jnp.int32)
        return jnp.clip(x, 0, 65535)

    x, y, z = (whole(c, 0.0, PLACE_STEP) for c in range(3))
    radius = whole(6, RADIUS_LEAST, RADIUS_STEP)
    scale = (SLIP_HALF - 1.0) / largest
    u, v, w = (
        (table[rows, 3 + c, :] * scale + (SLIP_HALF + 0.5)).astype(jnp.int32) for c in range(3)
    )
    coded = (
        x | (y << 16),
        z | (radius << 16),
        u | ((w & 2047) << 21),
        v | (lax.shift_right_logical(w, 11) << 21),
    )
    for k, word in enumerate(coded):
        words[pl.ds(n * 32 + k, ROWS, stride=4), :] = word


def decoded(words, largest):
    low = [x & 65535 for x in words[0:2]]
    high = [lax.shift_right_logical(x, 16) for x in words[0:2]]
    place = (low[0], high[0], low[1])
    radius = high[1].astype(jnp.float32) * RADIUS_STEP + RADIUS_LEAST
    mask = 2 * SLIP_HALF - 1
    third = lax.shift_right_logical(words[2], 21) | (lax.shift_right_logical(words[3], 21) << 11)
    scale = largest * (1.0 / (SLIP_HALF - 1.0))
    slip = [
        (x - SLIP_HALF).astype(jnp.float32) * scale for x in (words[2] & mask, words[3] & mask, third)
    ]
    return place, radius, slip


def fill_gas_rows(gas_ref, gas_rows):
    for r in range(16):
        rows = slice(r * ROWS, (r + 1) * ROWS)
        for c in range(3):
            for half in range(2):
                gas_rows[rows, half * 4 + c, :] = gas_ref[c, rows, half * LANES : (half + 1) * LANES]


def gas_index(block, keys_ref, slot):
    idx = slot[0]
    keys = keys_ref[rows_of(block), :]
    idx[0] = lax.shift_right_logical(keys, 19)
    idx[1] = lax.shift_right_logical(keys, 11) & (LANES - 1)


def gas_gather(block, g, ends, gas_rows, slot):
    idx, found = slot[0], slot[1]
    zero = jnp.zeros((ROWS, LANES), jnp.float32)
    first = ends[0, block * 16 + g]
    found[g] = window(gas_rows, first, GAS_WINDOW, wide(idx, 0, g), wide(idx, 1, g), zero)


def gas_rest(block, ends, gas_rows, slot):
    idx, found = slot[0], slot[1]

    @pl.when(ends[2, block * 16] >= GAS_WINDOW)
    def _():
        def one(g, carry):
            first = ends[0, block * 16 + g]
            row = jnp.broadcast_to(idx[0, pl.ds(g, 1), :], (ROWS, LANES))
            low = jnp.broadcast_to(idx[1, pl.ds(g, 1), :], (ROWS, LANES))

            def trip(t, total):
                base = jnp.minimum(first + GAS_WINDOW * t, LANES)
                return window(gas_rows, base, GAS_WINDOW, row, low, total)

            trips = (ends[1, block * 16 + g] - first) // GAS_WINDOW + 1
            found[g] = lax.fori_loop(1, trips, trip, found[g])
            return carry

        lax.fori_loop(0, 16, one, 0)


def seen_values(block, keys_ref, slot):
    idx, found, val = slot
    keys = keys_ref[rows_of(block), :]
    upper = (keys & (1 << 18)) != 0
    place_in = keys & (BLOCK - 1)
    val[0] = lax.shift_right_logical(place_in, 7).astype(jnp.float32)
    val[1] = (place_in & (LANES - 1)).astype(jnp.float32)
    for c in range(3):
        seen = jnp.where(upper, found[:, 4 + c, :], found[:, c, :])
        for n, part in enumerate(split_three(seen)):
            val[2 + 3 * c + n] = part


def seen_in_order(groups, slot, iota):
    val = slot[2]
    rows, hots = [], []
    for g in groups:
        parts = [[packed_row(val.at[2 + 3 * c + n], g) for c in range(3)] for n in range(3)]
        rows.append(spread_rows(packed_row(val.at[0], g), parts, iota))
        hots.append(one_hot_rows(packed_row(val.at[1], g), iota))
    return spread_add(rows, hots)


def write_states(block, total, pos_ref, vel_ref, diam_ref, out_ref, out_rows):
    rows = rows_of(block)
    for c in range(3):
        out_ref[out_rows, c, :] = pos_ref[c, rows, :]
        out_ref[out_rows, 3 + c, :] = total[16 * c : 16 * c + 16] - vel_ref[c, rows, :]
    out_ref[out_rows, 6, :] = 0.5 * diam_ref[rows, :]
    out_ref[out_rows, 7, :] = jnp.zeros((16, LANES), jnp.float32)


def states_step(gather, scatter, keys_ref, ends, gas_rows, iota, arrays):
    total = jnp.zeros((48, LANES), jnp.float32)
    if gather:
        gas_index(gather[0], keys_ref, gather[1])
    if scatter:
        seen_values(scatter[0], keys_ref, scatter[1])
    for g in range(16):
        if gather:
            gas_gather(gather[0], g, ends, gas_rows, gather[1])
        if scatter and g % 2:
            total = total + seen_in_order((g - 1, g), scatter[1], iota)
    if scatter:
        write_states(scatter[0], total, *arrays, *scatter[2:])
    if gather:
        gas_rest(gather[0], ends, gas_rows, gather[1])


def states_kernel(
    cell_hbm, gas_hbm, pos_hbm, vel_hbm, diam_hbm,
    keys_ref, ends_ref, table_ref, words_ref, largest_ref, one_ref, other_ref,
    cell_ref, gas_ref, pos_ref, vel_ref, diam_ref,
    gas_rows, iota, ends, idx_a, found_a, val_a, idx_b, found_b, val_b, sems,
):
    sources = (cell_hbm, gas_hbm, pos_hbm, vel_hbm, diam_hbm)
    places = (cell_ref, gas_ref, pos_ref, vel_ref, diam_ref)
    copies = [
        pltpu.make_async_copy(x, y, sems.at[n]) for n, (x, y) in enumerate(zip(sources, places))
    ]
    for copy in copies:
        copy.start()
    copies[0].wait()
    sub = lax.broadcasted_iota(jnp.int32, (ROWS, LANES), 0)
    lane = lax.broadcasted_iota(jnp.int32, (ROWS, LANES), 1)
    cells = cell_ref[...].T
    regs = []
    for v in range(16):
        own = (lane & 15) * LANES + v * ROWS + sub
        regs.append(cells[v * ROWS : (v + 1) * ROWS] * BLOCK + own)
    place = [("v", k) for k in range(4)] + [("s", k) for k in range(3)] + [("l", k) for k in range(4)]
    regs = sort_network(regs, place, 11)
    keys_ref[...] = jnp.concatenate(regs, axis=0).T
    least = functools.reduce(jnp.minimum, regs)
    most = functools.reduce(jnp.maximum, regs)
    least = lax.shift_right_logical(jnp.min(least, axis=0, keepdims=True), 19)
    most = lax.shift_right_logical(jnp.max(most, axis=0, keepdims=True), 19)
    ends_ref[0:1, :] = least
    ends_ref[1:2, :] = most
    ends_ref[2:8, :] = running_max(most - least, 16)[0:6]
    copy = pltpu.make_async_copy(ends_ref, ends, sems.at[5])
    copy.start()
    copies[1].wait()
    fill_gas_rows(gas_ref, gas_rows)
    for other in copies[2:]:
        other.wait()
    copy.wait()
    fill_iota(iota)
    a, b = (idx_a, found_a, val_a), (idx_b, found_b, val_b)
    step = functools.partial(
        states_step, keys_ref=keys_ref, ends=ends, gas_rows=gas_rows, iota=iota,
        arrays=(pos_ref, vel_ref, diam_ref),
    )
    step((0, a), None)

    def two(k, carry):
        block = 2 * k
        step((block + 1, b), (block, a, table_ref, rows_of(block)))
        step((block + 2, a), (block + 1, b, table_ref, rows_of(block + 1)))
        return carry

    lax.fori_loop(0, 3, two, 0)
    step((7, b), (6, a, table_ref, rows_of(6)))
    step(None, (7, b, table_ref, rows_of(7)))
    largest = largest_slip(table_ref, 128)
    largest_ref[...] = largest
    for n in range(16):
        code_rows(table_ref, n, largest, words_ref)
    words_ref[512:576, :] = jnp.zeros((64, LANES), jnp.int32)
    one_ref[...], other_ref[...] = by_partner("az", table_ref[0:16], table_ref[112:128])


def slots(rows, parts, dtype=jnp.float32):
    one = [VMEM((2, 16, LANES), jnp.int32), VMEM((16, ROWS, LANES), dtype), VMEM((parts, rows, LANES), dtype)]
    return one + one


def droplet_states(cells, gas, pos, vel, diam):
    f32, i32 = jnp.float32, jnp.int32
    arrays = (cells, gas, pos, vel, diam)
    return pl.pallas_call(
        states_kernel,
        name="droplet_states",
        out_shape=(
            jax.ShapeDtypeStruct((128, LANES), i32),
            jax.ShapeDtypeStruct((ROWS, LANES), i32),
            jax.ShapeDtypeStruct((128, ROWS, LANES), f32),
            jax.ShapeDtypeStruct((576, LANES), i32),
            jax.ShapeDtypeStruct((ROWS, LANES), f32),
            jax.ShapeDtypeStruct((16, ROWS, LANES), f32),
            jax.ShapeDtypeStruct((16, ROWS, LANES), f32),
        ),
        in_specs=[pl.BlockSpec(memory_space=pltpu.HBM)] * 5,
        scratch_shapes=[VMEM(x.shape, x.dtype) for x in arrays]
        + [VMEM((144, ROWS, LANES), f32), VMEM((LANES, LANES), jnp.bfloat16), SMEM((ROWS, LANES), i32)]
        + slots(16, 11)
        + [pltpu.SemaphoreType.DMA((6,))],
        compiler_params=params(),
    )(*[pltpu.with_memory_space_constraint(x, pltpu.HBM) for x in arrays])


def pair_sort_kernel(live_ref, pairs_ref, keys_ref, ends_ref):
    live = live_ref[0, 0]
    sub = lax.broadcasted_iota(jnp.int32, (ROWS, LANES), 0)
    lane = lax.broadcasted_iota(jnp.int32, (ROWS, LANES), 1)
    regs = []
    for v in range(32):
        rows = slice(v * ROWS, (v + 1) * ROWS)
        slot = v * 1024 + sub * LANES + lane
        head = pairs_ref[0, rows, :]
        tail = pairs_ref[1, rows, :] - 7 * BLOCK
        own = tail - BLOCK
        inside = (own >= 0) & (own < 8 * BLOCK)
        tail = jnp.where(inside, jnp.maximum(own, head) + BLOCK, tail)
        head = jnp.where(inside, jnp.minimum(own, head), head)
        bucket = lax.shift_right_logical(tail, 10)
        bucket = jnp.where(inside, bucket + 2, jnp.where(bucket >= 18, bucket - 16, bucket))
        turn = -(bucket & 1) & (8 * BLOCK - 1)
        key = (bucket << 24) | ((head ^ turn) << 10) | (tail & (BUCKET - 1))
        regs.append(jnp.where(slot < live, key, DEAD))
    place = (
        [("v", k) for k in range(4)]
        + [("s", k) for k in range(3)]
        + [("v", 4)]
        + [("l", k) for k in range(7)]
    )
    regs = sort_network(regs, place, 15)
    beyond = jnp.zeros((ROWS, LANES), jnp.float32)
    for key in regs:
        beyond = beyond + jnp.where(key < NEAR_BUCKETS << 24, 1.0, 0.0)
    beyond = jnp.sum(jnp.sum(beyond, axis=0, keepdims=True), axis=1, keepdims=True)
    ends_ref[8:16, :] = jnp.broadcast_to(beyond, (ROWS, LANES)).astype(jnp.int32)
    for half in range(2):
        rows = regs[16 * half : 16 * half + 16]
        keys_ref[half] = jnp.concatenate(rows, axis=0).T
        least_head = least_tail = jnp.full((ROWS, LANES), 1 << 20, jnp.int32)
        most_head = most_tail = jnp.full((ROWS, LANES), -1, jnp.int32)
        for key in rows:
            used = key < DEAD
            bucket = lax.shift_right_logical(key, 24)
            head = lax.shift_right_logical(key, 17) & (LANES - 1)
            head = head ^ (-(bucket & 1) & (LANES - 1))
            least_head = jnp.minimum(least_head, jnp.where(used, head, 1 << 20))
            most_head = jnp.maximum(most_head, jnp.where(used, head, -1))
            least_tail = jnp.minimum(least_tail, jnp.where(used, bucket, 1 << 20))
            most_tail = jnp.maximum(most_tail, jnp.where(used, bucket, -1))
        for n, x in enumerate((least_head, most_head, least_tail, most_tail)):
            reduce = jnp.max if n % 2 else jnp.min
            row = 4 * half + n
            bound = (LANES, LANES, BUCKETS, BUCKETS)[n]
            ends_ref[row : row + 1, :] = jnp.minimum(reduce(x, axis=0, keepdims=True), bound)


def pair_sort(live, pairs):
    return pl.pallas_call(
        pair_sort_kernel,
        name="pair_sort",
        out_shape=(
            jax.ShapeDtypeStruct((2, LANES, LANES), jnp.int32),
            jax.ShapeDtypeStruct((16, LANES), jnp.int32),
        ),
        in_specs=[pl.BlockSpec(memory_space=SMEM), pl.BlockSpec(memory_space=VMEM)],
        compiler_params=params(),
    )(live, pairs)


def group_ends(g, ends, part):
    g = jnp.minimum(g, 2 * LANES - 1)
    at, lane = 4 * (g & 1), g >> 1
    low, high, _ = part
    return (
        ends[at, lane] & -2,
        ends[at + 1, lane],
        jnp.maximum(ends[at + 2, lane], low),
        jnp.minimum(ends[at + 3, lane], high - 1),
    )


def take_items(state, groups, ends, part):
    low, high, heads = part
    items = []
    for _ in range(ROWS):
        g, bucket, head, now, later = state
        place = jnp.minimum(bucket, high) - low
        items.append((jnp.minimum(g, 2 * LANES - 1), jnp.where(g < groups, bucket, -1), head, place))
        ahead = group_ends(g + 2, ends, part)
        more_heads = head + heads <= now[1]
        stay = more_heads | (bucket < now[3])
        head = jnp.where(more_heads, head + heads, jnp.where(stay, now[0], later[0]))
        bucket = jnp.where(more_heads, bucket, jnp.where(stay, bucket + 1, later[2]))
        now = tuple(jnp.where(stay, x, y) for x, y in zip(now, later))
        later = tuple(jnp.where(stay, x, y) for x, y in zip(later, ahead))
        state = (jnp.where(stay, g, g + 1), bucket, head, now, later)
    return items, state


def word_window(words, first, count, pair, low):
    found = jnp.zeros((ROWS, LANES), jnp.int32)
    for u in range(count):
        rows = words[pl.ds(pl.multiple_of((first + u) * ROWS, ROWS), ROWS), :]
        found = jnp.where(pair == u, lane_gather(rows, low), found)
    return found


def pair_gather(k, item, keys_ref, near_words, far_words, heads, slot):
    key_rows, rel_rows, near, far = slot
    g, bucket, first, part = item
    keys = jnp.broadcast_to(keys_ref[g & 1, pl.ds(g >> 1, 1), :], (ROWS, LANES))
    of_bucket = lax.shift_right_logical(keys, 24)
    turn = -(of_bucket & 1) & (8 * BLOCK - 1)
    head = (lax.shift_right_logical(keys, 10) & (8 * BLOCK - 1)) ^ turn
    rel = lax.shift_right_logical(head, 7) - first
    used = (of_bucket == bucket) & (rel >= 0) & (rel < heads)
    key_rows[k : k + 1, :] = jnp.where(used, keys, DEAD)[0:1]
    rel_rows[k : k + 1, :] = rel[0:1]
    near[k] = word_window(near_words, first >> 1, heads // 2, rel >> 1, head & (LANES - 1))
    pair = lax.shift_right_logical(keys, 8) & 3
    far[k] = word_window(far_words, part * 4, 4, pair, keys & (LANES - 1))


def pair_values(slot, val, near_largest, far_largest):
    key_rows, rel_rows, near, far = slot
    keys, rel = key_rows[...], rel_rows[...]
    used = keys < DEAD
    turn = -(lax.shift_right_logical(keys, 24) & 1) & (LANES - 1)
    val[0] = rel.astype(jnp.float32)
    val[1] = ((lax.shift_right_logical(keys, 10) & (LANES - 1)) ^ turn).astype(jnp.float32)
    val[2] = (lax.shift_right_logical(keys, 7) & 7).astype(jnp.float32)
    val[3] = (keys & (LANES - 1)).astype(jnp.float32)

    def words(ref, odd):
        return [jnp.where(odd, ref[:, 4 + w, :], ref[:, w, :]) for w in range(4)]

    near_place, near_radius, near_slip = decoded(words(near, (rel & 1) == 1), near_largest)
    far_place, far_radius, far_slip = decoded(words(far, (keys & LANES) != 0), far_largest)
    gap = jnp.zeros((ROWS, LANES), jnp.float32)
    for x, y in zip(far_place, near_place):
        apart = (x - y).astype(jnp.float32)
        gap = gap + apart * apart
    gap = gap * (PLACE_STEP * PLACE_STEP)
    far_ratio = far_radius * lax.rsqrt(gap + far_radius * far_radius)
    near_ratio = near_radius * lax.rsqrt(gap + near_radius * near_radius)
    weight_far = jnp.where(used, piep_coef * far_ratio * far_ratio * far_ratio, 0.0)
    weight_near = jnp.where(used, piep_coef * near_ratio * near_ratio * near_ratio, 0.0)
    for c in range(3):
        for n, part in enumerate(split_two(weight_far * far_slip[c])):
            val[4 + 3 * n + c] = part
        for n, part in enumerate(split_two(weight_near * near_slip[c])):
            val[10 + 3 * n + c] = part


def pair_scatter(k, item, val, head_sum, tail_sum, iota, iota8):
    first, tail_first = item
    parts = [[packed_row(val.at[4 + 3 * n + c], k) for c in range(3)] for n in range(2)]
    heads = spread_rows(packed_row(val.at[0], k), parts, iota)
    hit = packed_row(val.at[2], k) == iota8[...]
    zero = jnp.zeros((16, LANES), jnp.bfloat16)
    tails = []
    for n in range(10, 16, 2):
        both = jnp.concatenate([wide(val, n, k), wide(val, n + 1, k)], axis=0)
        tails.append(jnp.where(hit, both.astype(jnp.bfloat16), zero))
    tails = jnp.concatenate(tails, axis=0)
    out = block_product(
        [heads, tails], [one_hot_rows(packed_row(val.at[n], k), iota) for n in (1, 3)]
    )
    for c in range(3):
        head_sum[c, pl.ds(first, 16), :] += out[16 * c : 16 * c + 16] + out[16 * c + 48 : 16 * c + 64]
    at = pl.ds(pl.multiple_of(tail_first, 8), 8)
    for c in range(3):
        tail_sum[c, at, :] += out[8 * c + 96 : 8 * c + 104] + out[8 * c + 120 : 8 * c + 128]


def run_pairs(groups, start, part, ends, keys_ref, near, far, sums, iota, iota8, scratch):
    fill_iota(iota)
    rows = lax.broadcasted_iota(jnp.int32, iota8.shape, 0) & 7
    iota8[...] = rows.astype(jnp.float32).astype(jnp.bfloat16)
    val, a, b = scratch[0], scratch[1:5], scratch[5:9]

    def step(state, slot, pending):
        items, state = take_items(state, groups, ends, part)
        if pending:
            pair_values(a, val, near[1], far[1])
        for k in range(ROWS):
            pair_gather(k, items[k], keys_ref, near[0], far[0], part[2], slot)
            if pending:
                pair_scatter(k, pending[k], val, *sums, iota, iota8)
        return tuple((item[2], item[3] * 8) for item in items), state, items[0][1] >= 0

    now, later = group_ends(start, ends, part), group_ends(start + 1, ends, part)
    state = (start, now[2], now[0], now, later)

    def one(carry):
        pending, state, _ = carry
        carry = step(state, b, pending)
        for x, y in zip(a, b):
            x[...] = y[...]
        return carry

    lax.while_loop(lambda carry: carry[2], one, step(state, a, None))


def near_pairs_kernel(
    ends, keys_ref, words_ref, largest_ref, one_in, other_in,
    heads_ref, one_ref, other_ref,
    shell, shell_words, head_sum, tail_sum, iota, iota8, *scratch,
):
    shell[0:16], shell[16:32] = from_partners("az", one_in[...], other_in[...], True)
    shell_largest = largest_slip(shell, 32)
    for n in range(4):
        code_rows(shell, n, shell_largest, shell_words)
    shell_words[128:160, :] = jnp.zeros((32, LANES), jnp.int32)
    head_sum[...] = jnp.zeros_like(head_sum)
    tail_sum[...] = jnp.zeros_like(tail_sum)
    groups = (ends[8, 0] + LANES - 1) // LANES
    run_pairs(
        groups, jnp.int32(0), (0, NEAR_BUCKETS, NEAR_HEADS), ends, keys_ref,
        (words_ref, largest_ref[...]), (shell_words, shell_largest),
        (head_sum, tail_sum), iota, iota8, scratch,
    )
    heads_ref[...] = head_sum[:, 0:128, :]
    one_ref[...], other_ref[...] = by_partner("az", tail_sum[:, 0:16, :], tail_sum[:, 16:32, :])


def own_pairs_kernel(
    live_ref, ends, keys_ref, words_ref, largest_ref, heads_ref,
    corr_ref,
    head_sum, tail_sum, iota, iota8, *scratch,
):
    head_sum[:, 0:128, :] = heads_ref[...]
    head_sum[:, 128:144, :] = jnp.zeros((3, 16, LANES), jnp.float32)
    tail_sum[...] = jnp.zeros_like(tail_sum)
    groups = (live_ref[0, 0] + LANES - 1) // LANES
    start = jnp.minimum(ends[8, 0] // LANES, 2 * LANES - 1)
    coded = (words_ref, largest_ref[...])
    run_pairs(
        groups, start, (NEAR_BUCKETS, BUCKETS, OWN_HEADS), ends, keys_ref, coded, coded,
        (head_sum, tail_sum), iota, iota8, scratch,
    )
    corr_ref[...] = head_sum[:, 0:128, :] + tail_sum[:, 0:128, :]


def pair_scratch(tail_rows):
    f32, i32 = jnp.float32, jnp.int32
    slot = [
        VMEM((ROWS, LANES), i32),
        VMEM((ROWS, LANES), i32),
        VMEM((ROWS, ROWS, LANES), i32),
        VMEM((ROWS, ROWS, LANES), i32),
    ]
    return [
        VMEM((3, 144, LANES), f32),
        VMEM((3, tail_rows, LANES), f32),
        VMEM((LANES, LANES), jnp.bfloat16),
        VMEM((16, LANES), jnp.bfloat16),
        VMEM((16, ROWS, LANES), f32),
        *slot,
        *slot,
    ]


def near_pairs(ends, keys, words, largest, one, other):
    f32 = jnp.float32
    smem, vmem = pl.BlockSpec(memory_space=SMEM), pl.BlockSpec(memory_space=VMEM)
    return pl.pallas_call(
        near_pairs_kernel,
        name="near_pairs",
        out_shape=(
            jax.ShapeDtypeStruct((3, 128, LANES), f32),
            jax.ShapeDtypeStruct((3, 16, LANES), f32),
            jax.ShapeDtypeStruct((3, 16, LANES), f32),
        ),
        in_specs=[smem, vmem, vmem, vmem, vmem, vmem],
        scratch_shapes=[VMEM((32, ROWS, LANES), f32), VMEM((160, LANES), jnp.int32)]
        + pair_scratch(40),
        compiler_params=params(),
    )(ends, keys, words, largest, one, other)


def own_pairs(live, ends, keys, words, largest, heads):
    smem, vmem = pl.BlockSpec(memory_space=SMEM), pl.BlockSpec(memory_space=VMEM)
    return pl.pallas_call(
        own_pairs_kernel,
        name="own_pairs",
        out_shape=jax.ShapeDtypeStruct((3, 128, LANES), jnp.float32),
        in_specs=[smem, smem, vmem, vmem, vmem, vmem],
        scratch_shapes=pair_scratch(136),
        compiler_params=params(),
    )(live, ends, keys, words, largest, heads)


def force_gather(block, keys_ref, table_ref, total_ref, slot):
    force, got, val = slot
    rows = rows_of(block)
    scale = (-2.0 * drag_coef) * table_ref[rows, 6, :]
    for c in range(3):
        push = scale * (table_ref[rows, 3 + c, :] + total_ref[c, rows, :])
        force[:, c, :] = push[0:8]
        force[:, 4 + c, :] = push[8:16]
    keys = keys_ref[rows, :]
    val[0] = lax.shift_right_logical(keys, 19).astype(jnp.float32)
    val[1] = (lax.shift_right_logical(keys, 11) & (2 * LANES - 1)).astype(jnp.float32)
    inner = lax.shift_right_logical(keys, 7) & 7
    low = keys & (LANES - 1)
    tables = [force[k] for k in range(ROWS)]
    for g in range(16):
        pick = jnp.broadcast_to(inner[g : g + 1, :], (ROWS, LANES))
        at = jnp.broadcast_to(low[g : g + 1, :], (ROWS, LANES))
        found = jnp.zeros((ROWS, LANES), jnp.float32)
        for k in range(ROWS):
            found = jnp.where(pick == k, lane_gather(tables[k], at), found)
        got[g] = found
    upper = (keys & 1024) != 0
    for c in range(3):
        pushed = jnp.where(upper, got[:, 4 + c, :], got[:, c, :])
        for n, part in enumerate(split_two(pushed)):
            val[2 + 2 * c + n] = part


def force_rows(g, base, slot, iota):
    val = slot[2]

    def row(n):
        if isinstance(g, int):
            return packed_row(val.at[n], g)
        return jnp.broadcast_to(val[n, pl.ds(g, 1), :], (16, LANES)).astype(jnp.bfloat16)

    rel = row(0) - base.astype(jnp.float32).astype(jnp.bfloat16)
    parts = [[row(2 + 2 * c + n) for c in range(3)] for n in range(2)]
    return spread_rows(rel, parts, iota), one_hot_rows(row(1), iota)


def force_add(groups, bases, slot, cells, iota):
    pieces = [force_rows(g, base, slot, iota) for g, base in zip(groups, bases)]
    out = block_product([p[0] for p in pieces], [p[1] for p in pieces])
    for n, base in enumerate(bases):
        for c in range(3):
            at = 96 * n + 16 * c
            total = out[at : at + 16] + out[at + 48 : at + 64]
            for half in range(2):
                part = total[:, half * LANES : (half + 1) * LANES]
                cells[2 * c + half, pl.ds(base, 16), :] += part


def force_rest(block, ends, slot, cells, iota):
    @pl.when(ends[2, block * 16] >= 16)
    def _():
        def one(g, carry):
            first, most = ends[0, block * 16 + g], ends[1, block * 16 + g]

            def trip(t, carry):
                force_add([g], [jnp.minimum(first + 16 * t, LANES)], slot, cells, iota)
                return carry

            lax.fori_loop(1, (most - first) // 16 + 1, trip, 0)
            return carry

        lax.fori_loop(0, 16, one, 0)


def deposit_step(gather, scatter, ends, keys_ref, table_ref, total_ref, cells, iota):
    if gather:
        force_gather(gather[0], keys_ref, table_ref, total_ref, gather[1])
    if scatter:
        for g in range(16):
            force_add([g], [ends[0, scatter[0] * 16 + g]], scatter[1], cells, iota)
        force_rest(scatter[0], ends, scatter[1], cells, iota)


def deposit_kernel(
    ends, keys_ref, table_ref, corr_ref, one_in, other_in,
    out_ref, total_ref, one_ref, other_ref,
    cells, iota, force_a, got_a, val_a, force_b, got_b, val_b,
):
    fill_iota(iota)
    cells[...] = jnp.zeros_like(cells)
    total_ref[...] = corr_ref[...]
    before, after = from_partners("az", one_in[...], other_in[...], True)
    total_ref[:, 0:16, :] += before
    total_ref[:, 112:128, :] += after
    a, b = (force_a, got_a, val_a), (force_b, got_b, val_b)
    step = functools.partial(
        deposit_step, ends=ends, keys_ref=keys_ref, table_ref=table_ref, total_ref=total_ref,
        cells=cells, iota=iota,
    )
    step((0, a), None)

    def two(k, carry):
        block = 2 * k
        step((block + 1, b), (block, a))
        step((block + 2, a), (block + 1, b))
        return carry

    lax.fori_loop(0, 3, two, 0)
    step((7, b), (6, a))
    step(None, (7, b))
    for c in range(3):
        for half in range(2):
            columns = slice(half * LANES, (half + 1) * LANES)
            out_ref[c, :, columns] = cells[2 * c + half, 0:128, :]
            one, other = by_partner(
                "ax", cells[2 * c + half, 0:32, :], cells[2 * c + half, 96:128, :]
            )
            one_ref[c, :, columns] = one
            other_ref[c, :, columns] = other


def deposits(ends, keys, table, corr, one, other):
    f32 = jnp.float32
    smem, vmem = pl.BlockSpec(memory_space=SMEM), pl.BlockSpec(memory_space=VMEM)
    slot = [VMEM((ROWS, ROWS, LANES), f32), VMEM((16, ROWS, LANES), f32), VMEM((8, 16, LANES), f32)]
    return pl.pallas_call(
        deposit_kernel,
        name="deposits",
        out_shape=(
            jax.ShapeDtypeStruct((3, 128, 2 * LANES), f32),
            jax.ShapeDtypeStruct((3, 128, LANES), f32),
            jax.ShapeDtypeStruct((3, 32, 2 * LANES), f32),
            jax.ShapeDtypeStruct((3, 32, 2 * LANES), f32),
        ),
        in_specs=[smem] + [vmem] * 5,
        scratch_shapes=[VMEM((6, 144, LANES), f32), VMEM((2 * LANES, LANES), jnp.bfloat16)]
        + slot
        + slot,
        compiler_params=params(),
    )(ends, keys, table, corr, one, other)


def axial_kernel(taps, cells_ref, one_in, other_in, out_ref, one_ref, other_ref, first_ref, last_ref):
    for c in range(3):
        before, after = from_partners("ax", one_in[c], other_in[c])
        padded = jnp.concatenate([before, cells_ref[c], after], axis=0)
        total = taps[0] * padded[0:128]
        for k in range(1, 5):
            total = total + taps[k] * padded[16 * k : 16 * k + 128]
        out_ref[c] = total
        for a in range(8):
            first_ref[2 * a : 2 * a + 2, :] = total[16 * a : 16 * a + 2]
            last_ref[2 * a : 2 * a + 2, :] = total[16 * a + 14 : 16 * a + 16]
        one_ref[c], other_ref[c] = by_partner("rad", first_ref[...], last_ref[...])


def radial_kernel(
    taps, cells_ref, one_in, other_in, out_ref, one_ref, other_ref, padded, before_ref, after_ref
):
    lane = lax.broadcasted_iota(jnp.int32, (LANES, LANES), 1)
    edges = jnp.zeros((LANES, LANES), jnp.float32)
    for c in range(3):
        before_ref[...], after_ref[...] = from_partners("rad", one_in[c], other_in[c])
        for a in range(8):
            padded[0:2, :] = before_ref[2 * a : 2 * a + 2, :]
            padded[2:18, :] = cells_ref[c, 16 * a : 16 * a + 16, :]
            padded[18:20, :] = after_ref[2 * a : 2 * a + 2, :]
            total = taps[0] * padded[0:16, :]
            for k in range(1, 5):
                total = total + taps[k] * padded[k : k + 16, :]
            out_ref[c, 16 * a : 16 * a + 16, :] = total
        left, right = out_ref[c, :, 0:LANES], out_ref[c, :, LANES:]
        if c:
            left = pltpu.roll(left, 2 * c, 1)
        right = pltpu.roll(right, 10 + 2 * c, 1)
        edges = jnp.where((lane >> 1) == c, left, edges)
        edges = jnp.where((lane >> 1) == 4 + c, right, edges)
    turned = edges.T
    one_ref[...], other_ref[...] = by_partner("az", turned[0:8], turned[8:16])


def inner_azimuthal_kernel(taps, cells_ref, out_ref):
    lane = lax.broadcasted_iota(jnp.int32, (LANES, LANES), 1)
    for c in range(3):
        left, right = cells_ref[c, :, 0:LANES], cells_ref[c, :, LANES:]
        out_left, out_right = taps[2] * left, taps[2] * right
        for k in (1, 2):
            tap = taps[2 + k]
            inner = lane < LANES - k
            x, y = (pltpu.roll(v, LANES - k, 1) for v in (left, right))
            out_left = out_left + tap * jnp.where(inner, x, y)
            out_right = out_right + tap * jnp.where(inner, y, 0.0)
            inner = lane >= k
            x, y = (pltpu.roll(v, k, 1) for v in (left, right))
            out_left = out_left + tap * jnp.where(inner, x, 0.0)
            out_right = out_right + tap * jnp.where(inner, y, x)
        out_ref[c, :, 0:LANES] = out_left
        out_ref[c, :, LANES:] = out_right


def azimuthal_kernel(taps, inner_ref, one_in, other_in, out_ref):
    lane = lax.broadcasted_iota(jnp.int32, (LANES, LANES), 1)
    rest = jnp.zeros((LANES - 16, LANES), jnp.float32)
    before, after = from_partners("az", one_in[...], other_in[...], True)
    edges = jnp.concatenate([after, before, rest], axis=0).T
    for c in range(3):
        out_left, out_right = inner_ref[c, :, 0:LANES], inner_ref[c, :, LANES:]
        for k in (1, 2):
            x = pltpu.roll(edges, (118 - 2 * c + k) % LANES, 1)
            out_left = out_left + taps[2 - k] * jnp.where(lane < k, x, 0.0)
            y = pltpu.roll(edges, LANES - 2 * c - k, 1)
            out_right = out_right + taps[2 + k] * jnp.where(lane >= LANES - k, y, 0.0)
        out_ref[c, :, 0:LANES] = out_left
        out_ref[c, :, LANES:] = out_right


def filtered(deposit, one, other):
    f32 = jnp.float32
    raw = [math.exp(-0.5 * k * k) for k in range(-2, 3)]
    taps = [x / sum(raw) for x in raw]
    whole = jax.ShapeDtypeStruct(deposit.shape, f32)
    radial_face = jax.ShapeDtypeStruct((3, 16, 2 * LANES), f32)
    edge = jax.ShapeDtypeStruct((8, LANES), f32)
    cells, one, other = pl.pallas_call(
        functools.partial(axial_kernel, taps),
        name="axial_filter",
        out_shape=(whole, radial_face, radial_face),
        scratch_shapes=[VMEM((16, 2 * LANES), f32)] * 2,
        compiler_params=params(),
    )(deposit, *swapped(one, other, "ax"))
    cells, one, other = pl.pallas_call(
        functools.partial(radial_kernel, taps),
        name="radial_filter",
        out_shape=(whole, edge, edge),
        scratch_shapes=[VMEM((24, 2 * LANES), f32)] + [VMEM((16, 2 * LANES), f32)] * 2,
        compiler_params=params(),
    )(cells, *swapped(one, other, "rad"))
    one, other = swapped(one, other, "az", True)
    inner = pl.pallas_call(
        functools.partial(inner_azimuthal_kernel, taps),
        name="inner_azimuthal_filter",
        out_shape=whole,
        compiler_params=params(),
    )(cells)
    return pl.pallas_call(
        functools.partial(azimuthal_kernel, taps),
        name="azimuthal_filter",
        out_shape=whole,
        compiler_params=params(),
    )(inner, one, other)


def swapped(one, other, axis, wrap=False):
    count = lax.axis_size(axis)

    def partner(i, odd):
        j = i + 1 if i % 2 == odd else i - 1
        return j % count if wrap or 0 <= j < count else i

    return [
        lax.ppermute(x, axis, [(i, partner(i, odd)) for i in range(count)])
        for odd, x in enumerate((one, other))
    ]


def per_device(positions, velocity, diameter, cell_index, pair_list, live_pairs, gas_velocity):
    live = live_pairs.reshape(1, 1)
    cells = cell_index.reshape(128, LANES)
    gas = gas_velocity.reshape(3, 128, 2 * LANES)
    pos = positions.reshape(3, 128, LANES)
    vel = velocity.reshape(3, 128, LANES)
    diam = diameter.reshape(128, LANES)
    cell_keys, cell_ends, table, words, largest, one, other = droplet_states(
        cells, gas, pos, vel, diam
    )
    one, other = swapped(one, other, "az", True)
    pair_keys, pair_ends = pair_sort(live, pair_list.reshape(2, 256, LANES))
    heads, one, other = near_pairs(pair_ends, pair_keys, words, largest, one, other)
    one, other = swapped(one, other, "az", True)
    corr = own_pairs(live, pair_ends, pair_keys, words, largest, heads)
    deposit, correction, one, other = deposits(cell_ends, cell_keys, table, corr, one, other)
    smoothed = filtered(deposit, one, other)
    return (correction.reshape(positions.shape), smoothed.reshape(gas_velocity.shape))


def solution(mesh):
    return jax.shard_map(
        per_device,
        mesh=mesh,
        in_specs=(
            P(None, "ax", "rad", "az"),
            P(None, "ax", "rad", "az"),
            P("ax", "rad", "az"),
            P("ax", "rad", "az"),
            P(None, "ax", "rad", "az"),
            P("ax", "rad", "az"),
            P(None, "ax", "rad", "az"),
        ),
        out_specs=(P(None, "ax", "rad", "az"), P(None, "ax", "rad", "az")),
        check_vma=False,
    )
```

```python
import functools
import math

import jax
import jax.numpy as jnp
from jax import lax
from jax.experimental import pallas as pl
from jax.experimental.pallas import tpu as pltpu
from jax.sharding import PartitionSpec as P

piep_coef = 1.0
drag_coef = 20.0

LANES = 128
ROWS = 8
BLOCK = 2048
GAS_WINDOW = 12
BUCKET = 1024
BUCKETS = 20
NEAR_BUCKETS = 4
NEAR_HEADS = 8
OWN_HEADS = 12
DEAD = 1 << 29

NT = (((1,), (1,)), ((), ()))
VMEM = pltpu.VMEM
SMEM = pltpu.SMEM


def params(megabytes=40):
    return pltpu.CompilerParams(vmem_limit_bytes=megabytes << 20)


def lane_gather(table, index):
    numbers = lax.GatherDimensionNumbers(
        offset_dims=(),
        collapsed_slice_dims=(1,),
        start_index_map=(1,),
        operand_batching_dims=(0,),
        start_indices_batching_dims=(0,),
    )
    return lax.gather(
        table,
        index[..., None],
        numbers,
        slice_sizes=(1, 1),
        mode=lax.GatherScatterMode.PROMISE_IN_BOUNDS,
    )


def sort_network(regs, place, levels):
    sub = lax.broadcasted_iota(jnp.int32, (ROWS, LANES), 0)
    lane = lax.broadcasted_iota(jnp.int32, (ROWS, LANES), 1)
    count = len(regs)

    def bit_fill(bit, v):
        if bit >= levels:
            return 0
        kind, k = place[bit]
        if kind == "v":
            return -((v >> k) & 1)
        return -(((sub if kind == "s" else lane) >> k) & 1)

    flip = [0] * count
    for level in range(1, levels + 1):
        fills = {}
        for v in range(count):
            kind, k = place[level] if level < levels else ("v", 99)
            key = (v >> k) & 1 if kind == "v" else 0
            if key not in fills:
                fills[key] = bit_fill(level, v)
            new = fills[key]
            if isinstance(new, int) and isinstance(flip[v], int):
                if new != flip[v]:
                    regs[v] = ~regs[v]
            else:
                regs[v] = regs[v] ^ (new ^ flip[v])
            flip[v] = new
        for bit in reversed(range(level)):
            kind, k = place[bit]
            step = 1 << k
            if kind == "v":
                for v in range(count):
                    if not v & step:
                        a, b = regs[v], regs[v | step]
                        regs[v], regs[v | step] = jnp.minimum(a, b), jnp.maximum(a, b)
            else:
                axis, size, where = (0, ROWS, sub) if kind == "s" else (1, LANES, lane)
                lower = (where & step) == 0
                for v in range(count):
                    x = regs[v]
                    ahead = pltpu.roll(x, size - step, axis)
                    behind = ahead if 2 * step == size else pltpu.roll(x, step, axis)
                    regs[v] = jnp.where(lower, jnp.minimum(x, ahead), jnp.maximum(x, behind))
    return regs


def split_two(x):
    high = x.astype(jnp.bfloat16).astype(jnp.float32)
    return high, x - high


def split_three(x):
    high, rest = split_two(x)
    mid, low = split_two(rest)
    return high, mid, low


def packed_row(ref, row):
    return jnp.broadcast_to(ref[row : row + 1, :], (16, LANES)).astype(jnp.bfloat16)


def one_hot_rows(low, iota):
    one = jnp.ones((16, LANES), jnp.bfloat16)
    zero = jnp.zeros((16, LANES), jnp.bfloat16)
    return jnp.concatenate(
        [jnp.where(low == iota[k : k + 16, :], one, zero) for k in range(0, iota.shape[0], 16)],
        axis=0,
    )


def spread_rows(rel, parts, iota):
    hit = rel == iota[0:16, :]
    zero = jnp.zeros((16, LANES), jnp.bfloat16)
    return jnp.concatenate([jnp.where(hit, p, zero) for part in parts for p in part], axis=0)


def block_product(rows, hots):
    zero = jnp.zeros
    lines = [
        jnp.concatenate(
            [x if m == n else zero(x.shape, x.dtype) for m in range(len(rows))], axis=1
        )
        for n, x in enumerate(rows)
    ]
    return lax.dot_general(
        jnp.concatenate(lines, axis=0),
        jnp.concatenate(hots, axis=1),
        NT,
        preferred_element_type=jnp.float32,
    )


def spread_add(rows, hots):
    out = lax.dot_general(
        jnp.concatenate(rows, axis=1) if len(rows) > 1 else rows[0],
        jnp.concatenate(hots, axis=1) if len(hots) > 1 else hots[0],
        NT,
        preferred_element_type=jnp.float32,
    )
    total = out[0:48]
    for s in range(48, out.shape[0], 48):
        total = total + out[s : s + 48]
    return total


def fill_iota(iota):
    rows = lax.broadcasted_iota(jnp.int32, iota.shape, 0)
    iota[...] = rows.astype(jnp.float32).astype(jnp.bfloat16)


def rows_of(block):
    start = block * 16
    return pl.ds(start if isinstance(block, int) else pl.multiple_of(start, 16), 16)


def wide(ref, *at):
    return jnp.broadcast_to(ref[at[:-1] + (slice(at[-1], at[-1] + 1),)], (ROWS, LANES))


def window(table, first, count, row, low, found):
    rel = row - first
    for u in range(count):
        found = jnp.where(rel == u, lane_gather(table[first + u], low), found)
    return found


def running_max(x, count):
    x = jnp.broadcast_to(x, (ROWS, LANES))
    step = 1
    while step < count:
        x = jnp.maximum(x, pltpu.roll(x, LANES - step, 1))
        step *= 2
    return x


def by_partner(axis, first, last):
    even = (lax.axis_index(axis) & 1) == 0
    return jnp.where(even, last, first), jnp.where(even, first, last)


def from_partners(axis, one, other, wrap=False):
    at, count = lax.axis_index(axis), lax.axis_size(axis)
    even = (at & 1) == 0
    before, after = jnp.where(even, other, one), jnp.where(even, one, other)
    if wrap:
        return before, after
    return jnp.where(at > 0, before, 0.0), jnp.where(at < count - 1, after, 0.0)


PLACE_STEP = 0.1 / 65535.0
RADIUS_LEAST = 0.01
RADIUS_STEP = 0.04 / 65535.0
SLIP_HALF = 1 << 20


def largest_slip(table, rows):
    most = jnp.zeros((ROWS, LANES), jnp.float32)
    for n in range(0, rows, ROWS):
        for c in range(3):
            most = jnp.maximum(most, jnp.abs(table[n : n + ROWS, 3 + c, :]))
    most = jnp.max(jnp.max(most, axis=0, keepdims=True), axis=1, keepdims=True)
    return jnp.broadcast_to(jnp.maximum(most, 1e-30), (ROWS, LANES))


def code_rows(table, n, largest, words):
    rows = pl.ds(n * ROWS, ROWS)

    def whole(c, least, step):
        x = ((table[rows, c, :] - least) * (1.0 / step) + 0.5).astype(jnp.int32)
        return jnp.clip(x, 0, 65535)

    x, y, z = (whole(c, 0.0, PLACE_STEP) for c in range(3))
    radius = whole(6, RADIUS_LEAST, RADIUS_STEP)
    scale = (SLIP_HALF - 1.0) / largest
    u, v, w = (
        (table[rows, 3 + c, :] * scale + (SLIP_HALF + 0.5)).astype(jnp.int32) for c in range(3)
    )
    coded = (
        x | (y << 16),
        z | (radius << 16),
        u | ((w & 2047) << 21),
        v | (lax.shift_right_logical(w, 11) << 21),
    )
    for k, word in enumerate(coded):
        words[pl.ds(n * 32 + k, ROWS, stride=4), :] = word


def decoded(words, largest):
    low = [x & 65535 for x in words[0:2]]
    high = [lax.shift_right_logical(x, 16) for x in words[0:2]]
    place = (low[0], high[0], low[1])
    radius = high[1].astype(jnp.float32) * RADIUS_STEP + RADIUS_LEAST
    mask = 2 * SLIP_HALF - 1
    third = lax.shift_right_logical(words[2], 21) | (lax.shift_right_logical(words[3], 21) << 11)
    scale = largest * (1.0 / (SLIP_HALF - 1.0))
    slip = [
        (x - SLIP_HALF).astype(jnp.float32) * scale for x in (words[2] & mask, words[3] & mask, third)
    ]
    return place, radius, slip


def fill_gas_rows(gas_ref, gas_rows):
    for r in range(16):
        rows = slice(r * ROWS, (r + 1) * ROWS)
        for c in range(3):
            for half in range(2):
                gas_rows[rows, half * 4 + c, :] = gas_ref[c, rows, half * LANES : (half + 1) * LANES]


def gas_index(block, keys_ref, slot):
    idx = slot[0]
    keys = keys_ref[rows_of(block), :]
    idx[0] = lax.shift_right_logical(keys, 19)
    idx[1] = lax.shift_right_logical(keys, 11) & (LANES - 1)


def gas_gather(block, g, ends, gas_rows, slot):
    idx, found = slot[0], slot[1]
    zero = jnp.zeros((ROWS, LANES), jnp.float32)
    first = ends[0, block * 16 + g]
    found[g] = window(gas_rows, first, GAS_WINDOW, wide(idx, 0, g), wide(idx, 1, g), zero)


def gas_rest(block, ends, gas_rows, slot):
    idx, found = slot[0], slot[1]

    @pl.when(ends[2, block * 16] >= GAS_WINDOW)
    def _():
        def one(g, carry):
            first = ends[0, block * 16 + g]
            row = jnp.broadcast_to(idx[0, pl.ds(g, 1), :], (ROWS, LANES))
            low = jnp.broadcast_to(idx[1, pl.ds(g, 1), :], (ROWS, LANES))

            def trip(t, total):
                base = jnp.minimum(first + GAS_WINDOW * t, LANES)
                return window(gas_rows, base, GAS_WINDOW, row, low, total)

            trips = (ends[1, block * 16 + g] - first) // GAS_WINDOW + 1
            found[g] = lax.fori_loop(1, trips, trip, found[g])
            return carry

        lax.fori_loop(0, 16, one, 0)


def seen_values(block, keys_ref, slot):
    idx, found, val = slot
    keys = keys_ref[rows_of(block), :]
    upper = (keys & (1 << 18)) != 0
    place_in = keys & (BLOCK - 1)
    val[0] = lax.shift_right_logical(place_in, 7).astype(jnp.float32)
    val[1] = (place_in & (LANES - 1)).astype(jnp.float32)
    for c in range(3):
        seen = jnp.where(upper, found[:, 4 + c, :], found[:, c, :])
        for n, part in enumerate(split_three(seen)):
            val[2 + 3 * c + n] = part


def seen_in_order(groups, slot, iota):
    val = slot[2]
    rows, hots = [], []
    for g in groups:
        parts = [[packed_row(val.at[2 + 3 * c + n], g) for c in range(3)] for n in range(3)]
        rows.append(spread_rows(packed_row(val.at[0], g), parts, iota))
        hots.append(one_hot_rows(packed_row(val.at[1], g), iota))
    return spread_add(rows, hots)


def write_states(block, total, pos_ref, vel_ref, diam_ref, out_ref, out_rows):
    rows = rows_of(block)
    for c in range(3):
        out_ref[out_rows, c, :] = pos_ref[c, rows, :]
        out_ref[out_rows, 3 + c, :] = total[16 * c : 16 * c + 16] - vel_ref[c, rows, :]
    out_ref[out_rows, 6, :] = 0.5 * diam_ref[rows, :]
    out_ref[out_rows, 7, :] = jnp.zeros((16, LANES), jnp.float32)


def states_step(gather, scatter, keys_ref, ends, gas_rows, iota, arrays):
    total = jnp.zeros((48, LANES), jnp.float32)
    if gather:
        gas_index(gather[0], keys_ref, gather[1])
    if scatter:
        seen_values(scatter[0], keys_ref, scatter[1])
    for g in range(16):
        if gather:
            gas_gather(gather[0], g, ends, gas_rows, gather[1])
        if scatter and g % 2:
            total = total + seen_in_order((g - 1, g), scatter[1], iota)
    if scatter:
        write_states(scatter[0], total, *arrays, *scatter[2:])
    if gather:
        gas_rest(gather[0], ends, gas_rows, gather[1])


def states_kernel(
    cell_hbm, gas_hbm, pos_hbm, vel_hbm, diam_hbm,
    keys_ref, ends_ref, table_ref, words_ref, largest_ref, sent_ref,
    cell_ref, gas_ref, pos_ref, vel_ref, diam_ref,
    gas_rows, iota, ends, idx_a, found_a, val_a, idx_b, found_b, val_b, sems,
):
    sources = (cell_hbm, gas_hbm, pos_hbm, vel_hbm, diam_hbm)
    places = (cell_ref, gas_ref, pos_ref, vel_ref, diam_ref)
    copies = [
        pltpu.make_async_copy(x, y, sems.at[n]) for n, (x, y) in enumerate(zip(sources, places))
    ]
    for copy in copies:
        copy.start()
    copies[0].wait()
    sub = lax.broadcasted_iota(jnp.int32, (ROWS, LANES), 0)
    lane = lax.broadcasted_iota(jnp.int32, (ROWS, LANES), 1)
    cells = cell_ref[...].T
    regs = []
    for v in range(16):
        own = (lane & 15) * LANES + v * ROWS + sub
        regs.append(cells[v * ROWS : (v + 1) * ROWS] * BLOCK + own)
    place = [("v", k) for k in range(4)] + [("s", k) for k in range(3)] + [("l", k) for k in range(4)]
    regs = sort_network(regs, place, 11)
    keys_ref[...] = jnp.concatenate(regs, axis=0).T
    least = functools.reduce(jnp.minimum, regs)
    most = functools.reduce(jnp.maximum, regs)
    least = lax.shift_right_logical(jnp.min(least, axis=0, keepdims=True), 19)
    most = lax.shift_right_logical(jnp.max(most, axis=0, keepdims=True), 19)
    ends_ref[0:1, :] = least
    ends_ref[1:2, :] = most
    ends_ref[2:8, :] = running_max(most - least, 16)[0:6]
    copy = pltpu.make_async_copy(ends_ref, ends, sems.at[5])
    copy.start()
    copies[1].wait()
    fill_gas_rows(gas_ref, gas_rows)
    for other in copies[2:]:
        other.wait()
    copy.wait()
    fill_iota(iota)
    a, b = (idx_a, found_a, val_a), (idx_b, found_b, val_b)
    step = functools.partial(
        states_step, keys_ref=keys_ref, ends=ends, gas_rows=gas_rows, iota=iota,
        arrays=(pos_ref, vel_ref, diam_ref),
    )
    step((0, a), None)

    def two(k, carry):
        block = 2 * k
        step((block + 1, b), (block, a, table_ref, rows_of(block)))
        step((block + 2, a), (block + 1, b, table_ref, rows_of(block + 1)))
        return carry

    lax.fori_loop(0, 3, two, 0)
    step((7, b), (6, a, table_ref, rows_of(6)))
    step(None, (7, b, table_ref, rows_of(7)))
    largest = largest_slip(table_ref, 128)
    largest_ref[...] = largest
    for n in range(16):
        code_rows(table_ref, n, largest, words_ref)
    words_ref[512:576, :] = jnp.zeros((64, LANES), jnp.int32)
    sent_ref[0], sent_ref[1] = by_partner("az", table_ref[0:16], table_ref[112:128])


def slots(rows, parts, dtype=jnp.float32):
    one = [VMEM((2, 16, LANES), jnp.int32), VMEM((16, ROWS, LANES), dtype), VMEM((parts, rows, LANES), dtype)]
    return one + one


def droplet_states(cells, gas, pos, vel, diam):
    f32, i32 = jnp.float32, jnp.int32
    arrays = (cells, gas, pos, vel, diam)
    return pl.pallas_call(
        states_kernel,
        name="droplet_states",
        out_shape=(
            jax.ShapeDtypeStruct((128, LANES), i32),
            jax.ShapeDtypeStruct((ROWS, LANES), i32),
            jax.ShapeDtypeStruct((128, ROWS, LANES), f32),
            jax.ShapeDtypeStruct((576, LANES), i32),
            jax.ShapeDtypeStruct((ROWS, LANES), f32),
            jax.ShapeDtypeStruct((2, 16, ROWS, LANES), f32),
        ),
        in_specs=[pl.BlockSpec(memory_space=pltpu.HBM)] * 5,
        scratch_shapes=[VMEM(x.shape, x.dtype) for x in arrays]
        + [VMEM((144, ROWS, LANES), f32), VMEM((LANES, LANES), jnp.bfloat16), SMEM((ROWS, LANES), i32)]
        + slots(16, 11)
        + [pltpu.SemaphoreType.DMA((6,))],
        compiler_params=params(),
    )(*[pltpu.with_memory_space_constraint(x, pltpu.HBM) for x in arrays])


def pair_sort_kernel(live_ref, pairs_ref, keys_ref, ends_ref):
    live = live_ref[0, 0]
    sub = lax.broadcasted_iota(jnp.int32, (ROWS, LANES), 0)
    lane = lax.broadcasted_iota(jnp.int32, (ROWS, LANES), 1)
    regs = []
    for v in range(32):
        rows = slice(v * ROWS, (v + 1) * ROWS)
        slot = v * 1024 + sub * LANES + lane
        head = pairs_ref[0, rows, :]
        tail = pairs_ref[1, rows, :] - 7 * BLOCK
        own = tail - BLOCK
        inside = (own >= 0) & (own < 8 * BLOCK)
        tail = jnp.where(inside, jnp.maximum(own, head) + BLOCK, tail)
        head = jnp.where(inside, jnp.minimum(own, head), head)
        bucket = lax.shift_right_logical(tail, 10)
        bucket = jnp.where(inside, bucket + 2, jnp.where(bucket >= 18, bucket - 16, bucket))
        turn = -(bucket & 1) & (8 * BLOCK - 1)
        key = (bucket << 24) | ((head ^ turn) << 10) | (tail & (BUCKET - 1))
        regs.append(jnp.where(slot < live, key, DEAD))
    place = (
        [("v", k) for k in range(4)]
        + [("s", k) for k in range(3)]
        + [("v", 4)]
        + [("l", k) for k in range(7)]
    )
    regs = sort_network(regs, place, 15)
    beyond = jnp.zeros((ROWS, LANES), jnp.float32)
    for key in regs:
        beyond = beyond + jnp.where(key < NEAR_BUCKETS << 24, 1.0, 0.0)
    beyond = jnp.sum(jnp.sum(beyond, axis=0, keepdims=True), axis=1, keepdims=True)
    ends_ref[8:16, :] = jnp.broadcast_to(beyond, (ROWS, LANES)).astype(jnp.int32)
    for half in range(2):
        rows = regs[16 * half : 16 * half + 16]
        keys_ref[half] = jnp.concatenate(rows, axis=0).T
        least_head = least_tail = jnp.full((ROWS, LANES), 1 << 20, jnp.int32)
        most_head = most_tail = jnp.full((ROWS, LANES), -1, jnp.int32)
        for key in rows:
            used = key < DEAD
            bucket = lax.shift_right_logical(key, 24)
            head = lax.shift_right_logical(key, 17) & (LANES - 1)
            head = head ^ (-(bucket & 1) & (LANES - 1))
            least_head = jnp.minimum(least_head, jnp.where(used, head, 1 << 20))
            most_head = jnp.maximum(most_head, jnp.where(used, head, -1))
            least_tail = jnp.minimum(least_tail, jnp.where(used, bucket, 1 << 20))
            most_tail = jnp.maximum(most_tail, jnp.where(used, bucket, -1))
        for n, x in enumerate((least_head, most_head, least_tail, most_tail)):
            reduce = jnp.max if n % 2 else jnp.min
            row = 4 * half + n
            bound = (LANES, LANES, BUCKETS, BUCKETS)[n]
            ends_ref[row : row + 1, :] = jnp.minimum(reduce(x, axis=0, keepdims=True), bound)


def pair_sort(live, pairs):
    return pl.pallas_call(
        pair_sort_kernel,
        name="pair_sort",
        out_shape=(
            jax.ShapeDtypeStruct((2, LANES, LANES), jnp.int32),
            jax.ShapeDtypeStruct((16, LANES), jnp.int32),
        ),
        in_specs=[pl.BlockSpec(memory_space=SMEM), pl.BlockSpec(memory_space=VMEM)],
        compiler_params=params(),
    )(live, pairs)


def group_ends(g, ends, part):
    g = jnp.minimum(g, 2 * LANES - 1)
    at, lane = 4 * (g & 1), g >> 1
    low, high, _ = part
    return (
        ends[at, lane] & -2,
        ends[at + 1, lane],
        jnp.maximum(ends[at + 2, lane], low),
        jnp.minimum(ends[at + 3, lane], high - 1),
    )


def take_items(state, groups, ends, part):
    low, high, heads = part
    items = []
    for _ in range(ROWS):
        g, bucket, head, now, later = state
        place = jnp.minimum(bucket, high) - low
        items.append((jnp.minimum(g, 2 * LANES - 1), jnp.where(g < groups, bucket, -1), head, place))
        ahead = group_ends(g + 2, ends, part)
        more_heads = head + heads <= now[1]
        stay = more_heads | (bucket < now[3])
        head = jnp.where(more_heads, head + heads, jnp.where(stay, now[0], later[0]))
        bucket = jnp.where(more_heads, bucket, jnp.where(stay, bucket + 1, later[2]))
        now = tuple(jnp.where(stay, x, y) for x, y in zip(now, later))
        later = tuple(jnp.where(stay, x, y) for x, y in zip(later, ahead))
        state = (jnp.where(stay, g, g + 1), bucket, head, now, later)
    return items, state


def word_window(words, first, count, pair, low):
    found = jnp.zeros((ROWS, LANES), jnp.int32)
    for u in range(count):
        rows = words[pl.ds(pl.multiple_of((first + u) * ROWS, ROWS), ROWS), :]
        found = jnp.where(pair == u, lane_gather(rows, low), found)
    return found


def pair_gather(k, item, keys_ref, near_words, far_words, heads, slot):
    key_rows, rel_rows, near, far = slot
    g, bucket, first, part = item
    keys = jnp.broadcast_to(keys_ref[g & 1, pl.ds(g >> 1, 1), :], (ROWS, LANES))
    of_bucket = lax.shift_right_logical(keys, 24)
    turn = -(of_bucket & 1) & (8 * BLOCK - 1)
    head = (lax.shift_right_logical(keys, 10) & (8 * BLOCK - 1)) ^ turn
    rel = lax.shift_right_logical(head, 7) - first
    used = (of_bucket == bucket) & (rel >= 0) & (rel < heads)
    key_rows[k : k + 1, :] = jnp.where(used, keys, DEAD)[0:1]
    rel_rows[k : k + 1, :] = rel[0:1]
    near[k] = word_window(near_words, first >> 1, heads // 2, rel >> 1, head & (LANES - 1))
    pair = lax.shift_right_logical(keys, 8) & 3
    far[k] = word_window(far_words, part * 4, 4, pair, keys & (LANES - 1))


def pair_values(slot, val, near_largest, far_largest):
    key_rows, rel_rows, near, far = slot
    keys, rel = key_rows[...], rel_rows[...]
    used = keys < DEAD
    turn = -(lax.shift_right_logical(keys, 24) & 1) & (LANES - 1)
    val[0] = rel.astype(jnp.float32)
    val[1] = ((lax.shift_right_logical(keys, 10) & (LANES - 1)) ^ turn).astype(jnp.float32)
    val[2] = (lax.shift_right_logical(keys, 7) & 7).astype(jnp.float32)
    val[3] = (keys & (LANES - 1)).astype(jnp.float32)

    def words(ref, odd):
        return [jnp.where(odd, ref[:, 4 + w, :], ref[:, w, :]) for w in range(4)]

    near_place, near_radius, near_slip = decoded(words(near, (rel & 1) == 1), near_largest)
    far_place, far_radius, far_slip = decoded(words(far, (keys & LANES) != 0), far_largest)
    gap = jnp.zeros((ROWS, LANES), jnp.float32)
    for x, y in zip(far_place, near_place):
        apart = (x - y).astype(jnp.float32)
        gap = gap + apart * apart
    gap = gap * (PLACE_STEP * PLACE_STEP)
    far_ratio = far_radius * lax.rsqrt(gap + far_radius * far_radius)
    near_ratio = near_radius * lax.rsqrt(gap + near_radius * near_radius)
    weight_far = jnp.where(used, piep_coef * far_ratio * far_ratio * far_ratio, 0.0)
    weight_near = jnp.where(used, piep_coef * near_ratio * near_ratio * near_ratio, 0.0)
    for c in range(3):
        for n, part in enumerate(split_two(weight_far * far_slip[c])):
            val[4 + 3 * n + c] = part
        for n, part in enumerate(split_two(weight_near * near_slip[c])):
            val[10 + 3 * n + c] = part


def pair_scatter(k, item, val, head_sum, tail_sum, iota, iota8):
    first, tail_first = item
    parts = [[packed_row(val.at[4 + 3 * n + c], k) for c in range(3)] for n in range(2)]
    heads = spread_rows(packed_row(val.at[0], k), parts, iota)
    hit = packed_row(val.at[2], k) == iota8[...]
    zero = jnp.zeros((16, LANES), jnp.bfloat16)
    tails = []
    for n in range(10, 16, 2):
        both = jnp.concatenate([wide(val, n, k), wide(val, n + 1, k)], axis=0)
        tails.append(jnp.where(hit, both.astype(jnp.bfloat16), zero))
    tails = jnp.concatenate(tails, axis=0)
    out = block_product(
        [heads, tails], [one_hot_rows(packed_row(val.at[n], k), iota) for n in (1, 3)]
    )
    for c in range(3):
        head_sum[c, pl.ds(first, 16), :] += out[16 * c : 16 * c + 16] + out[16 * c + 48 : 16 * c + 64]
    at = pl.ds(pl.multiple_of(tail_first, 8), 8)
    for c in range(3):
        tail_sum[c, at, :] += out[8 * c + 96 : 8 * c + 104] + out[8 * c + 120 : 8 * c + 128]


def run_pairs(groups, start, part, ends, keys_ref, near, far, sums, iota, iota8, scratch):
    fill_iota(iota)
    rows = lax.broadcasted_iota(jnp.int32, iota8.shape, 0) & 7
    iota8[...] = rows.astype(jnp.float32).astype(jnp.bfloat16)
    val, a, b = scratch[0], scratch[1:5], scratch[5:9]

    def step(state, slot, pending):
        items, state = take_items(state, groups, ends, part)
        if pending:
            pair_values(a, val, near[1], far[1])
        for k in range(ROWS):
            pair_gather(k, items[k], keys_ref, near[0], far[0], part[2], slot)
            if pending:
                pair_scatter(k, pending[k], val, *sums, iota, iota8)
        return tuple((item[2], item[3] * 8) for item in items), state, items[0][1] >= 0

    now, later = group_ends(start, ends, part), group_ends(start + 1, ends, part)
    state = (start, now[2], now[0], now, later)

    def one(carry):
        pending, state, _ = carry
        carry = step(state, b, pending)
        for x, y in zip(a, b):
            x[...] = y[...]
        return carry

    lax.while_loop(lambda carry: carry[2], one, step(state, a, None))


def near_pairs_kernel(
    ends, keys_ref, words_ref, largest_ref, one_in, other_in,
    heads_ref, one_ref, other_ref,
    shell, shell_words, head_sum, tail_sum, iota, iota8, *scratch,
):
    shell[0:16], shell[16:32] = from_partners("az", one_in[0], other_in[...], True)
    shell_largest = largest_slip(shell, 32)
    for n in range(4):
        code_rows(shell, n, shell_largest, shell_words)
    shell_words[128:160, :] = jnp.zeros((32, LANES), jnp.int32)
    head_sum[...] = jnp.zeros_like(head_sum)
    tail_sum[...] = jnp.zeros_like(tail_sum)
    groups = (ends[8, 0] + LANES - 1) // LANES
    run_pairs(
        groups, jnp.int32(0), (0, NEAR_BUCKETS, NEAR_HEADS), ends, keys_ref,
        (words_ref, largest_ref[...]), (shell_words, shell_largest),
        (head_sum, tail_sum), iota, iota8, scratch,
    )
    heads_ref[...] = head_sum[:, 0:128, :]
    one_ref[...], other_ref[...] = by_partner("az", tail_sum[:, 0:16, :], tail_sum[:, 16:32, :])


def own_pairs_kernel(
    live_ref, ends, keys_ref, words_ref, largest_ref, heads_ref,
    corr_ref,
    head_sum, tail_sum, iota, iota8, *scratch,
):
    head_sum[:, 0:128, :] = heads_ref[...]
    head_sum[:, 128:144, :] = jnp.zeros((3, 16, LANES), jnp.float32)
    tail_sum[...] = jnp.zeros_like(tail_sum)
    groups = (live_ref[0, 0] + LANES - 1) // LANES
    start = jnp.minimum(ends[8, 0] // LANES, 2 * LANES - 1)
    coded = (words_ref, largest_ref[...])
    run_pairs(
        groups, start, (NEAR_BUCKETS, BUCKETS, OWN_HEADS), ends, keys_ref, coded, coded,
        (head_sum, tail_sum), iota, iota8, scratch,
    )
    corr_ref[...] = head_sum[:, 0:128, :] + tail_sum[:, 0:128, :]


def pair_scratch(tail_rows):
    f32, i32 = jnp.float32, jnp.int32
    slot = [
        VMEM((ROWS, LANES), i32),
        VMEM((ROWS, LANES), i32),
        VMEM((ROWS, ROWS, LANES), i32),
        VMEM((ROWS, ROWS, LANES), i32),
    ]
    return [
        VMEM((3, 144, LANES), f32),
        VMEM((3, tail_rows, LANES), f32),
        VMEM((LANES, LANES), jnp.bfloat16),
        VMEM((16, LANES), jnp.bfloat16),
        VMEM((16, ROWS, LANES), f32),
        *slot,
        *slot,
    ]


def near_pairs(ends, keys, words, largest, one, other):
    f32 = jnp.float32
    smem, vmem = pl.BlockSpec(memory_space=SMEM), pl.BlockSpec(memory_space=VMEM)
    return pl.pallas_call(
        near_pairs_kernel,
        name="near_pairs",
        out_shape=(
            jax.ShapeDtypeStruct((3, 128, LANES), f32),
            jax.ShapeDtypeStruct((3, 16, LANES), f32),
            jax.ShapeDtypeStruct((3, 16, LANES), f32),
        ),
        in_specs=[smem, vmem, vmem, vmem, vmem, vmem],
        scratch_shapes=[VMEM((32, ROWS, LANES), f32), VMEM((160, LANES), jnp.int32)]
        + pair_scratch(40),
        compiler_params=params(),
    )(ends, keys, words, largest, one, other)


def own_pairs(live, ends, keys, words, largest, heads):
    smem, vmem = pl.BlockSpec(memory_space=SMEM), pl.BlockSpec(memory_space=VMEM)
    return pl.pallas_call(
        own_pairs_kernel,
        name="own_pairs",
        out_shape=jax.ShapeDtypeStruct((3, 128, LANES), jnp.float32),
        in_specs=[smem, smem, vmem, vmem, vmem, vmem],
        scratch_shapes=pair_scratch(136),
        compiler_params=params(),
    )(live, ends, keys, words, largest, heads)


def force_gather(block, keys_ref, table_ref, total_ref, slot):
    force, got, val = slot
    rows = rows_of(block)
    scale = (-2.0 * drag_coef) * table_ref[rows, 6, :]
    for c in range(3):
        push = scale * (table_ref[rows, 3 + c, :] + total_ref[c, rows, :])
        force[:, c, :] = push[0:8]
        force[:, 4 + c, :] = push[8:16]
    keys = keys_ref[rows, :]
    val[0] = lax.shift_right_logical(keys, 19).astype(jnp.float32)
    val[1] = (lax.shift_right_logical(keys, 11) & (2 * LANES - 1)).astype(jnp.float32)
    inner = lax.shift_right_logical(keys, 7) & 7
    low = keys & (LANES - 1)
    tables = [force[k] for k in range(ROWS)]
    for g in range(16):
        pick = jnp.broadcast_to(inner[g : g + 1, :], (ROWS, LANES))
        at = jnp.broadcast_to(low[g : g + 1, :], (ROWS, LANES))
        found = jnp.zeros((ROWS, LANES), jnp.float32)
        for k in range(ROWS):
            found = jnp.where(pick == k, lane_gather(tables[k], at), found)
        got[g] = found
    upper = (keys & 1024) != 0
    for c in range(3):
        pushed = jnp.where(upper, got[:, 4 + c, :], got[:, c, :])
        for n, part in enumerate(split_two(pushed)):
            val[2 + 2 * c + n] = part


def force_rows(g, base, slot, iota):
    val = slot[2]

    def row(n):
        if isinstance(g, int):
            return packed_row(val.at[n], g)
        return jnp.broadcast_to(val[n, pl.ds(g, 1), :], (16, LANES)).astype(jnp.bfloat16)

    rel = row(0) - base.astype(jnp.float32).astype(jnp.bfloat16)
    parts = [[row(2 + 2 * c + n) for c in range(3)] for n in range(2)]
    return spread_rows(rel, parts, iota), one_hot_rows(row(1), iota)


def force_add(groups, bases, slot, cells, iota):
    pieces = [force_rows(g, base, slot, iota) for g, base in zip(groups, bases)]
    out = block_product([p[0] for p in pieces], [p[1] for p in pieces])
    for n, base in enumerate(bases):
        for c in range(3):
            at = 96 * n + 16 * c
            total = out[at : at + 16] + out[at + 48 : at + 64]
            for half in range(2):
                part = total[:, half * LANES : (half + 1) * LANES]
                cells[2 * c + half, pl.ds(base, 16), :] += part


def force_rest(block, ends, slot, cells, iota):
    @pl.when(ends[2, block * 16] >= 16)
    def _():
        def one(g, carry):
            first, most = ends[0, block * 16 + g], ends[1, block * 16 + g]

            def trip(t, carry):
                force_add([g], [jnp.minimum(first + 16 * t, LANES)], slot, cells, iota)
                return carry

            lax.fori_loop(1, (most - first) // 16 + 1, trip, 0)
            return carry

        lax.fori_loop(0, 16, one, 0)


def deposit_step(gather, scatter, ends, keys_ref, table_ref, total_ref, cells, iota):
    if gather:
        force_gather(gather[0], keys_ref, table_ref, total_ref, gather[1])
    if scatter:
        for g in range(16):
            force_add([g], [ends[0, scatter[0] * 16 + g]], scatter[1], cells, iota)
        force_rest(scatter[0], ends, scatter[1], cells, iota)


def deposit_kernel(
    ends, keys_ref, table_ref, corr_ref, one_in, other_in,
    out_ref, total_ref, one_ref, other_ref,
    cells, iota, force_a, got_a, val_a, force_b, got_b, val_b,
):
    fill_iota(iota)
    cells[...] = jnp.zeros_like(cells)
    total_ref[...] = corr_ref[...]
    before, after = from_partners("az", one_in[...], other_in[...], True)
    total_ref[:, 0:16, :] += before
    total_ref[:, 112:128, :] += after
    a, b = (force_a, got_a, val_a), (force_b, got_b, val_b)
    step = functools.partial(
        deposit_step, ends=ends, keys_ref=keys_ref, table_ref=table_ref, total_ref=total_ref,
        cells=cells, iota=iota,
    )
    step((0, a), None)

    def two(k, carry):
        block = 2 * k
        step((block + 1, b), (block, a))
        step((block + 2, a), (block + 1, b))
        return carry

    lax.fori_loop(0, 3, two, 0)
    step((7, b), (6, a))
    step(None, (7, b))
    for c in range(3):
        for half in range(2):
            columns = slice(half * LANES, (half + 1) * LANES)
            out_ref[c, :, columns] = cells[2 * c + half, 0:128, :]
            one, other = by_partner(
                "ax", cells[2 * c + half, 0:32, :], cells[2 * c + half, 96:128, :]
            )
            one_ref[c, :, columns] = one
            other_ref[c, :, columns] = other


def deposits(ends, keys, table, corr, one, other):
    f32 = jnp.float32
    smem, vmem = pl.BlockSpec(memory_space=SMEM), pl.BlockSpec(memory_space=VMEM)
    slot = [VMEM((ROWS, ROWS, LANES), f32), VMEM((16, ROWS, LANES), f32), VMEM((8, 16, LANES), f32)]
    return pl.pallas_call(
        deposit_kernel,
        name="deposits",
        out_shape=(
            jax.ShapeDtypeStruct((3, 128, 2 * LANES), f32),
            jax.ShapeDtypeStruct((3, 128, LANES), f32),
            jax.ShapeDtypeStruct((3, 32, 2 * LANES), f32),
            jax.ShapeDtypeStruct((3, 32, 2 * LANES), f32),
        ),
        in_specs=[smem] + [vmem] * 5,
        scratch_shapes=[VMEM((6, 144, LANES), f32), VMEM((2 * LANES, LANES), jnp.bfloat16)]
        + slot
        + slot,
        compiler_params=params(),
    )(ends, keys, table, corr, one, other)


def axial_kernel(taps, cells_ref, one_in, other_in, out_ref, one_ref, other_ref, first_ref, last_ref):
    for c in range(3):
        before, after = from_partners("ax", one_in[c], other_in[c])
        padded = jnp.concatenate([before, cells_ref[c], after], axis=0)
        total = taps[0] * padded[0:128]
        for k in range(1, 5):
            total = total + taps[k] * padded[16 * k : 16 * k + 128]
        out_ref[c] = total
        for a in range(8):
            first_ref[2 * a : 2 * a + 2, :] = total[16 * a : 16 * a + 2]
            last_ref[2 * a : 2 * a + 2, :] = total[16 * a + 14 : 16 * a + 16]
        one_ref[c], other_ref[c] = by_partner("rad", first_ref[...], last_ref[...])


def radial_kernel(
    taps, cells_ref, one_in, other_in, out_ref, sent_ref, padded, before_ref, after_ref
):
    lane = lax.broadcasted_iota(jnp.int32, (LANES, LANES), 1)
    edges = jnp.zeros((LANES, LANES), jnp.float32)
    for c in range(3):
        before_ref[...], after_ref[...] = from_partners("rad", one_in[c], other_in[c])
        for a in range(8):
            padded[0:2, :] = before_ref[2 * a : 2 * a + 2, :]
            padded[2:18, :] = cells_ref[c, 16 * a : 16 * a + 16, :]
            padded[18:20, :] = after_ref[2 * a : 2 * a + 2, :]
            total = taps[0] * padded[0:16, :]
            for k in range(1, 5):
                total = total + taps[k] * padded[k : k + 16, :]
            out_ref[c, 16 * a : 16 * a + 16, :] = total
        left, right = out_ref[c, :, 0:LANES], out_ref[c, :, LANES:]
        if c:
            left = pltpu.roll(left, 2 * c, 1)
        right = pltpu.roll(right, 10 + 2 * c, 1)
        edges = jnp.where((lane >> 1) == c, left, edges)
        edges = jnp.where((lane >> 1) == 4 + c, right, edges)
    turned = edges.T
    sent_ref[0], sent_ref[1] = by_partner("az", turned[0:8], turned[8:16])


def inner_azimuthal_kernel(taps, cells_ref, out_ref):
    lane = lax.broadcasted_iota(jnp.int32, (LANES, LANES), 1)
    for c in range(3):
        left, right = cells_ref[c, :, 0:LANES], cells_ref[c, :, LANES:]
        out_left, out_right = taps[2] * left, taps[2] * right
        for k in (1, 2):
            tap = taps[2 + k]
            inner = lane < LANES - k
            x, y = (pltpu.roll(v, LANES - k, 1) for v in (left, right))
            out_left = out_left + tap * jnp.where(inner, x, y)
            out_right = out_right + tap * jnp.where(inner, y, 0.0)
            inner = lane >= k
            x, y = (pltpu.roll(v, k, 1) for v in (left, right))
            out_left = out_left + tap * jnp.where(inner, x, 0.0)
            out_right = out_right + tap * jnp.where(inner, y, x)
        out_ref[c, :, 0:LANES] = out_left
        out_ref[c, :, LANES:] = out_right


def azimuthal_kernel(taps, inner_ref, one_in, other_in, out_ref):
    lane = lax.broadcasted_iota(jnp.int32, (LANES, LANES), 1)
    rest = jnp.zeros((LANES - 16, LANES), jnp.float32)
    before, after = from_partners("az", one_in[0], other_in[...], True)
    edges = jnp.concatenate([after, before, rest], axis=0).T
    for c in range(3):
        out_left, out_right = inner_ref[c, :, 0:LANES], inner_ref[c, :, LANES:]
        for k in (1, 2):
            x = pltpu.roll(edges, (118 - 2 * c + k) % LANES, 1)
            out_left = out_left + taps[2 - k] * jnp.where(lane < k, x, 0.0)
            y = pltpu.roll(edges, LANES - 2 * c - k, 1)
            out_right = out_right + taps[2 + k] * jnp.where(lane >= LANES - k, y, 0.0)
        out_ref[c, :, 0:LANES] = out_left
        out_ref[c, :, LANES:] = out_right


def filtered(deposit, one, other):
    f32 = jnp.float32
    raw = [math.exp(-0.5 * k * k) for k in range(-2, 3)]
    taps = [x / sum(raw) for x in raw]
    whole = jax.ShapeDtypeStruct(deposit.shape, f32)
    radial_face = jax.ShapeDtypeStruct((3, 16, 2 * LANES), f32)
    edges = jax.ShapeDtypeStruct((2, 8, LANES), f32)
    cells, one, other = pl.pallas_call(
        functools.partial(axial_kernel, taps),
        name="axial_filter",
        out_shape=(whole, radial_face, radial_face),
        scratch_shapes=[VMEM((16, 2 * LANES), f32)] * 2,
        compiler_params=params(),
    )(deposit, *swapped(one, other, "ax"))
    cells, sent = pl.pallas_call(
        functools.partial(radial_kernel, taps),
        name="radial_filter",
        out_shape=(whole, edges),
        scratch_shapes=[VMEM((24, 2 * LANES), f32)] + [VMEM((16, 2 * LANES), f32)] * 2,
        compiler_params=params(),
    )(cells, *swapped(one, other, "rad"))
    one, other, _ = passed_on(sent, "az")
    inner = pl.pallas_call(
        functools.partial(inner_azimuthal_kernel, taps),
        name="inner_azimuthal_filter",
        out_shape=whole,
        compiler_params=params(),
    )(cells)
    return pl.pallas_call(
        functools.partial(azimuthal_kernel, taps),
        name="azimuthal_filter",
        out_shape=whole,
        compiler_params=params(),
    )(inner, one, other)


def swapped(one, other, axis, wrap=False):
    count = lax.axis_size(axis)

    def partner(i, odd):
        j = i + 1 if i % 2 == odd else i - 1
        return j % count if wrap or 0 <= j < count else i

    return [
        lax.ppermute(x, axis, [(i, partner(i, odd)) for i in range(count)])
        for odd, x in enumerate((one, other))
    ]


def passed_on(both, axis, beside=None):
    count = lax.axis_size(axis)
    came = lax.ppermute(both, axis, [(i, i ^ 1) for i in range(count)])
    if beside is not None:
        came, beside = lax.optimization_barrier((came, beside))
    further = [(i, (i + (-2 if i % 2 else 2)) % count) for i in range(count)]
    return came, lax.ppermute(came[1], axis, further), beside


def per_device(positions, velocity, diameter, cell_index, pair_list, live_pairs, gas_velocity):
    live = live_pairs.reshape(1, 1)
    cells = cell_index.reshape(128, LANES)
    gas = gas_velocity.reshape(3, 128, 2 * LANES)
    pos = positions.reshape(3, 128, LANES)
    vel = velocity.reshape(3, 128, LANES)
    diam = diameter.reshape(128, LANES)
    cell_keys, cell_ends, table, words, largest, sent = droplet_states(cells, gas, pos, vel, diam)
    sorted_pairs = pair_sort(live, pair_list.reshape(2, 256, LANES))
    one, other, (pair_keys, pair_ends) = passed_on(sent, "az", sorted_pairs)
    heads, one, other = near_pairs(pair_ends, pair_keys, words, largest, one, other)
    one, other = swapped(one, other, "az", True)
    corr = own_pairs(live, pair_ends, pair_keys, words, largest, heads)
    deposit, correction, one, other = deposits(cell_ends, cell_keys, table, corr, one, other)
    smoothed = filtered(deposit, one, other)
    return (correction.reshape(positions.shape), smoothed.reshape(gas_velocity.shape))


def solution(mesh):
    return jax.shard_map(
        per_device,
        mesh=mesh,
        in_specs=(
            P(None, "ax", "rad", "az"),
            P(None, "ax", "rad", "az"),
            P("ax", "rad", "az"),
            P("ax", "rad", "az"),
            P(None, "ax", "rad", "az"),
            P("ax", "rad", "az"),
            P(None, "ax", "rad", "az"),
        ),
        out_specs=(P(None, "ax", "rad", "az"), P(None, "ax", "rad", "az")),
        check_vma=False,
    )
```

```python
import functools
import math

import jax
import jax.numpy as jnp
from jax import lax
from jax.experimental import pallas as pl
from jax.experimental.pallas import tpu as pltpu
from jax.sharding import PartitionSpec as P

piep_coef = 1.0
drag_coef = 20.0

LANES = 128
ROWS = 8
BLOCK = 2048
GAS_WINDOW = 12
BUCKET = 1024
BUCKETS = 20
NEAR_BUCKETS = 4
NEAR_HEADS = 8
OWN_HEADS = 12
DEAD = 1 << 29

NT = (((1,), (1,)), ((), ()))
VMEM = pltpu.VMEM
SMEM = pltpu.SMEM


def params(megabytes=40):
    return pltpu.CompilerParams(vmem_limit_bytes=megabytes << 20)


def lane_gather(table, index):
    numbers = lax.GatherDimensionNumbers(
        offset_dims=(),
        collapsed_slice_dims=(1,),
        start_index_map=(1,),
        operand_batching_dims=(0,),
        start_indices_batching_dims=(0,),
    )
    return lax.gather(
        table,
        index[..., None],
        numbers,
        slice_sizes=(1, 1),
        mode=lax.GatherScatterMode.PROMISE_IN_BOUNDS,
    )


def sort_network(regs, place, levels):
    sub = lax.broadcasted_iota(jnp.int32, (ROWS, LANES), 0)
    lane = lax.broadcasted_iota(jnp.int32, (ROWS, LANES), 1)
    count = len(regs)

    def bit_fill(bit, v):
        if bit >= levels:
            return 0
        kind, k = place[bit]
        if kind == "v":
            return -((v >> k) & 1)
        return -(((sub if kind == "s" else lane) >> k) & 1)

    flip = [0] * count
    for level in range(1, levels + 1):
        fills = {}
        for v in range(count):
            kind, k = place[level] if level < levels else ("v", 99)
            key = (v >> k) & 1 if kind == "v" else 0
            if key not in fills:
                fills[key] = bit_fill(level, v)
            new = fills[key]
            if isinstance(new, int) and isinstance(flip[v], int):
                if new != flip[v]:
                    regs[v] = ~regs[v]
            else:
                regs[v] = regs[v] ^ (new ^ flip[v])
            flip[v] = new
        for bit in reversed(range(level)):
            kind, k = place[bit]
            step = 1 << k
            if kind == "v":
                for v in range(count):
                    if not v & step:
                        a, b = regs[v], regs[v | step]
                        regs[v], regs[v | step] = jnp.minimum(a, b), jnp.maximum(a, b)
            else:
                axis, size, where = (0, ROWS, sub) if kind == "s" else (1, LANES, lane)
                lower = (where & step) == 0
                for v in range(count):
                    x = regs[v]
                    ahead = pltpu.roll(x, size - step, axis)
                    behind = ahead if 2 * step == size else pltpu.roll(x, step, axis)
                    regs[v] = jnp.where(lower, jnp.minimum(x, ahead), jnp.maximum(x, behind))
    return regs


def split_two(x):
    high = x.astype(jnp.bfloat16).astype(jnp.float32)
    return high, x - high


def split_three(x):
    high, rest = split_two(x)
    mid, low = split_two(rest)
    return high, mid, low


def packed_row(ref, row):
    return jnp.broadcast_to(ref[row : row + 1, :], (16, LANES)).astype(jnp.bfloat16)


def one_hot(x, k):
    return jnp.maximum(jnp.minimum((x + 1) - k, k - (x - 1)), 0)


def one_hot_rows(low, iota):
    return jnp.concatenate(
        [one_hot(low, iota[k : k + 16, :]) for k in range(0, iota.shape[0], 16)], axis=0
    )


def spread_rows(rel, parts, iota):
    hit = one_hot(rel, iota[0:16, :])
    return jnp.concatenate([hit * p for part in parts for p in part], axis=0)


def block_product(rows, hots):
    zero = jnp.zeros
    lines = [
        jnp.concatenate(
            [x if m == n else zero(x.shape, x.dtype) for m in range(len(rows))], axis=1
        )
        for n, x in enumerate(rows)
    ]
    return lax.dot_general(
        jnp.concatenate(lines, axis=0),
        jnp.concatenate(hots, axis=1),
        NT,
        preferred_element_type=jnp.float32,
    )


def spread_add(rows, hots):
    out = lax.dot_general(
        jnp.concatenate(rows, axis=1) if len(rows) > 1 else rows[0],
        jnp.concatenate(hots, axis=1) if len(hots) > 1 else hots[0],
        NT,
        preferred_element_type=jnp.float32,
    )
    total = out[0:48]
    for s in range(48, out.shape[0], 48):
        total = total + out[s : s + 48]
    return total


def fill_iota(iota):
    rows = lax.broadcasted_iota(jnp.int32, iota.shape, 0)
    iota[...] = rows.astype(jnp.float32).astype(jnp.bfloat16)


def rows_of(block):
    start = block * 16
    return pl.ds(start if isinstance(block, int) else pl.multiple_of(start, 16), 16)


def wide(ref, *at):
    return jnp.broadcast_to(ref[at[:-1] + (slice(at[-1], at[-1] + 1),)], (ROWS, LANES))


def window(table, first, count, row, low, found):
    rel = row - first
    for u in range(count):
        found = jnp.where(rel == u, lane_gather(table[first + u], low), found)
    return found


def running_max(x, count):
    x = jnp.broadcast_to(x, (ROWS, LANES))
    step = 1
    while step < count:
        x = jnp.maximum(x, pltpu.roll(x, LANES - step, 1))
        step *= 2
    return x


def by_partner(axis, first, last):
    even = (lax.axis_index(axis) & 1) == 0
    return jnp.where(even, last, first), jnp.where(even, first, last)


def from_partners(axis, one, other, wrap=False):
    at, count = lax.axis_index(axis), lax.axis_size(axis)
    even = (at & 1) == 0
    before, after = jnp.where(even, other, one), jnp.where(even, one, other)
    if wrap:
        return before, after
    return jnp.where(at > 0, before, 0.0), jnp.where(at < count - 1, after, 0.0)


PLACE_STEP = 0.1 / 65535.0
RADIUS_LEAST = 0.01
RADIUS_STEP = 0.04 / 65535.0
SLIP_HALF = 1 << 20


def largest_slip(table, rows):
    most = jnp.zeros((ROWS, LANES), jnp.float32)
    for n in range(0, rows, ROWS):
        for c in range(3):
            most = jnp.maximum(most, jnp.abs(table[n : n + ROWS, 3 + c, :]))
    most = jnp.max(jnp.max(most, axis=0, keepdims=True), axis=1, keepdims=True)
    return jnp.broadcast_to(jnp.maximum(most, 1e-30), (ROWS, LANES))


def code_rows(table, n, largest, words):
    rows = pl.ds(n * ROWS, ROWS)

    def whole(c, least, step):
        x = ((table[rows, c, :] - least) * (1.0 / step) + 0.5).astype(jnp.int32)
        return jnp.clip(x, 0, 65535)

    x, y, z = (whole(c, 0.0, PLACE_STEP) for c in range(3))
    radius = whole(6, RADIUS_LEAST, RADIUS_STEP)
    scale = (SLIP_HALF - 1.0) / largest
    u, v, w = (
        (table[rows, 3 + c, :] * scale + (SLIP_HALF + 0.5)).astype(jnp.int32) for c in range(3)
    )
    coded = (
        x | (y << 16),
        z | (radius << 16),
        u | ((w & 2047) << 21),
        v | (lax.shift_right_logical(w, 11) << 21),
    )
    for k, word in enumerate(coded):
        words[pl.ds(n * 32 + k, ROWS, stride=4), :] = word


def decoded(words, largest):
    low = [x & 65535 for x in words[0:2]]
    high = [lax.shift_right_logical(x, 16) for x in words[0:2]]
    place = (low[0], high[0], low[1])
    radius = high[1].astype(jnp.float32) * RADIUS_STEP + RADIUS_LEAST
    mask = 2 * SLIP_HALF - 1
    third = lax.shift_right_logical(words[2], 21) | (lax.shift_right_logical(words[3], 21) << 11)
    scale = largest * (1.0 / (SLIP_HALF - 1.0))
    slip = [
        (x - SLIP_HALF).astype(jnp.float32) * scale for x in (words[2] & mask, words[3] & mask, third)
    ]
    return place, radius, slip


def fill_gas_rows(gas_ref, gas_rows):
    for r in range(16):
        rows = slice(r * ROWS, (r + 1) * ROWS)
        for c in range(3):
            for half in range(2):
                gas_rows[rows, half * 4 + c, :] = gas_ref[c, rows, half * LANES : (half + 1) * LANES]


def gas_index(block, keys_ref, slot):
    idx = slot[0]
    keys = keys_ref[rows_of(block), :]
    idx[0] = lax.shift_right_logical(keys, 19)
    idx[1] = lax.shift_right_logical(keys, 11) & (LANES - 1)


def gas_gather(block, g, ends, gas_rows, slot):
    idx, found = slot[0], slot[1]
    zero = jnp.zeros((ROWS, LANES), jnp.float32)
    first = ends[0, block * 16 + g]
    found[g] = window(gas_rows, first, GAS_WINDOW, wide(idx, 0, g), wide(idx, 1, g), zero)


def gas_rest(block, ends, gas_rows, slot):
    idx, found = slot[0], slot[1]

    @pl.when(ends[2, block * 16] >= GAS_WINDOW)
    def _():
        def one(g, carry):
            first = ends[0, block * 16 + g]
            row = jnp.broadcast_to(idx[0, pl.ds(g, 1), :], (ROWS, LANES))
            low = jnp.broadcast_to(idx[1, pl.ds(g, 1), :], (ROWS, LANES))

            def trip(t, total):
                base = jnp.minimum(first + GAS_WINDOW * t, LANES)
                return window(gas_rows, base, GAS_WINDOW, row, low, total)

            trips = (ends[1, block * 16 + g] - first) // GAS_WINDOW + 1
            found[g] = lax.fori_loop(1, trips, trip, found[g])
            return carry

        lax.fori_loop(0, 16, one, 0)


def seen_values(block, keys_ref, slot):
    idx, found, val = slot
    keys = keys_ref[rows_of(block), :]
    upper = (keys & (1 << 18)) != 0
    place_in = keys & (BLOCK - 1)
    val[0] = lax.shift_right_logical(place_in, 7).astype(jnp.float32)
    val[1] = (place_in & (LANES - 1)).astype(jnp.float32)
    for c in range(3):
        seen = jnp.where(upper, found[:, 4 + c, :], found[:, c, :])
        for n, part in enumerate(split_three(seen)):
            val[2 + 3 * c + n] = part


def seen_in_order(groups, slot, iota):
    val = slot[2]
    rows, hots = [], []
    for g in groups:
        parts = [[packed_row(val.at[2 + 3 * c + n], g) for c in range(3)] for n in range(3)]
        rows.append(spread_rows(packed_row(val.at[0], g), parts, iota))
        hots.append(one_hot_rows(packed_row(val.at[1], g), iota))
    return spread_add(rows, hots)


def write_states(block, total, pos_ref, vel_ref, diam_ref, out_ref, out_rows):
    rows = rows_of(block)
    for c in range(3):
        out_ref[out_rows, c, :] = pos_ref[c, rows, :]
        out_ref[out_rows, 3 + c, :] = total[16 * c : 16 * c + 16] - vel_ref[c, rows, :]
    out_ref[out_rows, 6, :] = 0.5 * diam_ref[rows, :]
    out_ref[out_rows, 7, :] = jnp.zeros((16, LANES), jnp.float32)


def states_step(gather, scatter, keys_ref, ends, gas_rows, iota, arrays):
    total = jnp.zeros((48, LANES), jnp.float32)
    if gather:
        gas_index(gather[0], keys_ref, gather[1])
    if scatter:
        seen_values(scatter[0], keys_ref, scatter[1])
    for g in range(16):
        if gather:
            gas_gather(gather[0], g, ends, gas_rows, gather[1])
        if scatter and g % 2:
            total = total + seen_in_order((g - 1, g), scatter[1], iota)
    if scatter:
        write_states(scatter[0], total, *arrays, *scatter[2:])
    if gather:
        gas_rest(gather[0], ends, gas_rows, gather[1])


def states_kernel(
    cell_hbm, gas_hbm, pos_hbm, vel_hbm, diam_hbm,
    keys_ref, ends_ref, table_ref, words_ref, largest_ref, one_ref, other_ref,
    cell_ref, gas_ref, pos_ref, vel_ref, diam_ref,
    gas_rows, iota, ends, idx_a, found_a, val_a, idx_b, found_b, val_b, sems,
):
    sources = (cell_hbm, gas_hbm, pos_hbm, vel_hbm, diam_hbm)
    places = (cell_ref, gas_ref, pos_ref, vel_ref, diam_ref)
    copies = [
        pltpu.make_async_copy(x, y, sems.at[n]) for n, (x, y) in enumerate(zip(sources, places))
    ]
    for copy in copies:
        copy.start()
    copies[0].wait()
    sub = lax.broadcasted_iota(jnp.int32, (ROWS, LANES), 0)
    lane = lax.broadcasted_iota(jnp.int32, (ROWS, LANES), 1)
    cells = cell_ref[...].T
    regs = []
    for v in range(16):
        own = (lane & 15) * LANES + v * ROWS + sub
        regs.append(cells[v * ROWS : (v + 1) * ROWS] * BLOCK + own)
    place = [("v", k) for k in range(4)] + [("s", k) for k in range(3)] + [("l", k) for k in range(4)]
    regs = sort_network(regs, place, 11)
    least = functools.reduce(jnp.minimum, regs)
    most = functools.reduce(jnp.maximum, regs)
    least = lax.shift_right_logical(jnp.min(least, axis=0, keepdims=True), 19)
    most = lax.shift_right_logical(jnp.max(most, axis=0, keepdims=True), 19)
    ends_ref[0:1, :] = least
    ends_ref[1:2, :] = most
    ends_ref[2:8, :] = running_max(most - least, 16)[0:6]
    copy = pltpu.make_async_copy(ends_ref, ends, sems.at[5])
    copy.start()
    keys_ref[...] = jnp.concatenate(regs, axis=0).T
    fill_iota(iota)
    copies[1].wait()
    fill_gas_rows(gas_ref, gas_rows)
    for other in copies[2:]:
        other.wait()
    copy.wait()
    a, b = (idx_a, found_a, val_a), (idx_b, found_b, val_b)
    step = functools.partial(
        states_step, keys_ref=keys_ref, ends=ends, gas_rows=gas_rows, iota=iota,
        arrays=(pos_ref, vel_ref, diam_ref),
    )
    step((0, a), None)

    def two(k, carry):
        block = 2 * k
        step((block + 1, b), (block, a, table_ref, rows_of(block)))
        step((block + 2, a), (block + 1, b, table_ref, rows_of(block + 1)))
        return carry

    lax.fori_loop(0, 3, two, 0)
    step((7, b), (6, a, table_ref, rows_of(6)))
    step(None, (7, b, table_ref, rows_of(7)))
    largest = largest_slip(table_ref, 128)
    largest_ref[...] = largest
    for n in range(16):
        code_rows(table_ref, n, largest, words_ref)
    words_ref[512:576, :] = jnp.zeros((64, LANES), jnp.int32)
    one_ref[...], other_ref[...] = by_partner("az", table_ref[0:16], table_ref[112:128])


def slots(rows, parts, dtype=jnp.float32):
    one = [VMEM((2, 16, LANES), jnp.int32), VMEM((16, ROWS, LANES), dtype), VMEM((parts, rows, LANES), dtype)]
    return one + one


def droplet_states(cells, gas, pos, vel, diam):
    f32, i32 = jnp.float32, jnp.int32
    arrays = (cells, gas, pos, vel, diam)
    return pl.pallas_call(
        states_kernel,
        name="droplet_states",
        out_shape=(
            jax.ShapeDtypeStruct((128, LANES), i32),
            jax.ShapeDtypeStruct((ROWS, LANES), i32),
            jax.ShapeDtypeStruct((128, ROWS, LANES), f32),
            jax.ShapeDtypeStruct((576, LANES), i32),
            jax.ShapeDtypeStruct((ROWS, LANES), f32),
            jax.ShapeDtypeStruct((16, ROWS, LANES), f32),
            jax.ShapeDtypeStruct((16, ROWS, LANES), f32),
        ),
        in_specs=[pl.BlockSpec(memory_space=pltpu.HBM)] * 5,
        scratch_shapes=[VMEM(x.shape, x.dtype) for x in arrays]
        + [VMEM((144, ROWS, LANES), f32), VMEM((LANES, LANES), jnp.bfloat16), SMEM((ROWS, LANES), i32)]
        + slots(16, 11)
        + [pltpu.SemaphoreType.DMA((6,))],
        compiler_params=params(),
    )(*[pltpu.with_memory_space_constraint(x, pltpu.HBM) for x in arrays])


def pair_sort_kernel(live_ref, pairs_ref, keys_ref, ends_ref):
    live = live_ref[0, 0]
    sub = lax.broadcasted_iota(jnp.int32, (ROWS, LANES), 0)
    lane = lax.broadcasted_iota(jnp.int32, (ROWS, LANES), 1)
    regs = []
    for v in range(32):
        rows = slice(v * ROWS, (v + 1) * ROWS)
        slot = v * 1024 + sub * LANES + lane
        head = pairs_ref[0, rows, :]
        tail = pairs_ref[1, rows, :] - 7 * BLOCK
        own = tail - BLOCK
        inside = (own >= 0) & (own < 8 * BLOCK)
        tail = jnp.where(inside, jnp.maximum(own, head) + BLOCK, tail)
        head = jnp.where(inside, jnp.minimum(own, head), head)
        bucket = lax.shift_right_logical(tail, 10)
        bucket = jnp.where(inside, bucket + 2, jnp.where(bucket >= 18, bucket - 16, bucket))
        turn = -(bucket & 1) & (8 * BLOCK - 1)
        key = (bucket << 24) | ((head ^ turn) << 10) | (tail & (BUCKET - 1))
        regs.append(jnp.where(slot < live, key, DEAD))
    place = (
        [("v", k) for k in range(4)]
        + [("s", k) for k in range(3)]
        + [("v", 4)]
        + [("l", k) for k in range(7)]
    )
    regs = sort_network(regs, place, 15)
    beyond = jnp.zeros((ROWS, LANES), jnp.float32)
    for key in regs:
        beyond = beyond + jnp.where(key < NEAR_BUCKETS << 24, 1.0, 0.0)
    beyond = jnp.sum(jnp.sum(beyond, axis=0, keepdims=True), axis=1, keepdims=True)
    ends_ref[8:16, :] = jnp.broadcast_to(beyond, (ROWS, LANES)).astype(jnp.int32)
    for half in range(2):
        rows = regs[16 * half : 16 * half + 16]
        keys_ref[half] = jnp.concatenate(rows, axis=0).T
        least_head = least_tail = jnp.full((ROWS, LANES), 1 << 20, jnp.int32)
        most_head = most_tail = jnp.full((ROWS, LANES), -1, jnp.int32)
        for key in rows:
            used = key < DEAD
            bucket = lax.shift_right_logical(key, 24)
            head = lax.shift_right_logical(key, 17) & (LANES - 1)
            head = head ^ (-(bucket & 1) & (LANES - 1))
            least_head = jnp.minimum(least_head, jnp.where(used, head, 1 << 20))
            most_head = jnp.maximum(most_head, jnp.where(used, head, -1))
            least_tail = jnp.minimum(least_tail, jnp.where(used, bucket, 1 << 20))
            most_tail = jnp.maximum(most_tail, jnp.where(used, bucket, -1))
        for n, x in enumerate((least_head, most_head, least_tail, most_tail)):
            reduce = jnp.max if n % 2 else jnp.min
            row = 4 * half + n
            bound = (LANES, LANES, BUCKETS, BUCKETS)[n]
            ends_ref[row : row + 1, :] = jnp.minimum(reduce(x, axis=0, keepdims=True), bound)


def pair_sort(live, pairs):
    return pl.pallas_call(
        pair_sort_kernel,
        name="pair_sort",
        out_shape=(
            jax.ShapeDtypeStruct((2, LANES, LANES), jnp.int32),
            jax.ShapeDtypeStruct((16, LANES), jnp.int32),
        ),
        in_specs=[pl.BlockSpec(memory_space=SMEM), pl.BlockSpec(memory_space=VMEM)],
        compiler_params=params(),
    )(live, pairs)


def group_ends(g, ends, part):
    g = jnp.minimum(g, 2 * LANES - 1)
    at, lane = 4 * (g & 1), g >> 1
    low, high, _ = part
    return (
        ends[at, lane] & -2,
        ends[at + 1, lane],
        jnp.maximum(ends[at + 2, lane], low),
        jnp.minimum(ends[at + 3, lane], high - 1),
    )


def take_items(state, groups, ends, part):
    low, high, heads = part
    items = []
    for _ in range(ROWS):
        g, bucket, head, now, later = state
        place = jnp.minimum(bucket, high) - low
        items.append((jnp.minimum(g, 2 * LANES - 1), jnp.where(g < groups, bucket, -1), head, place))
        ahead = group_ends(g + 2, ends, part)
        more_heads = head + heads <= now[1]
        stay = more_heads | (bucket < now[3])
        head = jnp.where(more_heads, head + heads, jnp.where(stay, now[0], later[0]))
        bucket = jnp.where(more_heads, bucket, jnp.where(stay, bucket + 1, later[2]))
        now = tuple(jnp.where(stay, x, y) for x, y in zip(now, later))
        later = tuple(jnp.where(stay, x, y) for x, y in zip(later, ahead))
        state = (jnp.where(stay, g, g + 1), bucket, head, now, later)
    return items, state


def word_window(words, first, count, pair, low):
    found = jnp.zeros((ROWS, LANES), jnp.int32)
    for u in range(count):
        rows = words[pl.ds(pl.multiple_of((first + u) * ROWS, ROWS), ROWS), :]
        found = jnp.where(pair == u, lane_gather(rows, low), found)
    return found


def pair_gather(k, item, keys_ref, near_words, far_words, heads, slot):
    key_rows, rel_rows, near, far = slot
    g, bucket, first, part = item
    keys = jnp.broadcast_to(keys_ref[g & 1, pl.ds(g >> 1, 1), :], (ROWS, LANES))
    of_bucket = lax.shift_right_logical(keys, 24)
    turn = -(of_bucket & 1) & (8 * BLOCK - 1)
    head = (lax.shift_right_logical(keys, 10) & (8 * BLOCK - 1)) ^ turn
    rel = lax.shift_right_logical(head, 7) - first
    used = (of_bucket == bucket) & (rel >= 0) & (rel < heads)
    key_rows[k : k + 1, :] = jnp.where(used, keys, DEAD)[0:1]
    rel_rows[k : k + 1, :] = rel[0:1]
    near[k] = word_window(near_words, first >> 1, heads // 2, rel >> 1, head & (LANES - 1))
    pair = lax.shift_right_logical(keys, 8) & 3
    far[k] = word_window(far_words, part * 4, 4, pair, keys & (LANES - 1))


def pair_values(slot, val, near_largest, far_largest):
    key_rows, rel_rows, near, far = slot
    keys, rel = key_rows[...], rel_rows[...]
    used = keys < DEAD
    turn = -(lax.shift_right_logical(keys, 24) & 1) & (LANES - 1)
    val[0] = rel.astype(jnp.float32)
    val[1] = ((lax.shift_right_logical(keys, 10) & (LANES - 1)) ^ turn).astype(jnp.float32)
    val[2] = (lax.shift_right_logical(keys, 7) & 7).astype(jnp.float32)
    val[3] = (keys & (LANES - 1)).astype(jnp.float32)

    def words(ref, odd):
        return [jnp.where(odd, ref[:, 4 + w, :], ref[:, w, :]) for w in range(4)]

    near_place, near_radius, near_slip = decoded(words(near, (rel & 1) == 1), near_largest)
    far_place, far_radius, far_slip = decoded(words(far, (keys & LANES) != 0), far_largest)
    gap = jnp.zeros((ROWS, LANES), jnp.float32)
    for x, y in zip(far_place, near_place):
        apart = (x - y).astype(jnp.float32)
        gap = gap + apart * apart
    gap = gap * (PLACE_STEP * PLACE_STEP)
    far_ratio = far_radius * lax.rsqrt(gap + far_radius * far_radius)
    near_ratio = near_radius * lax.rsqrt(gap + near_radius * near_radius)
    weight_far = jnp.where(used, piep_coef * far_ratio * far_ratio * far_ratio, 0.0)
    weight_near = jnp.where(used, piep_coef * near_ratio * near_ratio * near_ratio, 0.0)
    for c in range(3):
        for n, part in enumerate(split_two(weight_far * far_slip[c])):
            val[4 + 3 * n + c] = part
        for n, part in enumerate(split_two(weight_near * near_slip[c])):
            val[10 + 3 * n + c] = part


def pair_scatter(k, item, val, head_sum, tail_sum, iota, iota8):
    first, tail_first = item
    parts = [[packed_row(val.at[4 + 3 * n + c], k) for c in range(3)] for n in range(2)]
    heads = spread_rows(packed_row(val.at[0], k), parts, iota)
    hit = one_hot(packed_row(val.at[2], k), iota8[...])
    tails = []
    for n in range(10, 16, 2):
        both = jnp.concatenate([wide(val, n, k), wide(val, n + 1, k)], axis=0)
        tails.append(hit * both.astype(jnp.bfloat16))
    tails = jnp.concatenate(tails, axis=0)
    out = block_product(
        [heads, tails], [one_hot_rows(packed_row(val.at[n], k), iota) for n in (1, 3)]
    )
    for c in range(3):
        head_sum[c, pl.ds(first, 16), :] += out[16 * c : 16 * c + 16] + out[16 * c + 48 : 16 * c + 64]
    at = pl.ds(pl.multiple_of(tail_first, 8), 8)
    for c in range(3):
        tail_sum[c, at, :] += out[8 * c + 96 : 8 * c + 104] + out[8 * c + 120 : 8 * c + 128]


def run_pairs(groups, start, part, ends, keys_ref, near, far, sums, iota, iota8, scratch):
    fill_iota(iota)
    rows = lax.broadcasted_iota(jnp.int32, iota8.shape, 0) & 7
    iota8[...] = rows.astype(jnp.float32).astype(jnp.bfloat16)
    val, a, b = scratch[0], scratch[1:5], scratch[5:9]

    def step(state, slot, pending):
        items, state = take_items(state, groups, ends, part)
        if pending:
            pair_values(a, val, near[1], far[1])
        for k in range(ROWS):
            pair_gather(k, items[k], keys_ref, near[0], far[0], part[2], slot)
            if pending:
                pair_scatter(k, pending[k], val, *sums, iota, iota8)
        return tuple((item[2], item[3] * 8) for item in items), state, items[0][1] >= 0

    now, later = group_ends(start, ends, part), group_ends(start + 1, ends, part)
    state = (start, now[2], now[0], now, later)

    def one(carry):
        pending, state, _ = carry
        carry = step(state, b, pending)
        for x, y in zip(a, b):
            x[...] = y[...]
        return carry

    lax.while_loop(lambda carry: carry[2], one, step(state, a, None))


def near_pairs_kernel(
    ends, keys_ref, words_ref, largest_ref, one_in, other_in,
    heads_ref, one_ref, other_ref,
    shell, shell_words, head_sum, tail_sum, iota, iota8, *scratch,
):
    shell[0:16], shell[16:32] = from_partners("az", one_in[...], other_in[...], True)
    shell_largest = largest_slip(shell, 32)
    for n in range(4):
        code_rows(shell, n, shell_largest, shell_words)
    shell_words[128:160, :] = jnp.zeros((32, LANES), jnp.int32)
    head_sum[...] = jnp.zeros_like(head_sum)
    tail_sum[...] = jnp.zeros_like(tail_sum)
    groups = (ends[8, 0] + LANES - 1) // LANES
    run_pairs(
        groups, jnp.int32(0), (0, NEAR_BUCKETS, NEAR_HEADS), ends, keys_ref,
        (words_ref, largest_ref[...]), (shell_words, shell_largest),
        (head_sum, tail_sum), iota, iota8, scratch,
    )
    heads_ref[...] = head_sum[:, 0:128, :]
    one_ref[...], other_ref[...] = by_partner("az", tail_sum[:, 0:16, :], tail_sum[:, 16:32, :])


def own_pairs_kernel(
    live_ref, ends, keys_ref, words_ref, largest_ref, heads_ref,
    corr_ref,
    head_sum, tail_sum, iota, iota8, *scratch,
):
    head_sum[:, 0:128, :] = heads_ref[...]
    head_sum[:, 128:144, :] = jnp.zeros((3, 16, LANES), jnp.float32)
    tail_sum[...] = jnp.zeros_like(tail_sum)
    groups = (live_ref[0, 0] + LANES - 1) // LANES
    start = jnp.minimum(ends[8, 0] // LANES, 2 * LANES - 1)
    coded = (words_ref, largest_ref[...])
    run_pairs(
        groups, start, (NEAR_BUCKETS, BUCKETS, OWN_HEADS), ends, keys_ref, coded, coded,
        (head_sum, tail_sum), iota, iota8, scratch,
    )
    corr_ref[...] = head_sum[:, 0:128, :] + tail_sum[:, 0:128, :]


def pair_scratch(tail_rows):
    f32, i32 = jnp.float32, jnp.int32
    slot = [
        VMEM((ROWS, LANES), i32),
        VMEM((ROWS, LANES), i32),
        VMEM((ROWS, ROWS, LANES), i32),
        VMEM((ROWS, ROWS, LANES), i32),
    ]
    return [
        VMEM((3, 144, LANES), f32),
        VMEM((3, tail_rows, LANES), f32),
        VMEM((LANES, LANES), jnp.bfloat16),
        VMEM((16, LANES), jnp.bfloat16),
        VMEM((16, ROWS, LANES), f32),
        *slot,
        *slot,
    ]


def near_pairs(ends, keys, words, largest, one, other):
    f32 = jnp.float32
    smem, vmem = pl.BlockSpec(memory_space=SMEM), pl.BlockSpec(memory_space=VMEM)
    return pl.pallas_call(
        near_pairs_kernel,
        name="near_pairs",
        out_shape=(
            jax.ShapeDtypeStruct((3, 128, LANES), f32),
            jax.ShapeDtypeStruct((3, 16, LANES), f32),
            jax.ShapeDtypeStruct((3, 16, LANES), f32),
        ),
        in_specs=[smem, vmem, vmem, vmem, vmem, vmem],
        scratch_shapes=[VMEM((32, ROWS, LANES), f32), VMEM((160, LANES), jnp.int32)]
        + pair_scratch(40),
        compiler_params=params(),
    )(ends, keys, words, largest, one, other)


def own_pairs(live, ends, keys, words, largest, heads):
    smem, vmem = pl.BlockSpec(memory_space=SMEM), pl.BlockSpec(memory_space=VMEM)
    return pl.pallas_call(
        own_pairs_kernel,
        name="own_pairs",
        out_shape=jax.ShapeDtypeStruct((3, 128, LANES), jnp.float32),
        in_specs=[smem, smem, vmem, vmem, vmem, vmem],
        scratch_shapes=pair_scratch(136),
        compiler_params=params(),
    )(live, ends, keys, words, largest, heads)


def force_gather(block, keys_ref, table_ref, total_ref, slot):
    force, got, val = slot
    rows = rows_of(block)
    scale = (-2.0 * drag_coef) * table_ref[rows, 6, :]
    for c in range(3):
        push = scale * (table_ref[rows, 3 + c, :] + total_ref[c, rows, :])
        force[:, c, :] = push[0:8]
        force[:, 4 + c, :] = push[8:16]
    keys = keys_ref[rows, :]
    val[0] = lax.shift_right_logical(keys, 19).astype(jnp.float32)
    val[1] = (lax.shift_right_logical(keys, 11) & (2 * LANES - 1)).astype(jnp.float32)
    inner = lax.shift_right_logical(keys, 7) & 7
    low = keys & (LANES - 1)
    tables = [force[k] for k in range(ROWS)]
    for g in range(16):
        pick = jnp.broadcast_to(inner[g : g + 1, :], (ROWS, LANES))
        at = jnp.broadcast_to(low[g : g + 1, :], (ROWS, LANES))
        found = jnp.zeros((ROWS, LANES), jnp.float32)
        for k in range(ROWS):
            found = jnp.where(pick == k, lane_gather(tables[k], at), found)
        got[g] = found
    upper = (keys & 1024) != 0
    for c in range(3):
        pushed = jnp.where(upper, got[:, 4 + c, :], got[:, c, :])
        for n, part in enumerate(split_two(pushed)):
            val[2 + 2 * c + n] = part


def force_rows(g, base, slot, iota):
    val = slot[2]

    def row(n):
        if isinstance(g, int):
            return packed_row(val.at[n], g)
        return jnp.broadcast_to(val[n, pl.ds(g, 1), :], (16, LANES)).astype(jnp.bfloat16)

    rel = row(0) - base.astype(jnp.float32).astype(jnp.bfloat16)
    parts = [[row(2 + 2 * c + n) for c in range(3)] for n in range(2)]
    return spread_rows(rel, parts, iota), one_hot_rows(row(1), iota)


def force_add(groups, bases, slot, cells, iota):
    pieces = [force_rows(g, base, slot, iota) for g, base in zip(groups, bases)]
    out = block_product([p[0] for p in pieces], [p[1] for p in pieces])
    for n, base in enumerate(bases):
        for c in range(3):
            at = 96 * n + 16 * c
            total = out[at : at + 16] + out[at + 48 : at + 64]
            for half in range(2):
                part = total[:, half * LANES : (half + 1) * LANES]
                cells[2 * c + half, pl.ds(base, 16), :] += part


def force_rest(block, ends, slot, cells, iota):
    @pl.when(ends[2, block * 16] >= 16)
    def _():
        def one(g, carry):
            first, most = ends[0, block * 16 + g], ends[1, block * 16 + g]

            def trip(t, carry):
                force_add([g], [jnp.minimum(first + 16 * t, LANES)], slot, cells, iota)
                return carry

            lax.fori_loop(1, (most - first) // 16 + 1, trip, 0)
            return carry

        lax.fori_loop(0, 16, one, 0)


def deposit_step(gather, scatter, ends, keys_ref, table_ref, total_ref, cells, iota):
    if gather:
        force_gather(gather[0], keys_ref, table_ref, total_ref, gather[1])
    if scatter:
        for g in range(16):
            force_add([g], [ends[0, scatter[0] * 16 + g]], scatter[1], cells, iota)
        force_rest(scatter[0], ends, scatter[1], cells, iota)


def deposit_kernel(
    ends, keys_ref, table_ref, corr_ref, one_in, other_in,
    out_ref, total_ref, one_ref, other_ref,
    cells, iota, force_a, got_a, val_a, force_b, got_b, val_b,
):
    fill_iota(iota)
    cells[...] = jnp.zeros_like(cells)
    total_ref[...] = corr_ref[...]
    before, after = from_partners("az", one_in[...], other_in[...], True)
    total_ref[:, 0:16, :] += before
    total_ref[:, 112:128, :] += after
    a, b = (force_a, got_a, val_a), (force_b, got_b, val_b)
    step = functools.partial(
        deposit_step, ends=ends, keys_ref=keys_ref, table_ref=table_ref, total_ref=total_ref,
        cells=cells, iota=iota,
    )
    step((0, a), None)

    def two(k, carry):
        block = 2 * k
        step((block + 1, b), (block, a))
        step((block + 2, a), (block + 1, b))
        return carry

    lax.fori_loop(0, 3, two, 0)
    step((7, b), (6, a))
    step(None, (7, b))
    for c in range(3):
        for half in range(2):
            columns = slice(half * LANES, (half + 1) * LANES)
            out_ref[c, :, columns] = cells[2 * c + half, 0:128, :]
            one, other = by_partner(
                "ax", cells[2 * c + half, 0:32, :], cells[2 * c + half, 96:128, :]
            )
            one_ref[c, :, columns] = one
            other_ref[c, :, columns] = other


def deposits(ends, keys, table, corr, one, other):
    f32 = jnp.float32
    smem, vmem = pl.BlockSpec(memory_space=SMEM), pl.BlockSpec(memory_space=VMEM)
    slot = [VMEM((ROWS, ROWS, LANES), f32), VMEM((16, ROWS, LANES), f32), VMEM((8, 16, LANES), f32)]
    return pl.pallas_call(
        deposit_kernel,
        name="deposits",
        out_shape=(
            jax.ShapeDtypeStruct((3, 128, 2 * LANES), f32),
            jax.ShapeDtypeStruct((3, 128, LANES), f32),
            jax.ShapeDtypeStruct((3, 32, 2 * LANES), f32),
            jax.ShapeDtypeStruct((3, 32, 2 * LANES), f32),
        ),
        in_specs=[smem] + [vmem] * 5,
        scratch_shapes=[VMEM((6, 144, LANES), f32), VMEM((2 * LANES, LANES), jnp.bfloat16)]
        + slot
        + slot,
        compiler_params=params(),
    )(ends, keys, table, corr, one, other)


def axial_kernel(taps, cells_ref, one_in, other_in, out_ref, one_ref, other_ref, first_ref, last_ref):
    for c in range(3):
        before, after = from_partners("ax", one_in[c], other_in[c])
        padded = jnp.concatenate([before, cells_ref[c], after], axis=0)
        total = taps[0] * padded[0:128]
        for k in range(1, 5):
            total = total + taps[k] * padded[16 * k : 16 * k + 128]
        out_ref[c] = total
        for a in range(8):
            first_ref[2 * a : 2 * a + 2, :] = total[16 * a : 16 * a + 2]
            last_ref[2 * a : 2 * a + 2, :] = total[16 * a + 14 : 16 * a + 16]
        one_ref[c], other_ref[c] = by_partner("rad", first_ref[...], last_ref[...])


def radial_kernel(
    taps, cells_ref, one_in, other_in, out_ref, one_ref, other_ref, padded, before_ref, after_ref
):
    lane = lax.broadcasted_iota(jnp.int32, (LANES, LANES), 1)
    edges = jnp.zeros((LANES, LANES), jnp.float32)
    for c in range(3):
        before_ref[...], after_ref[...] = from_partners("rad", one_in[c], other_in[c])
        for a in range(8):
            padded[0:2, :] = before_ref[2 * a : 2 * a + 2, :]
            padded[2:18, :] = cells_ref[c, 16 * a : 16 * a + 16, :]
            padded[18:20, :] = after_ref[2 * a : 2 * a + 2, :]
            total = taps[0] * padded[0:16, :]
            for k in range(1, 5):
                total = total + taps[k] * padded[k : k + 16, :]
            out_ref[c, 16 * a : 16 * a + 16, :] = total
        left, right = out_ref[c, :, 0:LANES], out_ref[c, :, LANES:]
        if c:
            left = pltpu.roll(left, 2 * c, 1)
        right = pltpu.roll(right, 10 + 2 * c, 1)
        edges = jnp.where((lane >> 1) == c, left, edges)
        edges = jnp.where((lane >> 1) == 4 + c, right, edges)
    turned = edges.T
    one_ref[...], other_ref[...] = by_partner("az", turned[0:8], turned[8:16])


def inner_azimuthal_kernel(taps, cells_ref, out_ref):
    lane = lax.broadcasted_iota(jnp.int32, (LANES, LANES), 1)
    for c in range(3):
        left, right = cells_ref[c, :, 0:LANES], cells_ref[c, :, LANES:]
        out_left, out_right = taps[2] * left, taps[2] * right
        for k in (1, 2):
            tap = taps[2 + k]
            inner = lane < LANES - k
            x, y = (pltpu.roll(v, LANES - k, 1) for v in (left, right))
            out_left = out_left + tap * jnp.where(inner, x, y)
            out_right = out_right + tap * jnp.where(inner, y, 0.0)
            inner = lane >= k
            x, y = (pltpu.roll(v, k, 1) for v in (left, right))
            out_left = out_left + tap * jnp.where(inner, x, 0.0)
            out_right = out_right + tap * jnp.where(inner, y, x)
        out_ref[c, :, 0:LANES] = out_left
        out_ref[c, :, LANES:] = out_right


def azimuthal_kernel(taps, inner_ref, one_in, other_in, out_ref):
    lane = lax.broadcasted_iota(jnp.int32, (LANES, LANES), 1)
    rest = jnp.zeros((LANES - 16, LANES), jnp.float32)
    before, after = from_partners("az", one_in[...], other_in[...], True)
    edges = jnp.concatenate([after, before, rest], axis=0).T
    for c in range(3):
        out_left, out_right = inner_ref[c, :, 0:LANES], inner_ref[c, :, LANES:]
        for k in (1, 2):
            x = pltpu.roll(edges, (118 - 2 * c + k) % LANES, 1)
            out_left = out_left + taps[2 - k] * jnp.where(lane < k, x, 0.0)
            y = pltpu.roll(edges, LANES - 2 * c - k, 1)
            out_right = out_right + taps[2 + k] * jnp.where(lane >= LANES - k, y, 0.0)
        out_ref[c, :, 0:LANES] = out_left
        out_ref[c, :, LANES:] = out_right


def filtered(deposit, one, other):
    f32 = jnp.float32
    raw = [math.exp(-0.5 * k * k) for k in range(-2, 3)]
    taps = [x / sum(raw) for x in raw]
    whole = jax.ShapeDtypeStruct(deposit.shape, f32)
    radial_face = jax.ShapeDtypeStruct((3, 16, 2 * LANES), f32)
    edge = jax.ShapeDtypeStruct((8, LANES), f32)
    cells, one, other = pl.pallas_call(
        functools.partial(axial_kernel, taps),
        name="axial_filter",
        out_shape=(whole, radial_face, radial_face),
        scratch_shapes=[VMEM((16, 2 * LANES), f32)] * 2,
        compiler_params=params(),
    )(deposit, *swapped(one, other, "ax"))
    cells, one, other = pl.pallas_call(
        functools.partial(radial_kernel, taps),
        name="radial_filter",
        out_shape=(whole, edge, edge),
        scratch_shapes=[VMEM((24, 2 * LANES), f32)] + [VMEM((16, 2 * LANES), f32)] * 2,
        compiler_params=params(),
    )(cells, *swapped(one, other, "rad"))
    one, other = swapped(one, other, "az", True)
    inner = pl.pallas_call(
        functools.partial(inner_azimuthal_kernel, taps),
        name="inner_azimuthal_filter",
        out_shape=whole,
        compiler_params=params(),
    )(cells)
    return pl.pallas_call(
        functools.partial(azimuthal_kernel, taps),
        name="azimuthal_filter",
        out_shape=whole,
        compiler_params=params(),
    )(inner, one, other)


def swapped(one, other, axis, wrap=False):
    count = lax.axis_size(axis)

    def partner(i, odd):
        j = i + 1 if i % 2 == odd else i - 1
        return j % count if wrap or 0 <= j < count else i

    return [
        lax.ppermute(x, axis, [(i, partner(i, odd)) for i in range(count)])
        for odd, x in enumerate((one, other))
    ]


def per_device(positions, velocity, diameter, cell_index, pair_list, live_pairs, gas_velocity):
    live = live_pairs.reshape(1, 1)
    cells = cell_index.reshape(128, LANES)
    gas = gas_velocity.reshape(3, 128, 2 * LANES)
    pos = positions.reshape(3, 128, LANES)
    vel = velocity.reshape(3, 128, LANES)
    diam = diameter.reshape(128, LANES)
    cell_keys, cell_ends, table, words, largest, one, other = droplet_states(
        cells, gas, pos, vel, diam
    )
    one, other = swapped(one, other, "az", True)
    pair_keys, pair_ends = pair_sort(live, pair_list.reshape(2, 256, LANES))
    heads, one, other = near_pairs(pair_ends, pair_keys, words, largest, one, other)
    one, other = swapped(one, other, "az", True)
    corr = own_pairs(live, pair_ends, pair_keys, words, largest, heads)
    deposit, correction, one, other = deposits(cell_ends, cell_keys, table, corr, one, other)
    smoothed = filtered(deposit, one, other)
    return (correction.reshape(positions.shape), smoothed.reshape(gas_velocity.shape))


def solution(mesh):
    return jax.shard_map(
        per_device,
        mesh=mesh,
        in_specs=(
            P(None, "ax", "rad", "az"),
            P(None, "ax", "rad", "az"),
            P("ax", "rad", "az"),
            P("ax", "rad", "az"),
            P(None, "ax", "rad", "az"),
            P("ax", "rad", "az"),
            P(None, "ax", "rad", "az"),
        ),
        out_specs=(P(None, "ax", "rad", "az"), P(None, "ax", "rad", "az")),
        check_vma=False,
    )
```

```python
import functools
import math

import jax
import jax.numpy as jnp
from jax import lax
from jax.experimental import pallas as pl
from jax.experimental.pallas import tpu as pltpu
from jax.sharding import PartitionSpec as P

piep_coef = 1.0
drag_coef = 20.0

LANES = 128
ROWS = 8
BLOCK = 2048
GAS_WINDOW = 12
BUCKET = 1024
BUCKETS = 20
NEAR_BUCKETS = 4
NEAR_HEADS = 8
OWN_HEADS = 12
DEAD = 1 << 29

NT = (((1,), (1,)), ((), ()))
VMEM = pltpu.VMEM
SMEM = pltpu.SMEM


def params(megabytes=40):
    return pltpu.CompilerParams(vmem_limit_bytes=megabytes << 20)


def lane_gather(table, index):
    numbers = lax.GatherDimensionNumbers(
        offset_dims=(),
        collapsed_slice_dims=(1,),
        start_index_map=(1,),
        operand_batching_dims=(0,),
        start_indices_batching_dims=(0,),
    )
    return lax.gather(
        table,
        index[..., None],
        numbers,
        slice_sizes=(1, 1),
        mode=lax.GatherScatterMode.PROMISE_IN_BOUNDS,
    )


def sort_network(regs, place, levels):
    sub = lax.broadcasted_iota(jnp.int32, (ROWS, LANES), 0)
    lane = lax.broadcasted_iota(jnp.int32, (ROWS, LANES), 1)
    count = len(regs)

    def bit_fill(bit, v):
        if bit >= levels:
            return 0
        kind, k = place[bit]
        if kind == "v":
            return -((v >> k) & 1)
        return -(((sub if kind == "s" else lane) >> k) & 1)

    flip = [0] * count
    for level in range(1, levels + 1):
        fills = {}
        for v in range(count):
            kind, k = place[level] if level < levels else ("v", 99)
            key = (v >> k) & 1 if kind == "v" else 0
            if key not in fills:
                fills[key] = bit_fill(level, v)
            new = fills[key]
            if isinstance(new, int) and isinstance(flip[v], int):
                if new != flip[v]:
                    regs[v] = ~regs[v]
            else:
                regs[v] = regs[v] ^ (new ^ flip[v])
            flip[v] = new
        for bit in reversed(range(level)):
            kind, k = place[bit]
            step = 1 << k
            if kind == "v":
                for v in range(count):
                    if not v & step:
                        a, b = regs[v], regs[v | step]
                        regs[v], regs[v | step] = jnp.minimum(a, b), jnp.maximum(a, b)
            else:
                axis, size, where = (0, ROWS, sub) if kind == "s" else (1, LANES, lane)
                lower = (where & step) == 0
                for v in range(count):
                    x = regs[v]
                    ahead = pltpu.roll(x, size - step, axis)
                    behind = ahead if 2 * step == size else pltpu.roll(x, step, axis)
                    regs[v] = jnp.where(lower, jnp.minimum(x, ahead), jnp.maximum(x, behind))
    return regs


def split_two(x):
    high = x.astype(jnp.bfloat16).astype(jnp.float32)
    return high, x - high


def split_three(x):
    high, rest = split_two(x)
    mid, low = split_two(rest)
    return high, mid, low


def packed_row(ref, row):
    return jnp.broadcast_to(ref[row : row + 1, :], (16, LANES)).astype(jnp.bfloat16)


def one_hot_rows(low, iota):
    one = jnp.ones((16, LANES), jnp.bfloat16)
    zero = jnp.zeros((16, LANES), jnp.bfloat16)
    return jnp.concatenate(
        [jnp.where(low == iota[k : k + 16, :], one, zero) for k in range(0, iota.shape[0], 16)],
        axis=0,
    )


def spread_rows(rel, parts, iota):
    hit = rel == iota[0:16, :]
    zero = jnp.zeros((16, LANES), jnp.bfloat16)
    return jnp.concatenate([jnp.where(hit, p, zero) for part in parts for p in part], axis=0)


def block_product(rows, hots):
    zero = jnp.zeros
    lines = [
        jnp.concatenate(
            [x if m == n else zero(x.shape, x.dtype) for m in range(len(rows))], axis=1
        )
        for n, x in enumerate(rows)
    ]
    return lax.dot_general(
        jnp.concatenate(lines, axis=0),
        jnp.concatenate(hots, axis=1),
        NT,
        preferred_element_type=jnp.float32,
    )


def spread_add(rows, hots):
    out = lax.dot_general(
        jnp.concatenate(rows, axis=1) if len(rows) > 1 else rows[0],
        jnp.concatenate(hots, axis=1) if len(hots) > 1 else hots[0],
        NT,
        preferred_element_type=jnp.float32,
    )
    total = out[0:48]
    for s in range(48, out.shape[0], 48):
        total = total + out[s : s + 48]
    return total


def fill_iota(iota):
    rows = lax.broadcasted_iota(jnp.int32, iota.shape, 0)
    iota[...] = rows.astype(jnp.float32).astype(jnp.bfloat16)


def rows_of(block):
    start = block * 16
    return pl.ds(start if isinstance(block, int) else pl.multiple_of(start, 16), 16)


def wide(ref, *at):
    return jnp.broadcast_to(ref[at[:-1] + (slice(at[-1], at[-1] + 1),)], (ROWS, LANES))


def window(table, first, count, row, low, found):
    rel = row - first
    for u in range(count):
        found = jnp.where(rel == u, lane_gather(table[first + u], low), found)
    return found


def running_max(x, count):
    x = jnp.broadcast_to(x, (ROWS, LANES))
    step = 1
    while step < count:
        x = jnp.maximum(x, pltpu.roll(x, LANES - step, 1))
        step *= 2
    return x


def by_partner(axis, first, last):
    even = (lax.axis_index(axis) & 1) == 0
    return jnp.where(even, last, first), jnp.where(even, first, last)


def from_partners(axis, one, other, wrap=False):
    at, count = lax.axis_index(axis), lax.axis_size(axis)
    even = (at & 1) == 0
    before, after = jnp.where(even, other, one), jnp.where(even, one, other)
    if wrap:
        return before, after
    return jnp.where(at > 0, before, 0.0), jnp.where(at < count - 1, after, 0.0)


PLACE_STEP = 0.1 / 65535.0
RADIUS_LEAST = 0.01
RADIUS_STEP = 0.04 / 65535.0
SLIP_HALF = 1 << 20


def largest_slip(table, rows):
    most = jnp.zeros((ROWS, LANES), jnp.float32)
    for n in range(0, rows, ROWS):
        for c in range(3):
            most = jnp.maximum(most, jnp.abs(table[n : n + ROWS, 3 + c, :]))
    most = jnp.max(jnp.max(most, axis=0, keepdims=True), axis=1, keepdims=True)
    return jnp.broadcast_to(jnp.maximum(most, 1e-30), (ROWS, LANES))


def code_rows(table, n, largest, words):
    rows = pl.ds(n * ROWS, ROWS)

    def whole(c, least, step):
        x = ((table[rows, c, :] - least) * (1.0 / step) + 0.5).astype(jnp.int32)
        return jnp.clip(x, 0, 65535)

    x, y, z = (whole(c, 0.0, PLACE_STEP) for c in range(3))
    radius = whole(6, RADIUS_LEAST, RADIUS_STEP)
    scale = (SLIP_HALF - 1.0) / largest
    u, v, w = (
        (table[rows, 3 + c, :] * scale + (SLIP_HALF + 0.5)).astype(jnp.int32) for c in range(3)
    )
    coded = (
        x | (y << 16),
        z | (radius << 16),
        u | ((w & 2047) << 21),
        v | (lax.shift_right_logical(w, 11) << 21),
    )
    for k, word in enumerate(coded):
        words[pl.ds(n * 32 + k, ROWS, stride=4), :] = word


def decoded(words, largest):
    low = [x & 65535 for x in words[0:2]]
    high = [lax.shift_right_logical(x, 16) for x in words[0:2]]
    place = (low[0], high[0], low[1])
    radius = high[1].astype(jnp.float32) * RADIUS_STEP + RADIUS_LEAST
    mask = 2 * SLIP_HALF - 1
    third = lax.shift_right_logical(words[2], 21) | (lax.shift_right_logical(words[3], 21) << 11)
    scale = largest * (1.0 / (SLIP_HALF - 1.0))
    slip = [
        (x - SLIP_HALF).astype(jnp.float32) * scale for x in (words[2] & mask, words[3] & mask, third)
    ]
    return place, radius, slip


def fill_gas_rows(gas_ref, gas_rows):
    for r in range(16):
        rows = slice(r * ROWS, (r + 1) * ROWS)
        for c in range(3):
            for half in range(2):
                gas_rows[rows, half * 4 + c, :] = gas_ref[c, rows, half * LANES : (half + 1) * LANES]


def gas_index(block, keys_ref, slot):
    idx = slot[0]
    keys = keys_ref[rows_of(block), :]
    idx[0] = lax.shift_right_logical(keys, 19)
    idx[1] = lax.shift_right_logical(keys, 11) & (LANES - 1)


def gas_gather(block, g, ends, gas_rows, slot):
    idx, found = slot[0], slot[1]
    zero = jnp.zeros((ROWS, LANES), jnp.float32)
    first = ends[0, block * 16 + g]
    found[g] = window(gas_rows, first, GAS_WINDOW, wide(idx, 0, g), wide(idx, 1, g), zero)


def gas_rest(block, ends, gas_rows, slot):
    idx, found = slot[0], slot[1]

    @pl.when(ends[2, block * 16] >= GAS_WINDOW)
    def _():
        def one(g, carry):
            first = ends[0, block * 16 + g]
            row = jnp.broadcast_to(idx[0, pl.ds(g, 1), :], (ROWS, LANES))
            low = jnp.broadcast_to(idx[1, pl.ds(g, 1), :], (ROWS, LANES))

            def trip(t, total):
                base = jnp.minimum(first + GAS_WINDOW * t, LANES)
                return window(gas_rows, base, GAS_WINDOW, row, low, total)

            trips = (ends[1, block * 16 + g] - first) // GAS_WINDOW + 1
            found[g] = lax.fori_loop(1, trips, trip, found[g])
            return carry

        lax.fori_loop(0, 16, one, 0)


def seen_values(block, keys_ref, slot):
    idx, found, val = slot
    keys = keys_ref[rows_of(block), :]
    upper = (keys & (1 << 18)) != 0
    place_in = keys & (BLOCK - 1)
    val[0] = lax.shift_right_logical(place_in, 7).astype(jnp.float32)
    val[1] = (place_in & (LANES - 1)).astype(jnp.float32)
    for c in range(3):
        seen = jnp.where(upper, found[:, 4 + c, :], found[:, c, :])
        for n, part in enumerate(split_three(seen)):
            val[2 + 3 * c + n] = part


def seen_in_order(groups, slot, iota):
    val = slot[2]
    rows, hots = [], []
    for g in groups:
        parts = [[packed_row(val.at[2 + 3 * c + n], g) for c in range(3)] for n in range(3)]
        rows.append(spread_rows(packed_row(val.at[0], g), parts, iota))
        hots.append(one_hot_rows(packed_row(val.at[1], g), iota))
    return spread_add(rows, hots)


def write_states(block, total, pos_ref, vel_ref, diam_ref, out_ref, out_rows):
    rows = rows_of(block)
    for c in range(3):
        out_ref[out_rows, c, :] = pos_ref[c, rows, :]
        out_ref[out_rows, 3 + c, :] = total[16 * c : 16 * c + 16] - vel_ref[c, rows, :]
    out_ref[out_rows, 6, :] = 0.5 * diam_ref[rows, :]
    out_ref[out_rows, 7, :] = jnp.zeros((16, LANES), jnp.float32)


def states_step(gather, scatter, keys_ref, ends, gas_rows, iota, arrays):
    total = jnp.zeros((48, LANES), jnp.float32)
    if gather:
        gas_index(gather[0], keys_ref, gather[1])
    if scatter:
        seen_values(scatter[0], keys_ref, scatter[1])
    for g in range(16):
        if gather:
            gas_gather(gather[0], g, ends, gas_rows, gather[1])
        if scatter and g % 2:
            total = total + seen_in_order((g - 1, g), scatter[1], iota)
    if scatter:
        write_states(scatter[0], total, *arrays, *scatter[2:])
    if gather:
        gas_rest(gather[0], ends, gas_rows, gather[1])


def edge_states_kernel(
    cell_hbm, gas_hbm, pos_hbm, vel_hbm, diam_hbm,
    keys_ref, ends_ref, edges_ref, one_ref, other_ref,
    cell_ref, gas_ref, pos_ref, vel_ref, diam_ref,
    gas_rows, iota, ends, idx_a, found_a, val_a, idx_b, found_b, val_b, sems,
):
    sources = (cell_hbm, gas_hbm, pos_hbm, vel_hbm, diam_hbm)
    places = (cell_ref, gas_ref, pos_ref, vel_ref, diam_ref)
    copies = [
        pltpu.make_async_copy(x, y, sems.at[n]) for n, (x, y) in enumerate(zip(sources, places))
    ]
    for copy in copies:
        copy.start()
    copies[0].wait()
    sub = lax.broadcasted_iota(jnp.int32, (ROWS, LANES), 0)
    lane = lax.broadcasted_iota(jnp.int32, (ROWS, LANES), 1)
    cells = cell_ref[...].T
    regs = []
    for v in range(16):
        own = (lane & 15) * LANES + v * ROWS + sub
        regs.append(cells[v * ROWS : (v + 1) * ROWS] * BLOCK + own)
    place = [("v", k) for k in range(4)] + [("s", k) for k in range(3)] + [("l", k) for k in range(4)]
    regs = sort_network(regs, place, 11)
    keys_ref[...] = jnp.concatenate(regs, axis=0).T
    least = functools.reduce(jnp.minimum, regs)
    most = functools.reduce(jnp.maximum, regs)
    least = lax.shift_right_logical(jnp.min(least, axis=0, keepdims=True), 19)
    most = lax.shift_right_logical(jnp.max(most, axis=0, keepdims=True), 19)
    ends_ref[0:1, :] = least
    ends_ref[1:2, :] = most
    ends_ref[2:8, :] = running_max(most - least, 16)[0:6]
    copy = pltpu.make_async_copy(ends_ref, ends, sems.at[5])
    copy.start()
    copies[1].wait()
    fill_gas_rows(gas_ref, gas_rows)
    for other in copies[2:]:
        other.wait()
    copy.wait()
    fill_iota(iota)
    a, b = (idx_a, found_a, val_a), (idx_b, found_b, val_b)
    step = functools.partial(
        states_step, keys_ref=keys_ref, ends=ends, gas_rows=gas_rows, iota=iota,
        arrays=(pos_ref, vel_ref, diam_ref),
    )
    whole = slice(0, 16)
    step((0, a), None)
    step((7, b), (0, a, edges_ref.at[0], whole))
    step(None, (7, b, edges_ref.at[1], whole))
    one_ref[...], other_ref[...] = by_partner("az", edges_ref[0], edges_ref[1])


def inner_states_kernel(
    live_ref, ends, pairs_ref, keys_ref, edges_ref, gas_hbm, pos_hbm, vel_hbm, diam_hbm,
    pair_keys_ref, pair_ends_ref, table_ref, words_ref, largest_ref,
    gas_ref, pos_ref, vel_ref, diam_ref,
    gas_rows, iota, idx_a, found_a, val_a, idx_b, found_b, val_b, sems,
):
    sources = (gas_hbm, pos_hbm, vel_hbm, diam_hbm)
    places = (gas_ref, pos_ref, vel_ref, diam_ref)
    copies = [
        pltpu.make_async_copy(x, y, sems.at[n]) for n, (x, y) in enumerate(zip(sources, places))
    ]
    for copy in copies:
        copy.start()
    pair_sort(live_ref, pairs_ref, pair_keys_ref, pair_ends_ref)
    for copy in copies:
        copy.wait()
    fill_gas_rows(gas_ref, gas_rows)
    fill_iota(iota)
    a, b = (idx_a, found_a, val_a), (idx_b, found_b, val_b)
    step = functools.partial(
        states_step, keys_ref=keys_ref, ends=ends, gas_rows=gas_rows, iota=iota,
        arrays=(pos_ref, vel_ref, diam_ref),
    )
    table_ref[0:16] = edges_ref[0]
    table_ref[112:128] = edges_ref[1]
    step((1, a), None)

    def two(k, carry):
        block = 2 * k + 1
        step((block + 1, b), (block, a, table_ref, rows_of(block)))
        step((block + 2, a), (block + 1, b, table_ref, rows_of(block + 1)))
        return carry

    lax.fori_loop(0, 2, two, 0)
    step((6, b), (5, a, table_ref, rows_of(5)))
    step(None, (6, b, table_ref, rows_of(6)))
    largest = largest_slip(table_ref, 128)
    largest_ref[...] = largest
    for n in range(16):
        code_rows(table_ref, n, largest, words_ref)
    words_ref[512:576, :] = jnp.zeros((64, LANES), jnp.int32)


def slots(rows, parts, dtype=jnp.float32):
    one = [VMEM((2, 16, LANES), jnp.int32), VMEM((16, ROWS, LANES), dtype), VMEM((parts, rows, LANES), dtype)]
    return one + one


def in_hbm(arrays):
    return [pltpu.with_memory_space_constraint(x, pltpu.HBM) for x in arrays]


def edge_states(cells, gas, pos, vel, diam):
    f32, i32 = jnp.float32, jnp.int32
    arrays = (cells, gas, pos, vel, diam)
    return pl.pallas_call(
        edge_states_kernel,
        name="edge_states",
        out_shape=(
            jax.ShapeDtypeStruct((128, LANES), i32),
            jax.ShapeDtypeStruct((ROWS, LANES), i32),
            jax.ShapeDtypeStruct((2, 16, ROWS, LANES), f32),
            jax.ShapeDtypeStruct((16, ROWS, LANES), f32),
            jax.ShapeDtypeStruct((16, ROWS, LANES), f32),
        ),
        in_specs=[pl.BlockSpec(memory_space=pltpu.HBM)] * 5,
        scratch_shapes=[VMEM(x.shape, x.dtype) for x in arrays]
        + [VMEM((144, ROWS, LANES), f32), VMEM((LANES, LANES), jnp.bfloat16), SMEM((ROWS, LANES), i32)]
        + slots(16, 11)
        + [pltpu.SemaphoreType.DMA((6,))],
        compiler_params=params(),
    )(*in_hbm(arrays))


def inner_states(live, ends, pairs, keys, edges, *arrays):
    f32, i32 = jnp.float32, jnp.int32
    smem, vmem = pl.BlockSpec(memory_space=SMEM), pl.BlockSpec(memory_space=VMEM)
    return pl.pallas_call(
        inner_states_kernel,
        name="inner_states",
        out_shape=(
            jax.ShapeDtypeStruct((2, LANES, LANES), i32),
            jax.ShapeDtypeStruct((16, LANES), i32),
            jax.ShapeDtypeStruct((128, ROWS, LANES), f32),
            jax.ShapeDtypeStruct((576, LANES), i32),
            jax.ShapeDtypeStruct((ROWS, LANES), f32),
        ),
        in_specs=[smem, smem, vmem, vmem, vmem] + [pl.BlockSpec(memory_space=pltpu.HBM)] * 4,
        scratch_shapes=[VMEM(x.shape, x.dtype) for x in arrays]
        + [VMEM((144, ROWS, LANES), f32), VMEM((LANES, LANES), jnp.bfloat16)]
        + slots(16, 11)
        + [pltpu.SemaphoreType.DMA((4,))],
        compiler_params=params(),
    )(live, ends, pairs, keys, edges, *in_hbm(arrays))


def pair_sort(live_ref, pairs_ref, keys_ref, ends_ref):
    live = live_ref[0, 0]
    sub = lax.broadcasted_iota(jnp.int32, (ROWS, LANES), 0)
    lane = lax.broadcasted_iota(jnp.int32, (ROWS, LANES), 1)
    regs = []
    for v in range(32):
        rows = slice(v * ROWS, (v + 1) * ROWS)
        slot = v * 1024 + sub * LANES + lane
        head = pairs_ref[0, rows, :]
        tail = pairs_ref[1, rows, :] - 7 * BLOCK
        own = tail - BLOCK
        inside = (own >= 0) & (own < 8 * BLOCK)
        tail = jnp.where(inside, jnp.maximum(own, head) + BLOCK, tail)
        head = jnp.where(inside, jnp.minimum(own, head), head)
        bucket = lax.shift_right_logical(tail, 10)
        bucket = jnp.where(inside, bucket + 2, jnp.where(bucket >= 18, bucket - 16, bucket))
        turn = -(bucket & 1) & (8 * BLOCK - 1)
        key = (bucket << 24) | ((head ^ turn) << 10) | (tail & (BUCKET - 1))
        regs.append(jnp.where(slot < live, key, DEAD))
    place = (
        [("v", k) for k in range(4)]
        + [("s", k) for k in range(3)]
        + [("v", 4)]
        + [("l", k) for k in range(7)]
    )
    regs = sort_network(regs, place, 15)
    beyond = jnp.zeros((ROWS, LANES), jnp.float32)
    for key in regs:
        beyond = beyond + jnp.where(key < NEAR_BUCKETS << 24, 1.0, 0.0)
    beyond = jnp.sum(jnp.sum(beyond, axis=0, keepdims=True), axis=1, keepdims=True)
    ends_ref[8:16, :] = jnp.broadcast_to(beyond, (ROWS, LANES)).astype(jnp.int32)
    for half in range(2):
        rows = regs[16 * half : 16 * half + 16]
        keys_ref[half] = jnp.concatenate(rows, axis=0).T
        least_head = least_tail = jnp.full((ROWS, LANES), 1 << 20, jnp.int32)
        most_head = most_tail = jnp.full((ROWS, LANES), -1, jnp.int32)
        for key in rows:
            used = key < DEAD
            bucket = lax.shift_right_logical(key, 24)
            head = lax.shift_right_logical(key, 17) & (LANES - 1)
            head = head ^ (-(bucket & 1) & (LANES - 1))
            least_head = jnp.minimum(least_head, jnp.where(used, head, 1 << 20))
            most_head = jnp.maximum(most_head, jnp.where(used, head, -1))
            least_tail = jnp.minimum(least_tail, jnp.where(used, bucket, 1 << 20))
            most_tail = jnp.maximum(most_tail, jnp.where(used, bucket, -1))
        for n, x in enumerate((least_head, most_head, least_tail, most_tail)):
            reduce = jnp.max if n % 2 else jnp.min
            row = 4 * half + n
            bound = (LANES, LANES, BUCKETS, BUCKETS)[n]
            ends_ref[row : row + 1, :] = jnp.minimum(reduce(x, axis=0, keepdims=True), bound)


def group_ends(g, ends, part):
    g = jnp.minimum(g, 2 * LANES - 1)
    at, lane = 4 * (g & 1), g >> 1
    low, high, _ = part
    return (
        ends[at, lane] & -2,
        ends[at + 1, lane],
        jnp.maximum(ends[at + 2, lane], low),
        jnp.minimum(ends[at + 3, lane], high - 1),
    )


def take_items(state, groups, ends, part):
    low, high, heads = part
    items = []
    for _ in range(ROWS):
        g, bucket, head, now, later = state
        place = jnp.minimum(bucket, high) - low
        items.append((jnp.minimum(g, 2 * LANES - 1), jnp.where(g < groups, bucket, -1), head, place))
        ahead = group_ends(g + 2, ends, part)
        more_heads = head + heads <= now[1]
        stay = more_heads | (bucket < now[3])
        head = jnp.where(more_heads, head + heads, jnp.where(stay, now[0], later[0]))
        bucket = jnp.where(more_heads, bucket, jnp.where(stay, bucket + 1, later[2]))
        now = tuple(jnp.where(stay, x, y) for x, y in zip(now, later))
        later = tuple(jnp.where(stay, x, y) for x, y in zip(later, ahead))
        state = (jnp.where(stay, g, g + 1), bucket, head, now, later)
    return items, state


def word_window(words, first, count, pair, low):
    found = jnp.zeros((ROWS, LANES), jnp.int32)
    for u in range(count):
        rows = words[pl.ds(pl.multiple_of((first + u) * ROWS, ROWS), ROWS), :]
        found = jnp.where(pair == u, lane_gather(rows, low), found)
    return found


def pair_gather(k, item, keys_ref, near_words, far_words, heads, slot):
    key_rows, rel_rows, near, far = slot
    g, bucket, first, part = item
    keys = jnp.broadcast_to(keys_ref[g & 1, pl.ds(g >> 1, 1), :], (ROWS, LANES))
    of_bucket = lax.shift_right_logical(keys, 24)
    turn = -(of_bucket & 1) & (8 * BLOCK - 1)
    head = (lax.shift_right_logical(keys, 10) & (8 * BLOCK - 1)) ^ turn
    rel = lax.shift_right_logical(head, 7) - first
    used = (of_bucket == bucket) & (rel >= 0) & (rel < heads)
    key_rows[k : k + 1, :] = jnp.where(used, keys, DEAD)[0:1]
    rel_rows[k : k + 1, :] = rel[0:1]
    near[k] = word_window(near_words, first >> 1, heads // 2, rel >> 1, head & (LANES - 1))
    pair = lax.shift_right_logical(keys, 8) & 3
    far[k] = word_window(far_words, part * 4, 4, pair, keys & (LANES - 1))


def pair_values(slot, val, near_largest, far_largest):
    key_rows, rel_rows, near, far = slot
    keys, rel = key_rows[...], rel_rows[...]
    used = keys < DEAD
    turn = -(lax.shift_right_logical(keys, 24) & 1) & (LANES - 1)
    val[0] = rel.astype(jnp.float32)
    val[1] = ((lax.shift_right_logical(keys, 10) & (LANES - 1)) ^ turn).astype(jnp.float32)
    val[2] = (lax.shift_right_logical(keys, 7) & 7).astype(jnp.float32)
    val[3] = (keys & (LANES - 1)).astype(jnp.float32)

    def words(ref, odd):
        return [jnp.where(odd, ref[:, 4 + w, :], ref[:, w, :]) for w in range(4)]

    near_place, near_radius, near_slip = decoded(words(near, (rel & 1) == 1), near_largest)
    far_place, far_radius, far_slip = decoded(words(far, (keys & LANES) != 0), far_largest)
    gap = jnp.zeros((ROWS, LANES), jnp.float32)
    for x, y in zip(far_place, near_place):
        apart = (x - y).astype(jnp.float32)
        gap = gap + apart * apart
    gap = gap * (PLACE_STEP * PLACE_STEP)
    far_ratio = far_radius * lax.rsqrt(gap + far_radius * far_radius)
    near_ratio = near_radius * lax.rsqrt(gap + near_radius * near_radius)
    weight_far = jnp.where(used, piep_coef * far_ratio * far_ratio * far_ratio, 0.0)
    weight_near = jnp.where(used, piep_coef * near_ratio * near_ratio * near_ratio, 0.0)
    for c in range(3):
        for n, part in enumerate(split_two(weight_far * far_slip[c])):
            val[4 + 3 * n + c] = part
        for n, part in enumerate(split_two(weight_near * near_slip[c])):
            val[10 + 3 * n + c] = part


def pair_scatter(k, item, val, head_sum, tail_sum, iota, iota8):
    first, tail_first = item
    parts = [[packed_row(val.at[4 + 3 * n + c], k) for c in range(3)] for n in range(2)]
    heads = spread_rows(packed_row(val.at[0], k), parts, iota)
    hit = packed_row(val.at[2], k) == iota8[...]
    zero = jnp.zeros((16, LANES), jnp.bfloat16)
    tails = []
    for n in range(10, 16, 2):
        both = jnp.concatenate([wide(val, n, k), wide(val, n + 1, k)], axis=0)
        tails.append(jnp.where(hit, both.astype(jnp.bfloat16), zero))
    tails = jnp.concatenate(tails, axis=0)
    out = block_product(
        [heads, tails], [one_hot_rows(packed_row(val.at[n], k), iota) for n in (1, 3)]
    )
    for c in range(3):
        head_sum[c, pl.ds(first, 16), :] += out[16 * c : 16 * c + 16] + out[16 * c + 48 : 16 * c + 64]
    at = pl.ds(pl.multiple_of(tail_first, 8), 8)
    for c in range(3):
        tail_sum[c, at, :] += out[8 * c + 96 : 8 * c + 104] + out[8 * c + 120 : 8 * c + 128]


def run_pairs(groups, start, part, ends, keys_ref, near, far, sums, iota, iota8, scratch):
    fill_iota(iota)
    rows = lax.broadcasted_iota(jnp.int32, iota8.shape, 0) & 7
    iota8[...] = rows.astype(jnp.float32).astype(jnp.bfloat16)
    val, a, b = scratch[0], scratch[1:5], scratch[5:9]

    def step(state, slot, pending):
        items, state = take_items(state, groups, ends, part)
        if pending:
            pair_values(a, val, near[1], far[1])
        for k in range(ROWS):
            pair_gather(k, items[k], keys_ref, near[0], far[0], part[2], slot)
            if pending:
                pair_scatter(k, pending[k], val, *sums, iota, iota8)
        return tuple((item[2], item[3] * 8) for item in items), state, items[0][1] >= 0

    now, later = group_ends(start, ends, part), group_ends(start + 1, ends, part)
    state = (start, now[2], now[0], now, later)

    def one(carry):
        pending, state, _ = carry
        carry = step(state, b, pending)
        for x, y in zip(a, b):
            x[...] = y[...]
        return carry

    lax.while_loop(lambda carry: carry[2], one, step(state, a, None))


def near_pairs_kernel(
    ends, keys_ref, words_ref, largest_ref, one_in, other_in,
    heads_ref, one_ref, other_ref,
    shell, shell_words, head_sum, tail_sum, iota, iota8, *scratch,
):
    shell[0:16], shell[16:32] = from_partners("az", one_in[...], other_in[...], True)
    shell_largest = largest_slip(shell, 32)
    for n in range(4):
        code_rows(shell, n, shell_largest, shell_words)
    shell_words[128:160, :] = jnp.zeros((32, LANES), jnp.int32)
    head_sum[...] = jnp.zeros_like(head_sum)
    tail_sum[...] = jnp.zeros_like(tail_sum)
    groups = (ends[8, 0] + LANES - 1) // LANES
    run_pairs(
        groups, jnp.int32(0), (0, NEAR_BUCKETS, NEAR_HEADS), ends, keys_ref,
        (words_ref, largest_ref[...]), (shell_words, shell_largest),
        (head_sum, tail_sum), iota, iota8, scratch,
    )
    heads_ref[...] = head_sum[:, 0:128, :]
    one_ref[...], other_ref[...] = by_partner("az", tail_sum[:, 0:16, :], tail_sum[:, 16:32, :])


def own_pairs_kernel(
    live_ref, ends, keys_ref, words_ref, largest_ref, heads_ref,
    corr_ref,
    head_sum, tail_sum, iota, iota8, *scratch,
):
    head_sum[:, 0:128, :] = heads_ref[...]
    head_sum[:, 128:144, :] = jnp.zeros((3, 16, LANES), jnp.float32)
    tail_sum[...] = jnp.zeros_like(tail_sum)
    groups = (live_ref[0, 0] + LANES - 1) // LANES
    start = jnp.minimum(ends[8, 0] // LANES, 2 * LANES - 1)
    coded = (words_ref, largest_ref[...])
    run_pairs(
        groups, start, (NEAR_BUCKETS, BUCKETS, OWN_HEADS), ends, keys_ref, coded, coded,
        (head_sum, tail_sum), iota, iota8, scratch,
    )
    corr_ref[...] = head_sum[:, 0:128, :] + tail_sum[:, 0:128, :]


def pair_scratch(tail_rows):
    f32, i32 = jnp.float32, jnp.int32
    slot = [
        VMEM((ROWS, LANES), i32),
        VMEM((ROWS, LANES), i32),
        VMEM((ROWS, ROWS, LANES), i32),
        VMEM((ROWS, ROWS, LANES), i32),
    ]
    return [
        VMEM((3, 144, LANES), f32),
        VMEM((3, tail_rows, LANES), f32),
        VMEM((LANES, LANES), jnp.bfloat16),
        VMEM((16, LANES), jnp.bfloat16),
        VMEM((16, ROWS, LANES), f32),
        *slot,
        *slot,
    ]


def near_pairs(ends, keys, words, largest, one, other):
    f32 = jnp.float32
    smem, vmem = pl.BlockSpec(memory_space=SMEM), pl.BlockSpec(memory_space=VMEM)
    return pl.pallas_call(
        near_pairs_kernel,
        name="near_pairs",
        out_shape=(
            jax.ShapeDtypeStruct((3, 128, LANES), f32),
            jax.ShapeDtypeStruct((3, 16, LANES), f32),
            jax.ShapeDtypeStruct((3, 16, LANES), f32),
        ),
        in_specs=[smem, vmem, vmem, vmem, vmem, vmem],
        scratch_shapes=[VMEM((32, ROWS, LANES), f32), VMEM((160, LANES), jnp.int32)]
        + pair_scratch(40),
        compiler_params=params(),
    )(ends, keys, words, largest, one, other)


def own_pairs(live, ends, keys, words, largest, heads):
    smem, vmem = pl.BlockSpec(memory_space=SMEM), pl.BlockSpec(memory_space=VMEM)
    return pl.pallas_call(
        own_pairs_kernel,
        name="own_pairs",
        out_shape=jax.ShapeDtypeStruct((3, 128, LANES), jnp.float32),
        in_specs=[smem, smem, vmem, vmem, vmem, vmem],
        scratch_shapes=pair_scratch(136),
        compiler_params=params(),
    )(live, ends, keys, words, largest, heads)


def force_gather(block, keys_ref, table_ref, total_ref, slot):
    force, got, val = slot
    rows = rows_of(block)
    scale = (-2.0 * drag_coef) * table_ref[rows, 6, :]
    for c in range(3):
        push = scale * (table_ref[rows, 3 + c, :] + total_ref[c, rows, :])
        force[:, c, :] = push[0:8]
        force[:, 4 + c, :] = push[8:16]
    keys = keys_ref[rows, :]
    val[0] = lax.shift_right_logical(keys, 19).astype(jnp.float32)
    val[1] = (lax.shift_right_logical(keys, 11) & (2 * LANES - 1)).astype(jnp.float32)
    inner = lax.shift_right_logical(keys, 7) & 7
    low = keys & (LANES - 1)
    tables = [force[k] for k in range(ROWS)]
    for g in range(16):
        pick = jnp.broadcast_to(inner[g : g + 1, :], (ROWS, LANES))
        at = jnp.broadcast_to(low[g : g + 1, :], (ROWS, LANES))
        found = jnp.zeros((ROWS, LANES), jnp.float32)
        for k in range(ROWS):
            found = jnp.where(pick == k, lane_gather(tables[k], at), found)
        got[g] = found
    upper = (keys & 1024) != 0
    for c in range(3):
        pushed = jnp.where(upper, got[:, 4 + c, :], got[:, c, :])
        for n, part in enumerate(split_two(pushed)):
            val[2 + 2 * c + n] = part


def force_rows(g, base, slot, iota):
    val = slot[2]

    def row(n):
        if isinstance(g, int):
            return packed_row(val.at[n], g)
        return jnp.broadcast_to(val[n, pl.ds(g, 1), :], (16, LANES)).astype(jnp.bfloat16)

    rel = row(0) - base.astype(jnp.float32).astype(jnp.bfloat16)
    parts = [[row(2 + 2 * c + n) for c in range(3)] for n in range(2)]
    return spread_rows(rel, parts, iota), one_hot_rows(row(1), iota)


def force_add(groups, bases, slot, cells, iota):
    pieces = [force_rows(g, base, slot, iota) for g, base in zip(groups, bases)]
    out = block_product([p[0] for p in pieces], [p[1] for p in pieces])
    for n, base in enumerate(bases):
        for c in range(3):
            at = 96 * n + 16 * c
            total = out[at : at + 16] + out[at + 48 : at + 64]
            for half in range(2):
                part = total[:, half * LANES : (half + 1) * LANES]
                cells[2 * c + half, pl.ds(base, 16), :] += part


def force_rest(block, ends, slot, cells, iota):
    @pl.when(ends[2, block * 16] >= 16)
    def _():
        def one(g, carry):
            first, most = ends[0, block * 16 + g], ends[1, block * 16 + g]

            def trip(t, carry):
                force_add([g], [jnp.minimum(first + 16 * t, LANES)], slot, cells, iota)
                return carry

            lax.fori_loop(1, (most - first) // 16 + 1, trip, 0)
            return carry

        lax.fori_loop(0, 16, one, 0)


def deposit_step(gather, scatter, ends, keys_ref, table_ref, total_ref, cells, iota):
    if gather:
        force_gather(gather[0], keys_ref, table_ref, total_ref, gather[1])
    if scatter:
        for g in range(16):
            force_add([g], [ends[0, scatter[0] * 16 + g]], scatter[1], cells, iota)
        force_rest(scatter[0], ends, scatter[1], cells, iota)


def deposit_kernel(
    ends, keys_ref, table_ref, corr_ref, one_in, other_in,
    out_ref, total_ref, one_ref, other_ref,
    cells, iota, force_a, got_a, val_a, force_b, got_b, val_b,
):
    fill_iota(iota)
    cells[...] = jnp.zeros_like(cells)
    total_ref[...] = corr_ref[...]
    before, after = from_partners("az", one_in[...], other_in[...], True)
    total_ref[:, 0:16, :] += before
    total_ref[:, 112:128, :] += after
    a, b = (force_a, got_a, val_a), (force_b, got_b, val_b)
    step = functools.partial(
        deposit_step, ends=ends, keys_ref=keys_ref, table_ref=table_ref, total_ref=total_ref,
        cells=cells, iota=iota,
    )
    step((0, a), None)

    def two(k, carry):
        block = 2 * k
        step((block + 1, b), (block, a))
        step((block + 2, a), (block + 1, b))
        return carry

    lax.fori_loop(0, 3, two, 0)
    step((7, b), (6, a))
    step(None, (7, b))
    for c in range(3):
        for half in range(2):
            columns = slice(half * LANES, (half + 1) * LANES)
            out_ref[c, :, columns] = cells[2 * c + half, 0:128, :]
            one, other = by_partner(
                "ax", cells[2 * c + half, 0:32, :], cells[2 * c + half, 96:128, :]
            )
            one_ref[c, :, columns] = one
            other_ref[c, :, columns] = other


def deposits(ends, keys, table, corr, one, other):
    f32 = jnp.float32
    smem, vmem = pl.BlockSpec(memory_space=SMEM), pl.BlockSpec(memory_space=VMEM)
    slot = [VMEM((ROWS, ROWS, LANES), f32), VMEM((16, ROWS, LANES), f32), VMEM((8, 16, LANES), f32)]
    return pl.pallas_call(
        deposit_kernel,
        name="deposits",
        out_shape=(
            jax.ShapeDtypeStruct((3, 128, 2 * LANES), f32),
            jax.ShapeDtypeStruct((3, 128, LANES), f32),
            jax.ShapeDtypeStruct((3, 32, 2 * LANES), f32),
            jax.ShapeDtypeStruct((3, 32, 2 * LANES), f32),
        ),
        in_specs=[smem] + [vmem] * 5,
        scratch_shapes=[VMEM((6, 144, LANES), f32), VMEM((2 * LANES, LANES), jnp.bfloat16)]
        + slot
        + slot,
        compiler_params=params(),
    )(ends, keys, table, corr, one, other)


def axial_kernel(taps, cells_ref, one_in, other_in, out_ref, one_ref, other_ref, first_ref, last_ref):
    for c in range(3):
        before, after = from_partners("ax", one_in[c], other_in[c])
        padded = jnp.concatenate([before, cells_ref[c], after], axis=0)
        total = taps[0] * padded[0:128]
        for k in range(1, 5):
            total = total + taps[k] * padded[16 * k : 16 * k + 128]
        out_ref[c] = total
        for a in range(8):
            first_ref[2 * a : 2 * a + 2, :] = total[16 * a : 16 * a + 2]
            last_ref[2 * a : 2 * a + 2, :] = total[16 * a + 14 : 16 * a + 16]
        one_ref[c], other_ref[c] = by_partner("rad", first_ref[...], last_ref[...])


def radial_kernel(
    taps, cells_ref, one_in, other_in, out_ref, one_ref, other_ref, padded, before_ref, after_ref
):
    lane = lax.broadcasted_iota(jnp.int32, (LANES, LANES), 1)
    edges = jnp.zeros((LANES, LANES), jnp.float32)
    for c in range(3):
        before_ref[...], after_ref[...] = from_partners("rad", one_in[c], other_in[c])
        for a in range(8):
            padded[0:2, :] = before_ref[2 * a : 2 * a + 2, :]
            padded[2:18, :] = cells_ref[c, 16 * a : 16 * a + 16, :]
            padded[18:20, :] = after_ref[2 * a : 2 * a + 2, :]
            total = taps[0] * padded[0:16, :]
            for k in range(1, 5):
                total = total + taps[k] * padded[k : k + 16, :]
            out_ref[c, 16 * a : 16 * a + 16, :] = total
        left, right = out_ref[c, :, 0:LANES], out_ref[c, :, LANES:]
        if c:
            left = pltpu.roll(left, 2 * c, 1)
        right = pltpu.roll(right, 10 + 2 * c, 1)
        edges = jnp.where((lane >> 1) == c, left, edges)
        edges = jnp.where((lane >> 1) == 4 + c, right, edges)
    turned = edges.T
    one_ref[...], other_ref[...] = by_partner("az", turned[0:8], turned[8:16])


def inner_azimuthal_kernel(taps, cells_ref, out_ref):
    lane = lax.broadcasted_iota(jnp.int32, (LANES, LANES), 1)
    for c in range(3):
        left, right = cells_ref[c, :, 0:LANES], cells_ref[c, :, LANES:]
        out_left, out_right = taps[2] * left, taps[2] * right
        for k in (1, 2):
            tap = taps[2 + k]
            inner = lane < LANES - k
            x, y = (pltpu.roll(v, LANES - k, 1) for v in (left, right))
            out_left = out_left + tap * jnp.where(inner, x, y)
            out_right = out_right + tap * jnp.where(inner, y, 0.0)
            inner = lane >= k
            x, y = (pltpu.roll(v, k, 1) for v in (left, right))
            out_left = out_left + tap * jnp.where(inner, x, 0.0)
            out_right = out_right + tap * jnp.where(inner, y, x)
        out_ref[c, :, 0:LANES] = out_left
        out_ref[c, :, LANES:] = out_right


def azimuthal_kernel(taps, inner_ref, one_in, other_in, out_ref):
    lane = lax.broadcasted_iota(jnp.int32, (LANES, LANES), 1)
    rest = jnp.zeros((LANES - 16, LANES), jnp.float32)
    before, after = from_partners("az", one_in[...], other_in[...], True)
    edges = jnp.concatenate([after, before, rest], axis=0).T
    for c in range(3):
        out_left, out_right = inner_ref[c, :, 0:LANES], inner_ref[c, :, LANES:]
        for k in (1, 2):
            x = pltpu.roll(edges, (118 - 2 * c + k) % LANES, 1)
            out_left = out_left + taps[2 - k] * jnp.where(lane < k, x, 0.0)
            y = pltpu.roll(edges, LANES - 2 * c - k, 1)
            out_right = out_right + taps[2 + k] * jnp.where(lane >= LANES - k, y, 0.0)
        out_ref[c, :, 0:LANES] = out_left
        out_ref[c, :, LANES:] = out_right


def filtered(deposit, one, other):
    f32 = jnp.float32
    raw = [math.exp(-0.5 * k * k) for k in range(-2, 3)]
    taps = [x / sum(raw) for x in raw]
    whole = jax.ShapeDtypeStruct(deposit.shape, f32)
    radial_face = jax.ShapeDtypeStruct((3, 16, 2 * LANES), f32)
    edge = jax.ShapeDtypeStruct((8, LANES), f32)
    cells, one, other = pl.pallas_call(
        functools.partial(axial_kernel, taps),
        name="axial_filter",
        out_shape=(whole, radial_face, radial_face),
        scratch_shapes=[VMEM((16, 2 * LANES), f32)] * 2,
        compiler_params=params(),
    )(deposit, *swapped(one, other, "ax"))
    cells, one, other = pl.pallas_call(
        functools.partial(radial_kernel, taps),
        name="radial_filter",
        out_shape=(whole, edge, edge),
        scratch_shapes=[VMEM((24, 2 * LANES), f32)] + [VMEM((16, 2 * LANES), f32)] * 2,
        compiler_params=params(),
    )(cells, *swapped(one, other, "rad"))
    one, other = swapped(one, other, "az", True)
    inner = pl.pallas_call(
        functools.partial(inner_azimuthal_kernel, taps),
        name="inner_azimuthal_filter",
        out_shape=whole,
        compiler_params=params(),
    )(cells)
    return pl.pallas_call(
        functools.partial(azimuthal_kernel, taps),
        name="azimuthal_filter",
        out_shape=whole,
        compiler_params=params(),
    )(inner, one, other)


def swapped(one, other, axis, wrap=False):
    count = lax.axis_size(axis)

    def partner(i, odd):
        j = i + 1 if i % 2 == odd else i - 1
        return j % count if wrap or 0 <= j < count else i

    return [
        lax.ppermute(x, axis, [(i, partner(i, odd)) for i in range(count)])
        for odd, x in enumerate((one, other))
    ]


def per_device(positions, velocity, diameter, cell_index, pair_list, live_pairs, gas_velocity):
    live = live_pairs.reshape(1, 1)
    cells = cell_index.reshape(128, LANES)
    gas = gas_velocity.reshape(3, 128, 2 * LANES)
    pos = positions.reshape(3, 128, LANES)
    vel = velocity.reshape(3, 128, LANES)
    diam = diameter.reshape(128, LANES)
    cell_keys, cell_ends, edges, one, other = edge_states(cells, gas, pos, vel, diam)
    one, other = swapped(one, other, "az", True)
    pairs = pair_list.reshape(2, 256, LANES)
    pair_keys, pair_ends, table, words, largest = inner_states(
        live, cell_ends, pairs, cell_keys, edges, gas, pos, vel, diam
    )
    heads, one, other = near_pairs(pair_ends, pair_keys, words, largest, one, other)
    one, other = swapped(one, other, "az", True)
    corr = own_pairs(live, pair_ends, pair_keys, words, largest, heads)
    deposit, correction, one, other = deposits(cell_ends, cell_keys, table, corr, one, other)
    smoothed = filtered(deposit, one, other)
    return (correction.reshape(positions.shape), smoothed.reshape(gas_velocity.shape))


def solution(mesh):
    return jax.shard_map(
        per_device,
        mesh=mesh,
        in_specs=(
            P(None, "ax", "rad", "az"),
            P(None, "ax", "rad", "az"),
            P("ax", "rad", "az"),
            P("ax", "rad", "az"),
            P(None, "ax", "rad", "az"),
            P("ax", "rad", "az"),
            P(None, "ax", "rad", "az"),
        ),
        out_specs=(P(None, "ax", "rad", "az"), P(None, "ax", "rad", "az")),
        check_vma=False,
    )
```

```python
import functools
import math

import jax
import jax.numpy as jnp
from jax import lax
from jax.experimental import pallas as pl
from jax.experimental.pallas import tpu as pltpu
from jax.sharding import PartitionSpec as P

piep_coef = 1.0
drag_coef = 20.0

LANES = 128
ROWS = 8
BLOCK = 2048
GAS_WINDOW = 12
BUCKET = 1024
BUCKETS = 20
NEAR_BUCKETS = 4
NEAR_HEADS = 8
OWN_HEADS = 12
DEAD = 1 << 29

NT = (((1,), (1,)), ((), ()))
VMEM = pltpu.VMEM
SMEM = pltpu.SMEM


def params(megabytes=40):
    return pltpu.CompilerParams(vmem_limit_bytes=megabytes << 20)


def lane_gather(table, index):
    numbers = lax.GatherDimensionNumbers(
        offset_dims=(),
        collapsed_slice_dims=(1,),
        start_index_map=(1,),
        operand_batching_dims=(0,),
        start_indices_batching_dims=(0,),
    )
    return lax.gather(
        table,
        index[..., None],
        numbers,
        slice_sizes=(1, 1),
        mode=lax.GatherScatterMode.PROMISE_IN_BOUNDS,
    )


def sort_network(regs, place, levels):
    sub = lax.broadcasted_iota(jnp.int32, (ROWS, LANES), 0)
    lane = lax.broadcasted_iota(jnp.int32, (ROWS, LANES), 1)
    count = len(regs)

    def bit_fill(bit, v):
        if bit >= levels:
            return 0
        kind, k = place[bit]
        if kind == "v":
            return -((v >> k) & 1)
        return -(((sub if kind == "s" else lane) >> k) & 1)

    flip = [0] * count
    for level in range(1, levels + 1):
        fills = {}
        for v in range(count):
            kind, k = place[level] if level < levels else ("v", 99)
            key = (v >> k) & 1 if kind == "v" else 0
            if key not in fills:
                fills[key] = bit_fill(level, v)
            new = fills[key]
            if isinstance(new, int) and isinstance(flip[v], int):
                if new != flip[v]:
                    regs[v] = ~regs[v]
            else:
                regs[v] = regs[v] ^ (new ^ flip[v])
            flip[v] = new
        for bit in reversed(range(level)):
            kind, k = place[bit]
            step = 1 << k
            if kind == "v":
                for v in range(count):
                    if not v & step:
                        a, b = regs[v], regs[v | step]
                        regs[v], regs[v | step] = jnp.minimum(a, b), jnp.maximum(a, b)
            else:
                axis, size, where = (0, ROWS, sub) if kind == "s" else (1, LANES, lane)
                lower = (where & step) == 0
                for v in range(count):
                    x = regs[v]
                    ahead = pltpu.roll(x, size - step, axis)
                    behind = ahead if 2 * step == size else pltpu.roll(x, step, axis)
                    regs[v] = jnp.where(lower, jnp.minimum(x, ahead), jnp.maximum(x, behind))
    return regs


def split_two(x):
    high = x.astype(jnp.bfloat16).astype(jnp.float32)
    return high, x - high


def split_three(x):
    high, rest = split_two(x)
    mid, low = split_two(rest)
    return high, mid, low


def packed_row(ref, row):
    return jnp.broadcast_to(ref[row : row + 1, :], (16, LANES)).astype(jnp.bfloat16)


def one_hot_rows(low, iota):
    one = jnp.ones((16, LANES), jnp.bfloat16)
    zero = jnp.zeros((16, LANES), jnp.bfloat16)
    return jnp.concatenate(
        [jnp.where(low == iota[k : k + 16, :], one, zero) for k in range(0, iota.shape[0], 16)],
        axis=0,
    )


def spread_rows(rel, parts, iota):
    hit = rel == iota[0:16, :]
    zero = jnp.zeros((16, LANES), jnp.bfloat16)
    return jnp.concatenate([jnp.where(hit, p, zero) for part in parts for p in part], axis=0)


def block_product(rows, hots):
    zero = jnp.zeros
    lines = [
        jnp.concatenate(
            [x if m == n else zero(x.shape, x.dtype) for m in range(len(rows))], axis=1
        )
        for n, x in enumerate(rows)
    ]
    return lax.dot_general(
        jnp.concatenate(lines, axis=0),
        jnp.concatenate(hots, axis=1),
        NT,
        preferred_element_type=jnp.float32,
    )


def spread_add(rows, hots):
    out = lax.dot_general(
        jnp.concatenate(rows, axis=1) if len(rows) > 1 else rows[0],
        jnp.concatenate(hots, axis=1) if len(hots) > 1 else hots[0],
        NT,
        preferred_element_type=jnp.float32,
    )
    total = out[0:48]
    for s in range(48, out.shape[0], 48):
        total = total + out[s : s + 48]
    return total


def fill_iota(iota):
    rows = lax.broadcasted_iota(jnp.int32, iota.shape, 0)
    iota[...] = rows.astype(jnp.float32).astype(jnp.bfloat16)


def rows_of(block):
    start = block * 16
    return pl.ds(start if isinstance(block, int) else pl.multiple_of(start, 16), 16)


def wide(ref, *at):
    return jnp.broadcast_to(ref[at[:-1] + (slice(at[-1], at[-1] + 1),)], (ROWS, LANES))


def window(table, first, count, row, low, found):
    rel = row - first
    for u in range(count):
        found = jnp.where(rel == u, lane_gather(table[first + u], low), found)
    return found


def running_max(x, count):
    x = jnp.broadcast_to(x, (ROWS, LANES))
    step = 1
    while step < count:
        x = jnp.maximum(x, pltpu.roll(x, LANES - step, 1))
        step *= 2
    return x


def by_partner(axis, first, last):
    even = (lax.axis_index(axis) & 1) == 0
    return jnp.where(even, last, first), jnp.where(even, first, last)


def from_partners(axis, one, other, wrap=False):
    at, count = lax.axis_index(axis), lax.axis_size(axis)
    even = (at & 1) == 0
    before, after = jnp.where(even, other, one), jnp.where(even, one, other)
    if wrap:
        return before, after
    return jnp.where(at > 0, before, 0.0), jnp.where(at < count - 1, after, 0.0)


PLACE_STEP = 0.1 / 65535.0
RADIUS_LEAST = 0.01
RADIUS_STEP = 0.04 / 65535.0
SLIP_HALF = 1 << 20


def largest_slip(table, rows):
    most = jnp.zeros((ROWS, LANES), jnp.float32)
    for n in range(0, rows, ROWS):
        for c in range(3):
            most = jnp.maximum(most, jnp.abs(table[n : n + ROWS, 3 + c, :]))
    most = jnp.max(jnp.max(most, axis=0, keepdims=True), axis=1, keepdims=True)
    return jnp.broadcast_to(jnp.maximum(most, 1e-30), (ROWS, LANES))


def code_rows(table, n, largest, words):
    rows = pl.ds(n * ROWS, ROWS)

    def whole(c, least, step):
        x = ((table[rows, c, :] - least) * (1.0 / step) + 0.5).astype(jnp.int32)
        return jnp.clip(x, 0, 65535)

    x, y, z = (whole(c, 0.0, PLACE_STEP) for c in range(3))
    radius = whole(6, RADIUS_LEAST, RADIUS_STEP)
    scale = (SLIP_HALF - 1.0) / largest
    u, v, w = (
        (table[rows, 3 + c, :] * scale + (SLIP_HALF + 0.5)).astype(jnp.int32) for c in range(3)
    )
    coded = (
        x | (y << 16),
        z | (radius << 16),
        u | ((w & 2047) << 21),
        v | (lax.shift_right_logical(w, 11) << 21),
    )
    for k, word in enumerate(coded):
        words[pl.ds(n * 32 + k, ROWS, stride=4), :] = word


def decoded(words, largest):
    low = [x & 65535 for x in words[0:2]]
    high = [lax.shift_right_logical(x, 16) for x in words[0:2]]
    place = (low[0], high[0], low[1])
    radius = high[1].astype(jnp.float32) * RADIUS_STEP + RADIUS_LEAST
    mask = 2 * SLIP_HALF - 1
    third = lax.shift_right_logical(words[2], 21) | (lax.shift_right_logical(words[3], 21) << 11)
    scale = largest * (1.0 / (SLIP_HALF - 1.0))
    slip = [
        (x - SLIP_HALF).astype(jnp.float32) * scale for x in (words[2] & mask, words[3] & mask, third)
    ]
    return place, radius, slip


def fill_gas_rows(gas_ref, gas_rows):
    for r in range(16):
        rows = slice(r * ROWS, (r + 1) * ROWS)
        for c in range(3):
            for half in range(2):
                gas_rows[rows, half * 4 + c, :] = gas_ref[c, rows, half * LANES : (half + 1) * LANES]


def gas_index(block, keys_ref, slot):
    idx = slot[0]
    keys = keys_ref[rows_of(block), :]
    idx[0] = lax.shift_right_logical(keys, 19)
    idx[1] = lax.shift_right_logical(keys, 11) & (LANES - 1)


def gas_gather(block, g, ends, gas_rows, slot):
    idx, found = slot[0], slot[1]
    zero = jnp.zeros((ROWS, LANES), jnp.float32)
    first = ends[0, block * 16 + g]
    found[g] = window(gas_rows, first, GAS_WINDOW, wide(idx, 0, g), wide(idx, 1, g), zero)


def gas_rest(block, ends, gas_rows, slot):
    idx, found = slot[0], slot[1]

    @pl.when(ends[2, block * 16] >= GAS_WINDOW)
    def _():
        def one(g, carry):
            first = ends[0, block * 16 + g]
            row = jnp.broadcast_to(idx[0, pl.ds(g, 1), :], (ROWS, LANES))
            low = jnp.broadcast_to(idx[1, pl.ds(g, 1), :], (ROWS, LANES))

            def trip(t, total):
                base = jnp.minimum(first + GAS_WINDOW * t, LANES)
                return window(gas_rows, base, GAS_WINDOW, row, low, total)

            trips = (ends[1, block * 16 + g] - first) // GAS_WINDOW + 1
            found[g] = lax.fori_loop(1, trips, trip, found[g])
            return carry

        lax.fori_loop(0, 16, one, 0)


def seen_values(block, keys_ref, slot):
    idx, found, val = slot
    keys = keys_ref[rows_of(block), :]
    upper = (keys & (1 << 18)) != 0
    place_in = keys & (BLOCK - 1)
    val[0] = lax.shift_right_logical(place_in, 7).astype(jnp.float32)
    val[1] = (place_in & (LANES - 1)).astype(jnp.float32)
    for c in range(3):
        seen = jnp.where(upper, found[:, 4 + c, :], found[:, c, :])
        for n, part in enumerate(split_three(seen)):
            val[2 + 3 * c + n] = part


def seen_in_order(groups, slot, iota):
    val = slot[2]
    rows, hots = [], []
    for g in groups:
        parts = [[packed_row(val.at[2 + 3 * c + n], g) for c in range(3)] for n in range(3)]
        rows.append(spread_rows(packed_row(val.at[0], g), parts, iota))
        hots.append(one_hot_rows(packed_row(val.at[1], g), iota))
    return spread_add(rows, hots)


def write_states(block, total, pos_ref, vel_ref, diam_ref, out_ref, out_rows):
    rows = rows_of(block)
    for c in range(3):
        out_ref[out_rows, c, :] = pos_ref[c, rows, :]
        out_ref[out_rows, 3 + c, :] = total[16 * c : 16 * c + 16] - vel_ref[c, rows, :]
    out_ref[out_rows, 6, :] = 0.5 * diam_ref[rows, :]
    out_ref[out_rows, 7, :] = jnp.zeros((16, LANES), jnp.float32)


def states_step(gather, scatter, keys_ref, ends, gas_rows, iota, arrays):
    total = jnp.zeros((48, LANES), jnp.float32)
    if gather:
        gas_index(gather[0], keys_ref, gather[1])
    if scatter:
        seen_values(scatter[0], keys_ref, scatter[1])
    for g in range(16):
        if gather:
            gas_gather(gather[0], g, ends, gas_rows, gather[1])
        if scatter and g % 2:
            total = total + seen_in_order((g - 1, g), scatter[1], iota)
    if scatter:
        write_states(scatter[0], total, *arrays, *scatter[2:])
    if gather:
        gas_rest(gather[0], ends, gas_rows, gather[1])


def states_kernel(
    cell_hbm, gas_hbm, pos_hbm, vel_hbm, diam_hbm,
    keys_ref, ends_ref, table_ref, one_ref, other_ref,
    cell_ref, gas_ref, pos_ref, vel_ref, diam_ref,
    gas_rows, iota, ends, idx_a, found_a, val_a, idx_b, found_b, val_b, sems,
):
    sources = (cell_hbm, gas_hbm, pos_hbm, vel_hbm, diam_hbm)
    places = (cell_ref, gas_ref, pos_ref, vel_ref, diam_ref)
    copies = [
        pltpu.make_async_copy(x, y, sems.at[n]) for n, (x, y) in enumerate(zip(sources, places))
    ]
    for copy in copies:
        copy.start()
    copies[0].wait()
    sub = lax.broadcasted_iota(jnp.int32, (ROWS, LANES), 0)
    lane = lax.broadcasted_iota(jnp.int32, (ROWS, LANES), 1)
    cells = cell_ref[...].T
    regs = []
    for v in range(16):
        own = (lane & 15) * LANES + v * ROWS + sub
        regs.append(cells[v * ROWS : (v + 1) * ROWS] * BLOCK + own)
    place = [("v", k) for k in range(4)] + [("s", k) for k in range(3)] + [("l", k) for k in range(4)]
    regs = sort_network(regs, place, 11)
    least = functools.reduce(jnp.minimum, regs)
    most = functools.reduce(jnp.maximum, regs)
    least = lax.shift_right_logical(jnp.min(least, axis=0, keepdims=True), 19)
    most = lax.shift_right_logical(jnp.max(most, axis=0, keepdims=True), 19)
    ends_ref[0:1, :] = least
    ends_ref[1:2, :] = most
    ends_ref[2:8, :] = running_max(most - least, 16)[0:6]
    copy = pltpu.make_async_copy(ends_ref, ends, sems.at[5])
    copy.start()
    keys_ref[...] = jnp.concatenate(regs, axis=0).T
    copies[1].wait()
    fill_gas_rows(gas_ref, gas_rows)
    for other in copies[2:]:
        other.wait()
    copy.wait()
    fill_iota(iota)
    a, b = (idx_a, found_a, val_a), (idx_b, found_b, val_b)
    step = functools.partial(
        states_step, keys_ref=keys_ref, ends=ends, gas_rows=gas_rows, iota=iota,
        arrays=(pos_ref, vel_ref, diam_ref),
    )
    step((0, a), None)

    def two(k, carry):
        block = 2 * k
        step((block + 1, b), (block, a, table_ref, rows_of(block)))
        step((block + 2, a), (block + 1, b, table_ref, rows_of(block + 1)))
        return carry

    lax.fori_loop(0, 3, two, 0)
    step((7, b), (6, a, table_ref, rows_of(6)))
    step(None, (7, b, table_ref, rows_of(7)))
    one_ref[...], other_ref[...] = by_partner("az", table_ref[0:16], table_ref[112:128])


def slots(rows, parts, dtype=jnp.float32):
    one = [VMEM((2, 16, LANES), jnp.int32), VMEM((16, ROWS, LANES), dtype), VMEM((parts, rows, LANES), dtype)]
    return one + one


def droplet_states(cells, gas, pos, vel, diam):
    f32, i32 = jnp.float32, jnp.int32
    arrays = (cells, gas, pos, vel, diam)
    return pl.pallas_call(
        states_kernel,
        name="droplet_states",
        out_shape=(
            jax.ShapeDtypeStruct((128, LANES), i32),
            jax.ShapeDtypeStruct((ROWS, LANES), i32),
            jax.ShapeDtypeStruct((128, ROWS, LANES), f32),
            jax.ShapeDtypeStruct((16, ROWS, LANES), f32),
            jax.ShapeDtypeStruct((16, ROWS, LANES), f32),
        ),
        in_specs=[pl.BlockSpec(memory_space=pltpu.HBM)] * 5,
        scratch_shapes=[VMEM(x.shape, x.dtype) for x in arrays]
        + [VMEM((144, ROWS, LANES), f32), VMEM((LANES, LANES), jnp.bfloat16), SMEM((ROWS, LANES), i32)]
        + slots(16, 11)
        + [pltpu.SemaphoreType.DMA((6,))],
        compiler_params=params(),
    )(*[pltpu.with_memory_space_constraint(x, pltpu.HBM) for x in arrays])


def pair_sort_kernel(live_ref, pairs_ref, table_ref, keys_ref, ends_ref, words_ref, largest_ref):
    largest = largest_slip(table_ref, 128)
    largest_ref[...] = largest
    for n in range(16):
        code_rows(table_ref, n, largest, words_ref)
    words_ref[512:576, :] = jnp.zeros((64, LANES), jnp.int32)
    live = live_ref[0, 0]
    sub = lax.broadcasted_iota(jnp.int32, (ROWS, LANES), 0)
    lane = lax.broadcasted_iota(jnp.int32, (ROWS, LANES), 1)
    regs = []
    for v in range(32):
        rows = slice(v * ROWS, (v + 1) * ROWS)
        slot = v * 1024 + sub * LANES + lane
        head = pairs_ref[0, rows, :]
        tail = pairs_ref[1, rows, :] - 7 * BLOCK
        own = tail - BLOCK
        inside = (own >= 0) & (own < 8 * BLOCK)
        tail = jnp.where(inside, jnp.maximum(own, head) + BLOCK, tail)
        head = jnp.where(inside, jnp.minimum(own, head), head)
        bucket = lax.shift_right_logical(tail, 10)
        bucket = jnp.where(inside, bucket + 2, jnp.where(bucket >= 18, bucket - 16, bucket))
        turn = -(bucket & 1) & (8 * BLOCK - 1)
        key = (bucket << 24) | ((head ^ turn) << 10) | (tail & (BUCKET - 1))
        regs.append(jnp.where(slot < live, key, DEAD))
    place = (
        [("v", k) for k in range(4)]
        + [("s", k) for k in range(3)]
        + [("v", 4)]
        + [("l", k) for k in range(7)]
    )
    regs = sort_network(regs, place, 15)
    beyond = jnp.zeros((ROWS, LANES), jnp.float32)
    for key in regs:
        beyond = beyond + jnp.where(key < NEAR_BUCKETS << 24, 1.0, 0.0)
    beyond = jnp.sum(jnp.sum(beyond, axis=0, keepdims=True), axis=1, keepdims=True)
    ends_ref[8:16, :] = jnp.broadcast_to(beyond, (ROWS, LANES)).astype(jnp.int32)
    for half in range(2):
        rows = regs[16 * half : 16 * half + 16]
        keys_ref[half] = jnp.concatenate(rows, axis=0).T
        least_head = least_tail = jnp.full((ROWS, LANES), 1 << 20, jnp.int32)
        most_head = most_tail = jnp.full((ROWS, LANES), -1, jnp.int32)
        for key in rows:
            used = key < DEAD
            bucket = lax.shift_right_logical(key, 24)
            head = lax.shift_right_logical(key, 17) & (LANES - 1)
            head = head ^ (-(bucket & 1) & (LANES - 1))
            least_head = jnp.minimum(least_head, jnp.where(used, head, 1 << 20))
            most_head = jnp.maximum(most_head, jnp.where(used, head, -1))
            least_tail = jnp.minimum(least_tail, jnp.where(used, bucket, 1 << 20))
            most_tail = jnp.maximum(most_tail, jnp.where(used, bucket, -1))
        for n, x in enumerate((least_head, most_head, least_tail, most_tail)):
            reduce = jnp.max if n % 2 else jnp.min
            row = 4 * half + n
            bound = (LANES, LANES, BUCKETS, BUCKETS)[n]
            ends_ref[row : row + 1, :] = jnp.minimum(reduce(x, axis=0, keepdims=True), bound)


def pair_sort(live, pairs, table):
    return pl.pallas_call(
        pair_sort_kernel,
        name="pair_sort",
        out_shape=(
            jax.ShapeDtypeStruct((2, LANES, LANES), jnp.int32),
            jax.ShapeDtypeStruct((16, LANES), jnp.int32),
            jax.ShapeDtypeStruct((576, LANES), jnp.int32),
            jax.ShapeDtypeStruct((ROWS, LANES), jnp.float32),
        ),
        in_specs=[pl.BlockSpec(memory_space=SMEM)] + [pl.BlockSpec(memory_space=VMEM)] * 2,
        compiler_params=params(),
    )(live, pairs, table)


def group_ends(g, ends, part):
    g = jnp.minimum(g, 2 * LANES - 1)
    at, lane = 4 * (g & 1), g >> 1
    low, high, _ = part
    return (
        ends[at, lane] & -2,
        ends[at + 1, lane],
        jnp.maximum(ends[at + 2, lane], low),
        jnp.minimum(ends[at + 3, lane], high - 1),
    )


def take_items(state, groups, ends, part):
    low, high, heads = part
    items = []
    for _ in range(ROWS):
        g, bucket, head, now, later = state
        place = jnp.minimum(bucket, high) - low
        items.append((jnp.minimum(g, 2 * LANES - 1), jnp.where(g < groups, bucket, -1), head, place))
        ahead = group_ends(g + 2, ends, part)
        more_heads = head + heads <= now[1]
        stay = more_heads | (bucket < now[3])
        head = jnp.where(more_heads, head + heads, jnp.where(stay, now[0], later[0]))
        bucket = jnp.where(more_heads, bucket, jnp.where(stay, bucket + 1, later[2]))
        now = tuple(jnp.where(stay, x, y) for x, y in zip(now, later))
        later = tuple(jnp.where(stay, x, y) for x, y in zip(later, ahead))
        state = (jnp.where(stay, g, g + 1), bucket, head, now, later)
    return items, state


def word_window(words, first, count, pair, low):
    found = jnp.zeros((ROWS, LANES), jnp.int32)
    for u in range(count):
        rows = words[pl.ds(pl.multiple_of((first + u) * ROWS, ROWS), ROWS), :]
        found = jnp.where(pair == u, lane_gather(rows, low), found)
    return found


def pair_gather(k, item, keys_ref, near_words, far_words, heads, slot):
    key_rows, rel_rows, near, far = slot
    g, bucket, first, part = item
    keys = jnp.broadcast_to(keys_ref[g & 1, pl.ds(g >> 1, 1), :], (ROWS, LANES))
    of_bucket = lax.shift_right_logical(keys, 24)
    turn = -(of_bucket & 1) & (8 * BLOCK - 1)
    head = (lax.shift_right_logical(keys, 10) & (8 * BLOCK - 1)) ^ turn
    rel = lax.shift_right_logical(head, 7) - first
    used = (of_bucket == bucket) & (rel >= 0) & (rel < heads)
    key_rows[k : k + 1, :] = jnp.where(used, keys, DEAD)[0:1]
    rel_rows[k : k + 1, :] = rel[0:1]
    near[k] = word_window(near_words, first >> 1, heads // 2, rel >> 1, head & (LANES - 1))
    pair = lax.shift_right_logical(keys, 8) & 3
    far[k] = word_window(far_words, part * 4, 4, pair, keys & (LANES - 1))


def pair_values(slot, val, near_largest, far_largest):
    key_rows, rel_rows, near, far = slot
    keys, rel = key_rows[...], rel_rows[...]
    used = keys < DEAD
    turn = -(lax.shift_right_logical(keys, 24) & 1) & (LANES - 1)
    val[0] = rel.astype(jnp.float32)
    val[1] = ((lax.shift_right_logical(keys, 10) & (LANES - 1)) ^ turn).astype(jnp.float32)
    val[2] = (lax.shift_right_logical(keys, 7) & 7).astype(jnp.float32)
    val[3] = (keys & (LANES - 1)).astype(jnp.float32)

    def words(ref, odd):
        return [jnp.where(odd, ref[:, 4 + w, :], ref[:, w, :]) for w in range(4)]

    near_place, near_radius, near_slip = decoded(words(near, (rel & 1) == 1), near_largest)
    far_place, far_radius, far_slip = decoded(words(far, (keys & LANES) != 0), far_largest)
    gap = jnp.zeros((ROWS, LANES), jnp.float32)
    for x, y in zip(far_place, near_place):
        apart = (x - y).astype(jnp.float32)
        gap = gap + apart * apart
    gap = gap * (PLACE_STEP * PLACE_STEP)
    far_ratio = far_radius * lax.rsqrt(gap + far_radius * far_radius)
    near_ratio = near_radius * lax.rsqrt(gap + near_radius * near_radius)
    weight_far = jnp.where(used, piep_coef * far_ratio * far_ratio * far_ratio, 0.0)
    weight_near = jnp.where(used, piep_coef * near_ratio * near_ratio * near_ratio, 0.0)
    for c in range(3):
        for n, part in enumerate(split_two(weight_far * far_slip[c])):
            val[4 + 3 * n + c] = part
        for n, part in enumerate(split_two(weight_near * near_slip[c])):
            val[10 + 3 * n + c] = part


def pair_scatter(k, item, val, head_sum, tail_sum, iota, iota8):
    first, tail_first = item
    parts = [[packed_row(val.at[4 + 3 * n + c], k) for c in range(3)] for n in range(2)]
    heads = spread_rows(packed_row(val.at[0], k), parts, iota)
    hit = packed_row(val.at[2], k) == iota8[...]
    zero = jnp.zeros((16, LANES), jnp.bfloat16)
    tails = []
    for n in range(10, 16, 2):
        both = jnp.concatenate([wide(val, n, k), wide(val, n + 1, k)], axis=0)
        tails.append(jnp.where(hit, both.astype(jnp.bfloat16), zero))
    tails = jnp.concatenate(tails, axis=0)
    out = block_product(
        [heads, tails], [one_hot_rows(packed_row(val.at[n], k), iota) for n in (1, 3)]
    )
    for c in range(3):
        head_sum[c, pl.ds(first, 16), :] += out[16 * c : 16 * c + 16] + out[16 * c + 48 : 16 * c + 64]
    at = pl.ds(pl.multiple_of(tail_first, 8), 8)
    for c in range(3):
        tail_sum[c, at, :] += out[8 * c + 96 : 8 * c + 104] + out[8 * c + 120 : 8 * c + 128]


def run_pairs(groups, start, part, ends, keys_ref, near, far, sums, iota, iota8, scratch):
    fill_iota(iota)
    rows = lax.broadcasted_iota(jnp.int32, iota8.shape, 0) & 7
    iota8[...] = rows.astype(jnp.float32).astype(jnp.bfloat16)
    val, a, b = scratch[0], scratch[1:5], scratch[5:9]

    def step(state, slot, pending):
        items, state = take_items(state, groups, ends, part)
        if pending:
            pair_values(a, val, near[1], far[1])
        for k in range(ROWS):
            pair_gather(k, items[k], keys_ref, near[0], far[0], part[2], slot)
            if pending:
                pair_scatter(k, pending[k], val, *sums, iota, iota8)
        return tuple((item[2], item[3] * 8) for item in items), state, items[0][1] >= 0

    now, later = group_ends(start, ends, part), group_ends(start + 1, ends, part)
    state = (start, now[2], now[0], now, later)

    def one(carry):
        pending, state, _ = carry
        carry = step(state, b, pending)
        for x, y in zip(a, b):
            x[...] = y[...]
        return carry

    lax.while_loop(lambda carry: carry[2], one, step(state, a, None))


def near_pairs_kernel(
    ends, keys_ref, words_ref, largest_ref, one_in, other_in,
    heads_ref, one_ref, other_ref,
    shell, shell_words, head_sum, tail_sum, iota, iota8, *scratch,
):
    shell[0:16], shell[16:32] = from_partners("az", one_in[...], other_in[...], True)
    shell_largest = largest_slip(shell, 32)
    for n in range(4):
        code_rows(shell, n, shell_largest, shell_words)
    shell_words[128:160, :] = jnp.zeros((32, LANES), jnp.int32)
    head_sum[...] = jnp.zeros_like(head_sum)
    tail_sum[...] = jnp.zeros_like(tail_sum)
    groups = (ends[8, 0] + LANES - 1) // LANES
    run_pairs(
        groups, jnp.int32(0), (0, NEAR_BUCKETS, NEAR_HEADS), ends, keys_ref,
        (words_ref, largest_ref[...]), (shell_words, shell_largest),
        (head_sum, tail_sum), iota, iota8, scratch,
    )
    heads_ref[...] = head_sum[:, 0:128, :]
    one_ref[...], other_ref[...] = by_partner("az", tail_sum[:, 0:16, :], tail_sum[:, 16:32, :])


def own_pairs_kernel(
    live_ref, ends, keys_ref, words_ref, largest_ref, heads_ref,
    corr_ref,
    head_sum, tail_sum, iota, iota8, *scratch,
):
    head_sum[:, 0:128, :] = heads_ref[...]
    head_sum[:, 128:144, :] = jnp.zeros((3, 16, LANES), jnp.float32)
    tail_sum[...] = jnp.zeros_like(tail_sum)
    groups = (live_ref[0, 0] + LANES - 1) // LANES
    start = jnp.minimum(ends[8, 0] // LANES, 2 * LANES - 1)
    coded = (words_ref, largest_ref[...])
    run_pairs(
        groups, start, (NEAR_BUCKETS, BUCKETS, OWN_HEADS), ends, keys_ref, coded, coded,
        (head_sum, tail_sum), iota, iota8, scratch,
    )
    corr_ref[...] = head_sum[:, 0:128, :] + tail_sum[:, 0:128, :]


def pair_scratch(tail_rows):
    f32, i32 = jnp.float32, jnp.int32
    slot = [
        VMEM((ROWS, LANES), i32),
        VMEM((ROWS, LANES), i32),
        VMEM((ROWS, ROWS, LANES), i32),
        VMEM((ROWS, ROWS, LANES), i32),
    ]
    return [
        VMEM((3, 144, LANES), f32),
        VMEM((3, tail_rows, LANES), f32),
        VMEM((LANES, LANES), jnp.bfloat16),
        VMEM((16, LANES), jnp.bfloat16),
        VMEM((16, ROWS, LANES), f32),
        *slot,
        *slot,
    ]


def near_pairs(ends, keys, words, largest, one, other):
    f32 = jnp.float32
    smem, vmem = pl.BlockSpec(memory_space=SMEM), pl.BlockSpec(memory_space=VMEM)
    return pl.pallas_call(
        near_pairs_kernel,
        name="near_pairs",
        out_shape=(
            jax.ShapeDtypeStruct((3, 128, LANES), f32),
            jax.ShapeDtypeStruct((3, 16, LANES), f32),
            jax.ShapeDtypeStruct((3, 16, LANES), f32),
        ),
        in_specs=[smem, vmem, vmem, vmem, vmem, vmem],
        scratch_shapes=[VMEM((32, ROWS, LANES), f32), VMEM((160, LANES), jnp.int32)]
        + pair_scratch(40),
        compiler_params=params(),
    )(ends, keys, words, largest, one, other)


def own_pairs(live, ends, keys, words, largest, heads):
    smem, vmem = pl.BlockSpec(memory_space=SMEM), pl.BlockSpec(memory_space=VMEM)
    return pl.pallas_call(
        own_pairs_kernel,
        name="own_pairs",
        out_shape=jax.ShapeDtypeStruct((3, 128, LANES), jnp.float32),
        in_specs=[smem, smem, vmem, vmem, vmem, vmem],
        scratch_shapes=pair_scratch(136),
        compiler_params=params(),
    )(live, ends, keys, words, largest, heads)


def force_gather(block, keys_ref, table_ref, total_ref, slot):
    force, got, val = slot
    rows = rows_of(block)
    scale = (-2.0 * drag_coef) * table_ref[rows, 6, :]
    for c in range(3):
        push = scale * (table_ref[rows, 3 + c, :] + total_ref[c, rows, :])
        force[:, c, :] = push[0:8]
        force[:, 4 + c, :] = push[8:16]
    keys = keys_ref[rows, :]
    val[0] = lax.shift_right_logical(keys, 19).astype(jnp.float32)
    val[1] = (lax.shift_right_logical(keys, 11) & (2 * LANES - 1)).astype(jnp.float32)
    inner = lax.shift_right_logical(keys, 7) & 7
    low = keys & (LANES - 1)
    tables = [force[k] for k in range(ROWS)]
    for g in range(16):
        pick = jnp.broadcast_to(inner[g : g + 1, :], (ROWS, LANES))
        at = jnp.broadcast_to(low[g : g + 1, :], (ROWS, LANES))
        found = jnp.zeros((ROWS, LANES), jnp.float32)
        for k in range(ROWS):
            found = jnp.where(pick == k, lane_gather(tables[k], at), found)
        got[g] = found
    upper = (keys & 1024) != 0
    for c in range(3):
        pushed = jnp.where(upper, got[:, 4 + c, :], got[:, c, :])
        for n, part in enumerate(split_two(pushed)):
            val[2 + 2 * c + n] = part


def force_rows(g, base, slot, iota):
    val = slot[2]

    def row(n):
        if isinstance(g, int):
            return packed_row(val.at[n], g)
        return jnp.broadcast_to(val[n, pl.ds(g, 1), :], (16, LANES)).astype(jnp.bfloat16)

    rel = row(0) - base.astype(jnp.float32).astype(jnp.bfloat16)
    parts = [[row(2 + 2 * c + n) for c in range(3)] for n in range(2)]
    return spread_rows(rel, parts, iota), one_hot_rows(row(1), iota)


def force_add(groups, bases, slot, cells, iota):
    pieces = [force_rows(g, base, slot, iota) for g, base in zip(groups, bases)]
    out = block_product([p[0] for p in pieces], [p[1] for p in pieces])
    for n, base in enumerate(bases):
        for c in range(3):
            at = 96 * n + 16 * c
            total = out[at : at + 16] + out[at + 48 : at + 64]
            for half in range(2):
                part = total[:, half * LANES : (half + 1) * LANES]
                cells[2 * c + half, pl.ds(base, 16), :] += part


def force_rest(block, ends, slot, cells, iota):
    @pl.when(ends[2, block * 16] >= 16)
    def _():
        def one(g, carry):
            first, most = ends[0, block * 16 + g], ends[1, block * 16 + g]

            def trip(t, carry):
                force_add([g], [jnp.minimum(first + 16 * t, LANES)], slot, cells, iota)
                return carry

            lax.fori_loop(1, (most - first) // 16 + 1, trip, 0)
            return carry

        lax.fori_loop(0, 16, one, 0)


def deposit_step(gather, scatter, ends, keys_ref, table_ref, total_ref, cells, iota):
    if gather:
        force_gather(gather[0], keys_ref, table_ref, total_ref, gather[1])
    if scatter:
        for g in range(16):
            force_add([g], [ends[0, scatter[0] * 16 + g]], scatter[1], cells, iota)
        force_rest(scatter[0], ends, scatter[1], cells, iota)


def deposit_kernel(
    ends, keys_ref, table_ref, corr_ref, one_in, other_in,
    out_ref, total_ref, one_ref, other_ref,
    cells, iota, force_a, got_a, val_a, force_b, got_b, val_b,
):
    fill_iota(iota)
    cells[...] = jnp.zeros_like(cells)
    total_ref[...] = corr_ref[...]
    before, after = from_partners("az", one_in[...], other_in[...], True)
    total_ref[:, 0:16, :] += before
    total_ref[:, 112:128, :] += after
    a, b = (force_a, got_a, val_a), (force_b, got_b, val_b)
    step = functools.partial(
        deposit_step, ends=ends, keys_ref=keys_ref, table_ref=table_ref, total_ref=total_ref,
        cells=cells, iota=iota,
    )
    step((0, a), None)

    def two(k, carry):
        block = 2 * k
        step((block + 1, b), (block, a))
        step((block + 2, a), (block + 1, b))
        return carry

    lax.fori_loop(0, 3, two, 0)
    step((7, b), (6, a))
    step(None, (7, b))
    for c in range(3):
        for half in range(2):
            columns = slice(half * LANES, (half + 1) * LANES)
            out_ref[c, :, columns] = cells[2 * c + half, 0:128, :]
            one, other = by_partner(
                "ax", cells[2 * c + half, 0:32, :], cells[2 * c + half, 96:128, :]
            )
            one_ref[c, :, columns] = one
            other_ref[c, :, columns] = other


def deposits(ends, keys, table, corr, one, other):
    f32 = jnp.float32
    smem, vmem = pl.BlockSpec(memory_space=SMEM), pl.BlockSpec(memory_space=VMEM)
    slot = [VMEM((ROWS, ROWS, LANES), f32), VMEM((16, ROWS, LANES), f32), VMEM((8, 16, LANES), f32)]
    return pl.pallas_call(
        deposit_kernel,
        name="deposits",
        out_shape=(
            jax.ShapeDtypeStruct((3, 128, 2 * LANES), f32),
            jax.ShapeDtypeStruct((3, 128, LANES), f32),
            jax.ShapeDtypeStruct((3, 32, 2 * LANES), f32),
            jax.ShapeDtypeStruct((3, 32, 2 * LANES), f32),
        ),
        in_specs=[smem] + [vmem] * 5,
        scratch_shapes=[VMEM((6, 144, LANES), f32), VMEM((2 * LANES, LANES), jnp.bfloat16)]
        + slot
        + slot,
        compiler_params=params(),
    )(ends, keys, table, corr, one, other)


def axial_kernel(taps, cells_ref, one_in, other_in, out_ref, one_ref, other_ref, first_ref, last_ref):
    for c in range(3):
        before, after = from_partners("ax", one_in[c], other_in[c])
        padded = jnp.concatenate([before, cells_ref[c], after], axis=0)
        total = taps[0] * padded[0:128]
        for k in range(1, 5):
            total = total + taps[k] * padded[16 * k : 16 * k + 128]
        out_ref[c] = total
        for a in range(8):
            first_ref[2 * a : 2 * a + 2, :] = total[16 * a : 16 * a + 2]
            last_ref[2 * a : 2 * a + 2, :] = total[16 * a + 14 : 16 * a + 16]
        one_ref[c], other_ref[c] = by_partner("rad", first_ref[...], last_ref[...])


def radial_kernel(
    taps, cells_ref, one_in, other_in, out_ref, one_ref, other_ref, padded, before_ref, after_ref
):
    lane = lax.broadcasted_iota(jnp.int32, (LANES, LANES), 1)
    edges = jnp.zeros((LANES, LANES), jnp.float32)
    for c in range(3):
        before_ref[...], after_ref[...] = from_partners("rad", one_in[c], other_in[c])
        for a in range(8):
            padded[0:2, :] = before_ref[2 * a : 2 * a + 2, :]
            padded[2:18, :] = cells_ref[c, 16 * a : 16 * a + 16, :]
            padded[18:20, :] = after_ref[2 * a : 2 * a + 2, :]
            total = taps[0] * padded[0:16, :]
            for k in range(1, 5):
                total = total + taps[k] * padded[k : k + 16, :]
            out_ref[c, 16 * a : 16 * a + 16, :] = total
        left, right = out_ref[c, :, 0:LANES], out_ref[c, :, LANES:]
        if c:
            left = pltpu.roll(left, 2 * c, 1)
        right = pltpu.roll(right, 10 + 2 * c, 1)
        edges = jnp.where((lane >> 1) == c, left, edges)
        edges = jnp.where((lane >> 1) == 4 + c, right, edges)
    turned = edges.T
    one_ref[...], other_ref[...] = by_partner("az", turned[0:8], turned[8:16])


def inner_azimuthal_kernel(taps, cells_ref, out_ref):
    lane = lax.broadcasted_iota(jnp.int32, (LANES, LANES), 1)
    for c in range(3):
        left, right = cells_ref[c, :, 0:LANES], cells_ref[c, :, LANES:]
        out_left, out_right = taps[2] * left, taps[2] * right
        for k in (1, 2):
            tap = taps[2 + k]
            inner = lane < LANES - k
            x, y = (pltpu.roll(v, LANES - k, 1) for v in (left, right))
            out_left = out_left + tap * jnp.where(inner, x, y)
            out_right = out_right + tap * jnp.where(inner, y, 0.0)
            inner = lane >= k
            x, y = (pltpu.roll(v, k, 1) for v in (left, right))
            out_left = out_left + tap * jnp.where(inner, x, 0.0)
            out_right = out_right + tap * jnp.where(inner, y, x)
        out_ref[c, :, 0:LANES] = out_left
        out_ref[c, :, LANES:] = out_right


def azimuthal_kernel(taps, inner_ref, one_in, other_in, out_ref):
    lane = lax.broadcasted_iota(jnp.int32, (LANES, LANES), 1)
    rest = jnp.zeros((LANES - 16, LANES), jnp.float32)
    before, after = from_partners("az", one_in[...], other_in[...], True)
    edges = jnp.concatenate([after, before, rest], axis=0).T
    for c in range(3):
        out_left, out_right = inner_ref[c, :, 0:LANES], inner_ref[c, :, LANES:]
        for k in (1, 2):
            x = pltpu.roll(edges, (118 - 2 * c + k) % LANES, 1)
            out_left = out_left + taps[2 - k] * jnp.where(lane < k, x, 0.0)
            y = pltpu.roll(edges, LANES - 2 * c - k, 1)
            out_right = out_right + taps[2 + k] * jnp.where(lane >= LANES - k, y, 0.0)
        out_ref[c, :, 0:LANES] = out_left
        out_ref[c, :, LANES:] = out_right


def filtered(deposit, one, other):
    f32 = jnp.float32
    raw = [math.exp(-0.5 * k * k) for k in range(-2, 3)]
    taps = [x / sum(raw) for x in raw]
    whole = jax.ShapeDtypeStruct(deposit.shape, f32)
    radial_face = jax.ShapeDtypeStruct((3, 16, 2 * LANES), f32)
    edge = jax.ShapeDtypeStruct((8, LANES), f32)
    cells, one, other = pl.pallas_call(
        functools.partial(axial_kernel, taps),
        name="axial_filter",
        out_shape=(whole, radial_face, radial_face),
        scratch_shapes=[VMEM((16, 2 * LANES), f32)] * 2,
        compiler_params=params(),
    )(deposit, *swapped(one, other, "ax"))
    cells, one, other = pl.pallas_call(
        functools.partial(radial_kernel, taps),
        name="radial_filter",
        out_shape=(whole, edge, edge),
        scratch_shapes=[VMEM((24, 2 * LANES), f32)] + [VMEM((16, 2 * LANES), f32)] * 2,
        compiler_params=params(),
    )(cells, *swapped(one, other, "rad"))
    one, other = swapped(one, other, "az", True)
    inner = pl.pallas_call(
        functools.partial(inner_azimuthal_kernel, taps),
        name="inner_azimuthal_filter",
        out_shape=whole,
        compiler_params=params(),
    )(cells)
    return pl.pallas_call(
        functools.partial(azimuthal_kernel, taps),
        name="azimuthal_filter",
        out_shape=whole,
        compiler_params=params(),
    )(inner, one, other)


def swapped(one, other, axis, wrap=False):
    count = lax.axis_size(axis)

    def partner(i, odd):
        j = i + 1 if i % 2 == odd else i - 1
        return j % count if wrap or 0 <= j < count else i

    return [
        lax.ppermute(x, axis, [(i, partner(i, odd)) for i in range(count)])
        for odd, x in enumerate((one, other))
    ]


def per_device(positions, velocity, diameter, cell_index, pair_list, live_pairs, gas_velocity):
    live = live_pairs.reshape(1, 1)
    cells = cell_index.reshape(128, LANES)
    gas = gas_velocity.reshape(3, 128, 2 * LANES)
    pos = positions.reshape(3, 128, LANES)
    vel = velocity.reshape(3, 128, LANES)
    diam = diameter.reshape(128, LANES)
    cell_keys, cell_ends, table, one, other = droplet_states(
        cells, gas, pos, vel, diam
    )
    one, other = swapped(one, other, "az", True)
    pairs = pair_list.reshape(2, 256, LANES)
    pair_keys, pair_ends, words, largest = pair_sort(live, pairs, table)
    heads, one, other = near_pairs(pair_ends, pair_keys, words, largest, one, other)
    one, other = swapped(one, other, "az", True)
    corr = own_pairs(live, pair_ends, pair_keys, words, largest, heads)
    deposit, correction, one, other = deposits(cell_ends, cell_keys, table, corr, one, other)
    smoothed = filtered(deposit, one, other)
    return (correction.reshape(positions.shape), smoothed.reshape(gas_velocity.shape))


def solution(mesh):
    return jax.shard_map(
        per_device,
        mesh=mesh,
        in_specs=(
            P(None, "ax", "rad", "az"),
            P(None, "ax", "rad", "az"),
            P("ax", "rad", "az"),
            P("ax", "rad", "az"),
            P(None, "ax", "rad", "az"),
            P("ax", "rad", "az"),
            P(None, "ax", "rad", "az"),
        ),
        out_specs=(P(None, "ax", "rad", "az"), P(None, "ax", "rad", "az")),
        check_vma=False,
    )
```
